32 devices in a mesh: dp: 16 (over z, y, core), mp: 2 (over x).
Axes of the slice: x: 2, y: 2, z: 4, core: 2. Of those that a mesh axis runs over, the one named last changes fastest.
Arguments:
- layer_input: bfloat16 [32, 64, 1024], P('dp', None, 'mp'), may hold values from -6 to 6
- labels: int32 [32], P('dp'), may hold values from 0 to 999
- text_ids: int32 [32, 64], P('dp'), may hold values from 0 to 999
- noise_seeds: int32 [32], P('dp'), may hold values from 0 to 999999
- penalty_mask: int32 [32], P('dp'), may hold values from 0 to 1, as said below
- class_table: bfloat16 [1000, 512], replicated, may hold values from -6 to 6
- token_table: bfloat16 [1000, 768], replicated, may hold values from -6 to 6
- sel_weight: bfloat16 [512, 8], replicated, may hold values from -0.25 to 0.25
- mod_weight: bfloat16 [512, 1024], replicated, may hold values from -0.09375 to 0.09375
- rgb_mod: bfloat16 [512, 1024], replicated, may hold values from -0.09375 to 0.09375
- rgb_weight: bfloat16 [3, 1024], replicated, may hold values from -0.1875 to 0.1875
- conv_bias: bfloat16 [1024], replicated, may hold values from -3 to 3
- noise_strength: bfloat16 [1024], replicated, may hold values from -4 to 4
- kernel_bank: bfloat16 [8, 9, 1024, 1024], P(None, None, 'dp', 'mp'), may hold values from -0.0625 to 0.0625
- qk_weight: bfloat16 [1024, 1024], P('dp', 'mp'), may hold values from -0.0625 to 0.0625
- value_weight: bfloat16 [1024, 1024], P('dp', 'mp'), may hold values from -0.1875 to 0.1875
- attn_out: bfloat16 [1024, 1024], P('mp', 'dp'), may hold values from -1.5 to 1.5
- cross_query: bfloat16 [1024, 1024], P('dp', 'mp'), may hold values from -0.1875 to 0.1875
- cross_key: bfloat16 [768, 1024], P('dp', 'mp'), may hold values from -0.21875 to 0.21875
- cross_value: bfloat16 [768, 1024], P('dp', 'mp'), may hold values from -0.21875 to 0.21875
- cross_out: bfloat16 [1024, 1024], P('mp', 'dp'), may hold values from -1 to 1
- mlp_in: bfloat16 [1024, 4096], P('dp', 'mp'), may hold values from -0.1875 to 0.1875
- mlp_out: bfloat16 [4096, 1024], P('mp', 'dp'), may hold values from -0.09375 to 0.09375
- cot_feat: bfloat16 [32, 256, 1024], P('dp', None, 'mp'), may hold values from -6 to 6
- cot_rgb: bfloat16 [32, 3, 256], P('dp'), may hold values from -6 to 6
- penalty_dir: bfloat16 [32, 3, 256], P('dp'), may hold values from -6 to 6
Outputs:
- layer_output: float32 [32, 256, 1024], P('dp', None, 'mp')
- rgb_output: float32 [32, 3, 256], P('dp')
- input_grad: float32 [32, 64, 1024], P('dp', None, 'mp')
- class_table_grad: float32 [1000, 512], replicated
- token_table_grad: float32 [1000, 768], replicated
- sel_weight_grad: float32 [512, 8], replicated
- mod_weight_grad: float32 [512, 1024], replicated
- rgb_mod_grad: float32 [512, 1024], replicated
- rgb_weight_grad: float32 [3, 1024], replicated
- conv_bias_grad: float32 [1024], replicated
- noise_strength_grad: float32 [1024], replicated
- kernel_bank_grad: float32 [8, 9, 1024, 1024], P(None, None, 'dp', 'mp')
- qk_weight_grad: float32 [1024, 1024], P('dp', 'mp')
- value_weight_grad: float32 [1024, 1024], P('dp', 'mp')
- attn_out_grad: float32 [1024, 1024], P('mp', 'dp')
- cross_query_grad: float32 [1024, 1024], P('dp', 'mp')
- cross_key_grad: float32 [768, 1024], P('dp', 'mp')
- cross_value_grad: float32 [768, 1024], P('dp', 'mp')
- cross_out_grad: float32 [1024, 1024], P('mp', 'dp')
- mlp_in_grad: float32 [1024, 4096], P('dp', 'mp')
- mlp_out_grad: float32 [4096, 1024], P('mp', 'dp')
The draws below stay inside these ranges and needn't reach their ends.
Inputs may be any that keep to these rules, and one draw needn't show every extreme that they name: `penalty_mask`: 1 marks a sample whose input-gradient penalty counts, 0 one whose does not.
All inputs are finite; a program needn't handle non-finite values.
Results may differ from the reference program's by a relative error of at most 0.025.
Values may be sent and summed in bfloat16 or wider, within the bound.
A program may use at most 512 MiB of HBM per device.

```python
import jax
import jax.numpy as jnp
from jax import lax

C = 1024
HEAD = 64
NK = 8
S = 512
FF = 4096
DT = 768
NCLASS = 1000
NWORD = 1000
TT = 64
SIDE = 16
SAMP_DEV = 2
SAMPLES = 32


def draw_penalty_mask(key, part):
    key = jax.random.fold_in(key, 7)
    drawn_ranks = jax.random.randint(key, (SAMPLES,), 0, SAMPLES)
    return (drawn_ranks <= jnp.arange(SAMPLES, dtype=jnp.int32)).astype(jnp.int32)


def set_ends(result, own_key, least, high):
    shape = result.shape
    index_at = [jax.random.randint(jax.random.fold_in(own_key, axis), (), 0, shape[axis]) for axis in range(len(shape))]
    result = result.at[tuple(index_at)].set(least)
    longest = shape.index(max(shape))
    index_at[longest] = (index_at[longest] + 1) % shape[longest]
    return result.at[tuple(index_at)].set(high)


def shard_levels(key, shape, cuts, smallest, top_value):
    factor_of = 1.0
    for dim, shards_of in cuts:
        steps = jax.random.uniform(jax.random.fold_in(jax.random.fold_in(key, 6), dim), (shards_of,), jnp.float32, smallest / len(cuts), top_value / len(cuts))
        factor_of = factor_of * jnp.repeat(jnp.exp(steps), shape[dim] // shards_of).reshape((-1,) + (1,) * (len(shape) - 1 - dim))
    return factor_of


def normal_values(key, dims, spread, most, cuts=(), kind=jnp.bfloat16):
    drawn = jax.random.normal(key, dims, jnp.float32) * spread
    if len(cuts) > 0:
        drawn = shard_levels(key, dims, cuts, -0.22, 0.18) * drawn
    return jnp.clip(drawn, min=-most, max=most).astype(kind)


def setup_inputs(seed: int = 0) -> dict:
    keys = jax.random.split(jax.random.key(seed), 27)
    layer_input = normal_values(keys[0], (SAMPLES, SIDE * SIDE // 4, C), 1.0, 6.0, ((0, 16), (2, 2)))
    labels = set_ends(jax.random.randint(keys[1], (SAMPLES,), 0, NCLASS), jax.random.fold_in(keys[1], 1), 0, NCLASS - 1).astype(jnp.int32)
    text_ids = set_ends(jax.random.randint(keys[2], (SAMPLES, TT), 0, NWORD), jax.random.fold_in(keys[2], 1), 0, NWORD - 1).astype(jnp.int32)
    noise_seeds = set_ends(jax.random.randint(keys[3], (SAMPLES,), 0, 1000000), jax.random.fold_in(keys[3], 1), 0, 999999).astype(jnp.int32)
    penalty_mask = draw_penalty_mask(jax.random.fold_in(keys[26], 71), 0)
    class_table = normal_values(keys[5], (NCLASS, S), 1.0, 6.0)
    token_table = normal_values(keys[6], (NWORD, DT), 1.0, 6.0)
    sel_weight = normal_values(keys[7], (S, NK), S ** -0.5, 0.25)
    mod_weight = normal_values(keys[8], (S, C), (9 * S) ** -0.5, 0.09375)
    rgb_mod = normal_values(keys[9], (S, C), (9 * S) ** -0.5, 0.09375)
    rgb_weight = normal_values(keys[10], (3, C), C ** -0.5, 0.1875)
    conv_bias = normal_values(keys[11], (C,), 0.5, 3.0)
    noise_strength = normal_values(keys[12], (C,), 1.0, 4.0)
    kernel_bank = normal_values(keys[13], (NK, 9, C, C), (9 * C) ** -0.5, 0.0625, ((2, 16), (3, 2)))
    qk_weight = normal_values(keys[14], (C, C), (8 * C) ** -0.5, 0.0625, ((0, 16), (1, 2)))
    value_weight = normal_values(keys[15], (C, C), C ** -0.5, 0.1875, ((0, 16), (1, 2)))
    attn_out = normal_values(keys[16], (C, C), (C // 64) ** -0.5, 1.5, ((0, 2), (1, 16)))
    cross_query = normal_values(keys[17], (C, C), C ** -0.5, 0.1875, ((0, 16), (1, 2)))
    cross_key = normal_values(keys[18], (DT, C), DT ** -0.5, 0.21875, ((0, 16), (1, 2)))
    cross_value = normal_values(keys[19], (DT, C), DT ** -0.5, 0.21875, ((0, 16), (1, 2)))
    cross_out = normal_values(keys[20], (C, C), (C // 32) ** -0.5, 1.0, ((0, 2), (1, 16)))
    mlp_in = normal_values(keys[21], (C, FF), C ** -0.5, 0.1875, ((0, 16), (1, 2)))
    mlp_out = normal_values(keys[22], (FF, C), FF ** -0.5, 0.09375, ((0, 2), (1, 16)))
    cot_feat = normal_values(keys[23], (SAMPLES, SIDE * SIDE, C), 1.0, 6.0, ((0, 16), (2, 2)))
    cot_rgb = normal_values(keys[24], (SAMPLES, 3, SIDE * SIDE), 1.0, 6.0, ((0, 16),))
    penalty_dir = normal_values(keys[25], (SAMPLES, 3, SIDE * SIDE), 1.0, 6.0, ((0, 16),))
    return dict(layer_input=layer_input, labels=labels, text_ids=text_ids, noise_seeds=noise_seeds, penalty_mask=penalty_mask, class_table=class_table, token_table=token_table, sel_weight=sel_weight, mod_weight=mod_weight, rgb_mod=rgb_mod, rgb_weight=rgb_weight, conv_bias=conv_bias, noise_strength=noise_strength, kernel_bank=kernel_bank, qk_weight=qk_weight, value_weight=value_weight, attn_out=attn_out, cross_query=cross_query, cross_key=cross_key, cross_value=cross_value, cross_out=cross_out, mlp_in=mlp_in, mlp_out=mlp_out, cot_feat=cot_feat, cot_rgb=cot_rgb, penalty_dir=penalty_dir)


penalty_weight = 1.0

@jax.custom_vjp
def low(v):
    return lax.optimization_barrier(v.astype(jnp.bfloat16)).astype(jnp.float32)

@jax.custom_vjp
def low_back(v):
    return v

def low_keep(v):
    return (low(v), None)

def low_pass(kept, grad):
    return (grad,)

def back_keep(v):
    return (v, None)

def back_low(kept, grad):
    return (low(grad),)
low.defvjp(low_keep, low_pass)
low_back.defvjp(back_keep, back_low)

def round_both(values):
    return low(low_back(values))

def matmul_high(left, right):
    return jnp.matmul(left, right, precision=lax.Precision.HIGHEST)

def einsum_high(form, *operands):
    return jnp.einsum(form, *operands, precision=lax.Precision.HIGHEST)

def noise_field(seed_ids, pixel_count):
    pixel_ids = jnp.arange(pixel_count, dtype=jnp.int32)
    mixed = seed_ids.astype(jnp.int32)[:, None] * 1103515245 + pixel_ids[None, :] * 40503
    mixed = jnp.bitwise_xor(mixed, jnp.right_shift(mixed, 13)) * 1664525 + 1013904223
    levels = jnp.bitwise_and(jnp.right_shift(mixed, 8), 65535)
    return levels.astype(jnp.float32) / 65536.0 - 0.5

def patches_of(flat_rows, side_len):
    samples_here, pixels, width_here = flat_rows.shape
    half_side = side_len // 2
    picture = flat_rows.reshape(samples_here, half_side, half_side, width_here)
    picture = jnp.repeat(jnp.repeat(picture, 2, axis=1), 2, axis=2)
    padded = jnp.pad(picture, ((0, 0), (1, 1), (1, 1), (0, 0)))
    pieces = [padded[:, shift_row:shift_row + side_len, shift_col:shift_col + side_len, :] for shift_row in range(3) for shift_col in range(3)]
    return jnp.concatenate(pieces, axis=-1).reshape(samples_here, side_len * side_len, 9 * width_here)

def rms_norm(values):
    return values * lax.rsqrt(lax.optimization_barrier(jnp.mean(values * values, axis=-1, keepdims=True)) + 1e-06)

def conv_part(gathered, select, scales, bias_local, strength_local, noise_map, bank_full):
    samples_here = gathered.shape[0]
    width_out = bank_full.shape[3]
    columns = patches_of(gathered, SIDE)
    kernel = round_both(matmul_high(select, bank_full.reshape(bank_full.shape[0], -1)))
    kernel = kernel.reshape(samples_here, -1, width_out)
    conv_out = einsum_high('bpr,bro->bpo', columns, kernel)
    squares = lax.optimization_barrier(jnp.sum((kernel * kernel).reshape(samples_here, 9, -1, width_out), axis=1))
    demodulate = lax.rsqrt(einsum_high('bi,bio->bo', scales * scales, squares) + 1e-08)
    before = conv_out * demodulate[:, None, :] + bias_local + noise_map[:, :, None] * strength_local
    return jax.nn.silu(before)

def self_attention(active, qk_w, value_w, out_w):
    normed = round_both(rms_norm(active))
    queries = round_both(matmul_high(normed, qk_w))
    values = round_both(matmul_high(normed, value_w))
    samples_here, pixels, width_here = queries.shape
    heads_here = width_here // HEAD
    q_heads = queries.reshape(samples_here, pixels, heads_here, HEAD)
    v_heads = values.reshape(samples_here, pixels, heads_here, HEAD)
    lengths = jnp.transpose(lax.optimization_barrier(jnp.sum(q_heads * q_heads, axis=-1)), (0, 2, 1))
    scores = (2.0 * einsum_high('bphd,bqhd->bhpq', q_heads, q_heads) - lengths[:, :, None, :]) * HEAD ** (-0.5)
    soft_weights = round_both(jax.nn.softmax(scores, axis=-1))
    mixture = round_both(einsum_high('bhpq,bqhd->bphd', soft_weights, v_heads).reshape(samples_here, pixels, width_here))
    return matmul_high(mixture, out_w)

def cross_attention(active, text_rows, query_w, key_w, value_w, out_w):
    normed = round_both(rms_norm(active))
    queries = round_both(matmul_high(normed, query_w))
    key_rows = round_both(matmul_high(text_rows, key_w))
    values = round_both(matmul_high(text_rows, value_w))
    samples_here, pixels, width_here = queries.shape
    tokens = key_rows.shape[1]
    heads_here = width_here // HEAD
    q_heads = queries.reshape(samples_here, pixels, heads_here, HEAD)
    k_heads = key_rows.reshape(samples_here, tokens, heads_here, HEAD)
    v_heads = values.reshape(samples_here, tokens, heads_here, HEAD)
    scores = einsum_high('bphd,bthd->bhpt', q_heads, k_heads) * HEAD ** (-0.5)
    soft_weights = round_both(jax.nn.softmax(scores, axis=-1))
    mixture = round_both(einsum_high('bhpt,bthd->bphd', soft_weights, v_heads).reshape(samples_here, pixels, width_here))
    return matmul_high(mixture, out_w)

def feed_forward(active, weight_in, weight_out):
    normed = round_both(rms_norm(active))
    inner = round_both(jax.nn.gelu(matmul_high(normed, weight_in)))
    return matmul_high(inner, weight_out)

def layer(params, inputs, labels, text_ids, noise_seeds):
    class_table, token_table, sel_weight, mod_weight, rgb_mod, rgb_weight, conv_bias, noise_strength, kernel_bank, qk_weight, value_weight, attn_out, cross_query, cross_key, cross_value, cross_out, mlp_in, mlp_out = params
    latent = class_table[labels]
    text_rows = token_table[text_ids]
    select = jax.nn.softmax(matmul_high(latent, sel_weight), axis=-1)
    scales = 1.0 + matmul_high(latent, mod_weight)
    rgb_scales = 1.0 + matmul_high(latent, rgb_mod)
    moduled = round_both(inputs * scales[:, None, :])
    noise_map = noise_field(noise_seeds, SIDE * SIDE)
    hidden_one = conv_part(moduled, select, scales, conv_bias, noise_strength, noise_map, kernel_bank)
    hidden_two = hidden_one + low_back(self_attention(round_both(hidden_one), qk_weight, value_weight, attn_out))
    hidden_three = hidden_two + low_back(cross_attention(round_both(hidden_two), text_rows, cross_query, cross_key, cross_value, cross_out))
    hidden_four = hidden_three + low_back(feed_forward(round_both(hidden_three), mlp_in, mlp_out))
    picture = einsum_high('bpc,bc,kc->bkp', hidden_four, rgb_scales, rgb_weight)
    return (hidden_four, picture)

def reference(layer_input, labels, text_ids, noise_seeds, penalty_mask, class_table, token_table, sel_weight, mod_weight, rgb_mod, rgb_weight, conv_bias, noise_strength, kernel_bank, qk_weight, value_weight, attn_out, cross_query, cross_key, cross_value, cross_out, mlp_in, mlp_out, cot_feat, cot_rgb, penalty_dir):
    params = tuple((entry.astype(jnp.float32) for entry in (class_table, token_table, sel_weight, mod_weight, rgb_mod, rgb_weight, conv_bias, noise_strength, kernel_bank, qk_weight, value_weight, attn_out, cross_query, cross_key, cross_value, cross_out, mlp_in, mlp_out)))
    groups = SAMPLES // SAMP_DEV

    def grouped(array):
        return array.reshape((groups, SAMP_DEV) + array.shape[1:])
    stacked = (grouped(layer_input.astype(jnp.float32)), grouped(labels), grouped(text_ids), grouped(noise_seeds), grouped(penalty_mask), grouped(cot_feat.astype(jnp.float32)), grouped(cot_rgb.astype(jnp.float32)), grouped(penalty_dir.astype(jnp.float32)))

    def one_group(totals, group_item):
        inputs, label_group, word_group, seed_group, mask_group, feat_cot, picture_cot, direction = group_item

        def objective(param_set, values):

            def forward(inner_x):
                return layer(param_set, inner_x, label_group, word_group, seed_group)
            (feature, picture), pullback = jax.vjp(forward, values)
            grad_in = pullback((jnp.zeros_like(feature), direction))[0]
            penalty = 0.5 * penalty_weight * jnp.sum(mask_group.astype(jnp.float32)[:, None, None] * grad_in * grad_in)
            return (jnp.sum(feat_cot * feature) + jnp.sum(picture_cot * picture) + penalty, (feature, picture))
        (grad_params, grad_inputs), (feature, picture) = jax.grad(objective, argnums=(0, 1), has_aux=True)(params, inputs)
        totals = jax.tree.map(jnp.add, totals, grad_params)
        return (totals, (feature, picture, grad_inputs))
    zero_grads = jax.tree.map(jnp.zeros_like, params)
    grad_sums, (feature, picture, grad_inputs) = lax.scan(one_group, zero_grads, stacked)
    return (feature.reshape(SAMPLES, SIDE * SIDE, C), picture.reshape(SAMPLES, 3, SIDE * SIDE), grad_inputs.reshape(SAMPLES, SIDE * SIDE // 4, C), grad_sums[0], grad_sums[1], grad_sums[2], grad_sums[3], grad_sums[4], grad_sums[5], grad_sums[6], grad_sums[7], grad_sums[8], grad_sums[9], grad_sums[10], grad_sums[11], grad_sums[12], grad_sums[13], grad_sums[14], grad_sums[15], grad_sums[16], grad_sums[17])
```

```python
import jax
import jax.numpy as jnp
from jax import lax
from jax.sharding import PartitionSpec as P

HEAD = 64
SIDE = 16


penalty_weight = 1.0


def rounded(values):
    return lax.optimization_barrier(values.astype(jnp.bfloat16)).astype(jnp.float32)


def matmul_high(left, right):
    return jnp.matmul(left, right, precision=lax.Precision.HIGHEST)


def einsum_high(form, *operands):
    return jnp.einsum(form, *operands, precision=lax.Precision.HIGHEST)


def einsum_low(form, left, right):
    return jnp.einsum(
        form,
        left.astype(jnp.bfloat16),
        right.astype(jnp.bfloat16),
        preferred_element_type=jnp.float32,
    )


def noise_field(seed_ids, pixel_count):
    pixel_ids = jnp.arange(pixel_count, dtype=jnp.int32)
    mixed = seed_ids[:, None] * 1103515245 + pixel_ids[None, :] * 40503
    mixed = jnp.bitwise_xor(mixed, jnp.right_shift(mixed, 13)) * 1664525 + 1013904223
    levels = jnp.bitwise_and(jnp.right_shift(mixed, 8), 65535)
    return levels.astype(jnp.float32) / 65536.0 - 0.5


def patches_of(flat_rows, side_len):
    samples_here, pixels, width_here = flat_rows.shape
    half_side = side_len // 2
    picture = flat_rows.reshape(samples_here, half_side, half_side, width_here)
    picture = jnp.repeat(jnp.repeat(picture, 2, axis=1), 2, axis=2)
    padded = jnp.pad(picture, ((0, 0), (1, 1), (1, 1), (0, 0)))
    pieces = [
        padded[:, shift_row : shift_row + side_len, shift_col : shift_col + side_len, :]
        for shift_row in range(3)
        for shift_col in range(3)
    ]
    return jnp.concatenate(pieces, axis=-1).reshape(
        samples_here, side_len * side_len, 9 * width_here
    )


def rms_norm(values):
    return values * lax.rsqrt(jnp.mean(values * values, axis=-1, keepdims=True) + 1e-06)


def conv_part(gathered, kernel, scales, bias_local, strength_local, noise_map):
    samples_here = gathered.shape[0]
    width_out = kernel.shape[2]
    columns = patches_of(gathered, SIDE)
    conv_out = einsum_low("bpr,bro->bpo", columns, kernel)
    squares = jnp.sum((kernel * kernel).reshape(samples_here, 9, -1, width_out), axis=1)
    demodulate = lax.rsqrt(einsum_high("bi,bio->bo", scales * scales, squares) + 1e-08)
    before = conv_out * demodulate[:, None, :] + bias_local + noise_map[:, :, None] * strength_local
    return jax.nn.silu(before)


def self_attention(active, qk_w, value_w, out_w):
    normed = rounded(rms_norm(active))
    queries = rounded(matmul_high(normed, qk_w))
    values = rounded(matmul_high(normed, value_w))
    samples_here, pixels, width_here = queries.shape
    heads_here = width_here // HEAD
    q_heads = queries.reshape(samples_here, pixels, heads_here, HEAD)
    v_heads = values.reshape(samples_here, pixels, heads_here, HEAD)
    lengths = jnp.transpose(jnp.sum(q_heads * q_heads, axis=-1), (0, 2, 1))
    scores = (
        2.0 * einsum_low("bphd,bqhd->bhpq", q_heads, q_heads) - lengths[:, :, None, :]
    ) * HEAD ** (-0.5)
    soft_weights = rounded(jax.nn.softmax(scores, axis=-1))
    mixture = rounded(
        einsum_low("bhpq,bqhd->bphd", soft_weights, v_heads).reshape(
            samples_here, pixels, width_here
        )
    )
    return matmul_high(mixture, out_w)


def cross_attention(active, text_rows, query_w, key_w, value_w, out_w):
    normed = rounded(rms_norm(active))
    queries = rounded(matmul_high(normed, query_w))
    key_rows = rounded(matmul_high(text_rows, key_w))
    values = rounded(matmul_high(text_rows, value_w))
    samples_here, pixels, width_here = queries.shape
    tokens = key_rows.shape[1]
    heads_here = width_here // HEAD
    q_heads = queries.reshape(samples_here, pixels, heads_here, HEAD)
    k_heads = key_rows.reshape(samples_here, tokens, heads_here, HEAD)
    v_heads = values.reshape(samples_here, tokens, heads_here, HEAD)
    scores = einsum_low("bphd,bthd->bhpt", q_heads, k_heads) * HEAD ** (-0.5)
    soft_weights = rounded(jax.nn.softmax(scores, axis=-1))
    mixture = rounded(
        einsum_low("bhpt,bthd->bphd", soft_weights, v_heads).reshape(
            samples_here, pixels, width_here
        )
    )
    return matmul_high(mixture, out_w)


def feed_forward(active, weight_in, weight_out):
    normed = rounded(rms_norm(active))
    inner = rounded(jax.nn.gelu(matmul_high(normed, weight_in)))
    return matmul_high(inner, weight_out)


def tree_add(first, second):
    return jax.tree.map(jnp.add, first, second)


def tensor_parallel(
    layer_input,
    labels,
    text_ids,
    noise_seeds,
    penalty_mask,
    class_table,
    token_table,
    sel_weight,
    mod_weight,
    rgb_mod,
    rgb_weight,
    conv_bias,
    noise_strength,
    kernel_bank,
    qk_weight,
    value_weight,
    attn_out,
    cross_query,
    cross_key,
    cross_value,
    cross_out,
    mlp_in,
    mlp_out,
    cot_feat,
    cot_rgb,
    penalty_dir,
):
    width_local = layer_input.shape[2]
    offset = lax.axis_index("mp") * width_local
    small_params = tuple(
        (
            entry.astype(jnp.float32)
            for entry in (
                class_table,
                token_table,
                sel_weight,
                mod_weight,
                rgb_mod,
                rgb_weight,
                conv_bias,
                noise_strength,
            )
        )
    )

    def fetch_proj():
        fetched = (
            lax.all_gather(qk_weight, "dp", axis=0, tiled=True),
            lax.all_gather(value_weight, "dp", axis=0, tiled=True),
            lax.all_gather(attn_out, "dp", axis=1, tiled=True),
            lax.all_gather(cross_query, "dp", axis=0, tiled=True),
            lax.all_gather(cross_key, "dp", axis=0, tiled=True),
            lax.all_gather(cross_value, "dp", axis=0, tiled=True),
            lax.all_gather(cross_out, "dp", axis=1, tiled=True),
            lax.all_gather(mlp_in, "dp", axis=0, tiled=True),
            lax.all_gather(mlp_out, "dp", axis=1, tiled=True),
        )
        return tuple((entry.astype(jnp.float32) for entry in fetched))

    def style_part(param_set):
        table_class, table_word, select_w, modul_w, rgbmod_w, rgbout_w, bias_w, strength_w = (
            param_set
        )
        onehot_class = (
            labels[:, None] == jnp.arange(table_class.shape[0], dtype=jnp.int32)[None, :]
        ).astype(jnp.float32)
        latent = matmul_high(onehot_class, table_class)
        onehot_word = (
            text_ids[:, :, None] == jnp.arange(table_word.shape[0], dtype=jnp.int32)
        ).astype(jnp.float32)
        text_rows = matmul_high(onehot_word, table_word)
        select = jax.nn.softmax(matmul_high(latent, select_w), axis=-1)
        scales = 1.0 + matmul_high(latent, modul_w)
        rgb_scales = 1.0 + matmul_high(
            latent, lax.dynamic_slice_in_dim(rgbmod_w, offset, width_local, 1)
        )
        bias_local = lax.dynamic_slice_in_dim(bias_w, offset, width_local, 0)
        strength_local = lax.dynamic_slice_in_dim(strength_w, offset, width_local, 0)
        colour_local = lax.dynamic_slice_in_dim(rgbout_w, offset, width_local, 1)
        return (select, scales, rgb_scales, text_rows, bias_local, strength_local, colour_local)

    styles, style_pull = jax.vjp(style_part, small_params)
    noise_map = noise_field(noise_seeds, SIDE * SIDE)

    def owned_sets():
        proj_set = fetch_proj()
        conv_set = (lax.all_gather(kernel_bank, "dp", axis=2, tiled=True).astype(jnp.float32),)
        return ((), conv_set, proj_set[0:3], proj_set[3:7], proj_set[7:9], ())

    def seg_in(active, styles_in, own_set):
        return active * lax.dynamic_slice_in_dim(styles_in[1], offset, width_local, 1)[:, None, :]

    def seg_conv(active, styles_in, own_set):
        bank_full = own_set[0]
        kernel = rounded(matmul_high(styles_in[0], bank_full.reshape(bank_full.shape[0], -1)))
        kernel = kernel.reshape(active.shape[0], -1, bank_full.shape[3])
        return conv_part(active, kernel, styles_in[1], styles_in[4], styles_in[5], noise_map)

    def seg_self(active, styles_in, own_set):
        return self_attention(active, own_set[0], own_set[1], own_set[2])

    def seg_cross(active, styles_in, own_set):
        return cross_attention(active, styles_in[3], own_set[0], own_set[1], own_set[2], own_set[3])

    def seg_mlp(active, styles_in, own_set):
        return feed_forward(active, own_set[0], own_set[1])

    def seg_rgb(active, styles_in, own_set):
        return einsum_high("bpc,bc,kc->bkp", active, styles_in[2], styles_in[6])

    def spread(stacked):
        return lax.all_gather(stacked, "mp", axis=3, tiled=True)

    def collect(stacked):
        return lax.psum_scatter(
            stacked.astype(jnp.bfloat16), "mp", scatter_dimension=3, tiled=True
        ).astype(jnp.float32)

    def spread_one(values):
        return spread(values.astype(jnp.bfloat16)[None])[0].astype(jnp.float32)

    def collect_one(values):
        return collect(values[None])[0]

    own_first = owned_sets()
    input_full = layer_input.astype(jnp.float32)
    gathered_x = spread_one(seg_in(input_full, styles, own_first[0]))
    hidden_one = seg_conv(gathered_x, styles, own_first[1])
    gathered_one = spread_one(hidden_one)
    hidden_two = hidden_one + collect_one(seg_self(gathered_one, styles, own_first[2]))
    gathered_two = spread_one(hidden_two)
    hidden_three = hidden_two + collect_one(seg_cross(gathered_two, styles, own_first[3]))
    gathered_three = spread_one(hidden_three)
    hidden_four = hidden_three + collect_one(seg_mlp(gathered_three, styles, own_first[4]))
    picture = lax.psum(seg_rgb(hidden_four, styles, own_first[5]), "mp")
    own_second = owned_sets()

    def pull_act(segment, active, own_set, cotan):
        return jax.vjp(lambda inner_x: segment(inner_x, styles, own_set), active)[1](cotan)[0]

    grad_four = pull_act(seg_rgb, hidden_four, own_second[5], penalty_dir.astype(jnp.float32))
    back_three = pull_act(seg_mlp, gathered_three, own_second[4], spread_one(grad_four))
    grad_three = grad_four + rounded(collect_one(back_three))
    back_two = pull_act(seg_cross, gathered_two, own_second[3], spread_one(grad_three))
    grad_two = grad_three + rounded(collect_one(back_two))
    back_one = pull_act(seg_self, gathered_one, own_second[2], spread_one(grad_two))
    grad_one = grad_two + rounded(collect_one(back_one))
    grad_moduled = rounded(collect_one(pull_act(seg_conv, gathered_x, own_second[1], grad_one)))
    penalty_grad = pull_act(seg_in, input_full, own_second[0], grad_moduled)
    tangent = penalty_weight * penalty_mask.astype(jnp.float32)[:, None, None] * penalty_grad
    own_third = owned_sets()

    def push(segment, active, own_set, tangent_in):
        return jax.jvp(lambda inner_x: segment(inner_x, styles, own_set), (active,), (tangent_in,))[
            1
        ]

    tan_x = spread_one(push(seg_in, input_full, own_third[0], tangent))
    tan_one = push(seg_conv, gathered_x, own_third[1], tan_x)
    tan_g1 = spread_one(tan_one)
    tan_two = tan_one + collect_one(push(seg_self, gathered_one, own_third[2], tan_g1))
    tan_g2 = spread_one(tan_two)
    tan_three = tan_two + collect_one(push(seg_cross, gathered_two, own_third[3], tan_g2))
    tan_g3 = spread_one(tan_three)
    tan_four = tan_three + collect_one(push(seg_mlp, gathered_three, own_third[4], tan_g3))
    own_fourth = owned_sets()

    def pull_both(segment, active, tangent_in, own_set, cotan, cotan_tangent):

        def joint(inner_x, inner_tangent, styles_in, own_in):
            return jax.jvp(
                lambda value_x: segment(value_x, styles_in, own_in), (inner_x,), (inner_tangent,)
            )

        return jax.vjp(joint, active, tangent_in, styles, own_set)[1]((cotan, cotan_tangent))

    grad_act, grad_tan, style_acc, ignored = pull_both(
        seg_rgb,
        hidden_four,
        tan_four,
        own_fourth[5],
        cot_rgb.astype(jnp.float32),
        penalty_dir.astype(jnp.float32),
    )
    main_now = cot_feat.astype(jnp.float32) + grad_act
    side_now = grad_tan
    layer_grads = []
    for segment, active, tangent_in, own_set in (
        (seg_mlp, gathered_three, tan_g3, own_fourth[4]),
        (seg_cross, gathered_two, tan_g2, own_fourth[3]),
        (seg_self, gathered_one, tan_g1, own_fourth[2]),
    ):
        both_wide = spread(jnp.stack([main_now, side_now]).astype(jnp.bfloat16)).astype(jnp.float32)
        grad_act, grad_tan, grad_sty, grad_own = pull_both(
            segment, active, tangent_in, own_set, both_wide[0], both_wide[1]
        )
        style_acc = tree_add(style_acc, grad_sty)
        layer_grads.append(grad_own)
        both_sums = collect(jnp.stack([grad_act, grad_tan]))
        main_now = main_now + rounded(both_sums[0])
        side_now = side_now + rounded(both_sums[1])
    grad_act, grad_tan, grad_sty, grads_conv = pull_both(
        seg_conv, gathered_x, tan_x, own_fourth[1], main_now, side_now
    )
    style_acc = tree_add(style_acc, grad_sty)
    both_sums = collect(jnp.stack([grad_act, grad_tan]))
    grad_act, grad_tan, grad_sty, ignored = pull_both(
        seg_in, input_full, tangent, own_fourth[0], rounded(both_sums[0]), rounded(both_sums[1])
    )
    style_acc = tree_add(style_acc, grad_sty)
    proj_terms = layer_grads[2] + layer_grads[1] + layer_grads[0]
    big_terms = grads_conv + proj_terms
    big_sums = (
        lax.psum_scatter(
            big_terms[0].astype(jnp.bfloat16), "dp", scatter_dimension=2, tiled=True
        ).astype(jnp.float32),
        lax.psum_scatter(
            big_terms[1].astype(jnp.bfloat16), "dp", scatter_dimension=0, tiled=True
        ).astype(jnp.float32),
        lax.psum_scatter(
            big_terms[2].astype(jnp.bfloat16), "dp", scatter_dimension=0, tiled=True
        ).astype(jnp.float32),
        lax.psum_scatter(
            big_terms[3].astype(jnp.bfloat16), "dp", scatter_dimension=1, tiled=True
        ).astype(jnp.float32),
        lax.psum_scatter(
            big_terms[4].astype(jnp.bfloat16), "dp", scatter_dimension=0, tiled=True
        ).astype(jnp.float32),
        lax.psum_scatter(
            big_terms[5].astype(jnp.bfloat16), "dp", scatter_dimension=0, tiled=True
        ).astype(jnp.float32),
        lax.psum_scatter(
            big_terms[6].astype(jnp.bfloat16), "dp", scatter_dimension=0, tiled=True
        ).astype(jnp.float32),
        lax.psum_scatter(
            big_terms[7].astype(jnp.bfloat16), "dp", scatter_dimension=1, tiled=True
        ).astype(jnp.float32),
        lax.psum_scatter(
            big_terms[8].astype(jnp.bfloat16), "dp", scatter_dimension=0, tiled=True
        ).astype(jnp.float32),
        lax.psum_scatter(
            big_terms[9].astype(jnp.bfloat16), "dp", scatter_dimension=1, tiled=True
        ).astype(jnp.float32),
    )
    small_terms = style_pull(style_acc)[0]
    small_sums = lax.psum(
        (
            small_terms[0],
            small_terms[1],
            small_terms[2],
            small_terms[3],
            small_terms[4],
            small_terms[5],
            small_terms[6],
            small_terms[7],
        ),
        ("dp", "mp"),
    )
    return (hidden_four, picture, grad_act) + tuple(small_sums) + tuple(big_sums)


def fits_samples(mesh):
    return mesh.shape["dp"] == 16 and mesh.shape["mp"] == 2


def dot_wide(left, right, left_dim, right_dim):
    return lax.dot_general(
        left.astype(jnp.bfloat16),
        right.astype(jnp.bfloat16),
        (((left_dim,), (right_dim,)), ((), ())),
        preferred_element_type=jnp.float32,
    )


def make_products(flip):
    depth = 1 if flip else 0

    def weight_grad(rows, cotan):
        if flip:
            return dot_wide(cotan, rows, 0, 0).astype(jnp.bfloat16)
        return dot_wide(rows, cotan, 0, 0).astype(jnp.bfloat16)

    @jax.custom_vjp
    def single(rows, weight):
        return dot_wide(rows, weight, 1, depth)

    def single_fwd(rows, weight):
        return single(rows, weight), (rows, weight)

    def single_bwd(kept, cotan):
        rows, weight = kept
        return dot_wide(cotan, weight, 1, 1 - depth), weight_grad(rows, cotan)

    single.defvjp(single_fwd, single_bwd)

    @jax.custom_vjp
    def pair(rows, tangents, weight):
        return dot_wide(rows, weight, 1, depth), dot_wide(tangents, weight, 1, depth)

    def pair_fwd(rows, tangents, weight):
        return pair(rows, tangents, weight), (rows, tangents, weight)

    def pair_bwd(kept, cotans):
        rows, tangents, weight = kept
        count = rows.shape[0]
        both = jnp.concatenate([entry.astype(jnp.bfloat16) for entry in cotans], axis=0)
        inputs = jnp.concatenate(
            [rows.astype(jnp.bfloat16), tangents.astype(jnp.bfloat16)], axis=0
        )
        back = dot_wide(both, weight, 1, 1 - depth)
        return back[:count], back[count:], weight_grad(inputs, both)

    pair.defvjp(pair_fwd, pair_bwd)
    return single, pair


product, product_pair = make_products(False)
product_flip, product_flip_pair = make_products(True)


def make_bilinear(left_ids, right_ids, out_ids):
    @jax.custom_vjp
    def form(left, right):
        return einsum_low(f"{left_ids},{right_ids}->{out_ids}", left, right)

    def form_fwd(left, right):
        return form(left, right), (left, right)

    def form_bwd(kept, cotan):
        left, right = kept
        return (
            einsum_low(f"{out_ids},{right_ids}->{left_ids}", cotan, right),
            einsum_low(f"{left_ids},{out_ids}->{right_ids}", left, cotan),
        )

    form.defvjp(form_fwd, form_bwd)
    return form


head_scores = make_bilinear("phd", "qhd", "hpq")
head_mix = make_bilinear("hpq", "qhd", "phd")


def heads_of(rows):
    return rows.reshape(rows.shape[0], -1, HEAD)


def with_tangent(fun, value, tangent):
    return jax.jvp(fun, (value,), (tangent,))


def self_scores(q_heads):
    short = q_heads.astype(jnp.bfloat16).astype(jnp.float32)
    return jnp.transpose(jnp.sum(short * short, axis=-1))


def last_softmax(scores):
    return jax.nn.softmax(scores, axis=-1)


def post_conv(conv_out, sums, bias, strength, noise):
    demodulate = lax.rsqrt(sums + 1e-08)
    return jax.nn.silu(conv_out * demodulate[None] + bias[None] + noise[:, None] * strength[None])


def picture_of(hidden, rgb_scales, rgb_weight):
    return einsum_high("pc,kc->kp", hidden, rgb_scales[None] * rgb_weight)


def layer_forward(conv_out, sums, text_rows, small, weights, noise):
    bias, strength, rgb_scales, rgb_weight = small
    qk_w, value_w, attn_w, query_w, key_w, cval_w, cout_w, mlp_w, mout_w = weights
    hidden_one = post_conv(conv_out, sums, bias, strength, noise)
    normed = rms_norm(hidden_one)
    queries = heads_of(product(normed, qk_w))
    values = heads_of(product(normed, value_w))
    scores = (2.0 * head_scores(queries, queries) - self_scores(queries)[:, None, :]) * HEAD ** (
        -0.5
    )
    mixture = head_mix(last_softmax(scores), values).reshape(normed.shape)
    hidden_two = hidden_one + product_flip(mixture, attn_w)
    normed = rms_norm(hidden_two)
    queries = heads_of(product(normed, query_w))
    key_rows = heads_of(product(text_rows, key_w))
    values = heads_of(product(text_rows, cval_w))
    scores = head_scores(queries, key_rows) * HEAD ** (-0.5)
    mixture = head_mix(last_softmax(scores), values).reshape(normed.shape)
    hidden_three = hidden_two + product_flip(mixture, cout_w)
    normed = rms_norm(hidden_three)
    inner = jax.nn.gelu(product(normed, mlp_w))
    hidden_four = hidden_three + product_flip(inner, mout_w)
    return hidden_four, picture_of(hidden_four, rgb_scales, rgb_weight)


def layer_joint(conv_out, conv_tan, sums, text_rows, small, weights, noise):
    bias, strength, rgb_scales, rgb_weight = small
    qk_w, value_w, attn_w, query_w, key_w, cval_w, cout_w, mlp_w, mout_w = weights
    hidden_one, tan_one = with_tangent(
        lambda value: post_conv(value, sums, bias, strength, noise), conv_out, conv_tan
    )
    normed, tan_normed = with_tangent(rms_norm, hidden_one, tan_one)
    queries, tan_queries = product_pair(normed, tan_normed, qk_w)
    queries, tan_queries = heads_of(queries), heads_of(tan_queries)
    values, tan_values = product_pair(normed, tan_normed, value_w)
    values, tan_values = heads_of(values), heads_of(tan_values)
    lengths, tan_lengths = with_tangent(self_scores, queries, tan_queries)
    scores = (2.0 * head_scores(queries, queries) - lengths[:, None, :]) * HEAD ** (-0.5)
    half = head_scores(tan_queries, queries)
    tan_scores = (2.0 * (half + jnp.swapaxes(half, 1, 2)) - tan_lengths[:, None, :]) * HEAD ** (
        -0.5
    )
    soft, tan_soft = with_tangent(last_softmax, scores, tan_scores)
    mixture = head_mix(soft, values).reshape(normed.shape)
    tan_mixture = (head_mix(tan_soft, values) + head_mix(soft, tan_values)).reshape(normed.shape)
    added, tan_added = product_flip_pair(mixture, tan_mixture, attn_w)
    hidden_two, tan_two = hidden_one + added, tan_one + tan_added
    normed, tan_normed = with_tangent(rms_norm, hidden_two, tan_two)
    queries, tan_queries = product_pair(normed, tan_normed, query_w)
    queries, tan_queries = heads_of(queries), heads_of(tan_queries)
    key_rows = heads_of(product(text_rows, key_w))
    values = heads_of(product(text_rows, cval_w))
    scores = head_scores(queries, key_rows) * HEAD ** (-0.5)
    tan_scores = head_scores(tan_queries, key_rows) * HEAD ** (-0.5)
    soft, tan_soft = with_tangent(last_softmax, scores, tan_scores)
    mixture = head_mix(soft, values).reshape(normed.shape)
    tan_mixture = head_mix(tan_soft, values).reshape(normed.shape)
    added, tan_added = product_flip_pair(mixture, tan_mixture, cout_w)
    hidden_three, tan_three = hidden_two + added, tan_two + tan_added
    normed, tan_normed = with_tangent(rms_norm, hidden_three, tan_three)
    before, tan_before = product_pair(normed, tan_normed, mlp_w)
    inner, tan_inner = with_tangent(jax.nn.gelu, before, tan_before)
    added, tan_added = product_flip_pair(inner, tan_inner, mout_w)
    hidden_four, tan_four = hidden_three + added, tan_three + tan_added
    return (
        hidden_four,
        picture_of(hidden_four, rgb_scales, rgb_weight),
        picture_of(tan_four, rgb_scales, rgb_weight),
    )


SWAP = ((0, 1), (1, 0))


def swap_mp(values):
    return lax.ppermute(values, "mp", SWAP)


def pick(values, index):
    return lax.dynamic_index_in_dim(values, index, 0, keepdims=False)


def own_whole(values, mp):
    mine, other = pick(values, mp), swap_mp(pick(values, 1 - mp))
    first = jnp.where(mp == 0, mine, other)
    second = jnp.where(mp == 0, other, mine)
    return jnp.concatenate([first, second], axis=-1)


def both_half(whole, mp):
    half = whole.shape[-1] // 2
    mine = lax.dynamic_slice_in_dim(whole, mp * half, half, whole.ndim - 1)
    other = swap_mp(lax.dynamic_slice_in_dim(whole, (1 - mp) * half, half, whole.ndim - 1))
    first = jnp.where(mp == 0, mine, other)
    second = jnp.where(mp == 0, other, mine)
    return jnp.stack([first, second])


def to_slabs(both):
    devices = lax.axis_size("dp")
    parts = both.reshape(2, both.shape[1], devices, -1).transpose(2, 0, 1, 3)
    parts = lax.all_to_all(parts, "dp", 0, 0, tiled=True)
    return parts.reshape(2 * devices, both.shape[1], -1)


def from_slabs(slabs, mp):
    devices = lax.axis_size("dp")
    rows = slabs.shape[1]
    parts = slabs.astype(jnp.bfloat16).reshape((devices, 2) + slabs.shape[1:])
    parts = lax.all_to_all(parts, "dp", 0, 0, tiled=True)
    parts = parts.transpose(1, 2, 0, 3).reshape(2, rows, -1)
    other = swap_mp(pick(parts, 1 - mp))
    return pick(parts, mp).astype(jnp.float32) + other.astype(jnp.float32)


def halve(values, axis_name, bit, dim):
    size = lax.axis_size(axis_name)
    side = (lax.axis_index(axis_name) // bit) % 2
    pairs = [(index, index ^ bit) for index in range(size)]
    sent = lax.dynamic_index_in_dim(values, 1 - side, dim, keepdims=False)
    kept = lax.dynamic_index_in_dim(values, side, dim, keepdims=False)
    return kept + lax.ppermute(sent, axis_name, pairs)


def line_sum(values, dim):
    place = lax.axis_index("dp") // 4
    up = down = None
    for step in range(1, 4):
        send_up = lax.dynamic_index_in_dim(
            values, jnp.clip(4 - step + place, 0, 3), dim, keepdims=False
        )
        send_down = lax.dynamic_index_in_dim(
            values, jnp.clip(place - 4 + step, 0, 3), dim, keepdims=False
        )
        if up is not None:
            send_up = send_up + up
            send_down = send_down + down
        up_pairs = [
            (z * 4 + rest, z * 4 + 4 + rest) for z in range(3) if z < step for rest in range(4)
        ]
        down_pairs = [
            (z * 4 + rest, z * 4 - 4 + rest) for z in range(1, 4) if 3 - z < step for rest in range(4)
        ]
        up = lax.ppermute(send_up, "dp", up_pairs)
        down = lax.ppermute(send_down, "dp", down_pairs)
    own = lax.dynamic_index_in_dim(values, place, dim, keepdims=False)
    return own + up + down


def sum_dp(partial):
    parts = partial.reshape((4, 2, 2, 2) + partial.shape[1:])
    parts = halve(parts, "dp", 1, 2)
    parts = halve(parts, "dp", 2, 1)
    return line_sum(parts, 0)


def sum_all(partial):
    parts = partial.reshape((4, 2, 2, 2) + partial.shape[2:])
    parts = halve(parts, "dp", 1, 2)
    rows = parts.shape[3]
    first, second = parts[:, :, :, : rows // 2], parts[:, :, :, rows // 2 :]
    first = halve(halve(first, "mp", 1, 2), "dp", 2, 1)
    second = halve(halve(second, "dp", 2, 1), "mp", 1, 1)
    return jnp.concatenate([line_sum(first, 0), line_sum(second, 0)], axis=0)


def gather_dp(values):
    return lax.all_gather(values, "dp", axis=0, tiled=True)


def pack_rows(entry, flip):
    if flip:
        entry = entry.T
    rows = entry.shape[0]
    return entry.reshape(rows, -1, 512).transpose(1, 0, 2).reshape(-1, 512)


def unpack_shard(entry, rows, flip):
    entry = entry.reshape(-1, rows, 512).transpose(1, 0, 2).reshape(rows, -1)
    return entry.T if flip else entry


def whole_weight(gathered, start, rows, count):
    piece = gathered[:, start : start + rows * count]
    piece = piece.reshape(16, 2, count, rows, 512).transpose(0, 3, 1, 2, 4)
    return piece.reshape(16 * rows, 2 * count * 512)


def spread_weight(grad, rows, count):
    piece = grad.reshape(16, rows, 2, count, 512).transpose(0, 2, 3, 1, 4)
    return piece.reshape(16, 2, count * rows, 512)


def sample_parallel(
    layer_input,
    labels,
    text_ids,
    noise_seeds,
    penalty_mask,
    class_table,
    token_table,
    sel_weight,
    mod_weight,
    rgb_mod,
    rgb_weight,
    conv_bias,
    noise_strength,
    kernel_bank,
    qk_weight,
    value_weight,
    attn_out,
    cross_query,
    cross_key,
    cross_value,
    cross_out,
    mlp_in,
    mlp_out,
    cot_feat,
    cot_rgb,
    penalty_dir,
):
    mp = lax.axis_index("mp")
    dp = lax.axis_index("dp")
    half_px = layer_input.shape[1]
    slab = kernel_bank.shape[2]
    width_out = kernel_bank.shape[3]
    float32, bfloat16 = jnp.float32, jnp.bfloat16

    flips = (False, False, True, False, False, False, True, False, True)
    shards = (
        qk_weight,
        value_weight,
        attn_out,
        cross_query,
        cross_key,
        cross_value,
        cross_out,
        mlp_in,
        mlp_out,
    )
    rows_of = [entry.shape[1] if flip else entry.shape[0] for entry, flip in zip(shards, flips)]
    packed = [pack_rows(entry, flip) for entry, flip in zip(shards, flips)]
    counts = [entry.shape[0] // rows for entry, rows in zip(packed, rows_of)]
    stacked = jnp.concatenate(packed, axis=0)
    gathered = lax.all_gather(stacked, ("dp", "mp"), axis=0, tiled=False)
    weights = []
    start = 0
    for rows, count in zip(rows_of, counts):
        weights.append(whole_weight(gathered, start, rows, count))
        start += rows * count
    weights = tuple(weights)

    labels_all = lax.all_gather(labels, "dp", axis=0, tiled=True)
    sample_count = labels_all.shape[0]
    classes = jnp.arange(class_table.shape[0], dtype=jnp.int32)
    onehot_class = (labels_all[:, None] == classes[None, :]).astype(bfloat16)
    latent = dot_wide(onehot_class, class_table, 1, 0)
    select_all, select_pull = jax.vjp(last_softmax, dot_wide(latent, sel_weight, 1, 0))
    scales_all = 1.0 + dot_wide(latent, mod_weight, 1, 0)
    rgb_scales_all = 1.0 + dot_wide(latent, rgb_mod, 1, 0)
    me = 2 * dp + mp
    scales = pick(scales_all, me)
    rgb_scales = pick(rgb_scales_all, me)
    scales_slab = lax.dynamic_slice_in_dim(scales_all, dp * slab, slab, 1)
    words = jnp.arange(token_table.shape[0], dtype=jnp.int32)
    text_own = pick(text_ids, mp)
    text_rows = dot_wide((text_own[:, None] == words[None, :]).astype(bfloat16), token_table, 1, 0)
    noise = noise_field(pick(noise_seeds, mp)[None], SIDE * SIDE)[0]
    small = (
        conv_bias.astype(float32),
        noise_strength.astype(float32),
        rgb_scales,
        rgb_weight.astype(float32),
    )

    bank_rows = kernel_bank.reshape(kernel_bank.shape[0], 9 * slab, width_out)
    kernel = jnp.einsum(
        "bk,kro->bro",
        select_all,
        bank_rows.astype(float32),
        precision=lax.Precision.HIGHEST,
    ).astype(bfloat16)
    kernel_wide = kernel.astype(float32)
    squares = jnp.sum(
        (kernel_wide * kernel_wide).reshape(sample_count, 9, slab, width_out), axis=1
    )
    scales_two = scales_slab * scales_slab
    sums_part = jnp.sum(scales_two[:, :, None] * squares, axis=1)

    def convolve(slabs):
        columns = patches_of(slabs, SIDE)
        return columns, einsum_low("bpr,bro->bpo", columns, kernel)

    input_own = own_whole(layer_input, mp).astype(float32)
    scales_pair = lax.dynamic_slice_in_dim(scales_all, 2 * dp, 2, 0)
    input_pair = lax.all_gather(layer_input, "mp", axis=2, tiled=True).astype(float32)
    slabs_x = to_slabs((input_pair * scales_pair[:, None, :]).astype(bfloat16))
    columns_x, conv_part_x = convolve(slabs_x)
    partial = jnp.concatenate([conv_part_x, sums_part[:, None, :]], axis=1).astype(bfloat16)
    summed = own_whole(sum_dp(partial), mp).astype(float32)
    conv_out, sums = summed[:-1], summed[-1]

    (hidden_four, picture), pull = jax.vjp(
        lambda value: layer_forward(value, sums, text_rows, small, weights, noise), conv_out
    )

    dir_own = pick(penalty_dir, mp).astype(float32)
    grad_conv = pull((jnp.zeros_like(hidden_four), dir_own))[0]
    grads_all = gather_dp(both_half(grad_conv.astype(bfloat16), mp))

    def pull_columns(cotans):
        return einsum_low("bpo,bro->bpr", cotans, kernel)

    fold = jax.linear_transpose(
        lambda slabs: patches_of(slabs, SIDE),
        jax.ShapeDtypeStruct((sample_count, half_px, slab), float32),
    )
    grad_moduled = from_slabs(fold(pull_columns(grads_all))[0], mp)
    mask_own = pick(penalty_mask, mp).astype(float32)
    tangent = penalty_weight * mask_own * grad_moduled.astype(bfloat16).astype(float32) * scales

    tan_moduled = (tangent * scales).astype(bfloat16)
    tan_other = swap_mp(tan_moduled)
    tan_pair = jnp.stack(
        [jnp.where(mp == 0, tan_moduled, tan_other), jnp.where(mp == 0, tan_other, tan_moduled)]
    )
    slabs_t = to_slabs(tan_pair)
    columns_t, conv_part_t = convolve(slabs_t)
    conv_tan = own_whole(sum_dp(conv_part_t.astype(bfloat16)), mp).astype(float32)

    (ignored_out, ignored_pic, ignored_tan), pull_joint = jax.vjp(
        lambda *given: layer_joint(*given, noise),
        conv_out,
        conv_tan,
        sums,
        text_rows,
        small,
        weights,
    )
    cot_own = own_whole(cot_feat, mp).astype(float32)
    grad_main, grad_side, grad_sums, grad_text, grad_small, grad_weights = pull_joint(
        (cot_own, pick(cot_rgb, mp).astype(float32), dir_own)
    )

    spreads = [
        spread_weight(grad, rows, count)
        for grad, rows, count in zip(grad_weights, rows_of, counts)
    ]
    mlp_sum = sum_all(jnp.concatenate(spreads[7:], axis=2))
    rest_sum = sum_all(jnp.concatenate(spreads[:7], axis=2))
    weight_sums = jnp.concatenate([rest_sum, mlp_sum], axis=0).astype(float32)
    big_sums = []
    start = 0
    for rows, count, flip in zip(rows_of, counts, flips):
        big_sums.append(unpack_shard(weight_sums[start : start + rows * count], rows, flip))
        start += rows * count

    wide = jnp.concatenate([grad_main, grad_side, grad_sums[None]], axis=0).astype(bfloat16)
    wide_all = gather_dp(both_half(wide, mp))
    pixels = SIDE * SIDE
    both_cot = wide_all[:, : 2 * pixels]
    sums_cot = wide_all[:, 2 * pixels].astype(float32)
    both_columns = jnp.concatenate([columns_x, columns_t], axis=1)
    grad_kernel = einsum_low("bpr,bpo->bro", both_columns, both_cot)
    scales_rows = jnp.tile(scales_two, (1, 9))
    grad_kernel = grad_kernel + 2.0 * kernel_wide * scales_rows[:, :, None] * sums_cot[:, None, :]
    grad_kernel = grad_kernel.astype(bfloat16)
    grad_scales_slab = (
        2.0 * scales_slab * jnp.sum(squares * sums_cot[:, None, :], axis=2)
    )
    bank_grad = jnp.einsum(
        "bk,bro->kro",
        select_all,
        grad_kernel.astype(float32),
        precision=lax.Precision.HIGHEST,
    ).reshape(kernel_bank.shape)
    grad_select = jnp.einsum(
        "bro,kro->bk", grad_kernel, bank_rows, preferred_element_type=float32
    )
    back_columns = pull_columns(both_cot)
    both_back = jnp.concatenate(
        [
            fold(back_columns[:, :pixels])[0],
            fold(back_columns[:, pixels:])[0],
        ],
        axis=1,
    )
    both_back = from_slabs(both_back, mp).astype(bfloat16).astype(float32)
    back_main, back_side = both_back[:half_px], both_back[half_px:]
    input_grad = back_main * scales
    grad_scales = jnp.sum(back_main * input_own + back_side * tangent, axis=0)

    grad_bias, grad_strength, grad_rgb_scales, grad_rgb_weight = grad_small
    row = jnp.concatenate(
        [
            grad_scales,
            grad_rgb_scales,
            grad_rgb_weight.reshape(-1),
            grad_bias,
            grad_strength,
            grad_scales_slab.reshape(-1),
            grad_select.reshape(-1),
        ]
    ).reshape(-1, 128)
    rows_all = lax.all_gather(row, ("dp", "mp"), axis=0, tiled=False).reshape(sample_count, -1)
    channels = scales.shape[0]
    scale_terms = rows_all[:, :channels]
    rgb_terms = rows_all[:, channels : 2 * channels]
    sums_all = jnp.sum(rows_all[:, 2 * channels : 7 * channels], axis=0)
    slab_terms = rows_all[:, 7 * channels : 7 * channels + sample_count * slab]
    slab_terms = slab_terms.reshape(-1, 2, sample_count, slab).sum(axis=1)
    scale_terms = scale_terms + slab_terms.transpose(1, 0, 2).reshape(sample_count, channels)
    select_terms = jnp.sum(rows_all[:, 7 * channels + sample_count * slab :], axis=0)
    logit_terms = select_pull(select_terms.reshape(sample_count, -1))[0]
    latent_terms = (
        matmul_high(scale_terms, mod_weight.astype(float32).T)
        + matmul_high(rgb_terms, rgb_mod.astype(float32).T)
        + matmul_high(logit_terms, sel_weight.astype(float32).T)
    )
    class_grad = matmul_high(onehot_class.astype(float32).T, latent_terms)
    sel_grad = matmul_high(latent.T, logit_terms)
    mod_grad = matmul_high(latent.T, scale_terms)
    rgb_mod_grad = matmul_high(latent.T, rgb_terms)
    text_all = lax.all_gather(grad_text.astype(bfloat16), ("dp", "mp"), axis=0, tiled=True)
    ids_all = lax.all_gather(text_ids, "dp", axis=0, tiled=True).reshape(-1)
    token_grad = dot_wide((ids_all[:, None] == words[None, :]).astype(bfloat16), text_all, 0, 0)

    picture_other = swap_mp(picture)
    pictures = jnp.stack(
        [jnp.where(mp == 0, picture, picture_other), jnp.where(mp == 0, picture_other, picture)]
    )
    return (
        both_half(hidden_four, mp),
        pictures,
        both_half(input_grad, mp),
        class_grad,
        token_grad,
        sel_grad,
        mod_grad,
        rgb_mod_grad,
        sums_all[: 3 * channels].reshape(3, channels),
        sums_all[3 * channels : 4 * channels],
        sums_all[4 * channels :],
        bank_grad,
    ) + tuple(big_sums)


def solution(mesh):
    in_specs = (
        P("dp", None, "mp"),
        P("dp"),
        P("dp", None),
        P("dp"),
        P("dp"),
        P(),
        P(),
        P(),
        P(),
        P(),
        P(),
        P(),
        P(),
        P(None, None, "dp", "mp"),
        P("dp", "mp"),
        P("dp", "mp"),
        P("mp", "dp"),
        P("dp", "mp"),
        P("dp", "mp"),
        P("dp", "mp"),
        P("mp", "dp"),
        P("dp", "mp"),
        P("mp", "dp"),
        P("dp", None, "mp"),
        P("dp", None, None),
        P("dp", None, None),
    )
    out_specs = (
        P("dp", None, "mp"),
        P("dp", None, None),
        P("dp", None, "mp"),
        P(),
        P(),
        P(),
        P(),
        P(),
        P(),
        P(),
        P(),
        P(None, None, "dp", "mp"),
        P("dp", "mp"),
        P("dp", "mp"),
        P("mp", "dp"),
        P("dp", "mp"),
        P("dp", "mp"),
        P("dp", "mp"),
        P("mp", "dp"),
        P("dp", "mp"),
        P("mp", "dp"),
    )
    return jax.shard_map(
        sample_parallel if fits_samples(mesh) else tensor_parallel,
        mesh=mesh, in_specs=in_specs, out_specs=out_specs, check_vma=False
    )
```

```python
import jax
import jax.numpy as jnp
import numpy as np
from jax import lax
from jax.experimental import pallas as pl
from jax.experimental.pallas import tpu as pltpu
from jax.sharding import PartitionSpec as P

HEAD = 64
SIDE = 16


penalty_weight = 1.0


def rounded(values):
    return lax.optimization_barrier(values.astype(jnp.bfloat16)).astype(jnp.float32)


def matmul_high(left, right):
    return jnp.matmul(left, right, precision=lax.Precision.HIGHEST)


def einsum_high(form, *operands):
    return jnp.einsum(form, *operands, precision=lax.Precision.HIGHEST)


def einsum_low(form, left, right):
    return jnp.einsum(
        form,
        left.astype(jnp.bfloat16),
        right.astype(jnp.bfloat16),
        preferred_element_type=jnp.float32,
    )


def noise_field(seed_ids, pixel_count):
    pixel_ids = jnp.arange(pixel_count, dtype=jnp.int32)
    mixed = seed_ids[:, None] * 1103515245 + pixel_ids[None, :] * 40503
    mixed = jnp.bitwise_xor(mixed, jnp.right_shift(mixed, 13)) * 1664525 + 1013904223
    levels = jnp.bitwise_and(jnp.right_shift(mixed, 8), 65535)
    return levels.astype(jnp.float32) / 65536.0 - 0.5


def patches_of(flat_rows, side_len):
    samples_here, pixels, width_here = flat_rows.shape
    half_side = side_len // 2
    picture = flat_rows.reshape(samples_here, half_side, half_side, width_here)
    picture = jnp.repeat(jnp.repeat(picture, 2, axis=1), 2, axis=2)
    padded = jnp.pad(picture, ((0, 0), (1, 1), (1, 1), (0, 0)))
    pieces = [
        padded[:, shift_row : shift_row + side_len, shift_col : shift_col + side_len, :]
        for shift_row in range(3)
        for shift_col in range(3)
    ]
    return jnp.concatenate(pieces, axis=-1).reshape(
        samples_here, side_len * side_len, 9 * width_here
    )


def rms_norm(values):
    return values * lax.rsqrt(jnp.mean(values * values, axis=-1, keepdims=True) + 1e-06)


def conv_part(gathered, kernel, scales, bias_local, strength_local, noise_map):
    samples_here = gathered.shape[0]
    width_out = kernel.shape[2]
    columns = patches_of(gathered, SIDE)
    conv_out = einsum_low("bpr,bro->bpo", columns, kernel)
    squares = jnp.sum((kernel * kernel).reshape(samples_here, 9, -1, width_out), axis=1)
    demodulate = lax.rsqrt(einsum_high("bi,bio->bo", scales * scales, squares) + 1e-08)
    before = conv_out * demodulate[:, None, :] + bias_local + noise_map[:, :, None] * strength_local
    return jax.nn.silu(before)


def self_attention(active, qk_w, value_w, out_w):
    normed = rounded(rms_norm(active))
    queries = rounded(matmul_high(normed, qk_w))
    values = rounded(matmul_high(normed, value_w))
    samples_here, pixels, width_here = queries.shape
    heads_here = width_here // HEAD
    q_heads = queries.reshape(samples_here, pixels, heads_here, HEAD)
    v_heads = values.reshape(samples_here, pixels, heads_here, HEAD)
    lengths = jnp.transpose(jnp.sum(q_heads * q_heads, axis=-1), (0, 2, 1))
    scores = (
        2.0 * einsum_low("bphd,bqhd->bhpq", q_heads, q_heads) - lengths[:, :, None, :]
    ) * HEAD ** (-0.5)
    soft_weights = rounded(jax.nn.softmax(scores, axis=-1))
    mixture = rounded(
        einsum_low("bhpq,bqhd->bphd", soft_weights, v_heads).reshape(
            samples_here, pixels, width_here
        )
    )
    return matmul_high(mixture, out_w)


def cross_attention(active, text_rows, query_w, key_w, value_w, out_w):
    normed = rounded(rms_norm(active))
    queries = rounded(matmul_high(normed, query_w))
    key_rows = rounded(matmul_high(text_rows, key_w))
    values = rounded(matmul_high(text_rows, value_w))
    samples_here, pixels, width_here = queries.shape
    tokens = key_rows.shape[1]
    heads_here = width_here // HEAD
    q_heads = queries.reshape(samples_here, pixels, heads_here, HEAD)
    k_heads = key_rows.reshape(samples_here, tokens, heads_here, HEAD)
    v_heads = values.reshape(samples_here, tokens, heads_here, HEAD)
    scores = einsum_low("bphd,bthd->bhpt", q_heads, k_heads) * HEAD ** (-0.5)
    soft_weights = rounded(jax.nn.softmax(scores, axis=-1))
    mixture = rounded(
        einsum_low("bhpt,bthd->bphd", soft_weights, v_heads).reshape(
            samples_here, pixels, width_here
        )
    )
    return matmul_high(mixture, out_w)


def feed_forward(active, weight_in, weight_out):
    normed = rounded(rms_norm(active))
    inner = rounded(jax.nn.gelu(matmul_high(normed, weight_in)))
    return matmul_high(inner, weight_out)


def tree_add(first, second):
    return jax.tree.map(jnp.add, first, second)


def tensor_parallel(
    layer_input,
    labels,
    text_ids,
    noise_seeds,
    penalty_mask,
    class_table,
    token_table,
    sel_weight,
    mod_weight,
    rgb_mod,
    rgb_weight,
    conv_bias,
    noise_strength,
    kernel_bank,
    qk_weight,
    value_weight,
    attn_out,
    cross_query,
    cross_key,
    cross_value,
    cross_out,
    mlp_in,
    mlp_out,
    cot_feat,
    cot_rgb,
    penalty_dir,
):
    width_local = layer_input.shape[2]
    offset = lax.axis_index("mp") * width_local
    small_params = tuple(
        (
            entry.astype(jnp.float32)
            for entry in (
                class_table,
                token_table,
                sel_weight,
                mod_weight,
                rgb_mod,
                rgb_weight,
                conv_bias,
                noise_strength,
            )
        )
    )

    def fetch_proj():
        fetched = (
            lax.all_gather(qk_weight, "dp", axis=0, tiled=True),
            lax.all_gather(value_weight, "dp", axis=0, tiled=True),
            lax.all_gather(attn_out, "dp", axis=1, tiled=True),
            lax.all_gather(cross_query, "dp", axis=0, tiled=True),
            lax.all_gather(cross_key, "dp", axis=0, tiled=True),
            lax.all_gather(cross_value, "dp", axis=0, tiled=True),
            lax.all_gather(cross_out, "dp", axis=1, tiled=True),
            lax.all_gather(mlp_in, "dp", axis=0, tiled=True),
            lax.all_gather(mlp_out, "dp", axis=1, tiled=True),
        )
        return tuple((entry.astype(jnp.float32) for entry in fetched))

    def style_part(param_set):
        table_class, table_word, select_w, modul_w, rgbmod_w, rgbout_w, bias_w, strength_w = (
            param_set
        )
        onehot_class = (
            labels[:, None] == jnp.arange(table_class.shape[0], dtype=jnp.int32)[None, :]
        ).astype(jnp.float32)
        latent = matmul_high(onehot_class, table_class)
        onehot_word = (
            text_ids[:, :, None] == jnp.arange(table_word.shape[0], dtype=jnp.int32)
        ).astype(jnp.float32)
        text_rows = matmul_high(onehot_word, table_word)
        select = jax.nn.softmax(matmul_high(latent, select_w), axis=-1)
        scales = 1.0 + matmul_high(latent, modul_w)
        rgb_scales = 1.0 + matmul_high(
            latent, lax.dynamic_slice_in_dim(rgbmod_w, offset, width_local, 1)
        )
        bias_local = lax.dynamic_slice_in_dim(bias_w, offset, width_local, 0)
        strength_local = lax.dynamic_slice_in_dim(strength_w, offset, width_local, 0)
        colour_local = lax.dynamic_slice_in_dim(rgbout_w, offset, width_local, 1)
        return (select, scales, rgb_scales, text_rows, bias_local, strength_local, colour_local)

    styles, style_pull = jax.vjp(style_part, small_params)
    noise_map = noise_field(noise_seeds, SIDE * SIDE)

    def owned_sets():
        proj_set = fetch_proj()
        conv_set = (lax.all_gather(kernel_bank, "dp", axis=2, tiled=True).astype(jnp.float32),)
        return ((), conv_set, proj_set[0:3], proj_set[3:7], proj_set[7:9], ())

    def seg_in(active, styles_in, own_set):
        return active * lax.dynamic_slice_in_dim(styles_in[1], offset, width_local, 1)[:, None, :]

    def seg_conv(active, styles_in, own_set):
        bank_full = own_set[0]
        kernel = rounded(matmul_high(styles_in[0], bank_full.reshape(bank_full.shape[0], -1)))
        kernel = kernel.reshape(active.shape[0], -1, bank_full.shape[3])
        return conv_part(active, kernel, styles_in[1], styles_in[4], styles_in[5], noise_map)

    def seg_self(active, styles_in, own_set):
        return self_attention(active, own_set[0], own_set[1], own_set[2])

    def seg_cross(active, styles_in, own_set):
        return cross_attention(active, styles_in[3], own_set[0], own_set[1], own_set[2], own_set[3])

    def seg_mlp(active, styles_in, own_set):
        return feed_forward(active, own_set[0], own_set[1])

    def seg_rgb(active, styles_in, own_set):
        return einsum_high("bpc,bc,kc->bkp", active, styles_in[2], styles_in[6])

    def spread(stacked):
        return lax.all_gather(stacked, "mp", axis=3, tiled=True)

    def collect(stacked):
        return lax.psum_scatter(
            stacked.astype(jnp.bfloat16), "mp", scatter_dimension=3, tiled=True
        ).astype(jnp.float32)

    def spread_one(values):
        return spread(values.astype(jnp.bfloat16)[None])[0].astype(jnp.float32)

    def collect_one(values):
        return collect(values[None])[0]

    own_first = owned_sets()
    input_full = layer_input.astype(jnp.float32)
    gathered_x = spread_one(seg_in(input_full, styles, own_first[0]))
    hidden_one = seg_conv(gathered_x, styles, own_first[1])
    gathered_one = spread_one(hidden_one)
    hidden_two = hidden_one + collect_one(seg_self(gathered_one, styles, own_first[2]))
    gathered_two = spread_one(hidden_two)
    hidden_three = hidden_two + collect_one(seg_cross(gathered_two, styles, own_first[3]))
    gathered_three = spread_one(hidden_three)
    hidden_four = hidden_three + collect_one(seg_mlp(gathered_three, styles, own_first[4]))
    picture = lax.psum(seg_rgb(hidden_four, styles, own_first[5]), "mp")
    own_second = owned_sets()

    def pull_act(segment, active, own_set, cotan):
        return jax.vjp(lambda inner_x: segment(inner_x, styles, own_set), active)[1](cotan)[0]

    grad_four = pull_act(seg_rgb, hidden_four, own_second[5], penalty_dir.astype(jnp.float32))
    back_three = pull_act(seg_mlp, gathered_three, own_second[4], spread_one(grad_four))
    grad_three = grad_four + rounded(collect_one(back_three))
    back_two = pull_act(seg_cross, gathered_two, own_second[3], spread_one(grad_three))
    grad_two = grad_three + rounded(collect_one(back_two))
    back_one = pull_act(seg_self, gathered_one, own_second[2], spread_one(grad_two))
    grad_one = grad_two + rounded(collect_one(back_one))
    grad_moduled = rounded(collect_one(pull_act(seg_conv, gathered_x, own_second[1], grad_one)))
    penalty_grad = pull_act(seg_in, input_full, own_second[0], grad_moduled)
    tangent = penalty_weight * penalty_mask.astype(jnp.float32)[:, None, None] * penalty_grad
    own_third = owned_sets()

    def push(segment, active, own_set, tangent_in):
        return jax.jvp(lambda inner_x: segment(inner_x, styles, own_set), (active,), (tangent_in,))[
            1
        ]

    tan_x = spread_one(push(seg_in, input_full, own_third[0], tangent))
    tan_one = push(seg_conv, gathered_x, own_third[1], tan_x)
    tan_g1 = spread_one(tan_one)
    tan_two = tan_one + collect_one(push(seg_self, gathered_one, own_third[2], tan_g1))
    tan_g2 = spread_one(tan_two)
    tan_three = tan_two + collect_one(push(seg_cross, gathered_two, own_third[3], tan_g2))
    tan_g3 = spread_one(tan_three)
    tan_four = tan_three + collect_one(push(seg_mlp, gathered_three, own_third[4], tan_g3))
    own_fourth = owned_sets()

    def pull_both(segment, active, tangent_in, own_set, cotan, cotan_tangent):

        def joint(inner_x, inner_tangent, styles_in, own_in):
            return jax.jvp(
                lambda value_x: segment(value_x, styles_in, own_in), (inner_x,), (inner_tangent,)
            )

        return jax.vjp(joint, active, tangent_in, styles, own_set)[1]((cotan, cotan_tangent))

    grad_act, grad_tan, style_acc, ignored = pull_both(
        seg_rgb,
        hidden_four,
        tan_four,
        own_fourth[5],
        cot_rgb.astype(jnp.float32),
        penalty_dir.astype(jnp.float32),
    )
    main_now = cot_feat.astype(jnp.float32) + grad_act
    side_now = grad_tan
    layer_grads = []
    for segment, active, tangent_in, own_set in (
        (seg_mlp, gathered_three, tan_g3, own_fourth[4]),
        (seg_cross, gathered_two, tan_g2, own_fourth[3]),
        (seg_self, gathered_one, tan_g1, own_fourth[2]),
    ):
        both_wide = spread(jnp.stack([main_now, side_now]).astype(jnp.bfloat16)).astype(jnp.float32)
        grad_act, grad_tan, grad_sty, grad_own = pull_both(
            segment, active, tangent_in, own_set, both_wide[0], both_wide[1]
        )
        style_acc = tree_add(style_acc, grad_sty)
        layer_grads.append(grad_own)
        both_sums = collect(jnp.stack([grad_act, grad_tan]))
        main_now = main_now + rounded(both_sums[0])
        side_now = side_now + rounded(both_sums[1])
    grad_act, grad_tan, grad_sty, grads_conv = pull_both(
        seg_conv, gathered_x, tan_x, own_fourth[1], main_now, side_now
    )
    style_acc = tree_add(style_acc, grad_sty)
    both_sums = collect(jnp.stack([grad_act, grad_tan]))
    grad_act, grad_tan, grad_sty, ignored = pull_both(
        seg_in, input_full, tangent, own_fourth[0], rounded(both_sums[0]), rounded(both_sums[1])
    )
    style_acc = tree_add(style_acc, grad_sty)
    proj_terms = layer_grads[2] + layer_grads[1] + layer_grads[0]
    big_terms = grads_conv + proj_terms
    big_sums = (
        lax.psum_scatter(
            big_terms[0].astype(jnp.bfloat16), "dp", scatter_dimension=2, tiled=True
        ).astype(jnp.float32),
        lax.psum_scatter(
            big_terms[1].astype(jnp.bfloat16), "dp", scatter_dimension=0, tiled=True
        ).astype(jnp.float32),
        lax.psum_scatter(
            big_terms[2].astype(jnp.bfloat16), "dp", scatter_dimension=0, tiled=True
        ).astype(jnp.float32),
        lax.psum_scatter(
            big_terms[3].astype(jnp.bfloat16), "dp", scatter_dimension=1, tiled=True
        ).astype(jnp.float32),
        lax.psum_scatter(
            big_terms[4].astype(jnp.bfloat16), "dp", scatter_dimension=0, tiled=True
        ).astype(jnp.float32),
        lax.psum_scatter(
            big_terms[5].astype(jnp.bfloat16), "dp", scatter_dimension=0, tiled=True
        ).astype(jnp.float32),
        lax.psum_scatter(
            big_terms[6].astype(jnp.bfloat16), "dp", scatter_dimension=0, tiled=True
        ).astype(jnp.float32),
        lax.psum_scatter(
            big_terms[7].astype(jnp.bfloat16), "dp", scatter_dimension=1, tiled=True
        ).astype(jnp.float32),
        lax.psum_scatter(
            big_terms[8].astype(jnp.bfloat16), "dp", scatter_dimension=0, tiled=True
        ).astype(jnp.float32),
        lax.psum_scatter(
            big_terms[9].astype(jnp.bfloat16), "dp", scatter_dimension=1, tiled=True
        ).astype(jnp.float32),
    )
    small_terms = style_pull(style_acc)[0]
    small_sums = lax.psum(
        (
            small_terms[0],
            small_terms[1],
            small_terms[2],
            small_terms[3],
            small_terms[4],
            small_terms[5],
            small_terms[6],
            small_terms[7],
        ),
        ("dp", "mp"),
    )
    return (hidden_four, picture, grad_act) + tuple(small_sums) + tuple(big_sums)


def fits_samples(mesh):
    return mesh.shape["dp"] == 16 and mesh.shape["mp"] == 2


def dot_wide(left, right, left_dim, right_dim):
    return lax.dot_general(
        left.astype(jnp.bfloat16),
        right.astype(jnp.bfloat16),
        (((left_dim,), (right_dim,)), ((), ())),
        preferred_element_type=jnp.float32,
    )


def make_products(flip):
    depth = 1 if flip else 0

    def weight_grad(rows, cotan):
        if flip:
            return dot_wide(cotan, rows, 0, 0).astype(jnp.bfloat16)
        return dot_wide(rows, cotan, 0, 0).astype(jnp.bfloat16)

    @jax.custom_vjp
    def single(rows, weight):
        return dot_wide(rows, weight, 1, depth)

    def single_fwd(rows, weight):
        return single(rows, weight), (rows, weight)

    def single_bwd(kept, cotan):
        rows, weight = kept
        return dot_wide(cotan, weight, 1, 1 - depth), weight_grad(rows, cotan)

    single.defvjp(single_fwd, single_bwd)

    @jax.custom_vjp
    def pair(rows, tangents, weight):
        return dot_wide(rows, weight, 1, depth), dot_wide(tangents, weight, 1, depth)

    def pair_fwd(rows, tangents, weight):
        return pair(rows, tangents, weight), (rows, tangents, weight)

    def pair_bwd(kept, cotans):
        rows, tangents, weight = kept
        count = rows.shape[0]
        both = jnp.concatenate([entry.astype(jnp.bfloat16) for entry in cotans], axis=0)
        inputs = jnp.concatenate(
            [rows.astype(jnp.bfloat16), tangents.astype(jnp.bfloat16)], axis=0
        )
        back = dot_wide(both, weight, 1, 1 - depth)
        return back[:count], back[count:], weight_grad(inputs, both)

    pair.defvjp(pair_fwd, pair_bwd)
    return single, pair


product, product_pair = make_products(False)
product_flip, product_flip_pair = make_products(True)


def make_bilinear(left_ids, right_ids, out_ids):
    @jax.custom_vjp
    def form(left, right):
        return einsum_low(f"{left_ids},{right_ids}->{out_ids}", left, right)

    def form_fwd(left, right):
        return form(left, right), (left, right)

    def form_bwd(kept, cotan):
        left, right = kept
        return (
            einsum_low(f"{out_ids},{right_ids}->{left_ids}", cotan, right),
            einsum_low(f"{left_ids},{out_ids}->{right_ids}", left, cotan),
        )

    form.defvjp(form_fwd, form_bwd)
    return form


head_scores = make_bilinear("phd", "qhd", "hpq")
head_mix = make_bilinear("hpq", "qhd", "phd")


def heads_of(rows):
    return rows.reshape(rows.shape[0], -1, HEAD)


def with_tangent(fun, value, tangent):
    return jax.jvp(fun, (value,), (tangent,))


def self_scores(q_heads):
    short = q_heads.astype(jnp.bfloat16).astype(jnp.float32)
    return jnp.transpose(jnp.sum(short * short, axis=-1))


def last_softmax(scores):
    return jax.nn.softmax(scores, axis=-1)


def post_conv(conv_out, sums, bias, strength, noise):
    demodulate = lax.rsqrt(sums + 1e-08)
    return jax.nn.silu(conv_out * demodulate[None] + bias[None] + noise[:, None] * strength[None])


def picture_of(hidden, rgb_scales, rgb_weight):
    return einsum_high("pc,kc->kp", hidden, rgb_scales[None] * rgb_weight)


def layer_forward(conv_out, sums, text_rows, small, weights, noise):
    bias, strength, rgb_scales, rgb_weight = small
    qk_w, value_w, attn_w, query_w, key_w, cval_w, cout_w, mlp_w, mout_w = weights
    hidden_one = post_conv(conv_out, sums, bias, strength, noise)
    normed = rms_norm(hidden_one)
    queries = heads_of(product(normed, qk_w))
    values = heads_of(product(normed, value_w))
    scores = (2.0 * head_scores(queries, queries) - self_scores(queries)[:, None, :]) * HEAD ** (
        -0.5
    )
    mixture = head_mix(last_softmax(scores), values).reshape(normed.shape)
    hidden_two = hidden_one + product_flip(mixture, attn_w)
    normed = rms_norm(hidden_two)
    queries = heads_of(product(normed, query_w))
    key_rows = heads_of(product(text_rows, key_w))
    values = heads_of(product(text_rows, cval_w))
    scores = head_scores(queries, key_rows) * HEAD ** (-0.5)
    mixture = head_mix(last_softmax(scores), values).reshape(normed.shape)
    hidden_three = hidden_two + product_flip(mixture, cout_w)
    normed = rms_norm(hidden_three)
    inner = jax.nn.gelu(product(normed, mlp_w))
    hidden_four = hidden_three + product_flip(inner, mout_w)
    return hidden_four, picture_of(hidden_four, rgb_scales, rgb_weight)


def layer_joint(conv_out, conv_tan, sums, text_rows, small, weights, noise):
    bias, strength, rgb_scales, rgb_weight = small
    qk_w, value_w, attn_w, query_w, key_w, cval_w, cout_w, mlp_w, mout_w = weights
    hidden_one, tan_one = with_tangent(
        lambda value: post_conv(value, sums, bias, strength, noise), conv_out, conv_tan
    )
    normed, tan_normed = with_tangent(rms_norm, hidden_one, tan_one)
    queries, tan_queries = product_pair(normed, tan_normed, qk_w)
    queries, tan_queries = heads_of(queries), heads_of(tan_queries)
    values, tan_values = product_pair(normed, tan_normed, value_w)
    values, tan_values = heads_of(values), heads_of(tan_values)
    lengths, tan_lengths = with_tangent(self_scores, queries, tan_queries)
    scores = (2.0 * head_scores(queries, queries) - lengths[:, None, :]) * HEAD ** (-0.5)
    half = head_scores(tan_queries, queries)
    tan_scores = (2.0 * (half + jnp.swapaxes(half, 1, 2)) - tan_lengths[:, None, :]) * HEAD ** (
        -0.5
    )
    soft, tan_soft = with_tangent(last_softmax, scores, tan_scores)
    mixture = head_mix(soft, values).reshape(normed.shape)
    tan_mixture = (head_mix(tan_soft, values) + head_mix(soft, tan_values)).reshape(normed.shape)
    added, tan_added = product_flip_pair(mixture, tan_mixture, attn_w)
    hidden_two, tan_two = hidden_one + added, tan_one + tan_added
    normed, tan_normed = with_tangent(rms_norm, hidden_two, tan_two)
    queries, tan_queries = product_pair(normed, tan_normed, query_w)
    queries, tan_queries = heads_of(queries), heads_of(tan_queries)
    key_rows = heads_of(product(text_rows, key_w))
    values = heads_of(product(text_rows, cval_w))
    scores = head_scores(queries, key_rows) * HEAD ** (-0.5)
    tan_scores = head_scores(tan_queries, key_rows) * HEAD ** (-0.5)
    soft, tan_soft = with_tangent(last_softmax, scores, tan_scores)
    mixture = head_mix(soft, values).reshape(normed.shape)
    tan_mixture = head_mix(tan_soft, values).reshape(normed.shape)
    added, tan_added = product_flip_pair(mixture, tan_mixture, cout_w)
    hidden_three, tan_three = hidden_two + added, tan_two + tan_added
    normed, tan_normed = with_tangent(rms_norm, hidden_three, tan_three)
    before, tan_before = product_pair(normed, tan_normed, mlp_w)
    inner, tan_inner = with_tangent(jax.nn.gelu, before, tan_before)
    added, tan_added = product_flip_pair(inner, tan_inner, mout_w)
    hidden_four, tan_four = hidden_three + added, tan_three + tan_added
    return (
        hidden_four,
        picture_of(hidden_four, rgb_scales, rgb_weight),
        picture_of(tan_four, rgb_scales, rgb_weight),
    )


CHUNK = 16
PAD_ROWS = (SIDE + 2) * SIDE
PIXELS = SIDE * SIDE


def placing(half_side):
    side = 2 * half_side
    table = np.zeros((side + 2, side, 3, half_side * half_side), np.float32)
    for row in range(1, side + 1):
        for col in range(side):
            for shift in range(3):
                at = col + shift - 1
                if 0 <= at < side:
                    table[row, col, shift, (row - 1) // 2 * half_side + at // 2] = 1.0
    return jnp.asarray(table.reshape((side + 2) * side, -1), jnp.bfloat16)


def dot_f32(left, right, left_dim, right_dim):
    return lax.dot_general(
        left, right, (((left_dim,), (right_dim,)), ((), ())), preferred_element_type=jnp.float32
    )


def mix_matrix(select):
    high = select.astype(jnp.bfloat16)
    low = (select - high.astype(jnp.float32)).astype(jnp.bfloat16)
    eye = jnp.eye(CHUNK, dtype=jnp.bfloat16)
    parts = jnp.stack([high, low], axis=1)
    wide = parts[:, None, :, :, None] * eye[None, :, None, None, :]
    return wide.reshape(select.shape[0] * CHUNK, -1)


def lanes_wide(column, width):
    return jnp.concatenate([column] * (width // column.shape[-1]), axis=-1)


def mix_body(pieces, mix_ref, bank_ref, squares_ref, kernel_ref, sums_ref):
    step = pl.program_id(0)

    @pl.when(step == 0)
    def _():
        sums_ref[...] = jnp.zeros_like(sums_ref)

    kernels, rows, width = bank_ref.shape
    samples = kernel_ref.shape[0]
    per_tap = squares_ref.shape[1]
    for piece in range(pieces):
        part = bank_ref[:, piece * CHUNK : (piece + 1) * CHUNK, :].reshape(kernels * CHUNK, width)
        mixed = dot_f32(mix_ref[...], jnp.concatenate([part, part], axis=0), 1, 0)
        mixed = mixed.astype(jnp.bfloat16).reshape(samples, CHUNK, width)
        kernel_ref[:, piece * CHUNK : (piece + 1) * CHUNK, :] = mixed
        first = lax.rem(step * rows + piece * CHUNK, per_tap)
        factor = squares_ref[:, pl.ds(pl.multiple_of(first, CHUNK), CHUNK), :]
        wide = mixed.astype(jnp.float32)
        sums_ref[...] += jnp.sum(wide * wide * lanes_wide(factor, width), axis=1)


def mix_kernels(mix, bank_rows, squares):
    kernels, depth, width = bank_rows.shape
    samples = squares.shape[0]
    pieces = 4
    rows = pieces * CHUNK
    return pl.pallas_call(
        lambda *refs: mix_body(pieces, *refs),
        grid=(depth // rows,),
        in_specs=[
            pl.BlockSpec(mix.shape, lambda step: (0, 0)),
            pl.BlockSpec((kernels, rows, width), lambda step: (0, step, 0)),
            pl.BlockSpec(squares.shape, lambda step: (0, 0, 0)),
        ],
        out_specs=[
            pl.BlockSpec((samples, rows, width), lambda step: (0, step, 0)),
            pl.BlockSpec((samples, width), lambda step: (0, 0)),
        ],
        out_shape=[
            jax.ShapeDtypeStruct((samples, depth, width), jnp.bfloat16),
            jax.ShapeDtypeStruct((samples, width), jnp.float32),
        ],
        compiler_params=pltpu.CompilerParams(vmem_limit_bytes=48 * 2**20),
        name="mix_kernels",
    )(mix, bank_rows, squares)


def place_rows(slab, place_ref, spot_ref):
    pixels, width = slab.shape
    for shift in range(3):
        spot_ref[
            shift * pixels : (shift + 1) * pixels, shift * width : (shift + 1) * width
        ] = slab
    return dot_f32(place_ref[...], spot_ref[...], 1, 0).astype(jnp.bfloat16)


def conv_body(extra, slab_ref, place_ref, kernel_ref, sums_ref, out_ref, spot_ref):
    sample = pl.program_id(0)

    @pl.when(sample == 0)
    def _():
        spot_ref[...] = jnp.zeros_like(spot_ref)

    rows = place_rows(slab_ref[0], place_ref, spot_ref)
    depth = rows.shape[1]
    total = None
    for shift in range(3):
        term = dot_f32(
            rows[shift * SIDE : shift * SIDE + PIXELS],
            kernel_ref[0, shift * depth : (shift + 1) * depth, :],
            1,
            0,
        )
        total = term if total is None else total + term
    out_ref[0, :PIXELS, :] = total.astype(jnp.bfloat16)
    if extra:
        line = sums_ref[pl.ds(sample, 1), :]
        out_ref[0, PIXELS:, :] = jnp.broadcast_to(line, (CHUNK, line.shape[1])).astype(jnp.bfloat16)


def convolve(slabs, place, kernel, sums, extra):
    samples, pixels, width = slabs.shape
    depth, width_out = kernel.shape[1:]
    rows = PIXELS + (CHUNK if extra else 0)
    return pl.pallas_call(
        lambda *refs: conv_body(extra, *refs),
        grid=(samples,),
        in_specs=[
            pl.BlockSpec((1, pixels, width), lambda step: (step, 0, 0)),
            pl.BlockSpec(place.shape, lambda step: (0, 0)),
            pl.BlockSpec((1, depth, width_out), lambda step: (step, 0, 0)),
            pl.BlockSpec(sums.shape, lambda step: (0, 0)),
        ],
        out_specs=pl.BlockSpec((1, rows, width_out), lambda step: (step, 0, 0)),
        out_shape=jax.ShapeDtypeStruct((samples, rows, width_out), jnp.bfloat16),
        scratch_shapes=[pltpu.VMEM((3 * pixels, 3 * width), jnp.bfloat16)],
        compiler_params=pltpu.CompilerParams(vmem_limit_bytes=32 * 2**20),
        name="conv_forward",
    )(slabs, place, kernel, sums)


def fold_back(cotan, place_ref, kernel_ref, wide_ref, pixels, width):
    depth = 3 * width
    wide_ref[...] = jnp.zeros_like(wide_ref)
    for shift in range(3):
        wide_ref[shift * SIDE : shift * SIDE + PIXELS, :] += dot_f32(
            cotan, kernel_ref[0, shift * depth : (shift + 1) * depth, :], 1, 1
        )
    back = dot_f32(place_ref[...], wide_ref[...].astype(jnp.bfloat16), 0, 0)
    total = None
    for shift in range(3):
        term = back[shift * pixels : (shift + 1) * pixels, shift * width : (shift + 1) * width]
        total = term if total is None else total + term
    return total.astype(jnp.bfloat16)


def back_body(cotan_ref, place_ref, kernel_ref, out_ref, wide_ref):
    pixels, width = out_ref.shape[1:]
    out_ref[0] = fold_back(cotan_ref[0], place_ref, kernel_ref, wide_ref, pixels, width)


def conv_back(cotans, place, kernel, pixels, width):
    samples, rows, width_out = cotans.shape
    depth = kernel.shape[1]
    return pl.pallas_call(
        back_body,
        grid=(samples,),
        in_specs=[
            pl.BlockSpec((1, rows, width_out), lambda step: (step, 0, 0)),
            pl.BlockSpec(place.shape, lambda step: (0, 0)),
            pl.BlockSpec((1, depth, width_out), lambda step: (step, 0, 0)),
        ],
        out_specs=pl.BlockSpec((1, pixels, width), lambda step: (step, 0, 0)),
        out_shape=jax.ShapeDtypeStruct((samples, pixels, width), jnp.bfloat16),
        scratch_shapes=[pltpu.VMEM((PAD_ROWS, 3 * width), jnp.float32)],
        compiler_params=pltpu.CompilerParams(vmem_limit_bytes=32 * 2**20),
        name="conv_back",
    )(cotans, place, kernel)


def second_body(
    slab_ref,
    tan_ref,
    place_ref,
    kernel_ref,
    cotan_ref,
    squares_ref,
    grad_ref,
    back_ref,
    scale_ref,
    spot_ref,
    wide_ref,
):
    @pl.when(pl.program_id(0) == 0)
    def _():
        spot_ref[...] = jnp.zeros_like(spot_ref)

    pixels, width = slab_ref.shape[1:]
    depth = 3 * width
    rows = place_rows(slab_ref[0], place_ref, spot_ref)
    tan_rows = place_rows(tan_ref[0], place_ref, spot_ref)
    line = cotan_ref[0, 2 * PIXELS : 2 * PIXELS + CHUNK, :][:1].astype(jnp.float32)
    factor = 2.0 * lanes_wide(squares_ref[0], line.shape[1]) * line
    totals = None
    for shift in range(3):
        span = slice(shift * SIDE, shift * SIDE + PIXELS)
        grad = dot_f32(rows[span], cotan_ref[0, :PIXELS, :], 0, 0)
        grad = grad + dot_f32(tan_rows[span], cotan_ref[0, PIXELS : 2 * PIXELS, :], 0, 0)
        for tap in range(3):
            at = shift * depth + tap * width
            own = kernel_ref[0, at : at + width, :].astype(jnp.float32)
            grad_ref[0, at : at + width, :] = (
                grad[tap * width : (tap + 1) * width] + own * factor
            ).astype(jnp.bfloat16)
            term = own * own
            totals = term if totals is None else totals + term
    summed = jnp.sum(totals * line, axis=1, keepdims=True)
    scale_ref[0] = jnp.broadcast_to(summed, scale_ref.shape[1:])
    for part in range(2):
        back_ref[0, part * pixels : (part + 1) * pixels, :] = fold_back(
            cotan_ref[0, part * PIXELS : (part + 1) * PIXELS, :],
            place_ref,
            kernel_ref,
            wide_ref,
            pixels,
            width,
        )


def conv_second(slabs, tans, place, kernel, cotans, squares):
    samples, pixels, width = slabs.shape
    depth, width_out = kernel.shape[1:]
    return pl.pallas_call(
        second_body,
        grid=(samples,),
        in_specs=[
            pl.BlockSpec((1, pixels, width), lambda step: (step, 0, 0)),
            pl.BlockSpec((1, pixels, width), lambda step: (step, 0, 0)),
            pl.BlockSpec(place.shape, lambda step: (0, 0)),
            pl.BlockSpec((1, depth, width_out), lambda step: (step, 0, 0)),
            pl.BlockSpec((1,) + cotans.shape[1:], lambda step: (step, 0, 0)),
            pl.BlockSpec((1,) + squares.shape[1:], lambda step: (step, 0, 0)),
        ],
        out_specs=[
            pl.BlockSpec((1, depth, width_out), lambda step: (step, 0, 0)),
            pl.BlockSpec((1, 2 * pixels, width), lambda step: (step, 0, 0)),
            pl.BlockSpec((1,) + squares.shape[1:], lambda step: (step, 0, 0)),
        ],
        out_shape=[
            jax.ShapeDtypeStruct((samples, depth, width_out), jnp.bfloat16),
            jax.ShapeDtypeStruct((samples, 2 * pixels, width), jnp.bfloat16),
            jax.ShapeDtypeStruct(squares.shape, jnp.float32),
        ],
        scratch_shapes=[
            pltpu.VMEM((3 * pixels, 3 * width), jnp.bfloat16),
            pltpu.VMEM((PAD_ROWS, 3 * width), jnp.float32),
        ],
        compiler_params=pltpu.CompilerParams(vmem_limit_bytes=32 * 2**20),
        name="conv_second",
    )(slabs, tans, place, kernel, cotans, squares)


def unmix_body(pieces, mix_ref, bank_ref, grad_ref, out_ref, select_ref):
    @pl.when(pl.program_id(0) == 0)
    def _():
        select_ref[...] = jnp.zeros_like(select_ref)

    kernels, _, width = bank_ref.shape
    samples = grad_ref.shape[0]
    for piece in range(pieces):
        span = slice(piece * CHUNK, (piece + 1) * CHUNK)
        grad = grad_ref[:, span, :].reshape(samples * CHUNK, width)
        mixed = dot_f32(mix_ref[...], grad, 0, 0)
        count = kernels * CHUNK
        out_ref[:, span, :] = (mixed[:count] + mixed[count:]).reshape(kernels, CHUNK, width)
        part = bank_ref[:, span, :].reshape(count, width)
        select_ref[...] += dot_f32(grad, part, 1, 1)


def unmix_kernels(mix, bank_rows, grad):
    kernels, depth, width = bank_rows.shape
    samples = grad.shape[0]
    pieces = 4
    rows = pieces * CHUNK
    return pl.pallas_call(
        lambda *refs: unmix_body(pieces, *refs),
        grid=(depth // rows,),
        in_specs=[
            pl.BlockSpec(mix.shape, lambda step: (0, 0)),
            pl.BlockSpec((kernels, rows, width), lambda step: (0, step, 0)),
            pl.BlockSpec((samples, rows, width), lambda step: (0, step, 0)),
        ],
        out_specs=[
            pl.BlockSpec((kernels, rows, width), lambda step: (0, step, 0)),
            pl.BlockSpec((samples * CHUNK, kernels * CHUNK), lambda step: (0, 0)),
        ],
        out_shape=[
            jax.ShapeDtypeStruct((kernels, depth, width), jnp.float32),
            jax.ShapeDtypeStruct((samples * CHUNK, kernels * CHUNK), jnp.float32),
        ],
        compiler_params=pltpu.CompilerParams(vmem_limit_bytes=48 * 2**20),
        name="unmix_kernels",
    )(mix, bank_rows, grad)


SWAP = ((0, 1), (1, 0))


def swap_mp(values):
    return lax.ppermute(values, "mp", SWAP)


def pick(values, index):
    return lax.dynamic_index_in_dim(values, index, 0, keepdims=False)


def own_whole(values, mp):
    mine, other = pick(values, mp), swap_mp(pick(values, 1 - mp))
    first = jnp.where(mp == 0, mine, other)
    second = jnp.where(mp == 0, other, mine)
    return jnp.concatenate([first, second], axis=-1)


def both_half(whole, mp):
    half = whole.shape[-1] // 2
    mine = lax.dynamic_slice_in_dim(whole, mp * half, half, whole.ndim - 1)
    other = swap_mp(lax.dynamic_slice_in_dim(whole, (1 - mp) * half, half, whole.ndim - 1))
    first = jnp.where(mp == 0, mine, other)
    second = jnp.where(mp == 0, other, mine)
    return jnp.stack([first, second])


def to_slabs(both):
    devices = lax.axis_size("dp")
    parts = both.reshape(2, both.shape[1], devices, -1).transpose(2, 0, 1, 3)
    parts = lax.all_to_all(parts, "dp", 0, 0, tiled=True)
    return parts.reshape(2 * devices, both.shape[1], -1)


def from_slabs(slabs, mp):
    devices = lax.axis_size("dp")
    rows = slabs.shape[1]
    parts = slabs.astype(jnp.bfloat16).reshape((devices, 2) + slabs.shape[1:])
    parts = lax.all_to_all(parts, "dp", 0, 0, tiled=True)
    parts = parts.transpose(1, 2, 0, 3).reshape(2, rows, -1)
    other = swap_mp(pick(parts, 1 - mp))
    return pick(parts, mp).astype(jnp.float32) + other.astype(jnp.float32)


PLANES = 4


class Place:
    def __init__(self):
        dp = lax.axis_index("dp")
        self.z, self.y, self.core = dp // 4, lax.rem(dp // 2, 2), lax.rem(dp, 2)
        self.x = lax.axis_index("mp")


def greet(place, axes):
    barrier = pltpu.get_barrier_semaphore()

    def tell(**there):
        at = dict(z=place.z, y=place.y, core=place.core, x=place.x)
        at.update(there)
        pl.semaphore_signal(
            barrier,
            inc=1,
            device_id=((at["z"] * 2 + at["y"]) * 2 + at["core"], at["x"]),
            device_id_type=pl.DeviceIdType.MESH,
        )

    tell(core=1 - place.core)
    count = 1
    for name in ("y", "x"):
        if name in axes:
            tell(**{name: 1 - getattr(place, name)})
            count += 1

    @pl.when(place.z > 0)
    def _():
        tell(z=place.z - 1)

    @pl.when(place.z < PLANES - 1)
    def _():
        tell(z=place.z + 1)

    between = (place.z > 0) & (place.z < PLANES - 1)
    pl.semaphore_wait(barrier, count + jnp.where(between, 2, 1))


def gather_body(pieces, inputs, outputs, axes, send_sem, recv_sem, own_sem):
    place = Place()
    greet(place, axes)
    sends = []

    def spot(z, y, core, x):
        return (z * 2 + y) * 2 + core, x

    def chip(z, y, x):
        return (z * 2 + y) * 2 + x

    def send(number, piece, source, target, slot, parity, first, condition):
        sz, sy, sx = source
        dp, mp = spot(sz, sy, place.core, sx)
        there = piece["to"](outputs, dp, mp)
        copy = pltpu.make_async_remote_copy(
            src_ref=piece["of"](inputs) if first else there,
            dst_ref=there,
            send_sem=send_sem.at[number, chip(sz, sy, sx), slot],
            recv_sem=recv_sem.at[number, chip(sz, sy, sx), parity],
            device_id=spot(*target),
            device_id_type=pl.DeviceIdType.MESH,
        )

        if condition is None:
            copy.start()
        else:
            pl.when(condition)(copy.start)
        sends.append((condition, copy))

    def onward(number, piece, source, came, first, condition):
        def both(more):
            if condition is None:
                return more
            return condition if more is None else condition & more

        order = piece["order"]
        later = order if came is None else order[order.index(came[0]) :]
        for name in later:
            here = dict(z=place.z, y=place.y, core=place.core, x=place.x)
            if name == "z":
                for way, slot in ((1, 0), (-1, 1)):
                    if came is not None and came[0] == "z" and came[1] != way:
                        continue
                    fits = place.z < PLANES - 1 if way == 1 else place.z > 0
                    target = (place.z + way, place.y, place.core, place.x)
                    send(number, piece, source, target, slot, 0, first, both(fits))
            elif came is None or came[0] != name:
                here[name] = 1 - here[name]
                target = (here["z"], here["y"], here["core"], here["x"])
                slot = 2 if name == "y" else 3
                send(number, piece, source, target, slot, 0, first, both(None))
        target = (place.z, place.y, 1 - place.core, place.x)
        send(number, piece, source, target, 4, 1, first, both(None))

    def arrive(number, piece, source, parity, condition):
        sz, sy, sx = source
        core = place.core if parity == 0 else 1 - place.core
        there = piece["to"](outputs, *spot(sz, sy, core, sx))

        def wait():
            pltpu.make_async_remote_copy(
                src_ref=there,
                dst_ref=there,
                send_sem=send_sem.at[number, chip(sz, sy, sx), 0],
                recv_sem=recv_sem.at[number, chip(sz, sy, sx), parity],
                device_id=spot(place.z, place.y, 1 - place.core, place.x),
                device_id_type=pl.DeviceIdType.MESH,
            ).wait_recv()

        if condition is None:
            wait()
        else:
            pl.when(condition)(wait)

    own = []
    for number, piece in enumerate(pieces):
        onward(number, piece, (place.z, place.y, place.x), None, True, None)
        copy = pltpu.make_async_copy(
            piece["of"](inputs),
            piece["to"](outputs, *spot(place.z, place.y, place.core, place.x)),
            own_sem.at[number],
        )
        copy.start()
        own.append(copy)
    flips = [(fy, fx) for fy in (0, 1) for fx in ((0, 1) if "x" in axes else (0,))]
    blocks = [(dz, fy, fx) for dz in (0, 1, -1, 2, -2, 3, -3) for fy, fx in flips]
    blocks = sorted(blocks, key=lambda block: abs(block[0]) + block[1] + block[2])
    for dz, fy, fx in blocks:
        if (dz, fy, fx) == (0, 0, 0):
            continue
        condition = None
        if dz > 0:
            condition = place.z >= dz
        elif dz < 0:
            condition = place.z < PLANES + dz
        source = (
            place.z - dz,
            1 - place.y if fy else place.y,
            1 - place.x if fx else place.x,
        )
        for number, piece in enumerate(pieces):
            arrive(number, piece, source, 0, condition)
            moved = dict(z=dz, y=fy, x=fx)
            last = [name for name in piece["order"] if moved[name]][-1]
            came = (last, (1 if dz > 0 else -1) if last == "z" else 0)
            onward(number, piece, source, came, False, condition)
    for number, piece in enumerate(pieces):
        for sz in range(PLANES):
            for sy in range(2):
                for sx in (0, 1) if "x" in axes else (place.x,):
                    arrive(number, piece, (sz, sy, sx), 1, None)
    for condition, copy in sends:
        if condition is None:
            copy.wait_send()
        else:
            pl.when(condition)(copy.wait_send)
    for copy in own:
        copy.wait()


def gather_call(pieces, axes, arrays, shapes, call_id, name):
    count = len(arrays)

    def body(*refs):
        inputs, outputs = refs[:count], refs[count : count + len(shapes)]
        gather_body(pieces, inputs, outputs, axes, *refs[count + len(shapes) :])

    return pl.pallas_call(
        body,
        in_specs=[pl.BlockSpec(memory_space=pl.ANY)] * count,
        out_specs=[pl.BlockSpec(memory_space=pl.ANY)] * len(shapes),
        out_shape=[jax.ShapeDtypeStruct(shape, jnp.bfloat16) for shape in shapes],
        scratch_shapes=[
            pltpu.SemaphoreType.DMA((len(pieces), 16, 5)),
            pltpu.SemaphoreType.DMA((len(pieces), 16, 2)),
            pltpu.SemaphoreType.DMA((len(pieces),)),
        ],
        compiler_params=pltpu.CompilerParams(collective_id=call_id, has_side_effects=True),
        name=name,
    )(*arrays)


def rows_at(index, rows):
    return pl.ds(pl.multiple_of(index * rows, rows), rows)


def lanes_at(index, lanes):
    return pl.ds(pl.multiple_of(index * lanes, lanes), lanes)


def gather_weights(stacks, call_id):
    def piece(number, first, last, order):
        rows, lanes = stacks[number].shape[1:]
        return dict(
            order=order,
            of=lambda refs: refs[number].at[first:last],
            to=lambda refs, dp, mp: refs[number].at[
                first:last, rows_at(dp, rows), lanes_at(mp, lanes)
            ],
        )

    pieces = [
        piece(0, 0, 2, ("x", "y", "z")),
        piece(0, 2, 5, ("z", "x", "y")),
        piece(1, 0, 2, ("z", "y", "x")),
        piece(2, 0, 1, ("z", "x", "y")),
        piece(2, 1, 2, ("z", "y", "x")),
    ]
    shapes = [(a.shape[0], a.shape[1] * 16, a.shape[2] * 2) for a in stacks]
    return gather_call(pieces, ("z", "y", "x"), stacks, shapes, call_id, "gather_weights")


def gather_dp(values, call_id):
    samples, rows, lanes = values.shape

    def piece(sample, first, last, order):
        return dict(
            order=order,
            of=lambda refs: refs[0].at[sample, :, first:last],
            to=lambda refs, dp, mp: refs[0].at[dp * samples + sample, :, first:last],
        )

    cut = lanes * 3 // 4
    pieces = [piece(sample, 0, cut, ("z", "y")) for sample in range(samples)]
    pieces += [piece(sample, cut, lanes, ("y", "z")) for sample in range(samples)]
    shapes = [(16 * samples, rows, lanes)]
    return gather_call(pieces, ("z", "y"), [values], shapes, call_id, "gather_samples")[0]


def add_rows(total, part):
    shape = total.shape[:-2]
    for number in range(int(np.prod(shape))):
        spot = tuple(int(place) for place in np.unravel_index(number, shape))
        total[spot] = (total[spot].astype(jnp.float32) + part[spot].astype(jnp.float32)).astype(
            jnp.bfloat16
        )


def sum_body(
    cut,
    part_ref,
    out_ref,
    acc,
    core_in,
    y_in,
    y_last,
    z_first,
    z_second,
    x_in,
    load_sem,
    core_send,
    core_recv,
    y_send,
    y_recv,
    z_send,
    z_recv,
    x_send,
    x_recv,
):
    place = Place()
    greet(place, ("z", "y", "x"))
    z, y, x = place.z, place.y, place.x
    wide, narrow = slice(0, cut), slice(cut, acc.shape[-1])
    finish = []

    def spot(z, y, core, x):
        return (z * 2 + y) * 2 + core, x

    def remote(source, target, send, recv, device):
        return pltpu.make_async_remote_copy(
            src_ref=source,
            dst_ref=target,
            send_sem=send,
            recv_sem=recv,
            device_id=spot(*device),
            device_id_type=pl.DeviceIdType.MESH,
        )

    other_core = (z, y, 1 - place.core, x)
    other_y = (z, 1 - y, place.core, x)
    other_x = (z, y, place.core, 1 - x)

    chunks = [(dest, 1 - y) for dest in (3, 0, 2, 1)] + [(dest, y) for dest in (3, 0, 2, 1)]
    first = []
    for number, (dest, side) in enumerate(chunks):
        sent = remote(
            part_ref.at[dest, side, 1 - place.core],
            core_in.at[dest, side],
            core_send.at[number],
            core_recv.at[number],
            other_core,
        )
        sent.start()
        mine = pltpu.make_async_copy(
            part_ref.at[dest, side, place.core], acc.at[dest, side], load_sem.at[number]
        )
        mine.start()
        first.append((sent, mine))

    y_copies = []
    for number, (dest, side) in enumerate(chunks):
        sent, mine = first[number]
        mine.wait()
        sent.wait_recv()
        add_rows(acc.at[dest, side], core_in.at[dest, side])
        finish.append(sent)
        if number < 4:
            copy = remote(
                acc.at[dest, side, :, :, wide],
                y_in.at[dest],
                y_send.at[dest],
                y_recv.at[dest],
                other_y,
            )
            copy.start()
            y_copies.append(copy)

    def along_z(slot, view, landing, dest):
        for way in (0, 1):
            near = dest > z if way == 0 else dest < z
            has_before = z > 0 if way == 0 else z < PLANES - 1
            copy = remote(
                view,
                landing.at[way, dest],
                z_send.at[slot, way, dest],
                z_recv.at[slot, way, dest],
                (z + (1 if way == 0 else -1), y, place.core, x),
            )

            @pl.when(near & has_before)
            def _():
                copy.wait_recv()
                add_rows(view, landing.at[way, dest])

            pl.when(near)(copy.start)
            finish.append((near, copy))

    def end_z(slot, view, landing):
        for way in (0, 1):
            copy = remote(
                view,
                landing.at[way, z],
                z_send.at[slot, way, z],
                z_recv.at[slot, way, z],
                other_core,
            )

            @pl.when(z > 0 if way == 0 else z < PLANES - 1)
            def _():
                copy.wait_recv()
                add_rows(view, landing.at[way, z])

    for number, dest in enumerate((3, 0, 2, 1)):
        along_z(1, acc.at[dest, :, :, :, narrow], z_second, dest)
        y_copies[number].wait_recv()
        finish.append(y_copies[number])
        view = acc.at[dest, y, :, :, wide]
        add_rows(view, y_in.at[dest])
        along_z(0, view, z_first, dest)
    end_z(1, acc.at[z, :, :, :, narrow], z_second)
    last = remote(
        acc.at[z, 1 - y, :, :, narrow], y_last, y_send.at[PLANES], y_recv.at[PLANES], other_y
    )
    last.start()
    finish.append(last)
    end_z(0, acc.at[z, y, :, :, wide], z_first)
    last.wait_recv()
    add_rows(acc.at[z, y, :, :, narrow], y_last)
    swap = remote(acc.at[z, y, 1 - x], x_in, x_send, x_recv, other_x)
    swap.start()
    lanes = acc.shape[-1]
    out_ref[:, lanes_at(x, lanes)] = acc[z, y, x]
    swap.wait_recv()
    out_ref[:, lanes_at(1 - x, lanes)] = x_in[...]
    finish.append(swap)
    for item in finish:
        if isinstance(item, tuple):
            pl.when(item[0])(item[1].wait_send)
        else:
            item.wait_send()


def sum_samples(partial, call_id):
    samples, rows, lanes = partial.shape
    cut = lanes * 3 // 4
    bf16, dma = jnp.bfloat16, pltpu.SemaphoreType.DMA
    return pl.pallas_call(
        lambda *refs: sum_body(cut, *refs),
        in_specs=[pl.BlockSpec(memory_space=pl.ANY)],
        out_specs=pl.BlockSpec(memory_space=pltpu.VMEM),
        out_shape=jax.ShapeDtypeStruct((rows, 2 * lanes), bf16),
        scratch_shapes=[
            pltpu.VMEM((PLANES, 2, 2, rows, lanes), bf16),
            pltpu.VMEM((PLANES, 2, 2, rows, lanes), bf16),
            pltpu.VMEM((PLANES, 2, rows, cut), bf16),
            pltpu.VMEM((2, rows, lanes - cut), bf16),
            pltpu.VMEM((2, PLANES, 2, rows, cut), bf16),
            pltpu.VMEM((2, PLANES, 2, 2, rows, lanes - cut), bf16),
            pltpu.VMEM((rows, lanes), bf16),
            dma((8,)),
            dma((8,)),
            dma((8,)),
            dma((PLANES + 1,)),
            dma((PLANES + 1,)),
            dma((2, 2, PLANES)),
            dma((2, 2, PLANES)),
            dma,
            dma,
        ],
        compiler_params=pltpu.CompilerParams(
            collective_id=call_id, has_side_effects=True, vmem_limit_bytes=40 * 2**20
        ),
        name="sum_samples",
    )(partial.reshape(PLANES, 2, 2, 2, rows, lanes))


def sum_weights_body(parts, count, refs):
    inputs, outputs, rest = refs[:count], refs[count : 2 * count], refs[2 * count :]
    acc, core_in, one_in, two_in, z_in = (rest[k * count : (k + 1) * count] for k in range(5))
    (
        load_sem,
        core_send,
        core_recv,
        one_send,
        one_recv,
        two_send,
        two_recv,
        z_send,
        z_recv,
    ) = rest[5 * count :]
    place = Place()
    greet(place, ("z", "y", "x"))
    z, y, x = place.z, place.y, place.x
    order = (3, 0, 2, 1)
    finish = []

    def remote(source, target, send, recv, device):
        dz, dy, core, dx = device
        return pltpu.make_async_remote_copy(
            src_ref=source,
            dst_ref=target,
            send_sem=send,
            recv_sem=recv,
            device_id=((dz * 2 + dy) * 2 + core, dx),
            device_id_type=pl.DeviceIdType.MESH,
        )

    other_core = (z, y, 1 - place.core, x)
    other_y = (z, 1 - y, place.core, x)
    other_x = (z, y, place.core, 1 - x)
    sides = (1 - y, y)

    first = {}
    for dest in order:
        for w in range(count):
            rows = acc[w].shape[2]
            for turn, side in enumerate(sides):
                at = ((dest * 2 + side) * 2 + (1 - place.core)) * rows
                mine = ((dest * 2 + side) * 2 + place.core) * rows
                sent = remote(
                    inputs[w].at[pl.ds(pl.multiple_of(at, rows), rows)],
                    core_in[w].at[dest, side],
                    core_send.at[w, dest, turn],
                    core_recv.at[w, dest, turn],
                    other_core,
                )
                sent.start()
                load = pltpu.make_async_copy(
                    inputs[w].at[pl.ds(pl.multiple_of(mine, rows), rows)],
                    acc[w].at[dest, side],
                    load_sem.at[w, dest, turn],
                )
                load.start()
                first[w, dest, turn] = (sent, load)

    def half(w, index):
        lanes = acc[w].shape[-1] // 2
        return lanes_at(index, lanes)

    ones, twos = {}, {}

    def stage_one(dest):
        for w in range(count):
            for turn, side in enumerate(sides):
                sent, load = first[w, dest, turn]
                load.wait()
                sent.wait_recv()
                finish.append((None, sent))
                add_rows(acc[w].at[dest, side], core_in[w].at[dest, side])
                if parts[w] == "xy":
                    copy = remote(
                        acc[w].at[dest, side, :, half(w, 1 - x)],
                        one_in[w].at[dest, side],
                        one_send.at[w, dest, turn],
                        one_recv.at[w, dest, turn],
                        other_x,
                    )
                elif turn == 0:
                    copy = remote(
                        acc[w].at[dest, side],
                        one_in[w].at[dest],
                        one_send.at[w, dest, turn],
                        one_recv.at[w, dest, turn],
                        other_y,
                    )
                else:
                    continue
                copy.start()
                ones[w, dest, turn] = copy

    def stage_two(dest):
        for w in range(count):
            if parts[w] == "xy":
                for turn, side in enumerate(sides):
                    copy = ones[w, dest, turn]
                    copy.wait_recv()
                    finish.append((None, copy))
                    view = acc[w].at[dest, side, :, half(w, x)]
                    add_rows(view, one_in[w].at[dest, side])
                    if turn == 0:
                        twos[w, dest] = remote(
                            view,
                            two_in[w].at[dest],
                            two_send.at[w, dest],
                            two_recv.at[w, dest],
                            other_y,
                        )
                        twos[w, dest].start()
            else:
                copy = ones[w, dest, 0]
                copy.wait_recv()
                finish.append((None, copy))
                add_rows(acc[w].at[dest, y], one_in[w].at[dest])
                twos[w, dest] = remote(
                    acc[w].at[dest, y, :, half(w, 1 - x)],
                    two_in[w].at[dest],
                    two_send.at[w, dest],
                    two_recv.at[w, dest],
                    other_x,
                )
                twos[w, dest].start()

    def z_copy(w, dest, way):
        return remote(
            acc[w].at[dest, y, :, half(w, x)],
            z_in[w].at[way, dest],
            z_send.at[w, way, dest],
            z_recv.at[w, way, dest],
            (z + (1 if way == 0 else -1), y, place.core, x),
        )

    def stage_z(dest):
        for w in range(count):
            copy = twos[w, dest]
            copy.wait_recv()
            finish.append((None, copy))
            view = acc[w].at[dest, y, :, half(w, x)]
            add_rows(view, two_in[w].at[dest])
            for way in (0, 1):
                near = dest > z if way == 0 else dest < z
                has_before = z > 0 if way == 0 else z < PLANES - 1
                copy = z_copy(w, dest, way)

                @pl.when(near & has_before)
                def _():
                    copy.wait_recv()
                    add_rows(view, z_in[w].at[way, dest])

                pl.when(near)(copy.start)
                finish.append((near, copy))

    for turn in range(PLANES + 2):
        if turn < PLANES:
            stage_one(order[turn])
        if 0 <= turn - 1 < PLANES:
            stage_two(order[turn - 1])
        if turn >= 2:
            stage_z(order[turn - 2])
    for w in range(count):
        view = acc[w].at[z, y, :, half(w, x)]
        for way in (0, 1):

            @pl.when(z > 0 if way == 0 else z < PLANES - 1)
            def _():
                remote(
                    view,
                    z_in[w].at[way, z],
                    z_send.at[w, way, z],
                    z_recv.at[w, way, z],
                    other_core,
                ).wait_recv()
                add_rows(view, z_in[w].at[way, z])

        outputs[w][...] = acc[w][z, y, :, half(w, x)].astype(jnp.float32)
    for condition, copy in finish:
        if condition is None:
            copy.wait_send()
        else:
            pl.when(condition)(copy.wait_send)


def sum_weights(grads, parts, call_id):
    count = len(grads)
    bf16, dma = jnp.bfloat16, pltpu.SemaphoreType.DMA
    blocks = [(grad.shape[0] // 16, grad.shape[1]) for grad in grads]
    ones = [
        (PLANES, 2, rows, lanes // 2) if part == "xy" else (PLANES, rows, lanes)
        for (rows, lanes), part in zip(blocks, parts)
    ]
    return pl.pallas_call(
        lambda *refs: sum_weights_body(parts, count, refs),
        in_specs=[pl.BlockSpec(memory_space=pl.ANY)] * count,
        out_specs=[pl.BlockSpec(memory_space=pltpu.VMEM)] * count,
        out_shape=[
            jax.ShapeDtypeStruct((rows, lanes // 2), jnp.float32) for rows, lanes in blocks
        ],
        scratch_shapes=[pltpu.VMEM((PLANES, 2, rows, lanes), bf16) for rows, lanes in blocks]
        + [pltpu.VMEM((PLANES, 2, rows, lanes), bf16) for rows, lanes in blocks]
        + [pltpu.VMEM(shape, bf16) for shape in ones]
        + [pltpu.VMEM((PLANES, rows, lanes // 2), bf16) for rows, lanes in blocks]
        + [pltpu.VMEM((2, PLANES, rows, lanes // 2), bf16) for rows, lanes in blocks]
        + [dma((count, PLANES, 2))] * 5
        + [dma((count, PLANES))] * 2
        + [dma((count, 2, PLANES))] * 2,
        compiler_params=pltpu.CompilerParams(
            collective_id=call_id, has_side_effects=True, vmem_limit_bytes=60 * 2**20
        ),
        name="sum_weights",
    )(*grads)


def sample_parallel(
    layer_input,
    labels,
    text_ids,
    noise_seeds,
    penalty_mask,
    class_table,
    token_table,
    sel_weight,
    mod_weight,
    rgb_mod,
    rgb_weight,
    conv_bias,
    noise_strength,
    kernel_bank,
    qk_weight,
    value_weight,
    attn_out,
    cross_query,
    cross_key,
    cross_value,
    cross_out,
    mlp_in,
    mlp_out,
    cot_feat,
    cot_rgb,
    penalty_dir,
):
    mp = lax.axis_index("mp")
    dp = lax.axis_index("dp")
    half_px = layer_input.shape[1]
    slab = kernel_bank.shape[2]
    width_out = kernel_bank.shape[3]
    float32, bfloat16 = jnp.float32, jnp.bfloat16

    stack_attn, stack_text, stack_mlp = gather_weights(
        [
            jnp.stack([qk_weight, value_weight, attn_out.T, cross_query, cross_out.T]),
            jnp.stack([cross_key, cross_value]),
            jnp.stack([mlp_in, mlp_out.T]),
        ],
        1,
    )
    weights = (
        stack_attn[0],
        stack_attn[1],
        stack_attn[2],
        stack_attn[3],
        stack_text[0],
        stack_text[1],
        stack_attn[4],
        stack_mlp[0],
        stack_mlp[1],
    )

    labels_all = lax.all_gather(labels, "dp", axis=0, tiled=True)
    sample_count = labels_all.shape[0]
    classes = jnp.arange(class_table.shape[0], dtype=jnp.int32)
    onehot_class = (labels_all[:, None] == classes[None, :]).astype(bfloat16)
    latent = dot_wide(onehot_class, class_table, 1, 0)
    select_all, select_pull = jax.vjp(last_softmax, dot_wide(latent, sel_weight, 1, 0))
    scales_all = 1.0 + dot_wide(latent, mod_weight, 1, 0)
    rgb_scales_all = 1.0 + dot_wide(latent, rgb_mod, 1, 0)
    me = 2 * dp + mp
    scales = pick(scales_all, me)
    rgb_scales = pick(rgb_scales_all, me)
    scales_slab = lax.dynamic_slice_in_dim(scales_all, dp * slab, slab, 1)
    words = jnp.arange(token_table.shape[0], dtype=jnp.int32)
    text_own = pick(text_ids, mp)
    text_rows = dot_wide((text_own[:, None] == words[None, :]).astype(bfloat16), token_table, 1, 0)
    noise = noise_field(pick(noise_seeds, mp)[None], SIDE * SIDE)[0]
    small = (
        conv_bias.astype(float32),
        noise_strength.astype(float32),
        rgb_scales,
        rgb_weight.astype(float32),
    )

    bank_rows = kernel_bank.reshape(kernel_bank.shape[0], 9 * slab, width_out)
    mix = mix_matrix(select_all)
    scales_two = jnp.broadcast_to(
        (scales_slab * scales_slab)[:, :, None], (sample_count, slab, 128)
    )
    kernel, sums_part = mix_kernels(mix, bank_rows, scales_two)
    place = placing(SIDE // 2)

    input_own = own_whole(layer_input, mp).astype(float32)
    scales_pair = lax.dynamic_slice_in_dim(scales_all, 2 * dp, 2, 0)
    input_pair = lax.all_gather(layer_input, "mp", axis=2, tiled=True).astype(float32)
    slabs_x = to_slabs((input_pair * scales_pair[:, None, :]).astype(bfloat16))
    partial = convolve(slabs_x, place, kernel, sums_part, True)
    summed = sum_samples(partial, 4).astype(float32)
    conv_out, sums = summed[:PIXELS], summed[PIXELS]

    (hidden_four, picture), pull = jax.vjp(
        lambda value: layer_forward(value, sums, text_rows, small, weights, noise), conv_out
    )

    dir_own = pick(penalty_dir, mp).astype(float32)
    grad_conv = pull((jnp.zeros_like(hidden_four), dir_own))[0]
    grads_all = gather_dp(both_half(grad_conv.astype(bfloat16), mp), 2)

    grad_moduled = from_slabs(conv_back(grads_all, place, kernel, half_px, slab), mp)
    mask_own = pick(penalty_mask, mp).astype(float32)
    tangent = penalty_weight * mask_own * grad_moduled.astype(bfloat16).astype(float32) * scales

    tan_moduled = (tangent * scales).astype(bfloat16)
    tan_other = swap_mp(tan_moduled)
    tan_pair = jnp.stack(
        [jnp.where(mp == 0, tan_moduled, tan_other), jnp.where(mp == 0, tan_other, tan_moduled)]
    )
    slabs_t = to_slabs(tan_pair)
    conv_tan = sum_samples(convolve(slabs_t, place, kernel, sums_part, False), 5).astype(float32)

    (ignored_out, ignored_pic, ignored_tan), pull_joint = jax.vjp(
        lambda *given: layer_joint(*given, noise),
        conv_out,
        conv_tan,
        sums,
        text_rows,
        small,
        weights,
    )
    cot_own = own_whole(cot_feat, mp).astype(float32)
    grad_main, grad_side, grad_sums, grad_text, grad_small, grad_weights = pull_joint(
        (cot_own, pick(cot_rgb, mp).astype(float32), dir_own)
    )

    orders = ("xy", "yx", "xy", "yx", "xy", "yx", "yx", "xy", "xy")
    d_qk, d_value, d_attn, d_query, d_key, d_cval, d_cout, d_mlp, d_mout = grad_weights
    mlp_grad, mout_grad, qk_grad, value_grad, attn_grad, query_grad, cout_grad, key_grad, cval_grad = (
        sum_weights(
            [d_mlp, d_mout, d_qk, d_value, d_attn, d_query, d_cout, d_key, d_cval], orders, 6
        )
    )
    big_sums = (
        qk_grad,
        value_grad,
        attn_grad.T,
        query_grad,
        key_grad,
        cval_grad,
        cout_grad.T,
        mlp_grad,
        mout_grad.T,
    )

    lines = jnp.broadcast_to(grad_sums[None], (CHUNK,) + grad_sums.shape)
    wide = jnp.concatenate(
        [grad_main.astype(bfloat16), grad_side.astype(bfloat16), lines.astype(bfloat16)], axis=0
    )
    wide_all = gather_dp(both_half(wide, mp), 3)
    grad_kernel, both_back, scale_sums = conv_second(
        slabs_x, slabs_t, place, kernel, wide_all, scales_two
    )
    grad_scales_slab = 2.0 * scales_slab * scale_sums[:, :, 0]
    bank_grad, select_products = unmix_kernels(mix, bank_rows, grad_kernel)
    bank_grad = bank_grad.reshape(kernel_bank.shape)
    grad_select = jnp.einsum(
        "brkr->bk", select_products.reshape(sample_count, CHUNK, -1, CHUNK)
    )
    both_back = from_slabs(both_back, mp).astype(bfloat16).astype(float32)
    back_main, back_side = both_back[:half_px], both_back[half_px:]
    input_grad = back_main * scales
    grad_scales = jnp.sum(back_main * input_own + back_side * tangent, axis=0)

    grad_bias, grad_strength, grad_rgb_scales, grad_rgb_weight = grad_small
    row = jnp.concatenate(
        [
            grad_scales,
            grad_rgb_scales,
            grad_rgb_weight.reshape(-1),
            grad_bias,
            grad_strength,
            grad_scales_slab.reshape(-1),
            grad_select.reshape(-1),
        ]
    ).reshape(-1, 128)
    rows_all = lax.all_gather(row, ("dp", "mp"), axis=0, tiled=False).reshape(sample_count, -1)
    channels = scales.shape[0]
    scale_terms = rows_all[:, :channels]
    rgb_terms = rows_all[:, channels : 2 * channels]
    sums_all = jnp.sum(rows_all[:, 2 * channels : 7 * channels], axis=0)
    slab_terms = rows_all[:, 7 * channels : 7 * channels + sample_count * slab]
    slab_terms = slab_terms.reshape(-1, 2, sample_count, slab).sum(axis=1)
    scale_terms = scale_terms + slab_terms.transpose(1, 0, 2).reshape(sample_count, channels)
    select_terms = jnp.sum(rows_all[:, 7 * channels + sample_count * slab :], axis=0)
    logit_terms = select_pull(select_terms.reshape(sample_count, -1))[0]
    latent_terms = (
        matmul_high(scale_terms, mod_weight.astype(float32).T)
        + matmul_high(rgb_terms, rgb_mod.astype(float32).T)
        + matmul_high(logit_terms, sel_weight.astype(float32).T)
    )
    class_grad = matmul_high(onehot_class.astype(float32).T, latent_terms)
    sel_grad = matmul_high(latent.T, logit_terms)
    mod_grad = matmul_high(latent.T, scale_terms)
    rgb_mod_grad = matmul_high(latent.T, rgb_terms)
    text_all = lax.all_gather(grad_text.astype(bfloat16), ("dp", "mp"), axis=0, tiled=True)
    ids_all = lax.all_gather(text_ids, "dp", axis=0, tiled=True).reshape(-1)
    token_grad = dot_wide((ids_all[:, None] == words[None, :]).astype(bfloat16), text_all, 0, 0)

    picture_other = swap_mp(picture)
    pictures = jnp.stack(
        [jnp.where(mp == 0, picture, picture_other), jnp.where(mp == 0, picture_other, picture)]
    )
    return (
        both_half(hidden_four, mp),
        pictures,
        both_half(input_grad, mp),
        class_grad,
        token_grad,
        sel_grad,
        mod_grad,
        rgb_mod_grad,
        sums_all[: 3 * channels].reshape(3, channels),
        sums_all[3 * channels : 4 * channels],
        sums_all[4 * channels :],
        bank_grad,
    ) + big_sums


def solution(mesh):
    in_specs = (
        P("dp", None, "mp"),
        P("dp"),
        P("dp", None),
        P("dp"),
        P("dp"),
        P(),
        P(),
        P(),
        P(),
        P(),
        P(),
        P(),
        P(),
        P(None, None, "dp", "mp"),
        P("dp", "mp"),
        P("dp", "mp"),
        P("mp", "dp"),
        P("dp", "mp"),
        P("dp", "mp"),
        P("dp", "mp"),
        P("mp", "dp"),
        P("dp", "mp"),
        P("mp", "dp"),
        P("dp", None, "mp"),
        P("dp", None, None),
        P("dp", None, None),
    )
    out_specs = (
        P("dp", None, "mp"),
        P("dp", None, None),
        P("dp", None, "mp"),
        P(),
        P(),
        P(),
        P(),
        P(),
        P(),
        P(),
        P(),
        P(None, None, "dp", "mp"),
        P("dp", "mp"),
        P("dp", "mp"),
        P("mp", "dp"),
        P("dp", "mp"),
        P("dp", "mp"),
        P("dp", "mp"),
        P("mp", "dp"),
        P("dp", "mp"),
        P("mp", "dp"),
    )
    return jax.shard_map(
        sample_parallel if fits_samples(mesh) else tensor_parallel,
        mesh=mesh, in_specs=in_specs, out_specs=out_specs, check_vma=False
    )
```

```python
import jax
import jax.numpy as jnp
import numpy as np
from jax import lax
from jax.experimental import pallas as pl
from jax.experimental.pallas import tpu as pltpu
from jax.sharding import PartitionSpec as P

HEAD = 64
SIDE = 16


penalty_weight = 1.0


def rounded(values):
    return lax.optimization_barrier(values.astype(jnp.bfloat16)).astype(jnp.float32)


def matmul_high(left, right):
    return jnp.matmul(left, right, precision=lax.Precision.HIGHEST)


def einsum_high(form, *operands):
    return jnp.einsum(form, *operands, precision=lax.Precision.HIGHEST)


def einsum_low(form, left, right):
    return jnp.einsum(
        form,
        left.astype(jnp.bfloat16),
        right.astype(jnp.bfloat16),
        preferred_element_type=jnp.float32,
    )


def noise_field(seed_ids, pixel_count):
    pixel_ids = jnp.arange(pixel_count, dtype=jnp.int32)
    mixed = seed_ids[:, None] * 1103515245 + pixel_ids[None, :] * 40503
    mixed = jnp.bitwise_xor(mixed, jnp.right_shift(mixed, 13)) * 1664525 + 1013904223
    levels = jnp.bitwise_and(jnp.right_shift(mixed, 8), 65535)
    return levels.astype(jnp.float32) / 65536.0 - 0.5


def patches_of(flat_rows, side_len):
    samples_here, pixels, width_here = flat_rows.shape
    half_side = side_len // 2
    picture = flat_rows.reshape(samples_here, half_side, half_side, width_here)
    picture = jnp.repeat(jnp.repeat(picture, 2, axis=1), 2, axis=2)
    padded = jnp.pad(picture, ((0, 0), (1, 1), (1, 1), (0, 0)))
    pieces = [
        padded[:, shift_row : shift_row + side_len, shift_col : shift_col + side_len, :]
        for shift_row in range(3)
        for shift_col in range(3)
    ]
    return jnp.concatenate(pieces, axis=-1).reshape(
        samples_here, side_len * side_len, 9 * width_here
    )


def rms_norm(values):
    return values * lax.rsqrt(jnp.mean(values * values, axis=-1, keepdims=True) + 1e-06)


def conv_part(gathered, kernel, scales, bias_local, strength_local, noise_map):
    samples_here = gathered.shape[0]
    width_out = kernel.shape[2]
    columns = patches_of(gathered, SIDE)
    conv_out = einsum_low("bpr,bro->bpo", columns, kernel)
    squares = jnp.sum((kernel * kernel).reshape(samples_here, 9, -1, width_out), axis=1)
    demodulate = lax.rsqrt(einsum_high("bi,bio->bo", scales * scales, squares) + 1e-08)
    before = conv_out * demodulate[:, None, :] + bias_local + noise_map[:, :, None] * strength_local
    return jax.nn.silu(before)


def self_attention(active, qk_w, value_w, out_w):
    normed = rounded(rms_norm(active))
    queries = rounded(matmul_high(normed, qk_w))
    values = rounded(matmul_high(normed, value_w))
    samples_here, pixels, width_here = queries.shape
    heads_here = width_here // HEAD
    q_heads = queries.reshape(samples_here, pixels, heads_here, HEAD)
    v_heads = values.reshape(samples_here, pixels, heads_here, HEAD)
    lengths = jnp.transpose(jnp.sum(q_heads * q_heads, axis=-1), (0, 2, 1))
    scores = (
        2.0 * einsum_low("bphd,bqhd->bhpq", q_heads, q_heads) - lengths[:, :, None, :]
    ) * HEAD ** (-0.5)
    soft_weights = rounded(jax.nn.softmax(scores, axis=-1))
    mixture = rounded(
        einsum_low("bhpq,bqhd->bphd", soft_weights, v_heads).reshape(
            samples_here, pixels, width_here
        )
    )
    return matmul_high(mixture, out_w)


def cross_attention(active, text_rows, query_w, key_w, value_w, out_w):
    normed = rounded(rms_norm(active))
    queries = rounded(matmul_high(normed, query_w))
    key_rows = rounded(matmul_high(text_rows, key_w))
    values = rounded(matmul_high(text_rows, value_w))
    samples_here, pixels, width_here = queries.shape
    tokens = key_rows.shape[1]
    heads_here = width_here // HEAD
    q_heads = queries.reshape(samples_here, pixels, heads_here, HEAD)
    k_heads = key_rows.reshape(samples_here, tokens, heads_here, HEAD)
    v_heads = values.reshape(samples_here, tokens, heads_here, HEAD)
    scores = einsum_low("bphd,bthd->bhpt", q_heads, k_heads) * HEAD ** (-0.5)
    soft_weights = rounded(jax.nn.softmax(scores, axis=-1))
    mixture = rounded(
        einsum_low("bhpt,bthd->bphd", soft_weights, v_heads).reshape(
            samples_here, pixels, width_here
        )
    )
    return matmul_high(mixture, out_w)


def feed_forward(active, weight_in, weight_out):
    normed = rounded(rms_norm(active))
    inner = rounded(jax.nn.gelu(matmul_high(normed, weight_in)))
    return matmul_high(inner, weight_out)


def tree_add(first, second):
    return jax.tree.map(jnp.add, first, second)


def tensor_parallel(
    layer_input,
    labels,
    text_ids,
    noise_seeds,
    penalty_mask,
    class_table,
    token_table,
    sel_weight,
    mod_weight,
    rgb_mod,
    rgb_weight,
    conv_bias,
    noise_strength,
    kernel_bank,
    qk_weight,
    value_weight,
    attn_out,
    cross_query,
    cross_key,
    cross_value,
    cross_out,
    mlp_in,
    mlp_out,
    cot_feat,
    cot_rgb,
    penalty_dir,
):
    width_local = layer_input.shape[2]
    offset = lax.axis_index("mp") * width_local
    small_params = tuple(
        (
            entry.astype(jnp.float32)
            for entry in (
                class_table,
                token_table,
                sel_weight,
                mod_weight,
                rgb_mod,
                rgb_weight,
                conv_bias,
                noise_strength,
            )
        )
    )

    def fetch_proj():
        fetched = (
            lax.all_gather(qk_weight, "dp", axis=0, tiled=True),
            lax.all_gather(value_weight, "dp", axis=0, tiled=True),
            lax.all_gather(attn_out, "dp", axis=1, tiled=True),
            lax.all_gather(cross_query, "dp", axis=0, tiled=True),
            lax.all_gather(cross_key, "dp", axis=0, tiled=True),
            lax.all_gather(cross_value, "dp", axis=0, tiled=True),
            lax.all_gather(cross_out, "dp", axis=1, tiled=True),
            lax.all_gather(mlp_in, "dp", axis=0, tiled=True),
            lax.all_gather(mlp_out, "dp", axis=1, tiled=True),
        )
        return tuple((entry.astype(jnp.float32) for entry in fetched))

    def style_part(param_set):
        table_class, table_word, select_w, modul_w, rgbmod_w, rgbout_w, bias_w, strength_w = (
            param_set
        )
        onehot_class = (
            labels[:, None] == jnp.arange(table_class.shape[0], dtype=jnp.int32)[None, :]
        ).astype(jnp.float32)
        latent = matmul_high(onehot_class, table_class)
        onehot_word = (
            text_ids[:, :, None] == jnp.arange(table_word.shape[0], dtype=jnp.int32)
        ).astype(jnp.float32)
        text_rows = matmul_high(onehot_word, table_word)
        select = jax.nn.softmax(matmul_high(latent, select_w), axis=-1)
        scales = 1.0 + matmul_high(latent, modul_w)
        rgb_scales = 1.0 + matmul_high(
            latent, lax.dynamic_slice_in_dim(rgbmod_w, offset, width_local, 1)
        )
        bias_local = lax.dynamic_slice_in_dim(bias_w, offset, width_local, 0)
        strength_local = lax.dynamic_slice_in_dim(strength_w, offset, width_local, 0)
        colour_local = lax.dynamic_slice_in_dim(rgbout_w, offset, width_local, 1)
        return (select, scales, rgb_scales, text_rows, bias_local, strength_local, colour_local)

    styles, style_pull = jax.vjp(style_part, small_params)
    noise_map = noise_field(noise_seeds, SIDE * SIDE)

    def owned_sets():
        proj_set = fetch_proj()
        conv_set = (lax.all_gather(kernel_bank, "dp", axis=2, tiled=True).astype(jnp.float32),)
        return ((), conv_set, proj_set[0:3], proj_set[3:7], proj_set[7:9], ())

    def seg_in(active, styles_in, own_set):
        return active * lax.dynamic_slice_in_dim(styles_in[1], offset, width_local, 1)[:, None, :]

    def seg_conv(active, styles_in, own_set):
        bank_full = own_set[0]
        kernel = rounded(matmul_high(styles_in[0], bank_full.reshape(bank_full.shape[0], -1)))
        kernel = kernel.reshape(active.shape[0], -1, bank_full.shape[3])
        return conv_part(active, kernel, styles_in[1], styles_in[4], styles_in[5], noise_map)

    def seg_self(active, styles_in, own_set):
        return self_attention(active, own_set[0], own_set[1], own_set[2])

    def seg_cross(active, styles_in, own_set):
        return cross_attention(active, styles_in[3], own_set[0], own_set[1], own_set[2], own_set[3])

    def seg_mlp(active, styles_in, own_set):
        return feed_forward(active, own_set[0], own_set[1])

    def seg_rgb(active, styles_in, own_set):
        return einsum_high("bpc,bc,kc->bkp", active, styles_in[2], styles_in[6])

    def spread(stacked):
        return lax.all_gather(stacked, "mp", axis=3, tiled=True)

    def collect(stacked):
        return lax.psum_scatter(
            stacked.astype(jnp.bfloat16), "mp", scatter_dimension=3, tiled=True
        ).astype(jnp.float32)

    def spread_one(values):
        return spread(values.astype(jnp.bfloat16)[None])[0].astype(jnp.float32)

    def collect_one(values):
        return collect(values[None])[0]

    own_first = owned_sets()
    input_full = layer_input.astype(jnp.float32)
    gathered_x = spread_one(seg_in(input_full, styles, own_first[0]))
    hidden_one = seg_conv(gathered_x, styles, own_first[1])
    gathered_one = spread_one(hidden_one)
    hidden_two = hidden_one + collect_one(seg_self(gathered_one, styles, own_first[2]))
    gathered_two = spread_one(hidden_two)
    hidden_three = hidden_two + collect_one(seg_cross(gathered_two, styles, own_first[3]))
    gathered_three = spread_one(hidden_three)
    hidden_four = hidden_three + collect_one(seg_mlp(gathered_three, styles, own_first[4]))
    picture = lax.psum(seg_rgb(hidden_four, styles, own_first[5]), "mp")
    own_second = owned_sets()

    def pull_act(segment, active, own_set, cotan):
        return jax.vjp(lambda inner_x: segment(inner_x, styles, own_set), active)[1](cotan)[0]

    grad_four = pull_act(seg_rgb, hidden_four, own_second[5], penalty_dir.astype(jnp.float32))
    back_three = pull_act(seg_mlp, gathered_three, own_second[4], spread_one(grad_four))
    grad_three = grad_four + rounded(collect_one(back_three))
    back_two = pull_act(seg_cross, gathered_two, own_second[3], spread_one(grad_three))
    grad_two = grad_three + rounded(collect_one(back_two))
    back_one = pull_act(seg_self, gathered_one, own_second[2], spread_one(grad_two))
    grad_one = grad_two + rounded(collect_one(back_one))
    grad_moduled = rounded(collect_one(pull_act(seg_conv, gathered_x, own_second[1], grad_one)))
    penalty_grad = pull_act(seg_in, input_full, own_second[0], grad_moduled)
    tangent = penalty_weight * penalty_mask.astype(jnp.float32)[:, None, None] * penalty_grad
    own_third = owned_sets()

    def push(segment, active, own_set, tangent_in):
        return jax.jvp(lambda inner_x: segment(inner_x, styles, own_set), (active,), (tangent_in,))[
            1
        ]

    tan_x = spread_one(push(seg_in, input_full, own_third[0], tangent))
    tan_one = push(seg_conv, gathered_x, own_third[1], tan_x)
    tan_g1 = spread_one(tan_one)
    tan_two = tan_one + collect_one(push(seg_self, gathered_one, own_third[2], tan_g1))
    tan_g2 = spread_one(tan_two)
    tan_three = tan_two + collect_one(push(seg_cross, gathered_two, own_third[3], tan_g2))
    tan_g3 = spread_one(tan_three)
    tan_four = tan_three + collect_one(push(seg_mlp, gathered_three, own_third[4], tan_g3))
    own_fourth = owned_sets()

    def pull_both(segment, active, tangent_in, own_set, cotan, cotan_tangent):

        def joint(inner_x, inner_tangent, styles_in, own_in):
            return jax.jvp(
                lambda value_x: segment(value_x, styles_in, own_in), (inner_x,), (inner_tangent,)
            )

        return jax.vjp(joint, active, tangent_in, styles, own_set)[1]((cotan, cotan_tangent))

    grad_act, grad_tan, style_acc, ignored = pull_both(
        seg_rgb,
        hidden_four,
        tan_four,
        own_fourth[5],
        cot_rgb.astype(jnp.float32),
        penalty_dir.astype(jnp.float32),
    )
    main_now = cot_feat.astype(jnp.float32) + grad_act
    side_now = grad_tan
    layer_grads = []
    for segment, active, tangent_in, own_set in (
        (seg_mlp, gathered_three, tan_g3, own_fourth[4]),
        (seg_cross, gathered_two, tan_g2, own_fourth[3]),
        (seg_self, gathered_one, tan_g1, own_fourth[2]),
    ):
        both_wide = spread(jnp.stack([main_now, side_now]).astype(jnp.bfloat16)).astype(jnp.float32)
        grad_act, grad_tan, grad_sty, grad_own = pull_both(
            segment, active, tangent_in, own_set, both_wide[0], both_wide[1]
        )
        style_acc = tree_add(style_acc, grad_sty)
        layer_grads.append(grad_own)
        both_sums = collect(jnp.stack([grad_act, grad_tan]))
        main_now = main_now + rounded(both_sums[0])
        side_now = side_now + rounded(both_sums[1])
    grad_act, grad_tan, grad_sty, grads_conv = pull_both(
        seg_conv, gathered_x, tan_x, own_fourth[1], main_now, side_now
    )
    style_acc = tree_add(style_acc, grad_sty)
    both_sums = collect(jnp.stack([grad_act, grad_tan]))
    grad_act, grad_tan, grad_sty, ignored = pull_both(
        seg_in, input_full, tangent, own_fourth[0], rounded(both_sums[0]), rounded(both_sums[1])
    )
    style_acc = tree_add(style_acc, grad_sty)
    proj_terms = layer_grads[2] + layer_grads[1] + layer_grads[0]
    big_terms = grads_conv + proj_terms
    big_sums = (
        lax.psum_scatter(
            big_terms[0].astype(jnp.bfloat16), "dp", scatter_dimension=2, tiled=True
        ).astype(jnp.float32),
        lax.psum_scatter(
            big_terms[1].astype(jnp.bfloat16), "dp", scatter_dimension=0, tiled=True
        ).astype(jnp.float32),
        lax.psum_scatter(
            big_terms[2].astype(jnp.bfloat16), "dp", scatter_dimension=0, tiled=True
        ).astype(jnp.float32),
        lax.psum_scatter(
            big_terms[3].astype(jnp.bfloat16), "dp", scatter_dimension=1, tiled=True
        ).astype(jnp.float32),
        lax.psum_scatter(
            big_terms[4].astype(jnp.bfloat16), "dp", scatter_dimension=0, tiled=True
        ).astype(jnp.float32),
        lax.psum_scatter(
            big_terms[5].astype(jnp.bfloat16), "dp", scatter_dimension=0, tiled=True
        ).astype(jnp.float32),
        lax.psum_scatter(
            big_terms[6].astype(jnp.bfloat16), "dp", scatter_dimension=0, tiled=True
        ).astype(jnp.float32),
        lax.psum_scatter(
            big_terms[7].astype(jnp.bfloat16), "dp", scatter_dimension=1, tiled=True
        ).astype(jnp.float32),
        lax.psum_scatter(
            big_terms[8].astype(jnp.bfloat16), "dp", scatter_dimension=0, tiled=True
        ).astype(jnp.float32),
        lax.psum_scatter(
            big_terms[9].astype(jnp.bfloat16), "dp", scatter_dimension=1, tiled=True
        ).astype(jnp.float32),
    )
    small_terms = style_pull(style_acc)[0]
    small_sums = lax.psum(
        (
            small_terms[0],
            small_terms[1],
            small_terms[2],
            small_terms[3],
            small_terms[4],
            small_terms[5],
            small_terms[6],
            small_terms[7],
        ),
        ("dp", "mp"),
    )
    return (hidden_four, picture, grad_act) + tuple(small_sums) + tuple(big_sums)


def fits_samples(mesh):
    return mesh.shape["dp"] == 16 and mesh.shape["mp"] == 2


def dot_wide(left, right, left_dim, right_dim):
    return lax.dot_general(
        left.astype(jnp.bfloat16),
        right.astype(jnp.bfloat16),
        (((left_dim,), (right_dim,)), ((), ())),
        preferred_element_type=jnp.float32,
    )


def make_products(flip):
    depth = 1 if flip else 0

    def weight_grad(rows, cotan):
        if flip:
            return dot_wide(cotan, rows, 0, 0).astype(jnp.bfloat16)
        return dot_wide(rows, cotan, 0, 0).astype(jnp.bfloat16)

    @jax.custom_vjp
    def single(rows, weight):
        return dot_wide(rows, weight, 1, depth)

    def single_fwd(rows, weight):
        return single(rows, weight), (rows, weight)

    def single_bwd(kept, cotan):
        rows, weight = kept
        return dot_wide(cotan, weight, 1, 1 - depth), weight_grad(rows, cotan)

    single.defvjp(single_fwd, single_bwd)

    @jax.custom_vjp
    def pair(rows, tangents, weight):
        return dot_wide(rows, weight, 1, depth), dot_wide(tangents, weight, 1, depth)

    def pair_fwd(rows, tangents, weight):
        return pair(rows, tangents, weight), (rows, tangents, weight)

    def pair_bwd(kept, cotans):
        rows, tangents, weight = kept
        count = rows.shape[0]
        both = jnp.concatenate([entry.astype(jnp.bfloat16) for entry in cotans], axis=0)
        inputs = jnp.concatenate(
            [rows.astype(jnp.bfloat16), tangents.astype(jnp.bfloat16)], axis=0
        )
        back = dot_wide(both, weight, 1, 1 - depth)
        return back[:count], back[count:], weight_grad(inputs, both)

    pair.defvjp(pair_fwd, pair_bwd)
    return single, pair


product, product_pair = make_products(False)
product_flip, product_flip_pair = make_products(True)


def with_tangent(fun, value, tangent):
    return jax.jvp(fun, (value,), (tangent,))


def last_softmax(scores):
    return jax.nn.softmax(scores, axis=-1)


def post_conv(conv_out, sums, bias, strength, noise):
    demodulate = lax.rsqrt(sums + 1e-08)
    return jax.nn.silu(conv_out * demodulate[None] + bias[None] + noise[:, None] * strength[None])


def picture_of(hidden, rgb_scales, rgb_weight):
    return einsum_high("pc,kc->kp", hidden, rgb_scales[None] * rgb_weight)


CHUNK = 16
PAD_ROWS = (SIDE + 2) * SIDE
PIXELS = SIDE * SIDE


def placing(half_side):
    side = 2 * half_side
    table = np.zeros((side + 2, side, 3, half_side * half_side), np.float32)
    for row in range(1, side + 1):
        for col in range(side):
            for shift in range(3):
                at = col + shift - 1
                if 0 <= at < side:
                    table[row, col, shift, (row - 1) // 2 * half_side + at // 2] = 1.0
    return jnp.asarray(table.reshape((side + 2) * side, -1), jnp.bfloat16)


def dot_f32(left, right, left_dim, right_dim):
    return lax.dot_general(
        left, right, (((left_dim,), (right_dim,)), ((), ())), preferred_element_type=jnp.float32
    )


def mix_matrix(select):
    high = select.astype(jnp.bfloat16)
    low = (select - high.astype(jnp.float32)).astype(jnp.bfloat16)
    eye = jnp.eye(CHUNK, dtype=jnp.bfloat16)
    parts = jnp.stack([high, low], axis=1)
    wide = parts[:, None, :, :, None] * eye[None, :, None, None, :]
    return wide.reshape(select.shape[0] * CHUNK, -1)


def lanes_wide(column, width):
    return jnp.concatenate([column] * (width // column.shape[-1]), axis=-1)


def mix_body(pieces, mix_ref, bank_ref, squares_ref, kernel_ref, sums_ref):
    step = pl.program_id(0)

    @pl.when(step == 0)
    def _():
        sums_ref[...] = jnp.zeros_like(sums_ref)

    kernels, rows, width = bank_ref.shape
    samples = kernel_ref.shape[0]
    per_tap = squares_ref.shape[1]
    for piece in range(pieces):
        part = bank_ref[:, piece * CHUNK : (piece + 1) * CHUNK, :].reshape(kernels * CHUNK, width)
        mixed = dot_f32(mix_ref[...], jnp.concatenate([part, part], axis=0), 1, 0)
        mixed = mixed.astype(jnp.bfloat16).reshape(samples, CHUNK, width)
        kernel_ref[:, piece * CHUNK : (piece + 1) * CHUNK, :] = mixed
        first = lax.rem(step * rows + piece * CHUNK, per_tap)
        factor = squares_ref[:, pl.ds(pl.multiple_of(first, CHUNK), CHUNK), :]
        wide = mixed.astype(jnp.float32)
        sums_ref[...] += jnp.sum(wide * wide * lanes_wide(factor, width), axis=1)


def mix_kernels(mix, bank_rows, squares):
    kernels, depth, width = bank_rows.shape
    samples = squares.shape[0]
    pieces = 4
    rows = pieces * CHUNK
    return pl.pallas_call(
        lambda *refs: mix_body(pieces, *refs),
        grid=(depth // rows,),
        in_specs=[
            pl.BlockSpec(mix.shape, lambda step: (0, 0)),
            pl.BlockSpec((kernels, rows, width), lambda step: (0, step, 0)),
            pl.BlockSpec(squares.shape, lambda step: (0, 0, 0)),
        ],
        out_specs=[
            pl.BlockSpec((samples, rows, width), lambda step: (0, step, 0)),
            pl.BlockSpec((samples, width), lambda step: (0, 0)),
        ],
        out_shape=[
            jax.ShapeDtypeStruct((samples, depth, width), jnp.bfloat16),
            jax.ShapeDtypeStruct((samples, width), jnp.float32),
        ],
        compiler_params=pltpu.CompilerParams(vmem_limit_bytes=48 * 2**20),
        name="mix_kernels",
    )(mix, bank_rows, squares)


def place_rows(slab, place_ref, spot_ref):
    pixels, width = slab.shape
    for shift in range(3):
        spot_ref[
            shift * pixels : (shift + 1) * pixels, shift * width : (shift + 1) * width
        ] = slab
    return dot_f32(place_ref[...], spot_ref[...], 1, 0).astype(jnp.bfloat16)


def conv_body(extra, slab_ref, place_ref, kernel_ref, sums_ref, out_ref, spot_ref):
    sample = pl.program_id(0)

    @pl.when(sample == 0)
    def _():
        spot_ref[...] = jnp.zeros_like(spot_ref)

    rows = place_rows(slab_ref[0], place_ref, spot_ref)
    depth = rows.shape[1]
    total = None
    for shift in range(3):
        term = dot_f32(
            rows[shift * SIDE : shift * SIDE + PIXELS],
            kernel_ref[0, shift * depth : (shift + 1) * depth, :],
            1,
            0,
        )
        total = term if total is None else total + term
    out_ref[0, :PIXELS, :] = total.astype(jnp.bfloat16)
    if extra:
        line = sums_ref[pl.ds(sample, 1), :]
        out_ref[0, PIXELS:, :] = jnp.broadcast_to(line, (CHUNK, line.shape[1])).astype(jnp.bfloat16)


def convolve(slabs, place, kernel, sums, extra):
    samples, pixels, width = slabs.shape
    depth, width_out = kernel.shape[1:]
    rows = PIXELS + (CHUNK if extra else 0)
    return pl.pallas_call(
        lambda *refs: conv_body(extra, *refs),
        grid=(samples,),
        in_specs=[
            pl.BlockSpec((1, pixels, width), lambda step: (step, 0, 0)),
            pl.BlockSpec(place.shape, lambda step: (0, 0)),
            pl.BlockSpec((1, depth, width_out), lambda step: (step, 0, 0)),
            pl.BlockSpec(sums.shape, lambda step: (0, 0)),
        ],
        out_specs=pl.BlockSpec((1, rows, width_out), lambda step: (step, 0, 0)),
        out_shape=jax.ShapeDtypeStruct((samples, rows, width_out), jnp.bfloat16),
        scratch_shapes=[pltpu.VMEM((3 * pixels, 3 * width), jnp.bfloat16)],
        compiler_params=pltpu.CompilerParams(vmem_limit_bytes=32 * 2**20),
        name="conv_forward",
    )(slabs, place, kernel, sums)


def fold_back(cotan, place_ref, kernel_ref, wide_ref, pixels, width):
    depth = 3 * width
    wide_ref[...] = jnp.zeros_like(wide_ref)
    for shift in range(3):
        wide_ref[shift * SIDE : shift * SIDE + PIXELS, :] += dot_f32(
            cotan, kernel_ref[0, shift * depth : (shift + 1) * depth, :], 1, 1
        )
    back = dot_f32(place_ref[...], wide_ref[...].astype(jnp.bfloat16), 0, 0)
    total = None
    for shift in range(3):
        term = back[shift * pixels : (shift + 1) * pixels, shift * width : (shift + 1) * width]
        total = term if total is None else total + term
    return total.astype(jnp.bfloat16)


def back_body(cotan_ref, place_ref, kernel_ref, out_ref, wide_ref):
    pixels, width = out_ref.shape[1:]
    out_ref[0] = fold_back(cotan_ref[0], place_ref, kernel_ref, wide_ref, pixels, width)


def conv_back(cotans, place, kernel, pixels, width):
    samples, rows, width_out = cotans.shape
    depth = kernel.shape[1]
    return pl.pallas_call(
        back_body,
        grid=(samples,),
        in_specs=[
            pl.BlockSpec((1, rows, width_out), lambda step: (step, 0, 0)),
            pl.BlockSpec(place.shape, lambda step: (0, 0)),
            pl.BlockSpec((1, depth, width_out), lambda step: (step, 0, 0)),
        ],
        out_specs=pl.BlockSpec((1, pixels, width), lambda step: (step, 0, 0)),
        out_shape=jax.ShapeDtypeStruct((samples, pixels, width), jnp.bfloat16),
        scratch_shapes=[pltpu.VMEM((PAD_ROWS, 3 * width), jnp.float32)],
        compiler_params=pltpu.CompilerParams(vmem_limit_bytes=32 * 2**20),
        name="conv_back",
    )(cotans, place, kernel)


def second_body(
    slab_ref,
    tan_ref,
    place_ref,
    kernel_ref,
    cotan_ref,
    squares_ref,
    grad_ref,
    back_ref,
    scale_ref,
    spot_ref,
    wide_ref,
):
    @pl.when(pl.program_id(0) == 0)
    def _():
        spot_ref[...] = jnp.zeros_like(spot_ref)

    pixels, width = slab_ref.shape[1:]
    depth = 3 * width
    rows = place_rows(slab_ref[0], place_ref, spot_ref)
    tan_rows = place_rows(tan_ref[0], place_ref, spot_ref)
    line = cotan_ref[0, 2 * PIXELS : 2 * PIXELS + CHUNK, :][:1].astype(jnp.float32)
    factor = 2.0 * lanes_wide(squares_ref[0], line.shape[1]) * line
    totals = None
    for shift in range(3):
        span = slice(shift * SIDE, shift * SIDE + PIXELS)
        grad = dot_f32(rows[span], cotan_ref[0, :PIXELS, :], 0, 0)
        grad = grad + dot_f32(tan_rows[span], cotan_ref[0, PIXELS : 2 * PIXELS, :], 0, 0)
        for tap in range(3):
            at = shift * depth + tap * width
            own = kernel_ref[0, at : at + width, :].astype(jnp.float32)
            grad_ref[0, at : at + width, :] = (
                grad[tap * width : (tap + 1) * width] + own * factor
            ).astype(jnp.bfloat16)
            term = own * own
            totals = term if totals is None else totals + term
    summed = jnp.sum(totals * line, axis=1, keepdims=True)
    scale_ref[0] = jnp.broadcast_to(summed, scale_ref.shape[1:])
    for part in range(2):
        back_ref[0, part * pixels : (part + 1) * pixels, :] = fold_back(
            cotan_ref[0, part * PIXELS : (part + 1) * PIXELS, :],
            place_ref,
            kernel_ref,
            wide_ref,
            pixels,
            width,
        )


def conv_second(slabs, tans, place, kernel, cotans, squares):
    samples, pixels, width = slabs.shape
    depth, width_out = kernel.shape[1:]
    return pl.pallas_call(
        second_body,
        grid=(samples,),
        in_specs=[
            pl.BlockSpec((1, pixels, width), lambda step: (step, 0, 0)),
            pl.BlockSpec((1, pixels, width), lambda step: (step, 0, 0)),
            pl.BlockSpec(place.shape, lambda step: (0, 0)),
            pl.BlockSpec((1, depth, width_out), lambda step: (step, 0, 0)),
            pl.BlockSpec((1,) + cotans.shape[1:], lambda step: (step, 0, 0)),
            pl.BlockSpec((1,) + squares.shape[1:], lambda step: (step, 0, 0)),
        ],
        out_specs=[
            pl.BlockSpec((1, depth, width_out), lambda step: (step, 0, 0)),
            pl.BlockSpec((1, 2 * pixels, width), lambda step: (step, 0, 0)),
            pl.BlockSpec((1,) + squares.shape[1:], lambda step: (step, 0, 0)),
        ],
        out_shape=[
            jax.ShapeDtypeStruct((samples, depth, width_out), jnp.bfloat16),
            jax.ShapeDtypeStruct((samples, 2 * pixels, width), jnp.bfloat16),
            jax.ShapeDtypeStruct(squares.shape, jnp.float32),
        ],
        scratch_shapes=[
            pltpu.VMEM((3 * pixels, 3 * width), jnp.bfloat16),
            pltpu.VMEM((PAD_ROWS, 3 * width), jnp.float32),
        ],
        compiler_params=pltpu.CompilerParams(vmem_limit_bytes=32 * 2**20),
        name="conv_second",
    )(slabs, tans, place, kernel, cotans, squares)


def unmix_body(pieces, mix_ref, bank_ref, grad_ref, out_ref, select_ref):
    @pl.when(pl.program_id(0) == 0)
    def _():
        select_ref[...] = jnp.zeros_like(select_ref)

    kernels, _, width = bank_ref.shape
    samples = grad_ref.shape[0]
    for piece in range(pieces):
        span = slice(piece * CHUNK, (piece + 1) * CHUNK)
        grad = grad_ref[:, span, :].reshape(samples * CHUNK, width)
        mixed = dot_f32(mix_ref[...], grad, 0, 0)
        count = kernels * CHUNK
        out_ref[:, span, :] = (mixed[:count] + mixed[count:]).reshape(kernels, CHUNK, width)
        part = bank_ref[:, span, :].reshape(count, width)
        select_ref[...] += dot_f32(grad, part, 1, 1)


def unmix_kernels(mix, bank_rows, grad):
    kernels, depth, width = bank_rows.shape
    samples = grad.shape[0]
    pieces = 4
    rows = pieces * CHUNK
    return pl.pallas_call(
        lambda *refs: unmix_body(pieces, *refs),
        grid=(depth // rows,),
        in_specs=[
            pl.BlockSpec(mix.shape, lambda step: (0, 0)),
            pl.BlockSpec((kernels, rows, width), lambda step: (0, step, 0)),
            pl.BlockSpec((samples, rows, width), lambda step: (0, step, 0)),
        ],
        out_specs=[
            pl.BlockSpec((kernels, rows, width), lambda step: (0, step, 0)),
            pl.BlockSpec((samples * CHUNK, kernels * CHUNK), lambda step: (0, 0)),
        ],
        out_shape=[
            jax.ShapeDtypeStruct((kernels, depth, width), jnp.float32),
            jax.ShapeDtypeStruct((samples * CHUNK, kernels * CHUNK), jnp.float32),
        ],
        compiler_params=pltpu.CompilerParams(vmem_limit_bytes=48 * 2**20),
        name="unmix_kernels",
    )(mix, bank_rows, grad)


@jax.custom_vjp
def row_products(left, right):
    return dot_f32(left.astype(jnp.bfloat16), right.astype(jnp.bfloat16), 1, 1)


def row_products_fwd(left, right):
    return row_products(left, right), (left, right)


def row_products_bwd(kept, cotan):
    left, right = (entry.astype(jnp.bfloat16) for entry in kept)
    short = cotan.astype(jnp.bfloat16)
    return dot_f32(short, right, 1, 0), dot_f32(short, left, 0, 0)


row_products.defvjp(row_products_fwd, row_products_bwd)


@jax.custom_vjp
def mixed_rows(soft, values):
    return dot_f32(soft.astype(jnp.bfloat16), values.astype(jnp.bfloat16), 1, 0)


def mixed_rows_fwd(soft, values):
    return mixed_rows(soft, values), (soft, values)


def mixed_rows_bwd(kept, cotan):
    soft, values = (entry.astype(jnp.bfloat16) for entry in kept)
    short = cotan.astype(jnp.bfloat16)
    return dot_f32(short, values, 1, 1), dot_f32(soft, short, 0, 0)


mixed_rows.defvjp(mixed_rows_fwd, mixed_rows_bwd)


@jax.custom_vjp
def as_row(column):
    count = column.shape[0]
    lane = lax.broadcasted_iota(jnp.int32, (count, 128), 1)
    rest, parts = column, jnp.zeros((count, 128), jnp.float32)
    for place in range(3):
        short = rest.astype(jnp.bfloat16).astype(jnp.float32)
        parts = jnp.where(lane == place, short, parts)
        rest = rest - short
    ones = jnp.ones((count, 128), jnp.bfloat16)
    return dot_f32(ones, parts.astype(jnp.bfloat16), 1, 1)


def as_row_fwd(column):
    return as_row(column), None


def as_row_bwd(kept, cotan):
    ones = jnp.ones((cotan.shape[0], 128), jnp.bfloat16)
    return (dot_f32(cotan.astype(jnp.bfloat16), ones, 0, 0)[:, :1],)


as_row.defvjp(as_row_fwd, as_row_bwd)


def soft_of(scores):
    top = lax.stop_gradient(jnp.max(scores, axis=1, keepdims=True))
    powers = jnp.exp(scores - top)
    return powers / jnp.sum(powers, axis=1, keepdims=True)


def soft_tangent(soft, tangent):
    return soft * (tangent - jnp.sum(soft * tangent, axis=1, keepdims=True))


def squared(left, right):
    return jnp.sum(left * right, axis=1, keepdims=True)


def self_head(queries, values):
    scores = 2.0 * row_products(queries, queries) - as_row(squared(queries, queries))
    return (mixed_rows(soft_of(scores * HEAD ** (-0.5)), values),)


def self_head_joint(queries, tan_queries, values, tan_values):
    scores = 2.0 * row_products(queries, queries) - as_row(squared(queries, queries))
    tan_scores = row_products(tan_queries, queries) + row_products(queries, tan_queries)
    tan_scores = 2.0 * (tan_scores - as_row(squared(queries, tan_queries)))
    soft = soft_of(scores * HEAD ** (-0.5))
    tan_soft = soft_tangent(soft, tan_scores * HEAD ** (-0.5))
    return (
        mixed_rows(soft, values),
        mixed_rows(tan_soft, values) + mixed_rows(soft, tan_values),
    )


def cross_head(queries, keys, values):
    return (mixed_rows(soft_of(row_products(queries, keys) * HEAD ** (-0.5)), values),)


def cross_head_joint(queries, tan_queries, keys, values):
    soft = soft_of(row_products(queries, keys) * HEAD ** (-0.5))
    tan_soft = soft_tangent(soft, row_products(tan_queries, keys) * HEAD ** (-0.5))
    return mixed_rows(soft, values), mixed_rows(tan_soft, values)


def per_head(fun, arrays, shapes, name):
    lanes = 2 * HEAD

    def body(*refs):
        inputs, outputs = refs[: len(arrays)], refs[len(arrays) :]
        for head in range(2):
            span = slice(head * HEAD, (head + 1) * HEAD)
            results = fun(*[ref[:, span].astype(jnp.float32) for ref in inputs])
            for ref, result in zip(outputs, results):
                ref[:, span] = result.astype(jnp.bfloat16)

    return pl.pallas_call(
        body,
        grid=(arrays[0].shape[1] // lanes,),
        in_specs=[pl.BlockSpec((entry.shape[0], lanes), lambda step: (0, step)) for entry in arrays],
        out_specs=[pl.BlockSpec((shape[0], lanes), lambda step: (0, step)) for shape in shapes],
        out_shape=[jax.ShapeDtypeStruct(shape, jnp.bfloat16) for shape in shapes],
        compiler_params=pltpu.CompilerParams(vmem_limit_bytes=32 * 2**20),
        name=name,
    )(*arrays)


def make_attention(fun, count, name):
    @jax.custom_vjp
    def attend(*arrays):
        return tuple(per_head(fun, arrays, [arrays[0].shape] * count, name))

    def attend_fwd(*arrays):
        return attend(*arrays), arrays

    def attend_bwd(arrays, cotans):
        def pull(*given):
            return jax.vjp(fun, *given[: len(arrays)])[1](tuple(given[len(arrays) :]))

        shapes = [entry.shape for entry in arrays]
        return tuple(per_head(pull, list(arrays) + list(cotans), shapes, name + "_pull"))

    attend.defvjp(attend_fwd, attend_bwd)
    return attend


self_attend = make_attention(self_head, 1, "self_heads")
self_attend_joint = make_attention(self_head_joint, 2, "self_heads_joint")
cross_attend = make_attention(cross_head, 1, "cross_heads")
cross_attend_joint = make_attention(cross_head_joint, 2, "cross_heads_joint")


def short_of(*arrays):
    return [entry.astype(jnp.bfloat16) for entry in arrays]


def layer_forward(conv_out, sums, text_rows, small, weights, noise):
    bias, strength, rgb_scales, rgb_weight = small
    qk_w, value_w, attn_w, query_w, key_w, cval_w, cout_w, mlp_w, mout_w = weights
    hidden_one = post_conv(conv_out, sums, bias, strength, noise)
    normed = rms_norm(hidden_one)
    (mixture,) = self_attend(*short_of(product(normed, qk_w), product(normed, value_w)))
    hidden_two = hidden_one + product_flip(mixture.astype(jnp.float32), attn_w)
    normed = rms_norm(hidden_two)
    (mixture,) = cross_attend(
        *short_of(
            product(normed, query_w), product(text_rows, key_w), product(text_rows, cval_w)
        )
    )
    hidden_three = hidden_two + product_flip(mixture.astype(jnp.float32), cout_w)
    normed = rms_norm(hidden_three)
    inner = jax.nn.gelu(product(normed, mlp_w))
    hidden_four = hidden_three + product_flip(inner, mout_w)
    return hidden_four, picture_of(hidden_four, rgb_scales, rgb_weight)


def layer_joint(conv_out, conv_tan, sums, text_rows, small, weights, noise):
    bias, strength, rgb_scales, rgb_weight = small
    qk_w, value_w, attn_w, query_w, key_w, cval_w, cout_w, mlp_w, mout_w = weights
    hidden_one, tan_one = with_tangent(
        lambda value: post_conv(value, sums, bias, strength, noise), conv_out, conv_tan
    )
    normed, tan_normed = with_tangent(rms_norm, hidden_one, tan_one)
    queries, tan_queries = product_pair(normed, tan_normed, qk_w)
    values, tan_values = product_pair(normed, tan_normed, value_w)
    mixture, tan_mixture = self_attend_joint(*short_of(queries, tan_queries, values, tan_values))
    added, tan_added = product_flip_pair(
        mixture.astype(jnp.float32), tan_mixture.astype(jnp.float32), attn_w
    )
    hidden_two, tan_two = hidden_one + added, tan_one + tan_added
    normed, tan_normed = with_tangent(rms_norm, hidden_two, tan_two)
    queries, tan_queries = product_pair(normed, tan_normed, query_w)
    mixture, tan_mixture = cross_attend_joint(
        *short_of(queries, tan_queries, product(text_rows, key_w), product(text_rows, cval_w))
    )
    added, tan_added = product_flip_pair(
        mixture.astype(jnp.float32), tan_mixture.astype(jnp.float32), cout_w
    )
    hidden_three, tan_three = hidden_two + added, tan_two + tan_added
    normed, tan_normed = with_tangent(rms_norm, hidden_three, tan_three)
    before, tan_before = product_pair(normed, tan_normed, mlp_w)
    inner, tan_inner = with_tangent(jax.nn.gelu, before, tan_before)
    added, tan_added = product_flip_pair(inner, tan_inner, mout_w)
    hidden_four, tan_four = hidden_three + added, tan_three + tan_added
    return (
        hidden_four,
        picture_of(hidden_four, rgb_scales, rgb_weight),
        picture_of(tan_four, rgb_scales, rgb_weight),
    )


SWAP = ((0, 1), (1, 0))


def swap_mp(values):
    return lax.ppermute(values, "mp", SWAP)


def pick(values, index):
    return lax.dynamic_index_in_dim(values, index, 0, keepdims=False)


def own_whole(values, mp):
    mine, other = pick(values, mp), swap_mp(pick(values, 1 - mp))
    first = jnp.where(mp == 0, mine, other)
    second = jnp.where(mp == 0, other, mine)
    return jnp.concatenate([first, second], axis=-1)


def both_half(whole, mp):
    half = whole.shape[-1] // 2
    mine = lax.dynamic_slice_in_dim(whole, mp * half, half, whole.ndim - 1)
    other = swap_mp(lax.dynamic_slice_in_dim(whole, (1 - mp) * half, half, whole.ndim - 1))
    first = jnp.where(mp == 0, mine, other)
    second = jnp.where(mp == 0, other, mine)
    return jnp.stack([first, second])


def to_slabs(both):
    devices = lax.axis_size("dp")
    parts = both.reshape(2, both.shape[1], devices, -1).transpose(2, 0, 1, 3)
    parts = lax.all_to_all(parts, "dp", 0, 0, tiled=True)
    return parts.reshape(2 * devices, both.shape[1], -1)


def from_slabs(slabs, mp):
    devices = lax.axis_size("dp")
    rows = slabs.shape[1]
    parts = slabs.astype(jnp.bfloat16).reshape((devices, 2) + slabs.shape[1:])
    parts = lax.all_to_all(parts, "dp", 0, 0, tiled=True)
    parts = parts.transpose(1, 2, 0, 3).reshape(2, rows, -1)
    other = swap_mp(pick(parts, 1 - mp))
    return pick(parts, mp).astype(jnp.float32) + other.astype(jnp.float32)


PLANES = 4


class Place:
    def __init__(self):
        dp = lax.axis_index("dp")
        self.z, self.y, self.core = dp // 4, lax.rem(dp // 2, 2), lax.rem(dp, 2)
        self.x = lax.axis_index("mp")


def greet(place, axes):
    barrier = pltpu.get_barrier_semaphore()

    def tell(**there):
        at = dict(z=place.z, y=place.y, core=place.core, x=place.x)
        at.update(there)
        pl.semaphore_signal(
            barrier,
            inc=1,
            device_id=((at["z"] * 2 + at["y"]) * 2 + at["core"], at["x"]),
            device_id_type=pl.DeviceIdType.MESH,
        )

    tell(core=1 - place.core)
    count = 1
    for name in ("y", "x"):
        if name in axes:
            tell(**{name: 1 - getattr(place, name)})
            count += 1

    @pl.when(place.z > 0)
    def _():
        tell(z=place.z - 1)

    @pl.when(place.z < PLANES - 1)
    def _():
        tell(z=place.z + 1)

    between = (place.z > 0) & (place.z < PLANES - 1)
    pl.semaphore_wait(barrier, count + jnp.where(between, 2, 1))


def gather_body(pieces, inputs, outputs, axes, send_sem, recv_sem, own_sem):
    place = Place()
    greet(place, axes)
    sends = []

    def spot(z, y, core, x):
        return (z * 2 + y) * 2 + core, x

    def chip(z, y, x):
        return (z * 2 + y) * 2 + x

    def send(number, piece, source, target, slot, parity, first, condition):
        sz, sy, sx = source
        dp, mp = spot(sz, sy, place.core, sx)
        there = piece["to"](outputs, dp, mp)
        copy = pltpu.make_async_remote_copy(
            src_ref=piece["of"](inputs) if first else there,
            dst_ref=there,
            send_sem=send_sem.at[number, chip(sz, sy, sx), slot],
            recv_sem=recv_sem.at[number, chip(sz, sy, sx), parity],
            device_id=spot(*target),
            device_id_type=pl.DeviceIdType.MESH,
        )

        if condition is None:
            copy.start()
        else:
            pl.when(condition)(copy.start)
        sends.append((condition, copy))

    def onward(number, piece, source, came, first, condition):
        def both(more):
            if condition is None:
                return more
            return condition if more is None else condition & more

        order = piece["order"]
        later = order if came is None else order[order.index(came[0]) :]
        for name in later:
            here = dict(z=place.z, y=place.y, core=place.core, x=place.x)
            if name == "z":
                for way, slot in ((1, 0), (-1, 1)):
                    if came is not None and came[0] == "z" and came[1] != way:
                        continue
                    fits = place.z < PLANES - 1 if way == 1 else place.z > 0
                    target = (place.z + way, place.y, place.core, place.x)
                    send(number, piece, source, target, slot, 0, first, both(fits))
            elif came is None or came[0] != name:
                here[name] = 1 - here[name]
                target = (here["z"], here["y"], here["core"], here["x"])
                slot = 2 if name == "y" else 3
                send(number, piece, source, target, slot, 0, first, both(None))
        target = (place.z, place.y, 1 - place.core, place.x)
        send(number, piece, source, target, 4, 1, first, both(None))

    def arrive(number, piece, source, parity, condition):
        sz, sy, sx = source
        core = place.core if parity == 0 else 1 - place.core
        there = piece["to"](outputs, *spot(sz, sy, core, sx))

        def wait():
            pltpu.make_async_remote_copy(
                src_ref=there,
                dst_ref=there,
                send_sem=send_sem.at[number, chip(sz, sy, sx), 0],
                recv_sem=recv_sem.at[number, chip(sz, sy, sx), parity],
                device_id=spot(place.z, place.y, 1 - place.core, place.x),
                device_id_type=pl.DeviceIdType.MESH,
            ).wait_recv()

        if condition is None:
            wait()
        else:
            pl.when(condition)(wait)

    own = []
    for number, piece in enumerate(pieces):
        onward(number, piece, (place.z, place.y, place.x), None, True, None)
        copy = pltpu.make_async_copy(
            piece["of"](inputs),
            piece["to"](outputs, *spot(place.z, place.y, place.core, place.x)),
            own_sem.at[number],
        )
        copy.start()
        own.append(copy)
    flips = [(fy, fx) for fy in (0, 1) for fx in ((0, 1) if "x" in axes else (0,))]
    blocks = [(dz, fy, fx) for dz in (0, 1, -1, 2, -2, 3, -3) for fy, fx in flips]
    blocks = sorted(blocks, key=lambda block: abs(block[0]) + block[1] + block[2])
    for dz, fy, fx in blocks:
        if (dz, fy, fx) == (0, 0, 0):
            continue
        condition = None
        if dz > 0:
            condition = place.z >= dz
        elif dz < 0:
            condition = place.z < PLANES + dz
        source = (
            place.z - dz,
            1 - place.y if fy else place.y,
            1 - place.x if fx else place.x,
        )
        for number, piece in enumerate(pieces):
            arrive(number, piece, source, 0, condition)
            moved = dict(z=dz, y=fy, x=fx)
            last = [name for name in piece["order"] if moved[name]][-1]
            came = (last, (1 if dz > 0 else -1) if last == "z" else 0)
            onward(number, piece, source, came, False, condition)
    for number, piece in enumerate(pieces):
        for sz in range(PLANES):
            for sy in range(2):
                for sx in (0, 1) if "x" in axes else (place.x,):
                    arrive(number, piece, (sz, sy, sx), 1, None)
    for condition, copy in sends:
        if condition is None:
            copy.wait_send()
        else:
            pl.when(condition)(copy.wait_send)
    for copy in own:
        copy.wait()


def gather_call(pieces, axes, arrays, shapes, call_id, name):
    count = len(arrays)

    def body(*refs):
        inputs, outputs = refs[:count], refs[count : count + len(shapes)]
        gather_body(pieces, inputs, outputs, axes, *refs[count + len(shapes) :])

    return pl.pallas_call(
        body,
        in_specs=[pl.BlockSpec(memory_space=pl.ANY)] * count,
        out_specs=[pl.BlockSpec(memory_space=pl.ANY)] * len(shapes),
        out_shape=[
            jax.ShapeDtypeStruct(shape, entry.dtype) for shape, entry in zip(shapes, arrays)
        ],
        scratch_shapes=[
            pltpu.SemaphoreType.DMA((len(pieces), 16, 5)),
            pltpu.SemaphoreType.DMA((len(pieces), 16, 2)),
            pltpu.SemaphoreType.DMA((len(pieces),)),
        ],
        compiler_params=pltpu.CompilerParams(collective_id=call_id, has_side_effects=True),
        name=name,
    )(*arrays)


def rows_at(index, rows):
    return pl.ds(pl.multiple_of(index * rows, rows), rows)


def lanes_at(index, lanes):
    return pl.ds(pl.multiple_of(index * lanes, lanes), lanes)


def gather_weights(shards, numbers, call_id):
    orders = dict(x=("z", "y", "x"), y=("z", "x", "y"), z=("x", "y", "z"))
    turns = ("x", "y", "x", "y", "x", "y", "z", "y", "z")

    def piece(number, turn):
        rows, lanes = arrays[number].shape
        stacked = number == len(shards)

        def to(refs, dp, mp):
            if stacked:
                return refs[number].at[rows_at(dp * 2 + mp, rows)]
            return refs[number].at[rows_at(dp, rows), lanes_at(mp, lanes)]

        return dict(order=orders[turn], of=lambda refs: refs[number], to=to)

    arrays = list(shards) + [numbers]
    pieces = [piece(len(shards), "x")]
    pieces += [piece(number, turn) for number, turn in enumerate(turns)]
    shapes = [(entry.shape[0] * 16, entry.shape[1] * 2) for entry in shards]
    shapes.append((numbers.shape[0] * 32, numbers.shape[1]))
    return gather_call(pieces, ("z", "y", "x"), arrays, shapes, call_id, "gather_weights")


def gather_dp(values, call_id):
    samples, rows, lanes = values.shape

    def piece(sample, first, last, order):
        return dict(
            order=order,
            of=lambda refs: refs[0].at[sample, :, first:last],
            to=lambda refs, dp, mp: refs[0].at[dp * samples + sample, :, first:last],
        )

    cut = lanes * 3 // 4
    pieces = [piece(sample, 0, cut, ("z", "y")) for sample in range(samples)]
    pieces += [piece(sample, cut, lanes, ("y", "z")) for sample in range(samples)]
    shapes = [(16 * samples, rows, lanes)]
    return gather_call(pieces, ("z", "y"), [values], shapes, call_id, "gather_samples")[0]


def add_rows(total, part):
    shape = total.shape[:-2]
    for number in range(int(np.prod(shape))):
        spot = tuple(int(place) for place in np.unravel_index(number, shape))
        total[spot] = (total[spot].astype(jnp.float32) + part[spot].astype(jnp.float32)).astype(
            jnp.bfloat16
        )


def sum_body(
    cut,
    part_ref,
    out_ref,
    acc,
    core_in,
    y_in,
    y_last,
    z_first,
    z_second,
    x_in,
    load_sem,
    core_send,
    core_recv,
    y_send,
    y_recv,
    z_send,
    z_recv,
    x_send,
    x_recv,
):
    place = Place()
    greet(place, ("z", "y", "x"))
    z, y, x = place.z, place.y, place.x
    wide, narrow = slice(0, cut), slice(cut, acc.shape[-1])
    finish = []

    def spot(z, y, core, x):
        return (z * 2 + y) * 2 + core, x

    def remote(source, target, send, recv, device):
        return pltpu.make_async_remote_copy(
            src_ref=source,
            dst_ref=target,
            send_sem=send,
            recv_sem=recv,
            device_id=spot(*device),
            device_id_type=pl.DeviceIdType.MESH,
        )

    other_core = (z, y, 1 - place.core, x)
    other_y = (z, 1 - y, place.core, x)
    other_x = (z, y, place.core, 1 - x)

    chunks = [(dest, 1 - y) for dest in (3, 0, 2, 1)] + [(dest, y) for dest in (3, 0, 2, 1)]
    first = []
    for number, (dest, side) in enumerate(chunks):
        sent = remote(
            part_ref.at[dest, side, 1 - place.core],
            core_in.at[dest, side],
            core_send.at[number],
            core_recv.at[number],
            other_core,
        )
        sent.start()
        mine = pltpu.make_async_copy(
            part_ref.at[dest, side, place.core], acc.at[dest, side], load_sem.at[number]
        )
        mine.start()
        first.append((sent, mine))

    y_copies = []
    for number, (dest, side) in enumerate(chunks):
        sent, mine = first[number]
        mine.wait()
        sent.wait_recv()
        add_rows(acc.at[dest, side], core_in.at[dest, side])
        finish.append(sent)
        if number < 4:
            copy = remote(
                acc.at[dest, side, :, :, wide],
                y_in.at[dest],
                y_send.at[dest],
                y_recv.at[dest],
                other_y,
            )
            copy.start()
            y_copies.append(copy)

    def along_z(slot, view, landing, dest):
        for way in (0, 1):
            near = dest > z if way == 0 else dest < z
            has_before = z > 0 if way == 0 else z < PLANES - 1
            copy = remote(
                view,
                landing.at[way, dest],
                z_send.at[slot, way, dest],
                z_recv.at[slot, way, dest],
                (z + (1 if way == 0 else -1), y, place.core, x),
            )

            @pl.when(near & has_before)
            def _():
                copy.wait_recv()
                add_rows(view, landing.at[way, dest])

            pl.when(near)(copy.start)
            finish.append((near, copy))

    def end_z(slot, view, landing):
        for way in (0, 1):
            copy = remote(
                view,
                landing.at[way, z],
                z_send.at[slot, way, z],
                z_recv.at[slot, way, z],
                other_core,
            )

            @pl.when(z > 0 if way == 0 else z < PLANES - 1)
            def _():
                copy.wait_recv()
                add_rows(view, landing.at[way, z])

    for number, dest in enumerate((3, 0, 2, 1)):
        along_z(1, acc.at[dest, :, :, :, narrow], z_second, dest)
        y_copies[number].wait_recv()
        finish.append(y_copies[number])
        view = acc.at[dest, y, :, :, wide]
        add_rows(view, y_in.at[dest])
        along_z(0, view, z_first, dest)
    end_z(1, acc.at[z, :, :, :, narrow], z_second)
    last = remote(
        acc.at[z, 1 - y, :, :, narrow], y_last, y_send.at[PLANES], y_recv.at[PLANES], other_y
    )
    last.start()
    finish.append(last)
    end_z(0, acc.at[z, y, :, :, wide], z_first)
    last.wait_recv()
    add_rows(acc.at[z, y, :, :, narrow], y_last)
    swap = remote(acc.at[z, y, 1 - x], x_in, x_send, x_recv, other_x)
    swap.start()
    lanes = acc.shape[-1]
    out_ref[:, lanes_at(x, lanes)] = acc[z, y, x]
    swap.wait_recv()
    out_ref[:, lanes_at(1 - x, lanes)] = x_in[...]
    finish.append(swap)
    for item in finish:
        if isinstance(item, tuple):
            pl.when(item[0])(item[1].wait_send)
        else:
            item.wait_send()


def sum_samples(partial, call_id):
    samples, rows, lanes = partial.shape
    cut = lanes * 3 // 4
    bf16, dma = jnp.bfloat16, pltpu.SemaphoreType.DMA
    return pl.pallas_call(
        lambda *refs: sum_body(cut, *refs),
        in_specs=[pl.BlockSpec(memory_space=pl.ANY)],
        out_specs=pl.BlockSpec(memory_space=pltpu.VMEM),
        out_shape=jax.ShapeDtypeStruct((rows, 2 * lanes), bf16),
        scratch_shapes=[
            pltpu.VMEM((PLANES, 2, 2, rows, lanes), bf16),
            pltpu.VMEM((PLANES, 2, 2, rows, lanes), bf16),
            pltpu.VMEM((PLANES, 2, rows, cut), bf16),
            pltpu.VMEM((2, rows, lanes - cut), bf16),
            pltpu.VMEM((2, PLANES, 2, rows, cut), bf16),
            pltpu.VMEM((2, PLANES, 2, 2, rows, lanes - cut), bf16),
            pltpu.VMEM((rows, lanes), bf16),
            dma((8,)),
            dma((8,)),
            dma((8,)),
            dma((PLANES + 1,)),
            dma((PLANES + 1,)),
            dma((2, 2, PLANES)),
            dma((2, 2, PLANES)),
            dma,
            dma,
        ],
        compiler_params=pltpu.CompilerParams(
            collective_id=call_id, has_side_effects=True, vmem_limit_bytes=40 * 2**20
        ),
        name="sum_samples",
    )(partial.reshape(PLANES, 2, 2, 2, rows, lanes))


def sum_weights_body(parts, count, refs):
    inputs, outputs, rest = refs[:count], refs[count : 2 * count], refs[2 * count :]
    acc, core_in, one_in, two_in, z_in = (rest[k * count : (k + 1) * count] for k in range(5))
    (
        load_sem,
        core_send,
        core_recv,
        one_send,
        one_recv,
        two_send,
        two_recv,
        z_send,
        z_recv,
    ) = rest[5 * count :]
    place = Place()
    greet(place, ("z", "y", "x"))
    z, y, x = place.z, place.y, place.x
    order = (3, 0, 2, 1)
    finish = []

    def remote(source, target, send, recv, device):
        dz, dy, core, dx = device
        return pltpu.make_async_remote_copy(
            src_ref=source,
            dst_ref=target,
            send_sem=send,
            recv_sem=recv,
            device_id=((dz * 2 + dy) * 2 + core, dx),
            device_id_type=pl.DeviceIdType.MESH,
        )

    other_core = (z, y, 1 - place.core, x)
    other_y = (z, 1 - y, place.core, x)
    other_x = (z, y, place.core, 1 - x)
    sides = (1 - y, y)

    first = {}
    for dest in order:
        for w in range(count):
            rows = acc[w].shape[2]
            for turn, side in enumerate(sides):
                at = ((dest * 2 + side) * 2 + (1 - place.core)) * rows
                mine = ((dest * 2 + side) * 2 + place.core) * rows
                sent = remote(
                    inputs[w].at[pl.ds(pl.multiple_of(at, rows), rows)],
                    core_in[w].at[dest, side],
                    core_send.at[w, dest, turn],
                    core_recv.at[w, dest, turn],
                    other_core,
                )
                sent.start()
                load = pltpu.make_async_copy(
                    inputs[w].at[pl.ds(pl.multiple_of(mine, rows), rows)],
                    acc[w].at[dest, side],
                    load_sem.at[w, dest, turn],
                )
                load.start()
                first[w, dest, turn] = (sent, load)

    def half(w, index):
        lanes = acc[w].shape[-1] // 2
        return lanes_at(index, lanes)

    ones, twos = {}, {}

    def stage_one(dest):
        for w in range(count):
            for turn, side in enumerate(sides):
                sent, load = first[w, dest, turn]
                load.wait()
                sent.wait_recv()
                finish.append((None, sent))
                add_rows(acc[w].at[dest, side], core_in[w].at[dest, side])
                if parts[w] == "xy":
                    copy = remote(
                        acc[w].at[dest, side, :, half(w, 1 - x)],
                        one_in[w].at[dest, side],
                        one_send.at[w, dest, turn],
                        one_recv.at[w, dest, turn],
                        other_x,
                    )
                elif turn == 0:
                    copy = remote(
                        acc[w].at[dest, side],
                        one_in[w].at[dest],
                        one_send.at[w, dest, turn],
                        one_recv.at[w, dest, turn],
                        other_y,
                    )
                else:
                    continue
                copy.start()
                ones[w, dest, turn] = copy

    def stage_two(dest):
        for w in range(count):
            if parts[w] == "xy":
                for turn, side in enumerate(sides):
                    copy = ones[w, dest, turn]
                    copy.wait_recv()
                    finish.append((None, copy))
                    view = acc[w].at[dest, side, :, half(w, x)]
                    add_rows(view, one_in[w].at[dest, side])
                    if turn == 0:
                        twos[w, dest] = remote(
                            view,
                            two_in[w].at[dest],
                            two_send.at[w, dest],
                            two_recv.at[w, dest],
                            other_y,
                        )
                        twos[w, dest].start()
            else:
                copy = ones[w, dest, 0]
                copy.wait_recv()
                finish.append((None, copy))
                add_rows(acc[w].at[dest, y], one_in[w].at[dest])
                twos[w, dest] = remote(
                    acc[w].at[dest, y, :, half(w, 1 - x)],
                    two_in[w].at[dest],
                    two_send.at[w, dest],
                    two_recv.at[w, dest],
                    other_x,
                )
                twos[w, dest].start()

    def z_copy(w, dest, way):
        return remote(
            acc[w].at[dest, y, :, half(w, x)],
            z_in[w].at[way, dest],
            z_send.at[w, way, dest],
            z_recv.at[w, way, dest],
            (z + (1 if way == 0 else -1), y, place.core, x),
        )

    def stage_z(dest):
        for w in range(count):
            copy = twos[w, dest]
            copy.wait_recv()
            finish.append((None, copy))
            view = acc[w].at[dest, y, :, half(w, x)]
            add_rows(view, two_in[w].at[dest])
            for way in (0, 1):
                near = dest > z if way == 0 else dest < z
                has_before = z > 0 if way == 0 else z < PLANES - 1
                copy = z_copy(w, dest, way)

                @pl.when(near & has_before)
                def _():
                    copy.wait_recv()
                    add_rows(view, z_in[w].at[way, dest])

                pl.when(near)(copy.start)
                finish.append((near, copy))

    for turn in range(PLANES + 2):
        if turn < PLANES:
            stage_one(order[turn])
        if 0 <= turn - 1 < PLANES:
            stage_two(order[turn - 1])
        if turn >= 2:
            stage_z(order[turn - 2])
    for w in range(count):
        view = acc[w].at[z, y, :, half(w, x)]
        for way in (0, 1):

            @pl.when(z > 0 if way == 0 else z < PLANES - 1)
            def _():
                remote(
                    view,
                    z_in[w].at[way, z],
                    z_send.at[w, way, z],
                    z_recv.at[w, way, z],
                    other_core,
                ).wait_recv()
                add_rows(view, z_in[w].at[way, z])

        outputs[w][...] = acc[w][z, y, :, half(w, x)].astype(jnp.float32)
    for condition, copy in finish:
        if condition is None:
            copy.wait_send()
        else:
            pl.when(condition)(copy.wait_send)


def sum_weights(grads, parts, call_id):
    count = len(grads)
    bf16, dma = jnp.bfloat16, pltpu.SemaphoreType.DMA
    blocks = [(grad.shape[0] // 16, grad.shape[1]) for grad in grads]
    ones = [
        (PLANES, 2, rows, lanes // 2) if part == "xy" else (PLANES, rows, lanes)
        for (rows, lanes), part in zip(blocks, parts)
    ]
    return pl.pallas_call(
        lambda *refs: sum_weights_body(parts, count, refs),
        in_specs=[pl.BlockSpec(memory_space=pl.ANY)] * count,
        out_specs=[pl.BlockSpec(memory_space=pltpu.VMEM)] * count,
        out_shape=[
            jax.ShapeDtypeStruct((rows, lanes // 2), jnp.float32) for rows, lanes in blocks
        ],
        scratch_shapes=[pltpu.VMEM((PLANES, 2, rows, lanes), bf16) for rows, lanes in blocks]
        + [pltpu.VMEM((PLANES, 2, rows, lanes), bf16) for rows, lanes in blocks]
        + [pltpu.VMEM(shape, bf16) for shape in ones]
        + [pltpu.VMEM((PLANES, rows, lanes // 2), bf16) for rows, lanes in blocks]
        + [pltpu.VMEM((2, PLANES, rows, lanes // 2), bf16) for rows, lanes in blocks]
        + [dma((count, PLANES, 2))] * 5
        + [dma((count, PLANES))] * 2
        + [dma((count, 2, PLANES))] * 2,
        compiler_params=pltpu.CompilerParams(
            collective_id=call_id, has_side_effects=True, vmem_limit_bytes=60 * 2**20
        ),
        name="sum_weights",
    )(*grads)


def sample_parallel(
    layer_input,
    labels,
    text_ids,
    noise_seeds,
    penalty_mask,
    class_table,
    token_table,
    sel_weight,
    mod_weight,
    rgb_mod,
    rgb_weight,
    conv_bias,
    noise_strength,
    kernel_bank,
    qk_weight,
    value_weight,
    attn_out,
    cross_query,
    cross_key,
    cross_value,
    cross_out,
    mlp_in,
    mlp_out,
    cot_feat,
    cot_rgb,
    penalty_dir,
):
    mp = lax.axis_index("mp")
    dp = lax.axis_index("dp")
    half_px = layer_input.shape[1]
    slab = kernel_bank.shape[2]
    width_out = kernel_bank.shape[3]
    float32, bfloat16 = jnp.float32, jnp.bfloat16

    input_whole = lax.all_gather(layer_input, "mp", axis=2, tiled=True)
    raw_slabs = to_slabs(input_whole)
    numbers = jnp.concatenate([jnp.pad(labels, (0, 126)), text_ids.reshape(-1)]).reshape(2, 128)
    gathered = gather_weights(
        [
            mlp_in,
            mlp_out.T,
            qk_weight,
            value_weight,
            attn_out.T,
            cross_query,
            cross_out.T,
            cross_key,
            cross_value,
        ],
        jnp.pad(numbers, ((0, 6), (0, 0))),
        1,
    )
    mlp_whole, mout_whole, qk_whole, value_whole, attn_whole, query_whole, cout_whole = gathered[:7]
    key_whole, cval_whole, numbers_all = gathered[7:]
    weights = (
        qk_whole,
        value_whole,
        attn_whole,
        query_whole,
        key_whole,
        cval_whole,
        cout_whole,
        mlp_whole,
        mout_whole,
    )

    numbers_all = numbers_all.reshape(16, 2, 8, 128)[:, 0]
    labels_all = numbers_all[:, 0, :2].reshape(-1)
    ids_all = numbers_all[:, 1].reshape(-1)
    sample_count = labels_all.shape[0]
    classes = jnp.arange(class_table.shape[0], dtype=jnp.int32)
    onehot_class = (labels_all[:, None] == classes[None, :]).astype(bfloat16)
    latent = dot_wide(onehot_class, class_table, 1, 0)
    select_all, select_pull = jax.vjp(last_softmax, dot_wide(latent, sel_weight, 1, 0))
    scales_all = 1.0 + dot_wide(latent, mod_weight, 1, 0)
    rgb_scales_all = 1.0 + dot_wide(latent, rgb_mod, 1, 0)
    me = 2 * dp + mp
    scales = pick(scales_all, me)
    rgb_scales = pick(rgb_scales_all, me)
    scales_slab = lax.dynamic_slice_in_dim(scales_all, dp * slab, slab, 1)
    words = jnp.arange(token_table.shape[0], dtype=jnp.int32)
    text_own = pick(text_ids, mp)
    text_rows = dot_wide((text_own[:, None] == words[None, :]).astype(bfloat16), token_table, 1, 0)
    noise = noise_field(pick(noise_seeds, mp)[None], SIDE * SIDE)[0]
    small = (
        conv_bias.astype(float32),
        noise_strength.astype(float32),
        rgb_scales,
        rgb_weight.astype(float32),
    )

    bank_rows = kernel_bank.reshape(kernel_bank.shape[0], 9 * slab, width_out)
    mix = mix_matrix(select_all)
    scales_two = jnp.broadcast_to(
        (scales_slab * scales_slab)[:, :, None], (sample_count, slab, 128)
    )
    kernel, sums_part = mix_kernels(mix, bank_rows, scales_two)
    place = placing(SIDE // 2)

    input_own = pick(input_whole, mp).astype(float32)
    slabs_x = (raw_slabs.astype(float32) * scales_slab[:, None, :]).astype(bfloat16)
    partial = convolve(slabs_x, place, kernel, sums_part, True)
    summed = sum_samples(partial, 4).astype(float32)
    conv_out, sums = summed[:PIXELS], summed[PIXELS]

    (hidden_four, picture), pull = jax.vjp(
        lambda value: layer_forward(value, sums, text_rows, small, weights, noise), conv_out
    )

    dir_own = pick(penalty_dir, mp).astype(float32)
    grad_conv = pull((jnp.zeros_like(hidden_four), dir_own))[0]
    grads_all = gather_dp(both_half(grad_conv.astype(bfloat16), mp), 2)

    grad_moduled = from_slabs(conv_back(grads_all, place, kernel, half_px, slab), mp)
    mask_own = pick(penalty_mask, mp).astype(float32)
    tangent = penalty_weight * mask_own * grad_moduled.astype(bfloat16).astype(float32) * scales

    tan_moduled = (tangent * scales).astype(bfloat16)
    tan_other = swap_mp(tan_moduled)
    tan_pair = jnp.stack(
        [jnp.where(mp == 0, tan_moduled, tan_other), jnp.where(mp == 0, tan_other, tan_moduled)]
    )
    slabs_t = to_slabs(tan_pair)
    conv_tan = sum_samples(convolve(slabs_t, place, kernel, sums_part, False), 5).astype(float32)

    (ignored_out, ignored_pic, ignored_tan), pull_joint = jax.vjp(
        lambda *given: layer_joint(*given, noise),
        conv_out,
        conv_tan,
        sums,
        text_rows,
        small,
        weights,
    )
    cot_own = own_whole(cot_feat, mp).astype(float32)
    grad_main, grad_side, grad_sums, grad_text, grad_small, grad_weights = pull_joint(
        (cot_own, pick(cot_rgb, mp).astype(float32), dir_own)
    )

    orders = ("xy", "yx", "xy", "yx", "xy", "yx", "yx", "xy", "xy")
    d_qk, d_value, d_attn, d_query, d_key, d_cval, d_cout, d_mlp, d_mout = grad_weights
    mlp_grad, mout_grad, qk_grad, value_grad, attn_grad, query_grad, cout_grad, key_grad, cval_grad = (
        sum_weights(
            [d_mlp, d_mout, d_qk, d_value, d_attn, d_query, d_cout, d_key, d_cval], orders, 6
        )
    )
    big_sums = (
        qk_grad,
        value_grad,
        attn_grad.T,
        query_grad,
        key_grad,
        cval_grad,
        cout_grad.T,
        mlp_grad,
        mout_grad.T,
    )

    lines = jnp.broadcast_to(grad_sums[None], (CHUNK,) + grad_sums.shape)
    wide = jnp.concatenate(
        [grad_main.astype(bfloat16), grad_side.astype(bfloat16), lines.astype(bfloat16)], axis=0
    )
    wide_all = gather_dp(both_half(wide, mp), 3)
    grad_kernel, both_back, scale_sums = conv_second(
        slabs_x, slabs_t, place, kernel, wide_all, scales_two
    )
    grad_scales_slab = 2.0 * scales_slab * scale_sums[:, :, 0]
    bank_grad, select_products = unmix_kernels(mix, bank_rows, grad_kernel)
    bank_grad = bank_grad.reshape(kernel_bank.shape)
    grad_select = jnp.einsum(
        "brkr->bk", select_products.reshape(sample_count, CHUNK, -1, CHUNK)
    )
    both_back = from_slabs(both_back, mp).astype(bfloat16).astype(float32)
    back_main, back_side = both_back[:half_px], both_back[half_px:]
    input_grad = back_main * scales
    grad_scales = jnp.sum(back_main * input_own + back_side * tangent, axis=0)

    grad_bias, grad_strength, grad_rgb_scales, grad_rgb_weight = grad_small
    row = jnp.concatenate(
        [
            grad_scales,
            grad_rgb_scales,
            grad_rgb_weight.reshape(-1),
            grad_bias,
            grad_strength,
            grad_scales_slab.reshape(-1),
            grad_select.reshape(-1),
        ]
    ).reshape(-1, 128)
    rows_all = lax.all_gather(row, ("dp", "mp"), axis=0, tiled=False).reshape(sample_count, -1)
    channels = scales.shape[0]
    scale_terms = rows_all[:, :channels]
    rgb_terms = rows_all[:, channels : 2 * channels]
    sums_all = jnp.sum(rows_all[:, 2 * channels : 7 * channels], axis=0)
    slab_terms = rows_all[:, 7 * channels : 7 * channels + sample_count * slab]
    slab_terms = slab_terms.reshape(-1, 2, sample_count, slab).sum(axis=1)
    scale_terms = scale_terms + slab_terms.transpose(1, 0, 2).reshape(sample_count, channels)
    select_terms = jnp.sum(rows_all[:, 7 * channels + sample_count * slab :], axis=0)
    logit_terms = select_pull(select_terms.reshape(sample_count, -1))[0]
    latent_terms = (
        matmul_high(scale_terms, mod_weight.astype(float32).T)
        + matmul_high(rgb_terms, rgb_mod.astype(float32).T)
        + matmul_high(logit_terms, sel_weight.astype(float32).T)
    )
    class_grad = matmul_high(onehot_class.astype(float32).T, latent_terms)
    sel_grad = matmul_high(latent.T, logit_terms)
    mod_grad = matmul_high(latent.T, scale_terms)
    rgb_mod_grad = matmul_high(latent.T, rgb_terms)
    text_all = lax.all_gather(grad_text.astype(bfloat16), ("dp", "mp"), axis=0, tiled=True)
    token_grad = dot_wide((ids_all[:, None] == words[None, :]).astype(bfloat16), text_all, 0, 0)

    picture_other = swap_mp(picture)
    pictures = jnp.stack(
        [jnp.where(mp == 0, picture, picture_other), jnp.where(mp == 0, picture_other, picture)]
    )
    return (
        both_half(hidden_four, mp),
        pictures,
        both_half(input_grad, mp),
        class_grad,
        token_grad,
        sel_grad,
        mod_grad,
        rgb_mod_grad,
        sums_all[: 3 * channels].reshape(3, channels),
        sums_all[3 * channels : 4 * channels],
        sums_all[4 * channels :],
        bank_grad,
    ) + big_sums


def solution(mesh):
    in_specs = (
        P("dp", None, "mp"),
        P("dp"),
        P("dp", None),
        P("dp"),
        P("dp"),
        P(),
        P(),
        P(),
        P(),
        P(),
        P(),
        P(),
        P(),
        P(None, None, "dp", "mp"),
        P("dp", "mp"),
        P("dp", "mp"),
        P("mp", "dp"),
        P("dp", "mp"),
        P("dp", "mp"),
        P("dp", "mp"),
        P("mp", "dp"),
        P("dp", "mp"),
        P("mp", "dp"),
        P("dp", None, "mp"),
        P("dp", None, None),
        P("dp", None, None),
    )
    out_specs = (
        P("dp", None, "mp"),
        P("dp", None, None),
        P("dp", None, "mp"),
        P(),
        P(),
        P(),
        P(),
        P(),
        P(),
        P(),
        P(),
        P(None, None, "dp", "mp"),
        P("dp", "mp"),
        P("dp", "mp"),
        P("mp", "dp"),
        P("dp", "mp"),
        P("dp", "mp"),
        P("dp", "mp"),
        P("mp", "dp"),
        P("dp", "mp"),
        P("mp", "dp"),
    )
    return jax.shard_map(
        sample_parallel if fits_samples(mesh) else tensor_parallel,
        mesh=mesh, in_specs=in_specs, out_specs=out_specs, check_vma=False
    )
```

```python
import jax
import jax.numpy as jnp
import numpy as np
from jax import lax
from jax.experimental import pallas as pl
from jax.experimental.pallas import tpu as pltpu
from jax.sharding import PartitionSpec as P

HEAD = 64
SIDE = 16


penalty_weight = 1.0


def rounded(values):
    return lax.optimization_barrier(values.astype(jnp.bfloat16)).astype(jnp.float32)


def matmul_high(left, right):
    return jnp.matmul(left, right, precision=lax.Precision.HIGHEST)


def einsum_high(form, *operands):
    return jnp.einsum(form, *operands, precision=lax.Precision.HIGHEST)


def einsum_low(form, left, right):
    return jnp.einsum(
        form,
        left.astype(jnp.bfloat16),
        right.astype(jnp.bfloat16),
        preferred_element_type=jnp.float32,
    )


def noise_field(seed_ids, pixel_count):
    pixel_ids = jnp.arange(pixel_count, dtype=jnp.int32)
    mixed = seed_ids[:, None] * 1103515245 + pixel_ids[None, :] * 40503
    mixed = jnp.bitwise_xor(mixed, jnp.right_shift(mixed, 13)) * 1664525 + 1013904223
    levels = jnp.bitwise_and(jnp.right_shift(mixed, 8), 65535)
    return levels.astype(jnp.float32) / 65536.0 - 0.5


def patches_of(flat_rows, side_len):
    samples_here, pixels, width_here = flat_rows.shape
    half_side = side_len // 2
    picture = flat_rows.reshape(samples_here, half_side, half_side, width_here)
    picture = jnp.repeat(jnp.repeat(picture, 2, axis=1), 2, axis=2)
    padded = jnp.pad(picture, ((0, 0), (1, 1), (1, 1), (0, 0)))
    pieces = [
        padded[:, shift_row : shift_row + side_len, shift_col : shift_col + side_len, :]
        for shift_row in range(3)
        for shift_col in range(3)
    ]
    return jnp.concatenate(pieces, axis=-1).reshape(
        samples_here, side_len * side_len, 9 * width_here
    )


def rms_norm(values):
    return values * lax.rsqrt(jnp.mean(values * values, axis=-1, keepdims=True) + 1e-06)


def conv_part(gathered, kernel, scales, bias_local, strength_local, noise_map):
    samples_here = gathered.shape[0]
    width_out = kernel.shape[2]
    columns = patches_of(gathered, SIDE)
    conv_out = einsum_low("bpr,bro->bpo", columns, kernel)
    squares = jnp.sum((kernel * kernel).reshape(samples_here, 9, -1, width_out), axis=1)
    demodulate = lax.rsqrt(einsum_high("bi,bio->bo", scales * scales, squares) + 1e-08)
    before = conv_out * demodulate[:, None, :] + bias_local + noise_map[:, :, None] * strength_local
    return jax.nn.silu(before)


def self_attention(active, qk_w, value_w, out_w):
    normed = rounded(rms_norm(active))
    queries = rounded(matmul_high(normed, qk_w))
    values = rounded(matmul_high(normed, value_w))
    samples_here, pixels, width_here = queries.shape
    heads_here = width_here // HEAD
    q_heads = queries.reshape(samples_here, pixels, heads_here, HEAD)
    v_heads = values.reshape(samples_here, pixels, heads_here, HEAD)
    lengths = jnp.transpose(jnp.sum(q_heads * q_heads, axis=-1), (0, 2, 1))
    scores = (
        2.0 * einsum_low("bphd,bqhd->bhpq", q_heads, q_heads) - lengths[:, :, None, :]
    ) * HEAD ** (-0.5)
    soft_weights = rounded(jax.nn.softmax(scores, axis=-1))
    mixture = rounded(
        einsum_low("bhpq,bqhd->bphd", soft_weights, v_heads).reshape(
            samples_here, pixels, width_here
        )
    )
    return matmul_high(mixture, out_w)


def cross_attention(active, text_rows, query_w, key_w, value_w, out_w):
    normed = rounded(rms_norm(active))
    queries = rounded(matmul_high(normed, query_w))
    key_rows = rounded(matmul_high(text_rows, key_w))
    values = rounded(matmul_high(text_rows, value_w))
    samples_here, pixels, width_here = queries.shape
    tokens = key_rows.shape[1]
    heads_here = width_here // HEAD
    q_heads = queries.reshape(samples_here, pixels, heads_here, HEAD)
    k_heads = key_rows.reshape(samples_here, tokens, heads_here, HEAD)
    v_heads = values.reshape(samples_here, tokens, heads_here, HEAD)
    scores = einsum_low("bphd,bthd->bhpt", q_heads, k_heads) * HEAD ** (-0.5)
    soft_weights = rounded(jax.nn.softmax(scores, axis=-1))
    mixture = rounded(
        einsum_low("bhpt,bthd->bphd", soft_weights, v_heads).reshape(
            samples_here, pixels, width_here
        )
    )
    return matmul_high(mixture, out_w)


def feed_forward(active, weight_in, weight_out):
    normed = rounded(rms_norm(active))
    inner = rounded(jax.nn.gelu(matmul_high(normed, weight_in)))
    return matmul_high(inner, weight_out)


def tree_add(first, second):
    return jax.tree.map(jnp.add, first, second)


def tensor_parallel(
    layer_input,
    labels,
    text_ids,
    noise_seeds,
    penalty_mask,
    class_table,
    token_table,
    sel_weight,
    mod_weight,
    rgb_mod,
    rgb_weight,
    conv_bias,
    noise_strength,
    kernel_bank,
    qk_weight,
    value_weight,
    attn_out,
    cross_query,
    cross_key,
    cross_value,
    cross_out,
    mlp_in,
    mlp_out,
    cot_feat,
    cot_rgb,
    penalty_dir,
):
    width_local = layer_input.shape[2]
    offset = lax.axis_index("mp") * width_local
    small_params = tuple(
        (
            entry.astype(jnp.float32)
            for entry in (
                class_table,
                token_table,
                sel_weight,
                mod_weight,
                rgb_mod,
                rgb_weight,
                conv_bias,
                noise_strength,
            )
        )
    )

    def fetch_proj():
        fetched = (
            lax.all_gather(qk_weight, "dp", axis=0, tiled=True),
            lax.all_gather(value_weight, "dp", axis=0, tiled=True),
            lax.all_gather(attn_out, "dp", axis=1, tiled=True),
            lax.all_gather(cross_query, "dp", axis=0, tiled=True),
            lax.all_gather(cross_key, "dp", axis=0, tiled=True),
            lax.all_gather(cross_value, "dp", axis=0, tiled=True),
            lax.all_gather(cross_out, "dp", axis=1, tiled=True),
            lax.all_gather(mlp_in, "dp", axis=0, tiled=True),
            lax.all_gather(mlp_out, "dp", axis=1, tiled=True),
        )
        return tuple((entry.astype(jnp.float32) for entry in fetched))

    def style_part(param_set):
        table_class, table_word, select_w, modul_w, rgbmod_w, rgbout_w, bias_w, strength_w = (
            param_set
        )
        onehot_class = (
            labels[:, None] == jnp.arange(table_class.shape[0], dtype=jnp.int32)[None, :]
        ).astype(jnp.float32)
        latent = matmul_high(onehot_class, table_class)
        onehot_word = (
            text_ids[:, :, None] == jnp.arange(table_word.shape[0], dtype=jnp.int32)
        ).astype(jnp.float32)
        text_rows = matmul_high(onehot_word, table_word)
        select = jax.nn.softmax(matmul_high(latent, select_w), axis=-1)
        scales = 1.0 + matmul_high(latent, modul_w)
        rgb_scales = 1.0 + matmul_high(
            latent, lax.dynamic_slice_in_dim(rgbmod_w, offset, width_local, 1)
        )
        bias_local = lax.dynamic_slice_in_dim(bias_w, offset, width_local, 0)
        strength_local = lax.dynamic_slice_in_dim(strength_w, offset, width_local, 0)
        colour_local = lax.dynamic_slice_in_dim(rgbout_w, offset, width_local, 1)
        return (select, scales, rgb_scales, text_rows, bias_local, strength_local, colour_local)

    styles, style_pull = jax.vjp(style_part, small_params)
    noise_map = noise_field(noise_seeds, SIDE * SIDE)

    def owned_sets():
        proj_set = fetch_proj()
        conv_set = (lax.all_gather(kernel_bank, "dp", axis=2, tiled=True).astype(jnp.float32),)
        return ((), conv_set, proj_set[0:3], proj_set[3:7], proj_set[7:9], ())

    def seg_in(active, styles_in, own_set):
        return active * lax.dynamic_slice_in_dim(styles_in[1], offset, width_local, 1)[:, None, :]

    def seg_conv(active, styles_in, own_set):
        bank_full = own_set[0]
        kernel = rounded(matmul_high(styles_in[0], bank_full.reshape(bank_full.shape[0], -1)))
        kernel = kernel.reshape(active.shape[0], -1, bank_full.shape[3])
        return conv_part(active, kernel, styles_in[1], styles_in[4], styles_in[5], noise_map)

    def seg_self(active, styles_in, own_set):
        return self_attention(active, own_set[0], own_set[1], own_set[2])

    def seg_cross(active, styles_in, own_set):
        return cross_attention(active, styles_in[3], own_set[0], own_set[1], own_set[2], own_set[3])

    def seg_mlp(active, styles_in, own_set):
        return feed_forward(active, own_set[0], own_set[1])

    def seg_rgb(active, styles_in, own_set):
        return einsum_high("bpc,bc,kc->bkp", active, styles_in[2], styles_in[6])

    def spread(stacked):
        return lax.all_gather(stacked, "mp", axis=3, tiled=True)

    def collect(stacked):
        return lax.psum_scatter(
            stacked.astype(jnp.bfloat16), "mp", scatter_dimension=3, tiled=True
        ).astype(jnp.float32)

    def spread_one(values):
        return spread(values.astype(jnp.bfloat16)[None])[0].astype(jnp.float32)

    def collect_one(values):
        return collect(values[None])[0]

    own_first = owned_sets()
    input_full = layer_input.astype(jnp.float32)
    gathered_x = spread_one(seg_in(input_full, styles, own_first[0]))
    hidden_one = seg_conv(gathered_x, styles, own_first[1])
    gathered_one = spread_one(hidden_one)
    hidden_two = hidden_one + collect_one(seg_self(gathered_one, styles, own_first[2]))
    gathered_two = spread_one(hidden_two)
    hidden_three = hidden_two + collect_one(seg_cross(gathered_two, styles, own_first[3]))
    gathered_three = spread_one(hidden_three)
    hidden_four = hidden_three + collect_one(seg_mlp(gathered_three, styles, own_first[4]))
    picture = lax.psum(seg_rgb(hidden_four, styles, own_first[5]), "mp")
    own_second = owned_sets()

    def pull_act(segment, active, own_set, cotan):
        return jax.vjp(lambda inner_x: segment(inner_x, styles, own_set), active)[1](cotan)[0]

    grad_four = pull_act(seg_rgb, hidden_four, own_second[5], penalty_dir.astype(jnp.float32))
    back_three = pull_act(seg_mlp, gathered_three, own_second[4], spread_one(grad_four))
    grad_three = grad_four + rounded(collect_one(back_three))
    back_two = pull_act(seg_cross, gathered_two, own_second[3], spread_one(grad_three))
    grad_two = grad_three + rounded(collect_one(back_two))
    back_one = pull_act(seg_self, gathered_one, own_second[2], spread_one(grad_two))
    grad_one = grad_two + rounded(collect_one(back_one))
    grad_moduled = rounded(collect_one(pull_act(seg_conv, gathered_x, own_second[1], grad_one)))
    penalty_grad = pull_act(seg_in, input_full, own_second[0], grad_moduled)
    tangent = penalty_weight * penalty_mask.astype(jnp.float32)[:, None, None] * penalty_grad
    own_third = owned_sets()

    def push(segment, active, own_set, tangent_in):
        return jax.jvp(lambda inner_x: segment(inner_x, styles, own_set), (active,), (tangent_in,))[
            1
        ]

    tan_x = spread_one(push(seg_in, input_full, own_third[0], tangent))
    tan_one = push(seg_conv, gathered_x, own_third[1], tan_x)
    tan_g1 = spread_one(tan_one)
    tan_two = tan_one + collect_one(push(seg_self, gathered_one, own_third[2], tan_g1))
    tan_g2 = spread_one(tan_two)
    tan_three = tan_two + collect_one(push(seg_cross, gathered_two, own_third[3], tan_g2))
    tan_g3 = spread_one(tan_three)
    tan_four = tan_three + collect_one(push(seg_mlp, gathered_three, own_third[4], tan_g3))
    own_fourth = owned_sets()

    def pull_both(segment, active, tangent_in, own_set, cotan, cotan_tangent):

        def joint(inner_x, inner_tangent, styles_in, own_in):
            return jax.jvp(
                lambda value_x: segment(value_x, styles_in, own_in), (inner_x,), (inner_tangent,)
            )

        return jax.vjp(joint, active, tangent_in, styles, own_set)[1]((cotan, cotan_tangent))

    grad_act, grad_tan, style_acc, ignored = pull_both(
        seg_rgb,
        hidden_four,
        tan_four,
        own_fourth[5],
        cot_rgb.astype(jnp.float32),
        penalty_dir.astype(jnp.float32),
    )
    main_now = cot_feat.astype(jnp.float32) + grad_act
    side_now = grad_tan
    layer_grads = []
    for segment, active, tangent_in, own_set in (
        (seg_mlp, gathered_three, tan_g3, own_fourth[4]),
        (seg_cross, gathered_two, tan_g2, own_fourth[3]),
        (seg_self, gathered_one, tan_g1, own_fourth[2]),
    ):
        both_wide = spread(jnp.stack([main_now, side_now]).astype(jnp.bfloat16)).astype(jnp.float32)
        grad_act, grad_tan, grad_sty, grad_own = pull_both(
            segment, active, tangent_in, own_set, both_wide[0], both_wide[1]
        )
        style_acc = tree_add(style_acc, grad_sty)
        layer_grads.append(grad_own)
        both_sums = collect(jnp.stack([grad_act, grad_tan]))
        main_now = main_now + rounded(both_sums[0])
        side_now = side_now + rounded(both_sums[1])
    grad_act, grad_tan, grad_sty, grads_conv = pull_both(
        seg_conv, gathered_x, tan_x, own_fourth[1], main_now, side_now
    )
    style_acc = tree_add(style_acc, grad_sty)
    both_sums = collect(jnp.stack([grad_act, grad_tan]))
    grad_act, grad_tan, grad_sty, ignored = pull_both(
        seg_in, input_full, tangent, own_fourth[0], rounded(both_sums[0]), rounded(both_sums[1])
    )
    style_acc = tree_add(style_acc, grad_sty)
    proj_terms = layer_grads[2] + layer_grads[1] + layer_grads[0]
    big_terms = grads_conv + proj_terms
    big_sums = (
        lax.psum_scatter(
            big_terms[0].astype(jnp.bfloat16), "dp", scatter_dimension=2, tiled=True
        ).astype(jnp.float32),
        lax.psum_scatter(
            big_terms[1].astype(jnp.bfloat16), "dp", scatter_dimension=0, tiled=True
        ).astype(jnp.float32),
        lax.psum_scatter(
            big_terms[2].astype(jnp.bfloat16), "dp", scatter_dimension=0, tiled=True
        ).astype(jnp.float32),
        lax.psum_scatter(
            big_terms[3].astype(jnp.bfloat16), "dp", scatter_dimension=1, tiled=True
        ).astype(jnp.float32),
        lax.psum_scatter(
            big_terms[4].astype(jnp.bfloat16), "dp", scatter_dimension=0, tiled=True
        ).astype(jnp.float32),
        lax.psum_scatter(
            big_terms[5].astype(jnp.bfloat16), "dp", scatter_dimension=0, tiled=True
        ).astype(jnp.float32),
        lax.psum_scatter(
            big_terms[6].astype(jnp.bfloat16), "dp", scatter_dimension=0, tiled=True
        ).astype(jnp.float32),
        lax.psum_scatter(
            big_terms[7].astype(jnp.bfloat16), "dp", scatter_dimension=1, tiled=True
        ).astype(jnp.float32),
        lax.psum_scatter(
            big_terms[8].astype(jnp.bfloat16), "dp", scatter_dimension=0, tiled=True
        ).astype(jnp.float32),
        lax.psum_scatter(
            big_terms[9].astype(jnp.bfloat16), "dp", scatter_dimension=1, tiled=True
        ).astype(jnp.float32),
    )
    small_terms = style_pull(style_acc)[0]
    small_sums = lax.psum(
        (
            small_terms[0],
            small_terms[1],
            small_terms[2],
            small_terms[3],
            small_terms[4],
            small_terms[5],
            small_terms[6],
            small_terms[7],
        ),
        ("dp", "mp"),
    )
    return (hidden_four, picture, grad_act) + tuple(small_sums) + tuple(big_sums)


def fits_samples(mesh):
    return mesh.shape["dp"] == 16 and mesh.shape["mp"] == 2


def dot_wide(left, right, left_dim, right_dim):
    return lax.dot_general(
        left.astype(jnp.bfloat16),
        right.astype(jnp.bfloat16),
        (((left_dim,), (right_dim,)), ((), ())),
        preferred_element_type=jnp.float32,
    )


def make_products(flip):
    depth = 1 if flip else 0

    def weight_grad(rows, cotan):
        if flip:
            return dot_wide(cotan, rows, 0, 0).astype(jnp.bfloat16)
        return dot_wide(rows, cotan, 0, 0).astype(jnp.bfloat16)

    @jax.custom_vjp
    def single(rows, weight):
        return dot_wide(rows, weight, 1, depth)

    def single_fwd(rows, weight):
        return single(rows, weight), (rows, weight)

    def single_bwd(kept, cotan):
        rows, weight = kept
        return dot_wide(cotan, weight, 1, 1 - depth), weight_grad(rows, cotan)

    single.defvjp(single_fwd, single_bwd)

    @jax.custom_vjp
    def pair(rows, tangents, weight):
        return dot_wide(rows, weight, 1, depth), dot_wide(tangents, weight, 1, depth)

    def pair_fwd(rows, tangents, weight):
        return pair(rows, tangents, weight), (rows, tangents, weight)

    def pair_bwd(kept, cotans):
        rows, tangents, weight = kept
        count = rows.shape[0]
        both = jnp.concatenate([entry.astype(jnp.bfloat16) for entry in cotans], axis=0)
        inputs = jnp.concatenate(
            [rows.astype(jnp.bfloat16), tangents.astype(jnp.bfloat16)], axis=0
        )
        back = dot_wide(both, weight, 1, 1 - depth)
        return back[:count], back[count:], weight_grad(inputs, both)

    pair.defvjp(pair_fwd, pair_bwd)
    return single, pair


product, product_pair = make_products(False)
product_flip, product_flip_pair = make_products(True)


def with_tangent(fun, value, tangent):
    return jax.jvp(fun, (value,), (tangent,))


def last_softmax(scores):
    return jax.nn.softmax(scores, axis=-1)


def post_conv(conv_out, sums, bias, strength, noise):
    demodulate = lax.rsqrt(sums + 1e-08)
    return jax.nn.silu(conv_out * demodulate[None] + bias[None] + noise[:, None] * strength[None])


def picture_of(hidden, rgb_scales, rgb_weight):
    return einsum_high("pc,kc->kp", hidden, rgb_scales[None] * rgb_weight)


CHUNK = 16
PAD_ROWS = (SIDE + 2) * SIDE
PIXELS = SIDE * SIDE


def placing(half_side):
    side = 2 * half_side
    table = np.zeros((side + 2, side, 3, half_side * half_side), np.float32)
    for row in range(1, side + 1):
        for col in range(side):
            for shift in range(3):
                at = col + shift - 1
                if 0 <= at < side:
                    table[row, col, shift, (row - 1) // 2 * half_side + at // 2] = 1.0
    return jnp.asarray(table.reshape((side + 2) * side, -1), jnp.bfloat16)


def dot_f32(left, right, left_dim, right_dim):
    return lax.dot_general(
        left, right, (((left_dim,), (right_dim,)), ((), ())), preferred_element_type=jnp.float32
    )


def mix_matrix(select):
    high = select.astype(jnp.bfloat16)
    low = (select - high.astype(jnp.float32)).astype(jnp.bfloat16)
    eye = jnp.eye(CHUNK, dtype=jnp.bfloat16)
    parts = jnp.stack([high, low], axis=1)
    wide = parts[:, None, :, :, None] * eye[None, :, None, None, :]
    return wide.reshape(select.shape[0] * CHUNK, -1)


def lanes_wide(column, width):
    return jnp.concatenate([column] * (width // column.shape[-1]), axis=-1)


def mix_body(pieces, mix_ref, bank_ref, squares_ref, kernel_ref, sums_ref):
    step = pl.program_id(0)

    @pl.when(step == 0)
    def _():
        sums_ref[...] = jnp.zeros_like(sums_ref)

    kernels, rows, width = bank_ref.shape
    samples = kernel_ref.shape[0]
    per_tap = squares_ref.shape[1]
    for piece in range(pieces):
        part = bank_ref[:, piece * CHUNK : (piece + 1) * CHUNK, :].reshape(kernels * CHUNK, width)
        mixed = dot_f32(mix_ref[...], jnp.concatenate([part, part], axis=0), 1, 0)
        mixed = mixed.astype(jnp.bfloat16).reshape(samples, CHUNK, width)
        kernel_ref[:, piece * CHUNK : (piece + 1) * CHUNK, :] = mixed
        first = lax.rem(step * rows + piece * CHUNK, per_tap)
        factor = squares_ref[:, pl.ds(pl.multiple_of(first, CHUNK), CHUNK), :]
        wide = mixed.astype(jnp.float32)
        sums_ref[...] += jnp.sum(wide * wide * lanes_wide(factor, width), axis=1)


def mix_kernels(mix, bank_rows, squares):
    kernels, depth, width = bank_rows.shape
    samples = squares.shape[0]
    pieces = 4
    rows = pieces * CHUNK
    return pl.pallas_call(
        lambda *refs: mix_body(pieces, *refs),
        grid=(depth // rows,),
        in_specs=[
            pl.BlockSpec(mix.shape, lambda step: (0, 0)),
            pl.BlockSpec((kernels, rows, width), lambda step: (0, step, 0)),
            pl.BlockSpec(squares.shape, lambda step: (0, 0, 0)),
        ],
        out_specs=[
            pl.BlockSpec((samples, rows, width), lambda step: (0, step, 0)),
            pl.BlockSpec((samples, width), lambda step: (0, 0)),
        ],
        out_shape=[
            jax.ShapeDtypeStruct((samples, depth, width), jnp.bfloat16),
            jax.ShapeDtypeStruct((samples, width), jnp.float32),
        ],
        compiler_params=pltpu.CompilerParams(vmem_limit_bytes=48 * 2**20),
        name="mix_kernels",
    )(mix, bank_rows, squares)


def place_rows(slab, place_ref, spot_ref):
    pixels, width = slab.shape
    for shift in range(3):
        spot_ref[
            shift * pixels : (shift + 1) * pixels, shift * width : (shift + 1) * width
        ] = slab
    return dot_f32(place_ref[...], spot_ref[...], 1, 0).astype(jnp.bfloat16)


def conv_step(extra, sample, slab_ref, place_ref, kernel_ref, sums_ref, out_ref, spot_ref):
    rows = place_rows(slab_ref[0], place_ref, spot_ref)
    depth = rows.shape[1]
    total = None
    for shift in range(3):
        term = dot_f32(
            rows[shift * SIDE : shift * SIDE + PIXELS],
            kernel_ref[0, shift * depth : (shift + 1) * depth, :],
            1,
            0,
        )
        total = term if total is None else total + term
    out_ref[0, :PIXELS, :] = total.astype(jnp.bfloat16)
    if extra:
        line = sums_ref[pl.ds(sample, 1), :]
        out_ref[0, PIXELS:, :] = jnp.broadcast_to(line, (CHUNK, line.shape[1])).astype(jnp.bfloat16)


def fold_back(cotan, place_ref, kernel_ref, wide_ref, pixels, width):
    depth = 3 * width
    wide_ref[...] = jnp.zeros_like(wide_ref)
    for shift in range(3):
        wide_ref[shift * SIDE : shift * SIDE + PIXELS, :] += dot_f32(
            cotan, kernel_ref[0, shift * depth : (shift + 1) * depth, :], 1, 1
        )
    back = dot_f32(place_ref[...], wide_ref[...].astype(jnp.bfloat16), 0, 0)
    total = None
    for shift in range(3):
        term = back[shift * pixels : (shift + 1) * pixels, shift * width : (shift + 1) * width]
        total = term if total is None else total + term
    return total.astype(jnp.bfloat16)


def second_step(
    slab_ref,
    tan_ref,
    place_ref,
    kernel_ref,
    cotan_ref,
    side_ref,
    squares_ref,
    grad_ref,
    back_ref,
    scale_ref,
    spot_ref,
    wide_ref,
):
    pixels, width = slab_ref.shape[1:]
    depth = 3 * width
    rows = place_rows(slab_ref[0], place_ref, spot_ref)
    tan_rows = place_rows(tan_ref[0], place_ref, spot_ref)
    line = cotan_ref[0, PIXELS : PIXELS + CHUNK, :][:1].astype(jnp.float32)
    factor = 2.0 * lanes_wide(squares_ref[0], line.shape[1]) * line
    totals = None
    for shift in range(3):
        span = slice(shift * SIDE, shift * SIDE + PIXELS)
        grad = dot_f32(rows[span], cotan_ref[0, :PIXELS, :], 0, 0)
        grad = grad + dot_f32(tan_rows[span], side_ref[0], 0, 0)
        for tap in range(3):
            at = shift * depth + tap * width
            own = kernel_ref[0, at : at + width, :].astype(jnp.float32)
            grad_ref[0, at : at + width, :] = (
                grad[tap * width : (tap + 1) * width] + own * factor
            ).astype(jnp.bfloat16)
            term = own * own
            totals = term if totals is None else totals + term
    summed = jnp.sum(totals * line, axis=1, keepdims=True)
    scale_ref[0] = jnp.broadcast_to(summed, scale_ref.shape[1:])
    back_ref[0] = fold_back(
        cotan_ref[0, :PIXELS, :], place_ref, kernel_ref, wide_ref, pixels, width
    )


def unmix_body(pieces, mix_ref, bank_ref, grad_ref, out_ref, select_ref):
    @pl.when(pl.program_id(0) == 0)
    def _():
        select_ref[...] = jnp.zeros_like(select_ref)

    kernels, _, width = bank_ref.shape
    samples = grad_ref.shape[0]
    for piece in range(pieces):
        span = slice(piece * CHUNK, (piece + 1) * CHUNK)
        grad = grad_ref[:, span, :].reshape(samples * CHUNK, width)
        mixed = dot_f32(mix_ref[...], grad, 0, 0)
        count = kernels * CHUNK
        out_ref[:, span, :] = (mixed[:count] + mixed[count:]).reshape(kernels, CHUNK, width)
        part = bank_ref[:, span, :].reshape(count, width)
        select_ref[...] += dot_f32(grad, part, 1, 1)


def unmix_kernels(mix, bank_rows, grad):
    kernels, depth, width = bank_rows.shape
    samples = grad.shape[0]
    pieces = 4
    rows = pieces * CHUNK
    return pl.pallas_call(
        lambda *refs: unmix_body(pieces, *refs),
        grid=(depth // rows,),
        in_specs=[
            pl.BlockSpec(mix.shape, lambda step: (0, 0)),
            pl.BlockSpec((kernels, rows, width), lambda step: (0, step, 0)),
            pl.BlockSpec((samples, rows, width), lambda step: (0, step, 0)),
        ],
        out_specs=[
            pl.BlockSpec((kernels, rows, width), lambda step: (0, step, 0)),
            pl.BlockSpec((samples * CHUNK, kernels * CHUNK), lambda step: (0, 0)),
        ],
        out_shape=[
            jax.ShapeDtypeStruct((kernels, depth, width), jnp.float32),
            jax.ShapeDtypeStruct((samples * CHUNK, kernels * CHUNK), jnp.float32),
        ],
        compiler_params=pltpu.CompilerParams(vmem_limit_bytes=48 * 2**20),
        name="unmix_kernels",
    )(mix, bank_rows, grad)


@jax.custom_vjp
def row_products(left, right):
    return dot_f32(left.astype(jnp.bfloat16), right.astype(jnp.bfloat16), 1, 1)


def row_products_fwd(left, right):
    return row_products(left, right), (left, right)


def row_products_bwd(kept, cotan):
    left, right = (entry.astype(jnp.bfloat16) for entry in kept)
    short = cotan.astype(jnp.bfloat16)
    return dot_f32(short, right, 1, 0), dot_f32(short, left, 0, 0)


row_products.defvjp(row_products_fwd, row_products_bwd)


@jax.custom_vjp
def mixed_rows(soft, values):
    return dot_f32(soft.astype(jnp.bfloat16), values.astype(jnp.bfloat16), 1, 0)


def mixed_rows_fwd(soft, values):
    return mixed_rows(soft, values), (soft, values)


def mixed_rows_bwd(kept, cotan):
    soft, values = (entry.astype(jnp.bfloat16) for entry in kept)
    short = cotan.astype(jnp.bfloat16)
    return dot_f32(short, values, 1, 1), dot_f32(soft, short, 0, 0)


mixed_rows.defvjp(mixed_rows_fwd, mixed_rows_bwd)


@jax.custom_vjp
def as_row(column):
    count = column.shape[0]
    lane = lax.broadcasted_iota(jnp.int32, (count, 128), 1)
    rest, parts = column, jnp.zeros((count, 128), jnp.float32)
    for place in range(3):
        short = rest.astype(jnp.bfloat16).astype(jnp.float32)
        parts = jnp.where(lane == place, short, parts)
        rest = rest - short
    ones = jnp.ones((count, 128), jnp.bfloat16)
    return dot_f32(ones, parts.astype(jnp.bfloat16), 1, 1)


def as_row_fwd(column):
    return as_row(column), None


def as_row_bwd(kept, cotan):
    ones = jnp.ones((cotan.shape[0], 128), jnp.bfloat16)
    return (dot_f32(cotan.astype(jnp.bfloat16), ones, 0, 0)[:, :1],)


as_row.defvjp(as_row_fwd, as_row_bwd)


def soft_of(scores):
    top = lax.stop_gradient(jnp.max(scores, axis=1, keepdims=True))
    powers = jnp.exp(scores - top)
    return powers / jnp.sum(powers, axis=1, keepdims=True)


def soft_tangent(soft, tangent):
    return soft * (tangent - jnp.sum(soft * tangent, axis=1, keepdims=True))


def squared(left, right):
    return jnp.sum(left * right, axis=1, keepdims=True)


def self_head(queries, values):
    scores = 2.0 * row_products(queries, queries) - as_row(squared(queries, queries))
    return (mixed_rows(soft_of(scores * HEAD ** (-0.5)), values),)


def self_head_joint(queries, tan_queries, values, tan_values):
    scores = 2.0 * row_products(queries, queries) - as_row(squared(queries, queries))
    tan_scores = row_products(tan_queries, queries) + row_products(queries, tan_queries)
    tan_scores = 2.0 * (tan_scores - as_row(squared(queries, tan_queries)))
    soft = soft_of(scores * HEAD ** (-0.5))
    tan_soft = soft_tangent(soft, tan_scores * HEAD ** (-0.5))
    return (
        mixed_rows(soft, values),
        mixed_rows(tan_soft, values) + mixed_rows(soft, tan_values),
    )


def cross_head(queries, keys, values):
    return (mixed_rows(soft_of(row_products(queries, keys) * HEAD ** (-0.5)), values),)


def cross_head_joint(queries, tan_queries, keys, values):
    soft = soft_of(row_products(queries, keys) * HEAD ** (-0.5))
    tan_soft = soft_tangent(soft, row_products(tan_queries, keys) * HEAD ** (-0.5))
    return mixed_rows(soft, values), mixed_rows(tan_soft, values)


def per_head(fun, arrays, shapes, name):
    lanes = 2 * HEAD

    def body(*refs):
        inputs, outputs = refs[: len(arrays)], refs[len(arrays) :]
        for head in range(2):
            span = slice(head * HEAD, (head + 1) * HEAD)
            results = fun(*[ref[:, span].astype(jnp.float32) for ref in inputs])
            for ref, result in zip(outputs, results):
                ref[:, span] = result.astype(jnp.bfloat16)

    return pl.pallas_call(
        body,
        grid=(arrays[0].shape[1] // lanes,),
        in_specs=[pl.BlockSpec((entry.shape[0], lanes), lambda step: (0, step)) for entry in arrays],
        out_specs=[pl.BlockSpec((shape[0], lanes), lambda step: (0, step)) for shape in shapes],
        out_shape=[jax.ShapeDtypeStruct(shape, jnp.bfloat16) for shape in shapes],
        compiler_params=pltpu.CompilerParams(vmem_limit_bytes=32 * 2**20),
        name=name,
    )(*arrays)


def make_attention(fun, count, name):
    @jax.custom_vjp
    def attend(*arrays):
        return tuple(per_head(fun, arrays, [arrays[0].shape] * count, name))

    def attend_fwd(*arrays):
        return attend(*arrays), arrays

    def attend_bwd(arrays, cotans):
        def pull(*given):
            return jax.vjp(fun, *given[: len(arrays)])[1](tuple(given[len(arrays) :]))

        shapes = [entry.shape for entry in arrays]
        return tuple(per_head(pull, list(arrays) + list(cotans), shapes, name + "_pull"))

    attend.defvjp(attend_fwd, attend_bwd)
    return attend


self_attend = make_attention(self_head, 1, "self_heads")
self_attend_joint = make_attention(self_head_joint, 2, "self_heads_joint")
cross_attend = make_attention(cross_head, 1, "cross_heads")
cross_attend_joint = make_attention(cross_head_joint, 2, "cross_heads_joint")


def short_of(*arrays):
    return [entry.astype(jnp.bfloat16) for entry in arrays]


def layer_forward(conv_out, sums, text_rows, small, weights, noise):
    bias, strength, rgb_scales, rgb_weight = small
    qk_w, value_w, attn_w, query_w, key_w, cval_w, cout_w, mlp_w, mout_w = weights
    hidden_one = post_conv(conv_out, sums, bias, strength, noise)
    normed = rms_norm(hidden_one)
    (mixture,) = self_attend(*short_of(product(normed, qk_w), product(normed, value_w)))
    hidden_two = hidden_one + product_flip(mixture.astype(jnp.float32), attn_w)
    normed = rms_norm(hidden_two)
    (mixture,) = cross_attend(
        *short_of(
            product(normed, query_w), product(text_rows, key_w), product(text_rows, cval_w)
        )
    )
    hidden_three = hidden_two + product_flip(mixture.astype(jnp.float32), cout_w)
    normed = rms_norm(hidden_three)
    inner = jax.nn.gelu(product(normed, mlp_w))
    hidden_four = hidden_three + product_flip(inner, mout_w)
    return hidden_four, picture_of(hidden_four, rgb_scales, rgb_weight)


def layer_joint(conv_out, conv_tan, sums, text_rows, small, weights, noise):
    bias, strength, rgb_scales, rgb_weight = small
    qk_w, value_w, attn_w, query_w, key_w, cval_w, cout_w, mlp_w, mout_w = weights
    hidden_one, tan_one = with_tangent(
        lambda value: post_conv(value, sums, bias, strength, noise), conv_out, conv_tan
    )
    normed, tan_normed = with_tangent(rms_norm, hidden_one, tan_one)
    queries, tan_queries = product_pair(normed, tan_normed, qk_w)
    values, tan_values = product_pair(normed, tan_normed, value_w)
    mixture, tan_mixture = self_attend_joint(*short_of(queries, tan_queries, values, tan_values))
    added, tan_added = product_flip_pair(
        mixture.astype(jnp.float32), tan_mixture.astype(jnp.float32), attn_w
    )
    hidden_two, tan_two = hidden_one + added, tan_one + tan_added
    normed, tan_normed = with_tangent(rms_norm, hidden_two, tan_two)
    queries, tan_queries = product_pair(normed, tan_normed, query_w)
    mixture, tan_mixture = cross_attend_joint(
        *short_of(queries, tan_queries, product(text_rows, key_w), product(text_rows, cval_w))
    )
    added, tan_added = product_flip_pair(
        mixture.astype(jnp.float32), tan_mixture.astype(jnp.float32), cout_w
    )
    hidden_three, tan_three = hidden_two + added, tan_two + tan_added
    normed, tan_normed = with_tangent(rms_norm, hidden_three, tan_three)
    before, tan_before = product_pair(normed, tan_normed, mlp_w)
    inner, tan_inner = with_tangent(jax.nn.gelu, before, tan_before)
    added, tan_added = product_flip_pair(inner, tan_inner, mout_w)
    hidden_four, tan_four = hidden_three + added, tan_three + tan_added
    return (
        hidden_four,
        picture_of(hidden_four, rgb_scales, rgb_weight),
        picture_of(tan_four, rgb_scales, rgb_weight),
    )


SWAP = ((0, 1), (1, 0))


def swap_mp(values):
    return lax.ppermute(values, "mp", SWAP)


def pick(values, index):
    return lax.dynamic_index_in_dim(values, index, 0, keepdims=False)


def own_whole(values, mp):
    mine, other = pick(values, mp), swap_mp(pick(values, 1 - mp))
    first = jnp.where(mp == 0, mine, other)
    second = jnp.where(mp == 0, other, mine)
    return jnp.concatenate([first, second], axis=-1)


def both_half(whole, mp):
    half = whole.shape[-1] // 2
    mine = lax.dynamic_slice_in_dim(whole, mp * half, half, whole.ndim - 1)
    other = swap_mp(lax.dynamic_slice_in_dim(whole, (1 - mp) * half, half, whole.ndim - 1))
    first = jnp.where(mp == 0, mine, other)
    second = jnp.where(mp == 0, other, mine)
    return jnp.stack([first, second])


def to_slabs(both):
    devices = lax.axis_size("dp")
    parts = both.reshape(2, both.shape[1], devices, -1).transpose(2, 0, 1, 3)
    parts = lax.all_to_all(parts, "dp", 0, 0, tiled=True)
    return parts.reshape(2 * devices, both.shape[1], -1)


def from_slabs(slabs, mp):
    devices = lax.axis_size("dp")
    rows = slabs.shape[1]
    parts = slabs.astype(jnp.bfloat16).reshape((devices, 2) + slabs.shape[1:])
    parts = lax.all_to_all(parts, "dp", 0, 0, tiled=True)
    parts = parts.transpose(1, 2, 0, 3).reshape(2, rows, -1)
    other = swap_mp(pick(parts, 1 - mp))
    return pick(parts, mp).astype(jnp.float32) + other.astype(jnp.float32)


PLANES = 4


class Place:
    def __init__(self):
        dp = lax.axis_index("dp")
        self.z, self.y, self.core = dp // 4, lax.rem(dp // 2, 2), lax.rem(dp, 2)
        self.x = lax.axis_index("mp")


def greet(place, axes):
    barrier = pltpu.get_barrier_semaphore()

    def tell(**there):
        at = dict(z=place.z, y=place.y, core=place.core, x=place.x)
        at.update(there)
        pl.semaphore_signal(
            barrier,
            inc=1,
            device_id=((at["z"] * 2 + at["y"]) * 2 + at["core"], at["x"]),
            device_id_type=pl.DeviceIdType.MESH,
        )

    tell(core=1 - place.core)
    count = 1
    for name in ("y", "x"):
        if name in axes:
            tell(**{name: 1 - getattr(place, name)})
            count += 1

    @pl.when(place.z > 0)
    def _():
        tell(z=place.z - 1)

    @pl.when(place.z < PLANES - 1)
    def _():
        tell(z=place.z + 1)

    between = (place.z > 0) & (place.z < PLANES - 1)
    pl.semaphore_wait(barrier, count + jnp.where(between, 2, 1))


def gather_body(pieces, inputs, outputs, axes, send_sem, recv_sem, own_sem):
    place = Place()
    greet(place, axes)
    sends = []

    def spot(z, y, core, x):
        return (z * 2 + y) * 2 + core, x

    def chip(z, y, x):
        return (z * 2 + y) * 2 + x

    def send(number, piece, source, target, slot, parity, first, condition):
        sz, sy, sx = source
        dp, mp = spot(sz, sy, place.core, sx)
        there = piece["to"](outputs, dp, mp)
        copy = pltpu.make_async_remote_copy(
            src_ref=piece["of"](inputs) if first else there,
            dst_ref=there,
            send_sem=send_sem.at[number, chip(sz, sy, sx), slot],
            recv_sem=recv_sem.at[number, chip(sz, sy, sx), parity],
            device_id=spot(*target),
            device_id_type=pl.DeviceIdType.MESH,
        )

        if condition is None:
            copy.start()
        else:
            pl.when(condition)(copy.start)
        sends.append((condition, copy))

    def onward(number, piece, source, came, first, condition):
        def both(more):
            if condition is None:
                return more
            return condition if more is None else condition & more

        order = piece["order"]
        later = order if came is None else order[order.index(came[0]) :]
        for name in later:
            here = dict(z=place.z, y=place.y, core=place.core, x=place.x)
            if name == "z":
                for way, slot in ((1, 0), (-1, 1)):
                    if came is not None and came[0] == "z" and came[1] != way:
                        continue
                    fits = place.z < PLANES - 1 if way == 1 else place.z > 0
                    target = (place.z + way, place.y, place.core, place.x)
                    send(number, piece, source, target, slot, 0, first, both(fits))
            elif came is None or came[0] != name:
                here[name] = 1 - here[name]
                target = (here["z"], here["y"], here["core"], here["x"])
                slot = 2 if name == "y" else 3
                send(number, piece, source, target, slot, 0, first, both(None))
        target = (place.z, place.y, 1 - place.core, place.x)
        send(number, piece, source, target, 4, 1, first, both(None))

    def arrive(number, piece, source, parity, condition):
        sz, sy, sx = source
        core = place.core if parity == 0 else 1 - place.core
        there = piece["to"](outputs, *spot(sz, sy, core, sx))

        def wait():
            pltpu.make_async_remote_copy(
                src_ref=there,
                dst_ref=there,
                send_sem=send_sem.at[number, chip(sz, sy, sx), 0],
                recv_sem=recv_sem.at[number, chip(sz, sy, sx), parity],
                device_id=spot(place.z, place.y, 1 - place.core, place.x),
                device_id_type=pl.DeviceIdType.MESH,
            ).wait_recv()

        if condition is None:
            wait()
        else:
            pl.when(condition)(wait)

    own = []
    for number, piece in enumerate(pieces):
        onward(number, piece, (place.z, place.y, place.x), None, True, None)
        copy = pltpu.make_async_copy(
            piece["of"](inputs),
            piece["to"](outputs, *spot(place.z, place.y, place.core, place.x)),
            own_sem.at[number],
        )
        copy.start()
        own.append(copy)
    flips = [(fy, fx) for fy in (0, 1) for fx in ((0, 1) if "x" in axes else (0,))]
    blocks = [(dz, fy, fx) for dz in (0, 1, -1, 2, -2, 3, -3) for fy, fx in flips]
    blocks = sorted(blocks, key=lambda block: abs(block[0]) + block[1] + block[2])
    for dz, fy, fx in blocks:
        if (dz, fy, fx) == (0, 0, 0):
            continue
        condition = None
        if dz > 0:
            condition = place.z >= dz
        elif dz < 0:
            condition = place.z < PLANES + dz
        source = (
            place.z - dz,
            1 - place.y if fy else place.y,
            1 - place.x if fx else place.x,
        )
        for number, piece in enumerate(pieces):
            arrive(number, piece, source, 0, condition)
            moved = dict(z=dz, y=fy, x=fx)
            last = [name for name in piece["order"] if moved[name]][-1]
            came = (last, (1 if dz > 0 else -1) if last == "z" else 0)
            onward(number, piece, source, came, False, condition)
    for number, piece in enumerate(pieces):
        for sz in range(PLANES):
            for sy in range(2):
                for sx in (0, 1) if "x" in axes else (place.x,):
                    arrive(number, piece, (sz, sy, sx), 1, None)
    for condition, copy in sends:
        if condition is None:
            copy.wait_send()
        else:
            pl.when(condition)(copy.wait_send)
    for copy in own:
        copy.wait()


def gather_call(pieces, axes, arrays, shapes, call_id, name):
    count = len(arrays)

    def body(*refs):
        inputs, outputs = refs[:count], refs[count : count + len(shapes)]
        gather_body(pieces, inputs, outputs, axes, *refs[count + len(shapes) :])

    return pl.pallas_call(
        body,
        in_specs=[pl.BlockSpec(memory_space=pl.ANY)] * count,
        out_specs=[pl.BlockSpec(memory_space=pl.ANY)] * len(shapes),
        out_shape=[
            jax.ShapeDtypeStruct(shape, entry.dtype) for shape, entry in zip(shapes, arrays)
        ],
        scratch_shapes=[
            pltpu.SemaphoreType.DMA((len(pieces), 16, 5)),
            pltpu.SemaphoreType.DMA((len(pieces), 16, 2)),
            pltpu.SemaphoreType.DMA((len(pieces),)),
        ],
        compiler_params=pltpu.CompilerParams(collective_id=call_id, has_side_effects=True),
        name=name,
    )(*arrays)


def rows_at(index, rows):
    return pl.ds(pl.multiple_of(index * rows, rows), rows)


def lanes_at(index, lanes):
    return pl.ds(pl.multiple_of(index * lanes, lanes), lanes)


def gather_weights(shards, numbers, call_id):
    orders = dict(x=("z", "y", "x"), y=("z", "x", "y"), z=("x", "y", "z"))
    turns = ("x", "y", "x", "y", "x", "y", "z", "y", "z")

    def piece(number, turn):
        rows, lanes = arrays[number].shape
        stacked = number == len(shards)

        def to(refs, dp, mp):
            if stacked:
                return refs[number].at[rows_at(dp * 2 + mp, rows)]
            return refs[number].at[rows_at(dp, rows), lanes_at(mp, lanes)]

        return dict(order=orders[turn], of=lambda refs: refs[number], to=to)

    arrays = list(shards) + [numbers]
    pieces = [piece(len(shards), "x")]
    pieces += [piece(number, turn) for number, turn in enumerate(turns)]
    shapes = [(entry.shape[0] * 16, entry.shape[1] * 2) for entry in shards]
    shapes.append((numbers.shape[0] * 32, numbers.shape[1]))
    return gather_call(pieces, ("z", "y", "x"), arrays, shapes, call_id, "gather_weights")


def plane_of(z, turn):
    low = jnp.where(turn < 2, 1 - turn, turn)
    high = jnp.where(turn < 2, 2 + turn, 3 - turn)
    between = jnp.where(z == 1, low, high)
    return jnp.where(z == 0, turn, jnp.where(z == PLANES - 1, PLANES - 1 - turn, between))


class Stream:
    def __init__(self, source, slots, sem, where):
        self.source, self.slots, self.sem, self.where = source, slots, sem, where

    def copy(self, turn):
        slot = lax.rem(turn, 2)
        return pltpu.make_async_copy(
            self.source.at[self.where(turn)], self.slots.at[slot], self.sem.at[slot]
        )

    def take(self, turn, count):
        self.copy(turn).wait()

        @pl.when(turn + 1 < count)
        def _():
            self.copy(turn + 1).start()

        return lax.rem(turn, 2)


def consume_body(cut, samples, value_ref, landing, kernel_ref, slots, sems, work):
    kernel_sem, send_sem, recv_sem, own_sem = sems
    place = Place()
    z, y, core, x = place.z, place.y, place.core, place.x
    lanes = landing.shape[-1]
    pieces = [(s, slice(0, cut), "zy") for s in range(samples)]
    pieces += [(s, slice(cut, lanes), "yz") for s in range(samples)]
    blocks = 2 * PLANES
    count = 2 * samples * blocks

    def chip_at(block):
        return plane_of(z, block // 2), jnp.where(lax.rem(block, 2) == 1, 1 - y, y)

    def first_sample(block, parity):
        plane, row = chip_at(block)
        other = jnp.where(parity == 1, 1 - core, core)
        return ((plane * 2 + row) * 2 + other) * samples

    def sample_at(turn):
        block = turn // (2 * samples)
        return first_sample(block, lax.rem(turn // samples, 2)) + lax.rem(turn, samples)

    def sends(block, act):
        plane, row = chip_at(block)
        same_row = lax.rem(block, 2) == 0
        up, down = (plane <= z) & (z < PLANES - 1), (plane >= z) & (z > 0)
        for number, (s, span, order) in enumerate(pieces):
            view = landing.at[first_sample(block, 0) + s, :, span]
            if order == "zy":
                ways = (up & same_row, down & same_row, same_row)
            else:
                ways = (up, down, block == 0)
            targets = (
                (z + 1, y, core, 0),
                (z - 1, y, core, 0),
                (z, 1 - y, core, 0),
                (z, y, 1 - core, 1),
            )
            for slot, (dz, dy, dcore, parity) in enumerate(targets):
                copy = pltpu.make_async_remote_copy(
                    src_ref=view,
                    dst_ref=view,
                    send_sem=send_sem.at[block, number, slot],
                    recv_sem=recv_sem.at[plane * 2 + row, number, parity],
                    device_id=((dz * 2 + dy) * 2 + dcore, x),
                    device_id_type=pl.DeviceIdType.MESH,
                )
                if slot < 3:
                    pl.when(ways[slot])(lambda copy=copy: act(copy))
                else:
                    act(copy)

    def arrive(block, parity):
        plane, row = chip_at(block)
        for number, (s, span, order) in enumerate(pieces):
            view = landing.at[first_sample(block, parity) + s, :, span]
            pltpu.make_async_remote_copy(
                src_ref=view,
                dst_ref=view,
                send_sem=send_sem.at[block, number, 3],
                recv_sem=recv_sem.at[plane * 2 + row, number, parity],
                device_id=((z * 2 + y) * 2 + 1 - core, x),
                device_id_type=pl.DeviceIdType.MESH,
            ).wait_recv()

    stream = Stream(kernel_ref, slots, kernel_sem, sample_at)
    stream.copy(0).start()
    own = pltpu.make_async_copy(
        value_ref, landing.at[pl.ds(first_sample(0, 0), samples)], own_sem
    )
    own.start()
    greet(place, ("z", "y"))
    own.wait()
    sends(0, lambda copy: copy.start())

    @pl.loop(0, count)
    def _(turn):
        block = turn // (2 * samples)
        step = lax.rem(turn, 2 * samples)

        @pl.when((step == 0) & (block > 0))
        def _():
            arrive(block, 0)
            sends(block, lambda copy: copy.start())

        @pl.when(step == samples)
        def _():
            arrive(block, 1)

        slot = stream.take(turn, count)
        work(turn, sample_at(turn), slot, sample_at)

    @pl.loop(0, blocks)
    def _(block):
        sends(block, lambda copy: copy.wait_send())


def consume_scratch(samples, rows, lanes, kernel):
    dma = pltpu.SemaphoreType.DMA
    pieces = 2 * samples
    return [
        pltpu.VMEM((16 * samples, rows, lanes), jnp.bfloat16),
        pltpu.VMEM((2,) + kernel.shape[1:], jnp.bfloat16),
        dma((2,)),
        dma((2 * PLANES, pieces, 4)),
        dma((2 * PLANES, pieces, 2)),
        dma,
    ]


def whole_specs(count):
    return [pl.BlockSpec(memory_space=pltpu.VMEM)] * count


HBM = pl.BlockSpec(memory_space=pl.ANY)


def gather_back(cotan, place, kernel, pixels, width, call_id):
    samples, rows, lanes = cotan.shape
    total = kernel.shape[0]

    def body(
        cotan_ref,
        kernel_ref,
        place_ref,
        out_ref,
        all_ref,
        landing,
        slots,
        s0,
        s1,
        s2,
        s3,
        wide_ref,
        all_sem,
    ):
        def work(turn, sample, slot, sample_at):
            out_ref[sample] = fold_back(
                landing[sample], place_ref, slots.at[pl.ds(slot, 1)], wide_ref, pixels, width
            )

        consume_body(
            lanes * 3 // 4,
            samples,
            cotan_ref,
            landing,
            kernel_ref,
            slots,
            (s0, s1, s2, s3),
            work,
        )
        keep = pltpu.make_async_copy(landing, all_ref, all_sem)
        keep.start()
        keep.wait()

    return pl.pallas_call(
        body,
        in_specs=[HBM, HBM] + whole_specs(1),
        out_specs=whole_specs(1) + [HBM],
        out_shape=[
            jax.ShapeDtypeStruct((total, pixels, width), jnp.bfloat16),
            jax.ShapeDtypeStruct((total, rows, lanes), jnp.bfloat16),
        ],
        scratch_shapes=consume_scratch(samples, rows, lanes, kernel)
        + [pltpu.VMEM((PAD_ROWS, 3 * width), jnp.float32), pltpu.SemaphoreType.DMA],
        compiler_params=pltpu.CompilerParams(
            collective_id=call_id, has_side_effects=True, vmem_limit_bytes=40 * 2**20
        ),
        name="gather_back",
    )(cotan, kernel, place)


def gather_second(slabs, tans, place, kernel, cotan, sides, squares, call_id):
    samples, rows, lanes = cotan.shape
    total, pixels, width = slabs.shape

    def body(
        cotan_ref,
        kernel_ref,
        sides_ref,
        slab_ref,
        tan_ref,
        place_ref,
        squares_ref,
        grad_ref,
        back_ref,
        scale_ref,
        landing,
        slots,
        s0,
        s1,
        s2,
        s3,
        side_slots,
        side_sem,
        grad_slots,
        grad_sem,
        spot_ref,
        wide_ref,
    ):
        spot_ref[...] = jnp.zeros_like(spot_ref)

        def leave(slot, sample):
            return pltpu.make_async_copy(
                grad_slots.at[slot], grad_ref.at[sample], grad_sem.at[slot]
            )

        def work(turn, sample, slot, sample_at):
            sides = Stream(sides_ref, side_slots, side_sem, sample_at)
            pl.when(turn == 0)(lambda: sides.copy(0).start())
            sides.take(turn, total)

            @pl.when(turn >= 2)
            def _():
                leave(slot, sample).wait()

            one = pl.ds(sample, 1)
            second_step(
                slab_ref.at[one],
                tan_ref.at[one],
                place_ref,
                slots.at[pl.ds(slot, 1)],
                landing.at[one],
                side_slots.at[pl.ds(slot, 1)],
                squares_ref.at[one],
                grad_slots.at[pl.ds(slot, 1)],
                back_ref.at[one],
                scale_ref.at[one],
                spot_ref,
                wide_ref,
            )
            leave(slot, sample).start()

        consume_body(
            lanes * 3 // 4,
            samples,
            cotan_ref,
            landing,
            kernel_ref,
            slots,
            (s0, s1, s2, s3),
            work,
        )
        for slot in range(2):
            leave(slot, 0).wait()

    return pl.pallas_call(
        body,
        in_specs=[HBM, HBM, HBM] + whole_specs(4),
        out_specs=[HBM] + whole_specs(2),
        out_shape=[
            jax.ShapeDtypeStruct(kernel.shape, jnp.bfloat16),
            jax.ShapeDtypeStruct((total, pixels, width), jnp.bfloat16),
            jax.ShapeDtypeStruct(squares.shape, jnp.float32),
        ],
        scratch_shapes=consume_scratch(samples, rows, lanes, kernel)
        + [
            pltpu.VMEM((2,) + sides.shape[1:], jnp.bfloat16),
            pltpu.SemaphoreType.DMA((2,)),
            pltpu.VMEM((2,) + kernel.shape[1:], jnp.bfloat16),
            pltpu.SemaphoreType.DMA((2,)),
            pltpu.VMEM((3 * pixels, 3 * width), jnp.bfloat16),
            pltpu.VMEM((PAD_ROWS, 3 * width), jnp.float32),
        ],
        compiler_params=pltpu.CompilerParams(
            collective_id=call_id, has_side_effects=True, vmem_limit_bytes=48 * 2**20
        ),
        name="gather_second",
    )(cotan, kernel, sides, slabs, tans, place, squares)


def add_rows(total, part):
    shape = total.shape[:-2]
    for number in range(int(np.prod(shape))):
        spot = tuple(int(place) for place in np.unravel_index(number, shape))
        total[spot] = (total[spot].astype(jnp.float32) + part[spot].astype(jnp.float32)).astype(
            jnp.bfloat16
        )


def sum_body(
    cut,
    extra,
    kernel_ref,
    slab_ref,
    place_ref,
    sums_ref,
    out_ref,
    slots,
    kernel_sem,
    spot_ref,
    acc,
    core_out,
    core_in,
    y_in,
    y_last,
    z_first,
    z_second,
    x_in,
    core_send,
    core_recv,
    y_send,
    y_recv,
    z_send,
    z_recv,
    x_send,
    x_recv,
):
    place = Place()
    z, y, x = place.z, place.y, place.x
    spot_ref[...] = jnp.zeros_like(spot_ref)
    wide, narrow = slice(0, cut), slice(cut, acc.shape[-1])
    finish = []

    def spot(z, y, core, x):
        return (z * 2 + y) * 2 + core, x

    def remote(source, target, send, recv, device):
        return pltpu.make_async_remote_copy(
            src_ref=source,
            dst_ref=target,
            send_sem=send,
            recv_sem=recv,
            device_id=spot(*device),
            device_id_type=pl.DeviceIdType.MESH,
        )

    other_core = (z, y, 1 - place.core, x)
    other_y = (z, 1 - y, place.core, x)
    other_x = (z, y, place.core, 1 - x)

    def chunk_at(chunk):
        turn = lax.rem(chunk, PLANES)
        dest = jnp.where(turn == 0, 3, jnp.where(turn == 1, 0, 4 - turn))
        return dest, jnp.where(chunk < PLANES, 1 - y, y)

    def sample_at(turn):
        dest, side = chunk_at(turn // 4)
        step = lax.rem(turn, 4)
        owner = jnp.where(step < 2, 1 - place.core, place.core)
        return ((dest * 2 + side) * 2 + owner) * 2 + lax.rem(step, 2)

    stream = Stream(kernel_ref, slots, kernel_sem, sample_at)
    stream.copy(0).start()
    greet(place, ("z", "y", "x"))

    def core_copy(chunk):
        dest, side = chunk_at(chunk)
        return remote(
            core_out.at[dest, side],
            core_in.at[dest, side],
            core_send.at[chunk],
            core_recv.at[chunk],
            other_core,
        )

    def y_copy(dest):
        return remote(
            acc.at[dest, 1 - y, :, :, wide], y_in.at[dest], y_send.at[dest], y_recv.at[dest], other_y
        )

    @pl.loop(0, 16 * 2)
    def _(turn):
        chunk, step = turn // 4, lax.rem(turn, 4)
        dest, side = chunk_at(chunk)
        sample = sample_at(turn)
        slot = stream.take(turn, 16 * 2)

        def convolve(target):
            conv_step(
                extra,
                sample,
                slab_ref.at[pl.ds(sample, 1)],
                place_ref,
                slots.at[pl.ds(slot, 1)],
                sums_ref,
                target.at[dest, side, pl.ds(lax.rem(step, 2), 1)],
                spot_ref,
            )

        pl.when(step < 2)(lambda: convolve(core_out))
        pl.when(step >= 2)(lambda: convolve(acc))
        pl.when(step == 1)(lambda: core_copy(chunk).start())

        @pl.when(step == 3)
        def _():
            core_copy(chunk).wait_recv()
            add_rows(acc.at[dest, side], core_in.at[dest, side])
            pl.when(chunk < PLANES)(lambda: y_copy(dest).start())

    y_copies = [y_copy(dest) for dest in (3, 0, 2, 1)]

    def along_z(slot, view, landing, dest):
        for way in (0, 1):
            near = dest > z if way == 0 else dest < z
            has_before = z > 0 if way == 0 else z < PLANES - 1
            copy = remote(
                view,
                landing.at[way, dest],
                z_send.at[slot, way, dest],
                z_recv.at[slot, way, dest],
                (z + (1 if way == 0 else -1), y, place.core, x),
            )

            @pl.when(near & has_before)
            def _():
                copy.wait_recv()
                add_rows(view, landing.at[way, dest])

            pl.when(near)(copy.start)
            finish.append((near, copy))

    def end_z(slot, view, landing):
        for way in (0, 1):
            copy = remote(
                view,
                landing.at[way, z],
                z_send.at[slot, way, z],
                z_recv.at[slot, way, z],
                other_core,
            )

            @pl.when(z > 0 if way == 0 else z < PLANES - 1)
            def _():
                copy.wait_recv()
                add_rows(view, landing.at[way, z])

    for number, dest in enumerate((3, 0, 2, 1)):
        along_z(1, acc.at[dest, :, :, :, narrow], z_second, dest)
        y_copies[number].wait_recv()
        finish.append(y_copies[number])
        view = acc.at[dest, y, :, :, wide]
        add_rows(view, y_in.at[dest])
        along_z(0, view, z_first, dest)
    end_z(1, acc.at[z, :, :, :, narrow], z_second)
    last = remote(
        acc.at[z, 1 - y, :, :, narrow], y_last, y_send.at[PLANES], y_recv.at[PLANES], other_y
    )
    last.start()
    finish.append(last)
    end_z(0, acc.at[z, y, :, :, wide], z_first)
    last.wait_recv()
    add_rows(acc.at[z, y, :, :, narrow], y_last)
    swap = remote(acc.at[z, y, 1 - x], x_in, x_send, x_recv, other_x)
    swap.start()
    lanes = acc.shape[-1]
    out_ref[:, lanes_at(x, lanes)] = acc[z, y, x]
    swap.wait_recv()
    out_ref[:, lanes_at(1 - x, lanes)] = x_in[...]
    finish.append(swap)
    for item in finish:
        if isinstance(item, tuple):
            pl.when(item[0])(item[1].wait_send)
        else:
            item.wait_send()

    @pl.loop(0, 2 * PLANES)
    def _(chunk):
        core_copy(chunk).wait_send()


def conv_sum(slabs, place, kernel, sums, extra, call_id):
    _, pixels, width = slabs.shape
    rows, lanes = PIXELS + (CHUNK if extra else 0), kernel.shape[2]
    cut = lanes * 3 // 4
    bf16, dma = jnp.bfloat16, pltpu.SemaphoreType.DMA
    return pl.pallas_call(
        lambda *refs: sum_body(cut, extra, *refs),
        in_specs=[HBM] + whole_specs(3),
        out_specs=pl.BlockSpec(memory_space=pltpu.VMEM),
        out_shape=jax.ShapeDtypeStruct((rows, 2 * lanes), bf16),
        scratch_shapes=[
            pltpu.VMEM((2,) + kernel.shape[1:], bf16),
            dma((2,)),
            pltpu.VMEM((3 * pixels, 3 * width), bf16),
            pltpu.VMEM((PLANES, 2, 2, rows, lanes), bf16),
            pltpu.VMEM((PLANES, 2, 2, rows, lanes), bf16),
            pltpu.VMEM((PLANES, 2, 2, rows, lanes), bf16),
            pltpu.VMEM((PLANES, 2, rows, cut), bf16),
            pltpu.VMEM((2, rows, lanes - cut), bf16),
            pltpu.VMEM((2, PLANES, 2, rows, cut), bf16),
            pltpu.VMEM((2, PLANES, 2, 2, rows, lanes - cut), bf16),
            pltpu.VMEM((rows, lanes), bf16),
            dma((8,)),
            dma((8,)),
            dma((PLANES + 1,)),
            dma((PLANES + 1,)),
            dma((2, 2, PLANES)),
            dma((2, 2, PLANES)),
            dma,
            dma,
        ],
        compiler_params=pltpu.CompilerParams(
            collective_id=call_id, has_side_effects=True, vmem_limit_bytes=48 * 2**20
        ),
        name="conv_sum",
    )(kernel, slabs, place, sums)


def sum_weights_body(parts, count, refs):
    inputs, outputs, rest = refs[:count], refs[count : 2 * count], refs[2 * count :]
    acc, core_in, one_in, two_in, z_in = (rest[k * count : (k + 1) * count] for k in range(5))
    (
        load_sem,
        core_send,
        core_recv,
        one_send,
        one_recv,
        two_send,
        two_recv,
        z_send,
        z_recv,
    ) = rest[5 * count :]
    place = Place()
    greet(place, ("z", "y", "x"))
    z, y, x = place.z, place.y, place.x
    order = (3, 0, 2, 1)
    finish = []

    def remote(source, target, send, recv, device):
        dz, dy, core, dx = device
        return pltpu.make_async_remote_copy(
            src_ref=source,
            dst_ref=target,
            send_sem=send,
            recv_sem=recv,
            device_id=((dz * 2 + dy) * 2 + core, dx),
            device_id_type=pl.DeviceIdType.MESH,
        )

    other_core = (z, y, 1 - place.core, x)
    other_y = (z, 1 - y, place.core, x)
    other_x = (z, y, place.core, 1 - x)
    sides = (1 - y, y)

    first = {}
    for dest in order:
        for w in range(count):
            rows = acc[w].shape[2]
            for turn, side in enumerate(sides):
                at = ((dest * 2 + side) * 2 + (1 - place.core)) * rows
                mine = ((dest * 2 + side) * 2 + place.core) * rows
                sent = remote(
                    inputs[w].at[pl.ds(pl.multiple_of(at, rows), rows)],
                    core_in[w].at[dest, side],
                    core_send.at[w, dest, turn],
                    core_recv.at[w, dest, turn],
                    other_core,
                )
                sent.start()
                load = pltpu.make_async_copy(
                    inputs[w].at[pl.ds(pl.multiple_of(mine, rows), rows)],
                    acc[w].at[dest, side],
                    load_sem.at[w, dest, turn],
                )
                load.start()
                first[w, dest, turn] = (sent, load)

    def half(w, index):
        lanes = acc[w].shape[-1] // 2
        return lanes_at(index, lanes)

    ones, twos = {}, {}

    def stage_one(dest):
        for w in range(count):
            for turn, side in enumerate(sides):
                sent, load = first[w, dest, turn]
                load.wait()
                sent.wait_recv()
                finish.append((None, sent))
                add_rows(acc[w].at[dest, side], core_in[w].at[dest, side])
                if parts[w] == "xy":
                    copy = remote(
                        acc[w].at[dest, side, :, half(w, 1 - x)],
                        one_in[w].at[dest, side],
                        one_send.at[w, dest, turn],
                        one_recv.at[w, dest, turn],
                        other_x,
                    )
                elif turn == 0:
                    copy = remote(
                        acc[w].at[dest, side],
                        one_in[w].at[dest],
                        one_send.at[w, dest, turn],
                        one_recv.at[w, dest, turn],
                        other_y,
                    )
                else:
                    continue
                copy.start()
                ones[w, dest, turn] = copy

    def stage_two(dest):
        for w in range(count):
            if parts[w] == "xy":
                for turn, side in enumerate(sides):
                    copy = ones[w, dest, turn]
                    copy.wait_recv()
                    finish.append((None, copy))
                    view = acc[w].at[dest, side, :, half(w, x)]
                    add_rows(view, one_in[w].at[dest, side])
                    if turn == 0:
                        twos[w, dest] = remote(
                            view,
                            two_in[w].at[dest],
                            two_send.at[w, dest],
                            two_recv.at[w, dest],
                            other_y,
                        )
                        twos[w, dest].start()
            else:
                copy = ones[w, dest, 0]
                copy.wait_recv()
                finish.append((None, copy))
                add_rows(acc[w].at[dest, y], one_in[w].at[dest])
                twos[w, dest] = remote(
                    acc[w].at[dest, y, :, half(w, 1 - x)],
                    two_in[w].at[dest],
                    two_send.at[w, dest],
                    two_recv.at[w, dest],
                    other_x,
                )
                twos[w, dest].start()

    def z_copy(w, dest, way):
        return remote(
            acc[w].at[dest, y, :, half(w, x)],
            z_in[w].at[way, dest],
            z_send.at[w, way, dest],
            z_recv.at[w, way, dest],
            (z + (1 if way == 0 else -1), y, place.core, x),
        )

    def stage_z(dest):
        for w in range(count):
            copy = twos[w, dest]
            copy.wait_recv()
            finish.append((None, copy))
            view = acc[w].at[dest, y, :, half(w, x)]
            add_rows(view, two_in[w].at[dest])
            for way in (0, 1):
                near = dest > z if way == 0 else dest < z
                has_before = z > 0 if way == 0 else z < PLANES - 1
                copy = z_copy(w, dest, way)

                @pl.when(near & has_before)
                def _():
                    copy.wait_recv()
                    add_rows(view, z_in[w].at[way, dest])

                pl.when(near)(copy.start)
                finish.append((near, copy))

    for turn in range(PLANES + 2):
        if turn < PLANES:
            stage_one(order[turn])
        if 0 <= turn - 1 < PLANES:
            stage_two(order[turn - 1])
        if turn >= 2:
            stage_z(order[turn - 2])
    for w in range(count):
        view = acc[w].at[z, y, :, half(w, x)]
        for way in (0, 1):

            @pl.when(z > 0 if way == 0 else z < PLANES - 1)
            def _():
                remote(
                    view,
                    z_in[w].at[way, z],
                    z_send.at[w, way, z],
                    z_recv.at[w, way, z],
                    other_core,
                ).wait_recv()
                add_rows(view, z_in[w].at[way, z])

        outputs[w][...] = acc[w][z, y, :, half(w, x)].astype(jnp.float32)
    for condition, copy in finish:
        if condition is None:
            copy.wait_send()
        else:
            pl.when(condition)(copy.wait_send)


def sum_weights(grads, parts, call_id):
    count = len(grads)
    bf16, dma = jnp.bfloat16, pltpu.SemaphoreType.DMA
    blocks = [(grad.shape[0] // 16, grad.shape[1]) for grad in grads]
    ones = [
        (PLANES, 2, rows, lanes // 2) if part == "xy" else (PLANES, rows, lanes)
        for (rows, lanes), part in zip(blocks, parts)
    ]
    return pl.pallas_call(
        lambda *refs: sum_weights_body(parts, count, refs),
        in_specs=[pl.BlockSpec(memory_space=pl.ANY)] * count,
        out_specs=[pl.BlockSpec(memory_space=pltpu.VMEM)] * count,
        out_shape=[
            jax.ShapeDtypeStruct((rows, lanes // 2), jnp.float32) for rows, lanes in blocks
        ],
        scratch_shapes=[pltpu.VMEM((PLANES, 2, rows, lanes), bf16) for rows, lanes in blocks]
        + [pltpu.VMEM((PLANES, 2, rows, lanes), bf16) for rows, lanes in blocks]
        + [pltpu.VMEM(shape, bf16) for shape in ones]
        + [pltpu.VMEM((PLANES, rows, lanes // 2), bf16) for rows, lanes in blocks]
        + [pltpu.VMEM((2, PLANES, rows, lanes // 2), bf16) for rows, lanes in blocks]
        + [dma((count, PLANES, 2))] * 5
        + [dma((count, PLANES))] * 2
        + [dma((count, 2, PLANES))] * 2,
        compiler_params=pltpu.CompilerParams(
            collective_id=call_id, has_side_effects=True, vmem_limit_bytes=60 * 2**20
        ),
        name="sum_weights",
    )(*grads)


def sample_parallel(
    layer_input,
    labels,
    text_ids,
    noise_seeds,
    penalty_mask,
    class_table,
    token_table,
    sel_weight,
    mod_weight,
    rgb_mod,
    rgb_weight,
    conv_bias,
    noise_strength,
    kernel_bank,
    qk_weight,
    value_weight,
    attn_out,
    cross_query,
    cross_key,
    cross_value,
    cross_out,
    mlp_in,
    mlp_out,
    cot_feat,
    cot_rgb,
    penalty_dir,
):
    mp = lax.axis_index("mp")
    dp = lax.axis_index("dp")
    half_px = layer_input.shape[1]
    slab = kernel_bank.shape[2]
    width_out = kernel_bank.shape[3]
    float32, bfloat16 = jnp.float32, jnp.bfloat16

    input_whole = lax.all_gather(layer_input, "mp", axis=2, tiled=True)
    raw_slabs = to_slabs(input_whole)
    numbers = jnp.concatenate([jnp.pad(labels, (0, 126)), text_ids.reshape(-1)]).reshape(2, 128)
    gathered = gather_weights(
        [
            mlp_in,
            mlp_out.T,
            qk_weight,
            value_weight,
            attn_out.T,
            cross_query,
            cross_out.T,
            cross_key,
            cross_value,
        ],
        jnp.pad(numbers, ((0, 6), (0, 0))),
        1,
    )
    mlp_whole, mout_whole, qk_whole, value_whole, attn_whole, query_whole, cout_whole = gathered[:7]
    key_whole, cval_whole, numbers_all = gathered[7:]
    weights = (
        qk_whole,
        value_whole,
        attn_whole,
        query_whole,
        key_whole,
        cval_whole,
        cout_whole,
        mlp_whole,
        mout_whole,
    )

    numbers_all = numbers_all.reshape(16, 2, 8, 128)[:, 0]
    labels_all = numbers_all[:, 0, :2].reshape(-1)
    ids_all = numbers_all[:, 1].reshape(-1)
    sample_count = labels_all.shape[0]
    classes = jnp.arange(class_table.shape[0], dtype=jnp.int32)
    onehot_class = (labels_all[:, None] == classes[None, :]).astype(bfloat16)
    latent = dot_wide(onehot_class, class_table, 1, 0)
    select_all, select_pull = jax.vjp(last_softmax, dot_wide(latent, sel_weight, 1, 0))
    scales_all = 1.0 + dot_wide(latent, mod_weight, 1, 0)
    rgb_scales_all = 1.0 + dot_wide(latent, rgb_mod, 1, 0)
    me = 2 * dp + mp
    scales = pick(scales_all, me)
    rgb_scales = pick(rgb_scales_all, me)
    scales_slab = lax.dynamic_slice_in_dim(scales_all, dp * slab, slab, 1)
    words = jnp.arange(token_table.shape[0], dtype=jnp.int32)
    text_own = pick(text_ids, mp)
    text_rows = dot_wide((text_own[:, None] == words[None, :]).astype(bfloat16), token_table, 1, 0)
    noise = noise_field(pick(noise_seeds, mp)[None], SIDE * SIDE)[0]
    small = (
        conv_bias.astype(float32),
        noise_strength.astype(float32),
        rgb_scales,
        rgb_weight.astype(float32),
    )

    bank_rows = kernel_bank.reshape(kernel_bank.shape[0], 9 * slab, width_out)
    mix = mix_matrix(select_all)
    scales_two = jnp.broadcast_to(
        (scales_slab * scales_slab)[:, :, None], (sample_count, slab, 128)
    )
    kernel, sums_part = mix_kernels(mix, bank_rows, scales_two)
    place = placing(SIDE // 2)

    input_own = pick(input_whole, mp).astype(float32)
    slabs_x = (raw_slabs.astype(float32) * scales_slab[:, None, :]).astype(bfloat16)
    summed = conv_sum(slabs_x, place, kernel, sums_part, True, 4).astype(float32)
    conv_out, sums = summed[:PIXELS], summed[PIXELS]

    (hidden_four, picture), pull = jax.vjp(
        lambda value: layer_forward(value, sums, text_rows, small, weights, noise), conv_out
    )

    dir_own = pick(penalty_dir, mp).astype(float32)
    grad_conv = pull((jnp.zeros_like(hidden_four), dir_own))[0]
    back_slabs, sides_all = gather_back(
        both_half(grad_conv.astype(bfloat16), mp), place, kernel, half_px, slab, 2
    )
    grad_moduled = from_slabs(back_slabs, mp).astype(bfloat16).astype(float32)
    mask_own = pick(penalty_mask, mp).astype(float32)
    tangent = penalty_weight * mask_own * grad_moduled * scales

    tan_moduled = (tangent * scales).astype(bfloat16)
    tan_other = swap_mp(tan_moduled)
    tan_pair = jnp.stack(
        [jnp.where(mp == 0, tan_moduled, tan_other), jnp.where(mp == 0, tan_other, tan_moduled)]
    )
    slabs_t = to_slabs(tan_pair)
    conv_tan = conv_sum(slabs_t, place, kernel, sums_part, False, 5).astype(float32)

    (ignored_out, ignored_pic, ignored_tan), pull_joint = jax.vjp(
        lambda *given: layer_joint(*given, noise),
        conv_out,
        conv_tan,
        sums,
        text_rows,
        small,
        weights,
    )
    cot_own = own_whole(cot_feat, mp).astype(float32)
    grad_main, _, grad_sums, grad_text, grad_small, grad_weights = pull_joint(
        (cot_own, pick(cot_rgb, mp).astype(float32), dir_own)
    )

    orders = ("xy", "yx", "xy", "yx", "xy", "yx", "yx", "xy", "xy")
    d_qk, d_value, d_attn, d_query, d_key, d_cval, d_cout, d_mlp, d_mout = grad_weights
    mlp_grad, mout_grad, qk_grad, value_grad, attn_grad, query_grad, cout_grad, key_grad, cval_grad = (
        sum_weights(
            [d_mlp, d_mout, d_qk, d_value, d_attn, d_query, d_cout, d_key, d_cval], orders, 6
        )
    )
    big_sums = (
        qk_grad,
        value_grad,
        attn_grad.T,
        query_grad,
        key_grad,
        cval_grad,
        cout_grad.T,
        mlp_grad,
        mout_grad.T,
    )

    lines = jnp.broadcast_to(grad_sums[None], (CHUNK,) + grad_sums.shape)
    wide = jnp.concatenate([grad_main.astype(bfloat16), lines.astype(bfloat16)], axis=0)
    grad_kernel, back_slabs, scale_sums = gather_second(
        slabs_x, slabs_t, place, kernel, both_half(wide, mp), sides_all, scales_two, 3
    )
    grad_scales_slab = 2.0 * scales_slab * scale_sums[:, :, 0]
    bank_grad, select_products = unmix_kernels(mix, bank_rows, grad_kernel)
    bank_grad = bank_grad.reshape(kernel_bank.shape)
    grad_select = jnp.einsum(
        "brkr->bk", select_products.reshape(sample_count, CHUNK, -1, CHUNK)
    )
    back_main = from_slabs(back_slabs, mp).astype(bfloat16).astype(float32)
    input_grad = back_main * scales
    grad_scales = jnp.sum(back_main * input_own + grad_moduled * tangent, axis=0)

    grad_bias, grad_strength, grad_rgb_scales, grad_rgb_weight = grad_small
    row = jnp.concatenate(
        [
            grad_scales,
            grad_rgb_scales,
            grad_rgb_weight.reshape(-1),
            grad_bias,
            grad_strength,
            grad_scales_slab.reshape(-1),
            grad_select.reshape(-1),
        ]
    ).reshape(-1, 128)
    rows_all = lax.all_gather(row, ("dp", "mp"), axis=0, tiled=False).reshape(sample_count, -1)
    channels = scales.shape[0]
    scale_terms = rows_all[:, :channels]
    rgb_terms = rows_all[:, channels : 2 * channels]
    sums_all = jnp.sum(rows_all[:, 2 * channels : 7 * channels], axis=0)
    slab_terms = rows_all[:, 7 * channels : 7 * channels + sample_count * slab]
    slab_terms = slab_terms.reshape(-1, 2, sample_count, slab).sum(axis=1)
    scale_terms = scale_terms + slab_terms.transpose(1, 0, 2).reshape(sample_count, channels)
    select_terms = jnp.sum(rows_all[:, 7 * channels + sample_count * slab :], axis=0)
    logit_terms = select_pull(select_terms.reshape(sample_count, -1))[0]
    latent_terms = (
        matmul_high(scale_terms, mod_weight.astype(float32).T)
        + matmul_high(rgb_terms, rgb_mod.astype(float32).T)
        + matmul_high(logit_terms, sel_weight.astype(float32).T)
    )
    class_grad = matmul_high(onehot_class.astype(float32).T, latent_terms)
    sel_grad = matmul_high(latent.T, logit_terms)
    mod_grad = matmul_high(latent.T, scale_terms)
    rgb_mod_grad = matmul_high(latent.T, rgb_terms)
    text_all = lax.all_gather(grad_text.astype(bfloat16), ("dp", "mp"), axis=0, tiled=True)
    token_grad = dot_wide((ids_all[:, None] == words[None, :]).astype(bfloat16), text_all, 0, 0)

    picture_other = swap_mp(picture)
    pictures = jnp.stack(
        [jnp.where(mp == 0, picture, picture_other), jnp.where(mp == 0, picture_other, picture)]
    )
    return (
        both_half(hidden_four, mp),
        pictures,
        both_half(input_grad, mp),
        class_grad,
        token_grad,
        sel_grad,
        mod_grad,
        rgb_mod_grad,
        sums_all[: 3 * channels].reshape(3, channels),
        sums_all[3 * channels : 4 * channels],
        sums_all[4 * channels :],
        bank_grad,
    ) + big_sums


def solution(mesh):
    in_specs = (
        P("dp", None, "mp"),
        P("dp"),
        P("dp", None),
        P("dp"),
        P("dp"),
        P(),
        P(),
        P(),
        P(),
        P(),
        P(),
        P(),
        P(),
        P(None, None, "dp", "mp"),
        P("dp", "mp"),
        P("dp", "mp"),
        P("mp", "dp"),
        P("dp", "mp"),
        P("dp", "mp"),
        P("dp", "mp"),
        P("mp", "dp"),
        P("dp", "mp"),
        P("mp", "dp"),
        P("dp", None, "mp"),
        P("dp", None, None),
        P("dp", None, None),
    )
    out_specs = (
        P("dp", None, "mp"),
        P("dp", None, None),
        P("dp", None, "mp"),
        P(),
        P(),
        P(),
        P(),
        P(),
        P(),
        P(),
        P(),
        P(None, None, "dp", "mp"),
        P("dp", "mp"),
        P("dp", "mp"),
        P("mp", "dp"),
        P("dp", "mp"),
        P("dp", "mp"),
        P("dp", "mp"),
        P("mp", "dp"),
        P("dp", "mp"),
        P("mp", "dp"),
    )
    return jax.shard_map(
        sample_parallel if fits_samples(mesh) else tensor_parallel,
        mesh=mesh, in_specs=in_specs, out_specs=out_specs, check_vma=False
    )
```

```python
import jax
import jax.numpy as jnp
import numpy as np
from jax import lax
from jax.experimental import pallas as pl
from jax.experimental.pallas import tpu as pltpu
from jax.sharding import PartitionSpec as P

HEAD = 64
SIDE = 16


penalty_weight = 1.0


def rounded(values):
    return lax.optimization_barrier(values.astype(jnp.bfloat16)).astype(jnp.float32)


def matmul_high(left, right):
    return jnp.matmul(left, right, precision=lax.Precision.HIGHEST)


def einsum_high(form, *operands):
    return jnp.einsum(form, *operands, precision=lax.Precision.HIGHEST)


def einsum_low(form, left, right):
    return jnp.einsum(
        form,
        left.astype(jnp.bfloat16),
        right.astype(jnp.bfloat16),
        preferred_element_type=jnp.float32,
    )


def noise_field(seed_ids, pixel_count):
    pixel_ids = jnp.arange(pixel_count, dtype=jnp.int32)
    mixed = seed_ids[:, None] * 1103515245 + pixel_ids[None, :] * 40503
    mixed = jnp.bitwise_xor(mixed, jnp.right_shift(mixed, 13)) * 1664525 + 1013904223
    levels = jnp.bitwise_and(jnp.right_shift(mixed, 8), 65535)
    return levels.astype(jnp.float32) / 65536.0 - 0.5


def patches_of(flat_rows, side_len):
    samples_here, pixels, width_here = flat_rows.shape
    half_side = side_len // 2
    picture = flat_rows.reshape(samples_here, half_side, half_side, width_here)
    picture = jnp.repeat(jnp.repeat(picture, 2, axis=1), 2, axis=2)
    padded = jnp.pad(picture, ((0, 0), (1, 1), (1, 1), (0, 0)))
    pieces = [
        padded[:, shift_row : shift_row + side_len, shift_col : shift_col + side_len, :]
        for shift_row in range(3)
        for shift_col in range(3)
    ]
    return jnp.concatenate(pieces, axis=-1).reshape(
        samples_here, side_len * side_len, 9 * width_here
    )


def rms_norm(values):
    return values * lax.rsqrt(jnp.mean(values * values, axis=-1, keepdims=True) + 1e-06)


def conv_part(gathered, kernel, scales, bias_local, strength_local, noise_map):
    samples_here = gathered.shape[0]
    width_out = kernel.shape[2]
    columns = patches_of(gathered, SIDE)
    conv_out = einsum_low("bpr,bro->bpo", columns, kernel)
    squares = jnp.sum((kernel * kernel).reshape(samples_here, 9, -1, width_out), axis=1)
    demodulate = lax.rsqrt(einsum_high("bi,bio->bo", scales * scales, squares) + 1e-08)
    before = conv_out * demodulate[:, None, :] + bias_local + noise_map[:, :, None] * strength_local
    return jax.nn.silu(before)


def self_attention(active, qk_w, value_w, out_w):
    normed = rounded(rms_norm(active))
    queries = rounded(matmul_high(normed, qk_w))
    values = rounded(matmul_high(normed, value_w))
    samples_here, pixels, width_here = queries.shape
    heads_here = width_here // HEAD
    q_heads = queries.reshape(samples_here, pixels, heads_here, HEAD)
    v_heads = values.reshape(samples_here, pixels, heads_here, HEAD)
    lengths = jnp.transpose(jnp.sum(q_heads * q_heads, axis=-1), (0, 2, 1))
    scores = (
        2.0 * einsum_low("bphd,bqhd->bhpq", q_heads, q_heads) - lengths[:, :, None, :]
    ) * HEAD ** (-0.5)
    soft_weights = rounded(jax.nn.softmax(scores, axis=-1))
    mixture = rounded(
        einsum_low("bhpq,bqhd->bphd", soft_weights, v_heads).reshape(
            samples_here, pixels, width_here
        )
    )
    return matmul_high(mixture, out_w)


def cross_attention(active, text_rows, query_w, key_w, value_w, out_w):
    normed = rounded(rms_norm(active))
    queries = rounded(matmul_high(normed, query_w))
    key_rows = rounded(matmul_high(text_rows, key_w))
    values = rounded(matmul_high(text_rows, value_w))
    samples_here, pixels, width_here = queries.shape
    tokens = key_rows.shape[1]
    heads_here = width_here // HEAD
    q_heads = queries.reshape(samples_here, pixels, heads_here, HEAD)
    k_heads = key_rows.reshape(samples_here, tokens, heads_here, HEAD)
    v_heads = values.reshape(samples_here, tokens, heads_here, HEAD)
    scores = einsum_low("bphd,bthd->bhpt", q_heads, k_heads) * HEAD ** (-0.5)
    soft_weights = rounded(jax.nn.softmax(scores, axis=-1))
    mixture = rounded(
        einsum_low("bhpt,bthd->bphd", soft_weights, v_heads).reshape(
            samples_here, pixels, width_here
        )
    )
    return matmul_high(mixture, out_w)


def feed_forward(active, weight_in, weight_out):
    normed = rounded(rms_norm(active))
    inner = rounded(jax.nn.gelu(matmul_high(normed, weight_in)))
    return matmul_high(inner, weight_out)


def tree_add(first, second):
    return jax.tree.map(jnp.add, first, second)


def tensor_parallel(
    layer_input,
    labels,
    text_ids,
    noise_seeds,
    penalty_mask,
    class_table,
    token_table,
    sel_weight,
    mod_weight,
    rgb_mod,
    rgb_weight,
    conv_bias,
    noise_strength,
    kernel_bank,
    qk_weight,
    value_weight,
    attn_out,
    cross_query,
    cross_key,
    cross_value,
    cross_out,
    mlp_in,
    mlp_out,
    cot_feat,
    cot_rgb,
    penalty_dir,
):
    width_local = layer_input.shape[2]
    offset = lax.axis_index("mp") * width_local
    small_params = tuple(
        (
            entry.astype(jnp.float32)
            for entry in (
                class_table,
                token_table,
                sel_weight,
                mod_weight,
                rgb_mod,
                rgb_weight,
                conv_bias,
                noise_strength,
            )
        )
    )

    def fetch_proj():
        fetched = (
            lax.all_gather(qk_weight, "dp", axis=0, tiled=True),
            lax.all_gather(value_weight, "dp", axis=0, tiled=True),
            lax.all_gather(attn_out, "dp", axis=1, tiled=True),
            lax.all_gather(cross_query, "dp", axis=0, tiled=True),
            lax.all_gather(cross_key, "dp", axis=0, tiled=True),
            lax.all_gather(cross_value, "dp", axis=0, tiled=True),
            lax.all_gather(cross_out, "dp", axis=1, tiled=True),
            lax.all_gather(mlp_in, "dp", axis=0, tiled=True),
            lax.all_gather(mlp_out, "dp", axis=1, tiled=True),
        )
        return tuple((entry.astype(jnp.float32) for entry in fetched))

    def style_part(param_set):
        table_class, table_word, select_w, modul_w, rgbmod_w, rgbout_w, bias_w, strength_w = (
            param_set
        )
        onehot_class = (
            labels[:, None] == jnp.arange(table_class.shape[0], dtype=jnp.int32)[None, :]
        ).astype(jnp.float32)
        latent = matmul_high(onehot_class, table_class)
        onehot_word = (
            text_ids[:, :, None] == jnp.arange(table_word.shape[0], dtype=jnp.int32)
        ).astype(jnp.float32)
        text_rows = matmul_high(onehot_word, table_word)
        select = jax.nn.softmax(matmul_high(latent, select_w), axis=-1)
        scales = 1.0 + matmul_high(latent, modul_w)
        rgb_scales = 1.0 + matmul_high(
            latent, lax.dynamic_slice_in_dim(rgbmod_w, offset, width_local, 1)
        )
        bias_local = lax.dynamic_slice_in_dim(bias_w, offset, width_local, 0)
        strength_local = lax.dynamic_slice_in_dim(strength_w, offset, width_local, 0)
        colour_local = lax.dynamic_slice_in_dim(rgbout_w, offset, width_local, 1)
        return (select, scales, rgb_scales, text_rows, bias_local, strength_local, colour_local)

    styles, style_pull = jax.vjp(style_part, small_params)
    noise_map = noise_field(noise_seeds, SIDE * SIDE)

    def owned_sets():
        proj_set = fetch_proj()
        conv_set = (lax.all_gather(kernel_bank, "dp", axis=2, tiled=True).astype(jnp.float32),)
        return ((), conv_set, proj_set[0:3], proj_set[3:7], proj_set[7:9], ())

    def seg_in(active, styles_in, own_set):
        return active * lax.dynamic_slice_in_dim(styles_in[1], offset, width_local, 1)[:, None, :]

    def seg_conv(active, styles_in, own_set):
        bank_full = own_set[0]
        kernel = rounded(matmul_high(styles_in[0], bank_full.reshape(bank_full.shape[0], -1)))
        kernel = kernel.reshape(active.shape[0], -1, bank_full.shape[3])
        return conv_part(active, kernel, styles_in[1], styles_in[4], styles_in[5], noise_map)

    def seg_self(active, styles_in, own_set):
        return self_attention(active, own_set[0], own_set[1], own_set[2])

    def seg_cross(active, styles_in, own_set):
        return cross_attention(active, styles_in[3], own_set[0], own_set[1], own_set[2], own_set[3])

    def seg_mlp(active, styles_in, own_set):
        return feed_forward(active, own_set[0], own_set[1])

    def seg_rgb(active, styles_in, own_set):
        return einsum_high("bpc,bc,kc->bkp", active, styles_in[2], styles_in[6])

    def spread(stacked):
        return lax.all_gather(stacked, "mp", axis=3, tiled=True)

    def collect(stacked):
        return lax.psum_scatter(
            stacked.astype(jnp.bfloat16), "mp", scatter_dimension=3, tiled=True
        ).astype(jnp.float32)

    def spread_one(values):
        return spread(values.astype(jnp.bfloat16)[None])[0].astype(jnp.float32)

    def collect_one(values):
        return collect(values[None])[0]

    own_first = owned_sets()
    input_full = layer_input.astype(jnp.float32)
    gathered_x = spread_one(seg_in(input_full, styles, own_first[0]))
    hidden_one = seg_conv(gathered_x, styles, own_first[1])
    gathered_one = spread_one(hidden_one)
    hidden_two = hidden_one + collect_one(seg_self(gathered_one, styles, own_first[2]))
    gathered_two = spread_one(hidden_two)
    hidden_three = hidden_two + collect_one(seg_cross(gathered_two, styles, own_first[3]))
    gathered_three = spread_one(hidden_three)
    hidden_four = hidden_three + collect_one(seg_mlp(gathered_three, styles, own_first[4]))
    picture = lax.psum(seg_rgb(hidden_four, styles, own_first[5]), "mp")
    own_second = owned_sets()

    def pull_act(segment, active, own_set, cotan):
        return jax.vjp(lambda inner_x: segment(inner_x, styles, own_set), active)[1](cotan)[0]

    grad_four = pull_act(seg_rgb, hidden_four, own_second[5], penalty_dir.astype(jnp.float32))
    back_three = pull_act(seg_mlp, gathered_three, own_second[4], spread_one(grad_four))
    grad_three = grad_four + rounded(collect_one(back_three))
    back_two = pull_act(seg_cross, gathered_two, own_second[3], spread_one(grad_three))
    grad_two = grad_three + rounded(collect_one(back_two))
    back_one = pull_act(seg_self, gathered_one, own_second[2], spread_one(grad_two))
    grad_one = grad_two + rounded(collect_one(back_one))
    grad_moduled = rounded(collect_one(pull_act(seg_conv, gathered_x, own_second[1], grad_one)))
    penalty_grad = pull_act(seg_in, input_full, own_second[0], grad_moduled)
    tangent = penalty_weight * penalty_mask.astype(jnp.float32)[:, None, None] * penalty_grad
    own_third = owned_sets()

    def push(segment, active, own_set, tangent_in):
        return jax.jvp(lambda inner_x: segment(inner_x, styles, own_set), (active,), (tangent_in,))[
            1
        ]

    tan_x = spread_one(push(seg_in, input_full, own_third[0], tangent))
    tan_one = push(seg_conv, gathered_x, own_third[1], tan_x)
    tan_g1 = spread_one(tan_one)
    tan_two = tan_one + collect_one(push(seg_self, gathered_one, own_third[2], tan_g1))
    tan_g2 = spread_one(tan_two)
    tan_three = tan_two + collect_one(push(seg_cross, gathered_two, own_third[3], tan_g2))
    tan_g3 = spread_one(tan_three)
    tan_four = tan_three + collect_one(push(seg_mlp, gathered_three, own_third[4], tan_g3))
    own_fourth = owned_sets()

    def pull_both(segment, active, tangent_in, own_set, cotan, cotan_tangent):

        def joint(inner_x, inner_tangent, styles_in, own_in):
            return jax.jvp(
                lambda value_x: segment(value_x, styles_in, own_in), (inner_x,), (inner_tangent,)
            )

        return jax.vjp(joint, active, tangent_in, styles, own_set)[1]((cotan, cotan_tangent))

    grad_act, grad_tan, style_acc, ignored = pull_both(
        seg_rgb,
        hidden_four,
        tan_four,
        own_fourth[5],
        cot_rgb.astype(jnp.float32),
        penalty_dir.astype(jnp.float32),
    )
    main_now = cot_feat.astype(jnp.float32) + grad_act
    side_now = grad_tan
    layer_grads = []
    for segment, active, tangent_in, own_set in (
        (seg_mlp, gathered_three, tan_g3, own_fourth[4]),
        (seg_cross, gathered_two, tan_g2, own_fourth[3]),
        (seg_self, gathered_one, tan_g1, own_fourth[2]),
    ):
        both_wide = spread(jnp.stack([main_now, side_now]).astype(jnp.bfloat16)).astype(jnp.float32)
        grad_act, grad_tan, grad_sty, grad_own = pull_both(
            segment, active, tangent_in, own_set, both_wide[0], both_wide[1]
        )
        style_acc = tree_add(style_acc, grad_sty)
        layer_grads.append(grad_own)
        both_sums = collect(jnp.stack([grad_act, grad_tan]))
        main_now = main_now + rounded(both_sums[0])
        side_now = side_now + rounded(both_sums[1])
    grad_act, grad_tan, grad_sty, grads_conv = pull_both(
        seg_conv, gathered_x, tan_x, own_fourth[1], main_now, side_now
    )
    style_acc = tree_add(style_acc, grad_sty)
    both_sums = collect(jnp.stack([grad_act, grad_tan]))
    grad_act, grad_tan, grad_sty, ignored = pull_both(
        seg_in, input_full, tangent, own_fourth[0], rounded(both_sums[0]), rounded(both_sums[1])
    )
    style_acc = tree_add(style_acc, grad_sty)
    proj_terms = layer_grads[2] + layer_grads[1] + layer_grads[0]
    big_terms = grads_conv + proj_terms
    big_sums = (
        lax.psum_scatter(
            big_terms[0].astype(jnp.bfloat16), "dp", scatter_dimension=2, tiled=True
        ).astype(jnp.float32),
        lax.psum_scatter(
            big_terms[1].astype(jnp.bfloat16), "dp", scatter_dimension=0, tiled=True
        ).astype(jnp.float32),
        lax.psum_scatter(
            big_terms[2].astype(jnp.bfloat16), "dp", scatter_dimension=0, tiled=True
        ).astype(jnp.float32),
        lax.psum_scatter(
            big_terms[3].astype(jnp.bfloat16), "dp", scatter_dimension=1, tiled=True
        ).astype(jnp.float32),
        lax.psum_scatter(
            big_terms[4].astype(jnp.bfloat16), "dp", scatter_dimension=0, tiled=True
        ).astype(jnp.float32),
        lax.psum_scatter(
            big_terms[5].astype(jnp.bfloat16), "dp", scatter_dimension=0, tiled=True
        ).astype(jnp.float32),
        lax.psum_scatter(
            big_terms[6].astype(jnp.bfloat16), "dp", scatter_dimension=0, tiled=True
        ).astype(jnp.float32),
        lax.psum_scatter(
            big_terms[7].astype(jnp.bfloat16), "dp", scatter_dimension=1, tiled=True
        ).astype(jnp.float32),
        lax.psum_scatter(
            big_terms[8].astype(jnp.bfloat16), "dp", scatter_dimension=0, tiled=True
        ).astype(jnp.float32),
        lax.psum_scatter(
            big_terms[9].astype(jnp.bfloat16), "dp", scatter_dimension=1, tiled=True
        ).astype(jnp.float32),
    )
    small_terms = style_pull(style_acc)[0]
    small_sums = lax.psum(
        (
            small_terms[0],
            small_terms[1],
            small_terms[2],
            small_terms[3],
            small_terms[4],
            small_terms[5],
            small_terms[6],
            small_terms[7],
        ),
        ("dp", "mp"),
    )
    return (hidden_four, picture, grad_act) + tuple(small_sums) + tuple(big_sums)


def fits_samples(mesh):
    return mesh.shape["dp"] == 16 and mesh.shape["mp"] == 2


def dot_wide(left, right, left_dim, right_dim):
    return lax.dot_general(
        left.astype(jnp.bfloat16),
        right.astype(jnp.bfloat16),
        (((left_dim,), (right_dim,)), ((), ())),
        preferred_element_type=jnp.float32,
    )


def make_products(flip):
    depth = 1 if flip else 0

    def weight_grad(rows, cotan):
        if flip:
            return dot_wide(cotan, rows, 0, 0).astype(jnp.bfloat16)
        return dot_wide(rows, cotan, 0, 0).astype(jnp.bfloat16)

    @jax.custom_vjp
    def single(rows, weight):
        return dot_wide(rows, weight, 1, depth)

    def single_fwd(rows, weight):
        return single(rows, weight), (rows, weight)

    def single_bwd(kept, cotan):
        rows, weight = kept
        return dot_wide(cotan, weight, 1, 1 - depth), weight_grad(rows, cotan)

    single.defvjp(single_fwd, single_bwd)

    @jax.custom_vjp
    def pair(rows, tangents, weight):
        return dot_wide(rows, weight, 1, depth), dot_wide(tangents, weight, 1, depth)

    def pair_fwd(rows, tangents, weight):
        return pair(rows, tangents, weight), (rows, tangents, weight)

    def pair_bwd(kept, cotans):
        rows, tangents, weight = kept
        count = rows.shape[0]
        both = jnp.concatenate([entry.astype(jnp.bfloat16) for entry in cotans], axis=0)
        inputs = jnp.concatenate(
            [rows.astype(jnp.bfloat16), tangents.astype(jnp.bfloat16)], axis=0
        )
        back = dot_wide(both, weight, 1, 1 - depth)
        return back[:count], back[count:], weight_grad(inputs, both)

    pair.defvjp(pair_fwd, pair_bwd)
    return single, pair


product, product_pair = make_products(False)
product_flip, product_flip_pair = make_products(True)


def with_tangent(fun, value, tangent):
    return jax.jvp(fun, (value,), (tangent,))


def last_softmax(scores):
    return jax.nn.softmax(scores, axis=-1)


def post_conv(conv_out, sums, bias, strength, noise):
    demodulate = lax.rsqrt(sums + 1e-08)
    return jax.nn.silu(conv_out * demodulate[None] + bias[None] + noise[:, None] * strength[None])


def picture_of(hidden, rgb_scales, rgb_weight):
    return einsum_high("pc,kc->kp", hidden, rgb_scales[None] * rgb_weight)


CHUNK = 16
PAD_ROWS = (SIDE + 2) * SIDE
PIXELS = SIDE * SIDE


def placing(half_side):
    side = 2 * half_side
    table = np.zeros((side + 2, side, 3, half_side * half_side), np.float32)
    for row in range(1, side + 1):
        for col in range(side):
            for shift in range(3):
                at = col + shift - 1
                if 0 <= at < side:
                    table[row, col, shift, (row - 1) // 2 * half_side + at // 2] = 1.0
    return jnp.asarray(table.reshape((side + 2) * side, -1), jnp.bfloat16)


def dot_f32(left, right, left_dim, right_dim):
    return lax.dot_general(
        left, right, (((left_dim,), (right_dim,)), ((), ())), preferred_element_type=jnp.float32
    )


def mix_matrix(select):
    high = select.astype(jnp.bfloat16)
    low = (select - high.astype(jnp.float32)).astype(jnp.bfloat16)
    eye = jnp.eye(CHUNK, dtype=jnp.bfloat16)
    parts = jnp.stack([high, low], axis=1)
    wide = parts[:, None, :, :, None] * eye[None, :, None, None, :]
    return wide.reshape(select.shape[0] * CHUNK, -1)


def lanes_wide(column, width):
    return jnp.concatenate([column] * (width // column.shape[-1]), axis=-1)


def mix_body(pieces, mix_ref, bank_ref, squares_ref, kernel_ref, sums_ref):
    step = pl.program_id(0)

    @pl.when(step == 0)
    def _():
        sums_ref[...] = jnp.zeros_like(sums_ref)

    kernels, rows, width = bank_ref.shape
    samples = kernel_ref.shape[0]
    per_tap = squares_ref.shape[1]
    for piece in range(pieces):
        part = bank_ref[:, piece * CHUNK : (piece + 1) * CHUNK, :].reshape(kernels * CHUNK, width)
        mixed = dot_f32(mix_ref[...], jnp.concatenate([part, part], axis=0), 1, 0)
        mixed = mixed.astype(jnp.bfloat16).reshape(samples, CHUNK, width)
        kernel_ref[:, piece * CHUNK : (piece + 1) * CHUNK, :] = mixed
        first = lax.rem(step * rows + piece * CHUNK, per_tap)
        factor = squares_ref[:, pl.ds(pl.multiple_of(first, CHUNK), CHUNK), :]
        wide = mixed.astype(jnp.float32)
        sums_ref[...] += jnp.sum(wide * wide * lanes_wide(factor, width), axis=1)


def mix_kernels(mix, bank_rows, squares):
    kernels, depth, width = bank_rows.shape
    samples = squares.shape[0]
    pieces = 4
    rows = pieces * CHUNK
    return pl.pallas_call(
        lambda *refs: mix_body(pieces, *refs),
        grid=(depth // rows,),
        in_specs=[
            pl.BlockSpec(mix.shape, lambda step: (0, 0)),
            pl.BlockSpec((kernels, rows, width), lambda step: (0, step, 0)),
            pl.BlockSpec(squares.shape, lambda step: (0, 0, 0)),
        ],
        out_specs=[
            pl.BlockSpec((samples, rows, width), lambda step: (0, step, 0)),
            pl.BlockSpec((samples, width), lambda step: (0, 0)),
        ],
        out_shape=[
            jax.ShapeDtypeStruct((samples, depth, width), jnp.bfloat16),
            jax.ShapeDtypeStruct((samples, width), jnp.float32),
        ],
        compiler_params=pltpu.CompilerParams(vmem_limit_bytes=48 * 2**20),
        name="mix_kernels",
    )(mix, bank_rows, squares)


def place_rows(slab, place_ref, spot_ref):
    pixels, width = slab.shape
    for shift in range(3):
        spot_ref[
            shift * pixels : (shift + 1) * pixels, shift * width : (shift + 1) * width
        ] = slab
    return dot_f32(place_ref[...], spot_ref[...], 1, 0).astype(jnp.bfloat16)


def conv_step(extra, sample, slab_ref, place_ref, kernel_ref, sums_ref, out_ref, spot_ref):
    rows = place_rows(slab_ref[0], place_ref, spot_ref)
    depth = rows.shape[1]
    total = None
    for shift in range(3):
        term = dot_f32(
            rows[shift * SIDE : shift * SIDE + PIXELS],
            kernel_ref[0, shift * depth : (shift + 1) * depth, :],
            1,
            0,
        )
        total = term if total is None else total + term
    out_ref[0, :PIXELS, :] = total.astype(jnp.bfloat16)
    if extra:
        line = sums_ref[pl.ds(sample, 1), :]
        out_ref[0, PIXELS:, :] = jnp.broadcast_to(line, (CHUNK, line.shape[1])).astype(jnp.bfloat16)


def fold_back(cotan, place_ref, kernel_ref, wide_ref, pixels, width):
    depth = 3 * width
    wide_ref[...] = jnp.zeros_like(wide_ref)
    for shift in range(3):
        wide_ref[shift * SIDE : shift * SIDE + PIXELS, :] += dot_f32(
            cotan, kernel_ref[0, shift * depth : (shift + 1) * depth, :], 1, 1
        )
    back = dot_f32(place_ref[...], wide_ref[...].astype(jnp.bfloat16), 0, 0)
    total = None
    for shift in range(3):
        term = back[shift * pixels : (shift + 1) * pixels, shift * width : (shift + 1) * width]
        total = term if total is None else total + term
    return total.astype(jnp.bfloat16)


def second_step(
    slab_ref,
    tan_ref,
    place_ref,
    kernel_ref,
    cotan_ref,
    side_ref,
    squares_ref,
    grad_ref,
    back_ref,
    scale_ref,
    spot_ref,
    wide_ref,
):
    pixels, width = slab_ref.shape[1:]
    depth = 3 * width
    rows = place_rows(slab_ref[0], place_ref, spot_ref)
    tan_rows = place_rows(tan_ref[0], place_ref, spot_ref)
    line = cotan_ref[0, PIXELS : PIXELS + CHUNK, :][:1].astype(jnp.float32)
    factor = 2.0 * lanes_wide(squares_ref[0], line.shape[1]) * line
    totals = None
    for shift in range(3):
        span = slice(shift * SIDE, shift * SIDE + PIXELS)
        grad = dot_f32(rows[span], cotan_ref[0, :PIXELS, :], 0, 0)
        grad = grad + dot_f32(tan_rows[span], side_ref[0], 0, 0)
        for tap in range(3):
            at = shift * depth + tap * width
            own = kernel_ref[0, at : at + width, :].astype(jnp.float32)
            grad_ref[0, at : at + width, :] = (
                grad[tap * width : (tap + 1) * width] + own * factor
            ).astype(jnp.bfloat16)
            term = own * own
            totals = term if totals is None else totals + term
    summed = jnp.sum(totals * line, axis=1, keepdims=True)
    scale_ref[0] = jnp.broadcast_to(summed, scale_ref.shape[1:])
    back_ref[0] = fold_back(
        cotan_ref[0, :PIXELS, :], place_ref, kernel_ref, wide_ref, pixels, width
    )


def unmix_body(pieces, mix_ref, bank_ref, grad_ref, out_ref, select_ref):
    @pl.when(pl.program_id(0) == 0)
    def _():
        select_ref[...] = jnp.zeros_like(select_ref)

    kernels, _, width = bank_ref.shape
    samples = grad_ref.shape[0]
    for piece in range(pieces):
        span = slice(piece * CHUNK, (piece + 1) * CHUNK)
        grad = grad_ref[:, span, :].reshape(samples * CHUNK, width)
        mixed = dot_f32(mix_ref[...], grad, 0, 0)
        count = kernels * CHUNK
        out_ref[:, span, :] = (mixed[:count] + mixed[count:]).reshape(kernels, CHUNK, width)
        part = bank_ref[:, span, :].reshape(count, width)
        select_ref[...] += dot_f32(grad, part, 1, 1)


def unmix_kernels(mix, bank_rows, grad):
    kernels, depth, width = bank_rows.shape
    samples = grad.shape[0]
    pieces = 4
    rows = pieces * CHUNK
    return pl.pallas_call(
        lambda *refs: unmix_body(pieces, *refs),
        grid=(depth // rows,),
        in_specs=[
            pl.BlockSpec(mix.shape, lambda step: (0, 0)),
            pl.BlockSpec((kernels, rows, width), lambda step: (0, step, 0)),
            pl.BlockSpec((samples, rows, width), lambda step: (0, step, 0)),
        ],
        out_specs=[
            pl.BlockSpec((kernels, rows, width), lambda step: (0, step, 0)),
            pl.BlockSpec((samples * CHUNK, kernels * CHUNK), lambda step: (0, 0)),
        ],
        out_shape=[
            jax.ShapeDtypeStruct((kernels, depth, width), jnp.float32),
            jax.ShapeDtypeStruct((samples * CHUNK, kernels * CHUNK), jnp.float32),
        ],
        compiler_params=pltpu.CompilerParams(vmem_limit_bytes=48 * 2**20),
        name="unmix_kernels",
    )(mix, bank_rows, grad)


@jax.custom_vjp
def row_products(left, right):
    return dot_f32(left.astype(jnp.bfloat16), right.astype(jnp.bfloat16), 1, 1)


def row_products_fwd(left, right):
    return row_products(left, right), (left, right)


def row_products_bwd(kept, cotan):
    left, right = (entry.astype(jnp.bfloat16) for entry in kept)
    short = cotan.astype(jnp.bfloat16)
    return dot_f32(short, right, 1, 0), dot_f32(short, left, 0, 0)


row_products.defvjp(row_products_fwd, row_products_bwd)


@jax.custom_vjp
def mixed_rows(soft, values):
    return dot_f32(soft.astype(jnp.bfloat16), values.astype(jnp.bfloat16), 1, 0)


def mixed_rows_fwd(soft, values):
    return mixed_rows(soft, values), (soft, values)


def mixed_rows_bwd(kept, cotan):
    soft, values = (entry.astype(jnp.bfloat16) for entry in kept)
    short = cotan.astype(jnp.bfloat16)
    return dot_f32(short, values, 1, 1), dot_f32(soft, short, 0, 0)


mixed_rows.defvjp(mixed_rows_fwd, mixed_rows_bwd)


@jax.custom_vjp
def as_row(column):
    count = column.shape[0]
    lane = lax.broadcasted_iota(jnp.int32, (count, 128), 1)
    rest, parts = column, jnp.zeros((count, 128), jnp.float32)
    for place in range(3):
        short = rest.astype(jnp.bfloat16).astype(jnp.float32)
        parts = jnp.where(lane == place, short, parts)
        rest = rest - short
    ones = jnp.ones((count, 128), jnp.bfloat16)
    return dot_f32(ones, parts.astype(jnp.bfloat16), 1, 1)


def as_row_fwd(column):
    return as_row(column), None


def as_row_bwd(kept, cotan):
    ones = jnp.ones((cotan.shape[0], 128), jnp.bfloat16)
    return (dot_f32(cotan.astype(jnp.bfloat16), ones, 0, 0)[:, :1],)


as_row.defvjp(as_row_fwd, as_row_bwd)


def soft_of(scores):
    top = lax.stop_gradient(jnp.max(scores, axis=1, keepdims=True))
    powers = jnp.exp(scores - top)
    return powers / jnp.sum(powers, axis=1, keepdims=True)


def soft_tangent(soft, tangent):
    return soft * (tangent - jnp.sum(soft * tangent, axis=1, keepdims=True))


def squared(left, right):
    return jnp.sum(left * right, axis=1, keepdims=True)


def self_head(queries, values):
    scores = 2.0 * row_products(queries, queries) - as_row(squared(queries, queries))
    return (mixed_rows(soft_of(scores * HEAD ** (-0.5)), values),)


def self_head_joint(queries, tan_queries, values, tan_values):
    scores = 2.0 * row_products(queries, queries) - as_row(squared(queries, queries))
    tan_scores = row_products(tan_queries, queries) + row_products(queries, tan_queries)
    tan_scores = 2.0 * (tan_scores - as_row(squared(queries, tan_queries)))
    soft = soft_of(scores * HEAD ** (-0.5))
    tan_soft = soft_tangent(soft, tan_scores * HEAD ** (-0.5))
    return (
        mixed_rows(soft, values),
        mixed_rows(tan_soft, values) + mixed_rows(soft, tan_values),
    )


def cross_head(queries, keys, values):
    return (mixed_rows(soft_of(row_products(queries, keys) * HEAD ** (-0.5)), values),)


def cross_head_joint(queries, tan_queries, keys, values):
    soft = soft_of(row_products(queries, keys) * HEAD ** (-0.5))
    tan_soft = soft_tangent(soft, row_products(tan_queries, keys) * HEAD ** (-0.5))
    return mixed_rows(soft, values), mixed_rows(tan_soft, values)


def per_head(fun, arrays, shapes, name):
    lanes = 2 * HEAD

    def body(*refs):
        inputs, outputs = refs[: len(arrays)], refs[len(arrays) :]
        for head in range(2):
            span = slice(head * HEAD, (head + 1) * HEAD)
            results = fun(*[ref[:, span].astype(jnp.float32) for ref in inputs])
            for ref, result in zip(outputs, results):
                ref[:, span] = result.astype(jnp.bfloat16)

    return pl.pallas_call(
        body,
        grid=(arrays[0].shape[1] // lanes,),
        in_specs=[pl.BlockSpec((entry.shape[0], lanes), lambda step: (0, step)) for entry in arrays],
        out_specs=[pl.BlockSpec((shape[0], lanes), lambda step: (0, step)) for shape in shapes],
        out_shape=[jax.ShapeDtypeStruct(shape, jnp.bfloat16) for shape in shapes],
        compiler_params=pltpu.CompilerParams(vmem_limit_bytes=32 * 2**20),
        name=name,
    )(*arrays)


def make_attention(fun, count, name):
    @jax.custom_vjp
    def attend(*arrays):
        return tuple(per_head(fun, arrays, [arrays[0].shape] * count, name))

    def attend_fwd(*arrays):
        return attend(*arrays), arrays

    def attend_bwd(arrays, cotans):
        def pull(*given):
            return jax.vjp(fun, *given[: len(arrays)])[1](tuple(given[len(arrays) :]))

        shapes = [entry.shape for entry in arrays]
        return tuple(per_head(pull, list(arrays) + list(cotans), shapes, name + "_pull"))

    attend.defvjp(attend_fwd, attend_bwd)
    return attend


self_attend = make_attention(self_head, 1, "self_heads")
self_attend_joint = make_attention(self_head_joint, 2, "self_heads_joint")
cross_attend = make_attention(cross_head, 1, "cross_heads")
cross_attend_joint = make_attention(cross_head_joint, 2, "cross_heads_joint")


def short_of(*arrays):
    return [entry.astype(jnp.bfloat16) for entry in arrays]


def gelu_parts(value):
    scale, cubic = (2.0 / np.pi) ** 0.5, 0.044715
    bend = jnp.tanh(scale * (value + cubic * value * value * value))
    slope = scale * (1.0 + 3.0 * cubic * value * value)
    steep = 1.0 - bend * bend
    once = steep * slope
    twice = steep * (6.0 * cubic * scale) * value - 2.0 * bend * once * slope
    return (
        0.5 * value * (1.0 + bend),
        0.5 * (1.0 + bend) + 0.5 * value * once,
        once + 0.5 * value * twice,
    )


@jax.custom_vjp
def gelu_kept(value):
    return gelu_parts(value)


def gelu_kept_fwd(value):
    result, first, second = lax.optimization_barrier(gelu_parts(value))
    return (result, first, second), first


def gelu_kept_bwd(first, cotans):
    return (cotans[0] * first,)


gelu_kept.defvjp(gelu_kept_fwd, gelu_kept_bwd)


@jax.custom_vjp
def gelu_joint(value, tangent, parts):
    return parts[0], tangent * parts[1]


def gelu_joint_fwd(value, tangent, parts):
    return gelu_joint(value, tangent, parts), (tangent, parts)


def gelu_joint_bwd(kept, cotans):
    tangent, parts = kept
    main, side = cotans
    back = main * parts[1] + side * tangent * parts[2]
    return back, side * parts[1], tuple(jnp.zeros_like(part) for part in parts)


gelu_joint.defvjp(gelu_joint_fwd, gelu_joint_bwd)


def layer_forward(conv_out, sums, text_rows, small, weights, noise):
    bias, strength, rgb_scales, rgb_weight = small
    qk_w, value_w, attn_w, query_w, key_w, cval_w, cout_w, mlp_w, mout_w = weights
    hidden_one = post_conv(conv_out, sums, bias, strength, noise)
    normed = rms_norm(hidden_one)
    (mixture,) = self_attend(*short_of(product(normed, qk_w), product(normed, value_w)))
    hidden_two = hidden_one + product_flip(mixture.astype(jnp.float32), attn_w)
    normed = rms_norm(hidden_two)
    (mixture,) = cross_attend(
        *short_of(
            product(normed, query_w), product(text_rows, key_w), product(text_rows, cval_w)
        )
    )
    hidden_three = hidden_two + product_flip(mixture.astype(jnp.float32), cout_w)
    normed = rms_norm(hidden_three)
    parts = gelu_kept(product(normed, mlp_w))
    hidden_four = hidden_three + product_flip(parts[0], mout_w)
    return (hidden_four, picture_of(hidden_four, rgb_scales, rgb_weight)), parts


def layer_joint(conv_out, conv_tan, sums, text_rows, small, weights, noise, parts):
    bias, strength, rgb_scales, rgb_weight = small
    qk_w, value_w, attn_w, query_w, key_w, cval_w, cout_w, mlp_w, mout_w = weights
    hidden_one, tan_one = with_tangent(
        lambda value: post_conv(value, sums, bias, strength, noise), conv_out, conv_tan
    )
    normed, tan_normed = with_tangent(rms_norm, hidden_one, tan_one)
    queries, tan_queries = product_pair(normed, tan_normed, qk_w)
    values, tan_values = product_pair(normed, tan_normed, value_w)
    mixture, tan_mixture = self_attend_joint(*short_of(queries, tan_queries, values, tan_values))
    added, tan_added = product_flip_pair(
        mixture.astype(jnp.float32), tan_mixture.astype(jnp.float32), attn_w
    )
    hidden_two, tan_two = hidden_one + added, tan_one + tan_added
    normed, tan_normed = with_tangent(rms_norm, hidden_two, tan_two)
    queries, tan_queries = product_pair(normed, tan_normed, query_w)
    mixture, tan_mixture = cross_attend_joint(
        *short_of(queries, tan_queries, product(text_rows, key_w), product(text_rows, cval_w))
    )
    added, tan_added = product_flip_pair(
        mixture.astype(jnp.float32), tan_mixture.astype(jnp.float32), cout_w
    )
    hidden_three, tan_three = hidden_two + added, tan_two + tan_added
    normed, tan_normed = with_tangent(rms_norm, hidden_three, tan_three)
    before, tan_before = product_pair(normed, tan_normed, mlp_w)
    inner, tan_inner = gelu_joint(before, tan_before, parts)
    added, tan_added = product_flip_pair(inner, tan_inner, mout_w)
    hidden_four, tan_four = hidden_three + added, tan_three + tan_added
    return (
        hidden_four,
        picture_of(hidden_four, rgb_scales, rgb_weight),
        picture_of(tan_four, rgb_scales, rgb_weight),
    )


SWAP = ((0, 1), (1, 0))


def swap_mp(values):
    return lax.ppermute(values, "mp", SWAP)


def pick(values, index):
    return lax.dynamic_index_in_dim(values, index, 0, keepdims=False)


def own_whole(values, mp):
    mine, other = pick(values, mp), swap_mp(pick(values, 1 - mp))
    first = jnp.where(mp == 0, mine, other)
    second = jnp.where(mp == 0, other, mine)
    return jnp.concatenate([first, second], axis=-1)


def both_half(whole, mp):
    half = whole.shape[-1] // 2
    mine = lax.dynamic_slice_in_dim(whole, mp * half, half, whole.ndim - 1)
    other = swap_mp(lax.dynamic_slice_in_dim(whole, (1 - mp) * half, half, whole.ndim - 1))
    first = jnp.where(mp == 0, mine, other)
    second = jnp.where(mp == 0, other, mine)
    return jnp.stack([first, second])


def to_slabs(both):
    devices = lax.axis_size("dp")
    parts = both.reshape(2, both.shape[1], devices, -1).transpose(2, 0, 1, 3)
    parts = lax.all_to_all(parts, "dp", 0, 0, tiled=True)
    return parts.reshape(2 * devices, both.shape[1], -1)


def from_slabs(slabs, mp):
    devices = lax.axis_size("dp")
    rows = slabs.shape[1]
    parts = slabs.astype(jnp.bfloat16).reshape((devices, 2) + slabs.shape[1:])
    parts = lax.all_to_all(parts, "dp", 0, 0, tiled=True)
    parts = parts.transpose(1, 2, 0, 3).reshape(2, rows, -1)
    other = swap_mp(pick(parts, 1 - mp))
    return pick(parts, mp).astype(jnp.float32) + other.astype(jnp.float32)


PLANES = 4


class Place:
    def __init__(self):
        dp = lax.axis_index("dp")
        self.z, self.y, self.core = dp // 4, lax.rem(dp // 2, 2), lax.rem(dp, 2)
        self.x = lax.axis_index("mp")


def greet(place, axes):
    barrier = pltpu.get_barrier_semaphore()

    def tell(**there):
        at = dict(z=place.z, y=place.y, core=place.core, x=place.x)
        at.update(there)
        pl.semaphore_signal(
            barrier,
            inc=1,
            device_id=((at["z"] * 2 + at["y"]) * 2 + at["core"], at["x"]),
            device_id_type=pl.DeviceIdType.MESH,
        )

    tell(core=1 - place.core)
    count = 1
    for name in ("y", "x"):
        if name in axes:
            tell(**{name: 1 - getattr(place, name)})
            count += 1

    @pl.when(place.z > 0)
    def _():
        tell(z=place.z - 1)

    @pl.when(place.z < PLANES - 1)
    def _():
        tell(z=place.z + 1)

    between = (place.z > 0) & (place.z < PLANES - 1)
    pl.semaphore_wait(barrier, count + jnp.where(between, 2, 1))


def gather_body(pieces, inputs, outputs, axes, send_sem, recv_sem, own_sem):
    place = Place()
    greet(place, axes)
    sends = []

    def spot(z, y, core, x):
        return (z * 2 + y) * 2 + core, x

    def chip(z, y, x):
        return (z * 2 + y) * 2 + x

    def send(number, piece, source, target, slot, parity, first, condition):
        sz, sy, sx = source
        dp, mp = spot(sz, sy, place.core, sx)
        there = piece["to"](outputs, dp, mp)
        copy = pltpu.make_async_remote_copy(
            src_ref=piece["of"](inputs) if first else there,
            dst_ref=there,
            send_sem=send_sem.at[number, chip(sz, sy, sx), slot],
            recv_sem=recv_sem.at[number, chip(sz, sy, sx), parity],
            device_id=spot(*target),
            device_id_type=pl.DeviceIdType.MESH,
        )

        if condition is None:
            copy.start()
        else:
            pl.when(condition)(copy.start)
        sends.append((condition, copy))

    def onward(number, piece, source, came, first, condition):
        def both(more):
            if condition is None:
                return more
            return condition if more is None else condition & more

        order = piece["order"]
        later = order if came is None else order[order.index(came[0]) :]
        for name in later:
            here = dict(z=place.z, y=place.y, core=place.core, x=place.x)
            if name == "z":
                for way, slot in ((1, 0), (-1, 1)):
                    if came is not None and came[0] == "z" and came[1] != way:
                        continue
                    fits = place.z < PLANES - 1 if way == 1 else place.z > 0
                    target = (place.z + way, place.y, place.core, place.x)
                    send(number, piece, source, target, slot, 0, first, both(fits))
            elif came is None or came[0] != name:
                here[name] = 1 - here[name]
                target = (here["z"], here["y"], here["core"], here["x"])
                slot = 2 if name == "y" else 3
                send(number, piece, source, target, slot, 0, first, both(None))
        target = (place.z, place.y, 1 - place.core, place.x)
        send(number, piece, source, target, 4, 1, first, both(None))

    def arrive(number, piece, source, parity, condition):
        sz, sy, sx = source
        core = place.core if parity == 0 else 1 - place.core
        there = piece["to"](outputs, *spot(sz, sy, core, sx))

        def wait():
            pltpu.make_async_remote_copy(
                src_ref=there,
                dst_ref=there,
                send_sem=send_sem.at[number, chip(sz, sy, sx), 0],
                recv_sem=recv_sem.at[number, chip(sz, sy, sx), parity],
                device_id=spot(place.z, place.y, 1 - place.core, place.x),
                device_id_type=pl.DeviceIdType.MESH,
            ).wait_recv()

        if condition is None:
            wait()
        else:
            pl.when(condition)(wait)

    own = []
    for number, piece in enumerate(pieces):
        onward(number, piece, (place.z, place.y, place.x), None, True, None)
        copy = pltpu.make_async_copy(
            piece["of"](inputs),
            piece["to"](outputs, *spot(place.z, place.y, place.core, place.x)),
            own_sem.at[number],
        )
        copy.start()
        own.append(copy)
    flips = [(fy, fx) for fy in (0, 1) for fx in ((0, 1) if "x" in axes else (0,))]
    blocks = [(dz, fy, fx) for dz in (0, 1, -1, 2, -2, 3, -3) for fy, fx in flips]
    blocks = sorted(blocks, key=lambda block: abs(block[0]) + block[1] + block[2])
    for dz, fy, fx in blocks:
        if (dz, fy, fx) == (0, 0, 0):
            continue
        condition = None
        if dz > 0:
            condition = place.z >= dz
        elif dz < 0:
            condition = place.z < PLANES + dz
        source = (
            place.z - dz,
            1 - place.y if fy else place.y,
            1 - place.x if fx else place.x,
        )
        for number, piece in enumerate(pieces):
            arrive(number, piece, source, 0, condition)
            moved = dict(z=dz, y=fy, x=fx)
            last = [name for name in piece["order"] if moved[name]][-1]
            came = (last, (1 if dz > 0 else -1) if last == "z" else 0)
            onward(number, piece, source, came, False, condition)
    for number, piece in enumerate(pieces):
        for sz in range(PLANES):
            for sy in range(2):
                for sx in (0, 1) if "x" in axes else (place.x,):
                    arrive(number, piece, (sz, sy, sx), 1, None)
    for condition, copy in sends:
        if condition is None:
            copy.wait_send()
        else:
            pl.when(condition)(copy.wait_send)
    for copy in own:
        copy.wait()


def gather_call(pieces, axes, arrays, shapes, call_id, name):
    count = len(arrays)

    def body(*refs):
        inputs, outputs = refs[:count], refs[count : count + len(shapes)]
        gather_body(pieces, inputs, outputs, axes, *refs[count + len(shapes) :])

    return pl.pallas_call(
        body,
        in_specs=[pl.BlockSpec(memory_space=pl.ANY)] * count,
        out_specs=[pl.BlockSpec(memory_space=pl.ANY)] * len(shapes),
        out_shape=[
            jax.ShapeDtypeStruct(shape, entry.dtype) for shape, entry in zip(shapes, arrays)
        ],
        scratch_shapes=[
            pltpu.SemaphoreType.DMA((len(pieces), 16, 5)),
            pltpu.SemaphoreType.DMA((len(pieces), 16, 2)),
            pltpu.SemaphoreType.DMA((len(pieces),)),
        ],
        compiler_params=pltpu.CompilerParams(collective_id=call_id, has_side_effects=True),
        name=name,
    )(*arrays)


def rows_at(index, rows):
    return pl.ds(pl.multiple_of(index * rows, rows), rows)


def lanes_at(index, lanes):
    return pl.ds(pl.multiple_of(index * lanes, lanes), lanes)


def gather_weights(shards, numbers, call_id):
    orders = dict(x=("z", "y", "x"), y=("z", "x", "y"), z=("x", "y", "z"))
    turns = ("x", "y", "x", "y", "x", "y", "z", "y", "z")

    def piece(number, turn):
        rows, lanes = arrays[number].shape
        stacked = number == len(shards)

        def to(refs, dp, mp):
            if stacked:
                return refs[number].at[rows_at(dp * 2 + mp, rows)]
            return refs[number].at[rows_at(dp, rows), lanes_at(mp, lanes)]

        return dict(order=orders[turn], of=lambda refs: refs[number], to=to)

    arrays = list(shards) + [numbers]
    pieces = [piece(len(shards), "x")]
    pieces += [piece(number, turn) for number, turn in enumerate(turns)]
    shapes = [(entry.shape[0] * 16, entry.shape[1] * 2) for entry in shards]
    shapes.append((numbers.shape[0] * 32, numbers.shape[1]))
    return gather_call(pieces, ("z", "y", "x"), arrays, shapes, call_id, "gather_weights")


def plane_of(z, turn):
    low = jnp.where(turn < 2, 1 - turn, turn)
    high = jnp.where(turn < 2, 2 + turn, 3 - turn)
    between = jnp.where(z == 1, low, high)
    return jnp.where(z == 0, turn, jnp.where(z == PLANES - 1, PLANES - 1 - turn, between))


class Stream:
    def __init__(self, source, slots, sem, where):
        self.source, self.slots, self.sem, self.where = source, slots, sem, where

    def copy(self, turn):
        slot = lax.rem(turn, 2)
        return pltpu.make_async_copy(
            self.source.at[self.where(turn)], self.slots.at[slot], self.sem.at[slot]
        )

    def take(self, turn, count):
        self.copy(turn).wait()

        @pl.when(turn + 1 < count)
        def _():
            self.copy(turn + 1).start()

        return lax.rem(turn, 2)


def consume_body(cut, samples, value_ref, landing, kernel_ref, slots, sems, work):
    kernel_sem, send_sem, recv_sem, own_sem = sems
    place = Place()
    z, y, core, x = place.z, place.y, place.core, place.x
    lanes = landing.shape[-1]
    pieces = [(s, slice(0, cut), "zy") for s in range(samples)]
    pieces += [(s, slice(cut, lanes), "yz") for s in range(samples)]
    blocks = 2 * PLANES
    count = 2 * samples * blocks

    def chip_at(block):
        return plane_of(z, block // 2), jnp.where(lax.rem(block, 2) == 1, 1 - y, y)

    def first_sample(block, parity):
        plane, row = chip_at(block)
        other = jnp.where(parity == 1, 1 - core, core)
        return ((plane * 2 + row) * 2 + other) * samples

    def sample_at(turn):
        block = turn // (2 * samples)
        return first_sample(block, lax.rem(turn // samples, 2)) + lax.rem(turn, samples)

    def sends(block, act):
        plane, row = chip_at(block)
        same_row = lax.rem(block, 2) == 0
        up, down = (plane <= z) & (z < PLANES - 1), (plane >= z) & (z > 0)
        for number, (s, span, order) in enumerate(pieces):
            view = landing.at[first_sample(block, 0) + s, :, span]
            if order == "zy":
                ways = (up & same_row, down & same_row, same_row)
            else:
                ways = (up, down, block == 0)
            targets = (
                (z + 1, y, core, 0),
                (z - 1, y, core, 0),
                (z, 1 - y, core, 0),
                (z, y, 1 - core, 1),
            )
            for slot, (dz, dy, dcore, parity) in enumerate(targets):
                copy = pltpu.make_async_remote_copy(
                    src_ref=view,
                    dst_ref=view,
                    send_sem=send_sem.at[block, number, slot],
                    recv_sem=recv_sem.at[plane * 2 + row, number, parity],
                    device_id=((dz * 2 + dy) * 2 + dcore, x),
                    device_id_type=pl.DeviceIdType.MESH,
                )
                if slot < 3:
                    pl.when(ways[slot])(lambda copy=copy: act(copy))
                else:
                    act(copy)

    def arrive(block, parity):
        plane, row = chip_at(block)
        for number, (s, span, order) in enumerate(pieces):
            view = landing.at[first_sample(block, parity) + s, :, span]
            pltpu.make_async_remote_copy(
                src_ref=view,
                dst_ref=view,
                send_sem=send_sem.at[block, number, 3],
                recv_sem=recv_sem.at[plane * 2 + row, number, parity],
                device_id=((z * 2 + y) * 2 + 1 - core, x),
                device_id_type=pl.DeviceIdType.MESH,
            ).wait_recv()

    stream = Stream(kernel_ref, slots, kernel_sem, sample_at)
    stream.copy(0).start()
    own = pltpu.make_async_copy(
        value_ref, landing.at[pl.ds(first_sample(0, 0), samples)], own_sem
    )
    own.start()
    greet(place, ("z", "y"))
    own.wait()
    sends(0, lambda copy: copy.start())

    @pl.loop(0, count)
    def _(turn):
        block = turn // (2 * samples)
        step = lax.rem(turn, 2 * samples)

        @pl.when((step == 0) & (block > 0))
        def _():
            arrive(block, 0)
            sends(block, lambda copy: copy.start())

        @pl.when(step == samples)
        def _():
            arrive(block, 1)

        slot = stream.take(turn, count)
        work(turn, sample_at(turn), slot, sample_at)

    @pl.loop(0, blocks)
    def _(block):
        sends(block, lambda copy: copy.wait_send())


def consume_scratch(samples, rows, lanes, kernel):
    dma = pltpu.SemaphoreType.DMA
    pieces = 2 * samples
    return [
        pltpu.VMEM((16 * samples, rows, lanes), jnp.bfloat16),
        pltpu.VMEM((2,) + kernel.shape[1:], jnp.bfloat16),
        dma((2,)),
        dma((2 * PLANES, pieces, 4)),
        dma((2 * PLANES, pieces, 2)),
        dma,
    ]


def whole_specs(count):
    return [pl.BlockSpec(memory_space=pltpu.VMEM)] * count


HBM = pl.BlockSpec(memory_space=pl.ANY)


def gather_back(cotan, place, kernel, pixels, width, call_id):
    samples, rows, lanes = cotan.shape
    total = kernel.shape[0]

    def body(
        cotan_ref,
        kernel_ref,
        place_ref,
        out_ref,
        all_ref,
        landing,
        slots,
        s0,
        s1,
        s2,
        s3,
        wide_ref,
        all_sem,
    ):
        def work(turn, sample, slot, sample_at):
            out_ref[sample] = fold_back(
                landing[sample], place_ref, slots.at[pl.ds(slot, 1)], wide_ref, pixels, width
            )

        consume_body(
            lanes * 3 // 4,
            samples,
            cotan_ref,
            landing,
            kernel_ref,
            slots,
            (s0, s1, s2, s3),
            work,
        )
        keep = pltpu.make_async_copy(landing, all_ref, all_sem)
        keep.start()
        keep.wait()

    return pl.pallas_call(
        body,
        in_specs=[HBM, HBM] + whole_specs(1),
        out_specs=whole_specs(1) + [HBM],
        out_shape=[
            jax.ShapeDtypeStruct((total, pixels, width), jnp.bfloat16),
            jax.ShapeDtypeStruct((total, rows, lanes), jnp.bfloat16),
        ],
        scratch_shapes=consume_scratch(samples, rows, lanes, kernel)
        + [pltpu.VMEM((PAD_ROWS, 3 * width), jnp.float32), pltpu.SemaphoreType.DMA],
        compiler_params=pltpu.CompilerParams(
            collective_id=call_id, has_side_effects=True, vmem_limit_bytes=40 * 2**20
        ),
        name="gather_back",
    )(cotan, kernel, place)


def gather_second(slabs, tans, place, kernel, cotan, sides, squares, call_id):
    samples, rows, lanes = cotan.shape
    total, pixels, width = slabs.shape

    def body(
        cotan_ref,
        kernel_ref,
        sides_ref,
        slab_ref,
        tan_ref,
        place_ref,
        squares_ref,
        grad_ref,
        back_ref,
        scale_ref,
        landing,
        slots,
        s0,
        s1,
        s2,
        s3,
        side_slots,
        side_sem,
        grad_slots,
        grad_sem,
        spot_ref,
        wide_ref,
    ):
        spot_ref[...] = jnp.zeros_like(spot_ref)

        def leave(slot, sample):
            return pltpu.make_async_copy(
                grad_slots.at[slot], grad_ref.at[sample], grad_sem.at[slot]
            )

        def work(turn, sample, slot, sample_at):
            sides = Stream(sides_ref, side_slots, side_sem, sample_at)
            pl.when(turn == 0)(lambda: sides.copy(0).start())
            sides.take(turn, total)

            @pl.when(turn >= 2)
            def _():
                leave(slot, sample).wait()

            one = pl.ds(sample, 1)
            second_step(
                slab_ref.at[one],
                tan_ref.at[one],
                place_ref,
                slots.at[pl.ds(slot, 1)],
                landing.at[one],
                side_slots.at[pl.ds(slot, 1)],
                squares_ref.at[one],
                grad_slots.at[pl.ds(slot, 1)],
                back_ref.at[one],
                scale_ref.at[one],
                spot_ref,
                wide_ref,
            )
            leave(slot, sample).start()

        consume_body(
            lanes * 3 // 4,
            samples,
            cotan_ref,
            landing,
            kernel_ref,
            slots,
            (s0, s1, s2, s3),
            work,
        )
        for slot in range(2):
            leave(slot, 0).wait()

    return pl.pallas_call(
        body,
        in_specs=[HBM, HBM, HBM] + whole_specs(4),
        out_specs=[HBM] + whole_specs(2),
        out_shape=[
            jax.ShapeDtypeStruct(kernel.shape, jnp.bfloat16),
            jax.ShapeDtypeStruct((total, pixels, width), jnp.bfloat16),
            jax.ShapeDtypeStruct(squares.shape, jnp.float32),
        ],
        scratch_shapes=consume_scratch(samples, rows, lanes, kernel)
        + [
            pltpu.VMEM((2,) + sides.shape[1:], jnp.bfloat16),
            pltpu.SemaphoreType.DMA((2,)),
            pltpu.VMEM((2,) + kernel.shape[1:], jnp.bfloat16),
            pltpu.SemaphoreType.DMA((2,)),
            pltpu.VMEM((3 * pixels, 3 * width), jnp.bfloat16),
            pltpu.VMEM((PAD_ROWS, 3 * width), jnp.float32),
        ],
        compiler_params=pltpu.CompilerParams(
            collective_id=call_id, has_side_effects=True, vmem_limit_bytes=48 * 2**20
        ),
        name="gather_second",
    )(cotan, kernel, sides, slabs, tans, place, squares)


def add_rows(total, part):
    shape = total.shape[:-2]
    for number in range(int(np.prod(shape))):
        spot = tuple(int(place) for place in np.unravel_index(number, shape))
        total[spot] = (total[spot].astype(jnp.float32) + part[spot].astype(jnp.float32)).astype(
            jnp.bfloat16
        )


def sum_body(
    cut,
    extra,
    kernel_ref,
    slab_ref,
    place_ref,
    sums_ref,
    out_ref,
    slots,
    kernel_sem,
    spot_ref,
    acc,
    core_out,
    core_in,
    y_in,
    y_last,
    z_first,
    z_second,
    x_in,
    core_send,
    core_recv,
    y_send,
    y_recv,
    z_send,
    z_recv,
    x_send,
    x_recv,
):
    place = Place()
    z, y, x = place.z, place.y, place.x
    spot_ref[...] = jnp.zeros_like(spot_ref)
    wide, narrow = slice(0, cut), slice(cut, acc.shape[-1])

    def spot(z, y, core, x):
        return (z * 2 + y) * 2 + core, x

    def remote(source, target, send, recv, device):
        return pltpu.make_async_remote_copy(
            src_ref=source,
            dst_ref=target,
            send_sem=send,
            recv_sem=recv,
            device_id=spot(*device),
            device_id_type=pl.DeviceIdType.MESH,
        )

    other_core = (z, y, 1 - place.core, x)
    other_y = (z, 1 - y, place.core, x)
    other_x = (z, y, place.core, 1 - x)

    order = (3, 0, 2, 1)

    def chunk_at(chunk):
        turn = chunk // 2
        dest = jnp.where(turn == 0, 3, jnp.where(turn == 1, 0, 4 - turn))
        return dest, jnp.where(lax.rem(chunk, 2) == 0, 1 - y, y)

    def sample_at(turn):
        dest, side = chunk_at(turn // 4)
        step = lax.rem(turn, 4)
        owner = jnp.where(step < 2, 1 - place.core, place.core)
        return ((dest * 2 + side) * 2 + owner) * 2 + lax.rem(step, 2)

    stream = Stream(kernel_ref, slots, kernel_sem, sample_at)
    stream.copy(0).start()
    greet(place, ("z", "y", "x"))

    def core_copy(chunk):
        dest, side = chunk_at(chunk)
        return remote(
            core_out.at[dest, side],
            core_in.at[dest, side],
            core_send.at[chunk],
            core_recv.at[chunk],
            other_core,
        )

    def y_copy(dest):
        return remote(
            acc.at[dest, 1 - y, :, :, wide], y_in.at[dest], y_send.at[dest], y_recv.at[dest], other_y
        )

    def one_sample(turn):
        chunk, step = turn // 4, lax.rem(turn, 4)
        dest, side = chunk_at(chunk)
        sample = sample_at(turn)
        slot = stream.take(turn, 16 * 2)

        def convolve(target):
            conv_step(
                extra,
                sample,
                slab_ref.at[pl.ds(sample, 1)],
                place_ref,
                slots.at[pl.ds(slot, 1)],
                sums_ref,
                target.at[dest, side, pl.ds(lax.rem(step, 2), 1)],
                spot_ref,
            )

        pl.when(step < 2)(lambda: convolve(core_out))
        pl.when(step >= 2)(lambda: convolve(acc))
        pl.when(step == 1)(lambda: core_copy(chunk).start())

        @pl.when(step == 3)
        def _():
            core_copy(chunk).wait_recv()
            add_rows(acc.at[dest, side], core_in.at[dest, side])
            pl.when(lax.rem(chunk, 2) == 0)(lambda: y_copy(dest).start())

    views = (
        lambda dest: acc.at[dest, y, :, :, wide],
        lambda dest: acc.at[dest, :, :, :, narrow],
    )
    landings = (z_first, z_second)

    def z_copy(slot, way, dest, device):
        return remote(
            views[slot](dest),
            landings[slot].at[way, dest],
            z_send.at[slot, way, dest],
            z_recv.at[slot, way, dest],
            device,
        )

    def take_y(dest):
        y_copy(dest).wait_recv()
        add_rows(views[0](dest), y_in.at[dest])

    def along_z(slot, dest, act):
        for way in (0, 1):
            near = dest > z if way == 0 else dest < z
            has_before = z > 0 if way == 0 else z < PLANES - 1
            copy = z_copy(slot, way, dest, (z + (1 if way == 0 else -1), y, place.core, x))
            if act:

                @pl.when(near & has_before)
                def _():
                    copy.wait_recv()
                    add_rows(views[slot](dest), landings[slot].at[way, dest])

                pl.when(near)(copy.start)
            else:
                pl.when(near)(copy.wait_send)

    def end_z(slot):
        for way in (0, 1):

            @pl.when(z > 0 if way == 0 else z < PLANES - 1)
            def _():
                z_copy(slot, way, z, other_core).wait_recv()
                add_rows(views[slot](z), landings[slot].at[way, z])

    @pl.loop(0, 2 * PLANES)
    def _(turn):
        @pl.when(turn < PLANES)
        def _():
            pl.loop(0, 8)(lambda step: one_sample(turn * 8 + step))

        for number, dest in enumerate(order):
            due = number + jnp.where(dest > z, z, PLANES - 1 - z)

            @pl.when((turn == due) & (dest != z))
            def _():
                along_z(1, dest, True)

            @pl.when((turn == due + 1) & (dest != z))
            def _():
                take_y(dest)
                along_z(0, dest, True)

    take_y(z)
    end_z(1)
    last = remote(
        acc.at[z, 1 - y, :, :, narrow], y_last, y_send.at[PLANES], y_recv.at[PLANES], other_y
    )
    last.start()
    end_z(0)
    last.wait_recv()
    add_rows(acc.at[z, y, :, :, narrow], y_last)
    swap = remote(acc.at[z, y, 1 - x], x_in, x_send, x_recv, other_x)
    swap.start()
    lanes = acc.shape[-1]
    out_ref[:, lanes_at(x, lanes)] = acc[z, y, x]
    swap.wait_recv()
    out_ref[:, lanes_at(1 - x, lanes)] = x_in[...]
    swap.wait_send()
    last.wait_send()
    for dest in range(PLANES):
        y_copy(dest).wait_send()
        for slot in (0, 1):
            along_z(slot, dest, False)

    @pl.loop(0, 2 * PLANES)
    def _(chunk):
        core_copy(chunk).wait_send()


def conv_sum(slabs, place, kernel, sums, extra, call_id):
    _, pixels, width = slabs.shape
    rows, lanes = PIXELS + (CHUNK if extra else 0), kernel.shape[2]
    cut = lanes * 3 // 4
    bf16, dma = jnp.bfloat16, pltpu.SemaphoreType.DMA
    return pl.pallas_call(
        lambda *refs: sum_body(cut, extra, *refs),
        in_specs=[HBM] + whole_specs(3),
        out_specs=pl.BlockSpec(memory_space=pltpu.VMEM),
        out_shape=jax.ShapeDtypeStruct((rows, 2 * lanes), bf16),
        scratch_shapes=[
            pltpu.VMEM((2,) + kernel.shape[1:], bf16),
            dma((2,)),
            pltpu.VMEM((3 * pixels, 3 * width), bf16),
            pltpu.VMEM((PLANES, 2, 2, rows, lanes), bf16),
            pltpu.VMEM((PLANES, 2, 2, rows, lanes), bf16),
            pltpu.VMEM((PLANES, 2, 2, rows, lanes), bf16),
            pltpu.VMEM((PLANES, 2, rows, cut), bf16),
            pltpu.VMEM((2, rows, lanes - cut), bf16),
            pltpu.VMEM((2, PLANES, 2, rows, cut), bf16),
            pltpu.VMEM((2, PLANES, 2, 2, rows, lanes - cut), bf16),
            pltpu.VMEM((rows, lanes), bf16),
            dma((8,)),
            dma((8,)),
            dma((PLANES + 1,)),
            dma((PLANES + 1,)),
            dma((2, 2, PLANES)),
            dma((2, 2, PLANES)),
            dma,
            dma,
        ],
        compiler_params=pltpu.CompilerParams(
            collective_id=call_id, has_side_effects=True, vmem_limit_bytes=48 * 2**20
        ),
        name="conv_sum",
    )(kernel, slabs, place, sums)


def sum_weights_body(parts, count, refs):
    inputs, outputs, rest = refs[:count], refs[count : 2 * count], refs[2 * count :]
    acc, core_in, one_in, two_in, z_in = (rest[k * count : (k + 1) * count] for k in range(5))
    (
        load_sem,
        core_send,
        core_recv,
        one_send,
        one_recv,
        two_send,
        two_recv,
        z_send,
        z_recv,
    ) = rest[5 * count :]
    place = Place()
    greet(place, ("z", "y", "x"))
    z, y, x = place.z, place.y, place.x
    order = (3, 0, 2, 1)
    finish = []

    def remote(source, target, send, recv, device):
        dz, dy, core, dx = device
        return pltpu.make_async_remote_copy(
            src_ref=source,
            dst_ref=target,
            send_sem=send,
            recv_sem=recv,
            device_id=((dz * 2 + dy) * 2 + core, dx),
            device_id_type=pl.DeviceIdType.MESH,
        )

    other_core = (z, y, 1 - place.core, x)
    other_y = (z, 1 - y, place.core, x)
    other_x = (z, y, place.core, 1 - x)
    sides = (1 - y, y)

    first = {}
    for dest in order:
        for w in range(count):
            rows = acc[w].shape[2]
            for turn, side in enumerate(sides):
                at = ((dest * 2 + side) * 2 + (1 - place.core)) * rows
                mine = ((dest * 2 + side) * 2 + place.core) * rows
                sent = remote(
                    inputs[w].at[pl.ds(pl.multiple_of(at, rows), rows)],
                    core_in[w].at[dest, side],
                    core_send.at[w, dest, turn],
                    core_recv.at[w, dest, turn],
                    other_core,
                )
                sent.start()
                load = pltpu.make_async_copy(
                    inputs[w].at[pl.ds(pl.multiple_of(mine, rows), rows)],
                    acc[w].at[dest, side],
                    load_sem.at[w, dest, turn],
                )
                load.start()
                first[w, dest, turn] = (sent, load)

    def half(w, index):
        lanes = acc[w].shape[-1] // 2
        return lanes_at(index, lanes)

    ones, twos = {}, {}

    def stage_one(dest):
        for w in range(count):
            for turn, side in enumerate(sides):
                sent, load = first[w, dest, turn]
                load.wait()
                sent.wait_recv()
                finish.append((None, sent))
                add_rows(acc[w].at[dest, side], core_in[w].at[dest, side])
                if parts[w] == "z":
                    continue
                if parts[w] == "xy":
                    copy = remote(
                        acc[w].at[dest, side, :, half(w, 1 - x)],
                        one_in[w].at[dest, side],
                        one_send.at[w, dest, turn],
                        one_recv.at[w, dest, turn],
                        other_x,
                    )
                elif turn == 0:
                    copy = remote(
                        acc[w].at[dest, side],
                        one_in[w].at[dest],
                        one_send.at[w, dest, turn],
                        one_recv.at[w, dest, turn],
                        other_y,
                    )
                else:
                    continue
                copy.start()
                ones[w, dest, turn] = copy

    def stage_two(dest):
        for w in range(count):
            if parts[w] == "z":
                continue
            if parts[w] == "xy":
                for turn, side in enumerate(sides):
                    copy = ones[w, dest, turn]
                    copy.wait_recv()
                    finish.append((None, copy))
                    view = acc[w].at[dest, side, :, half(w, x)]
                    add_rows(view, one_in[w].at[dest, side])
                    if turn == 0:
                        twos[w, dest] = remote(
                            view,
                            two_in[w].at[dest],
                            two_send.at[w, dest],
                            two_recv.at[w, dest],
                            other_y,
                        )
                        twos[w, dest].start()
            else:
                copy = ones[w, dest, 0]
                copy.wait_recv()
                finish.append((None, copy))
                add_rows(acc[w].at[dest, y], one_in[w].at[dest])
                twos[w, dest] = remote(
                    acc[w].at[dest, y, :, half(w, 1 - x)],
                    two_in[w].at[dest],
                    two_send.at[w, dest],
                    two_recv.at[w, dest],
                    other_x,
                )
                twos[w, dest].start()

    def plane_copy(w, dest, way, device):
        return remote(
            acc[w].at[dest],
            z_in[w].at[way, dest],
            z_send.at[w, way, dest],
            z_recv.at[w, way, dest],
            device,
        )

    def planes_first(turn):
        for number, dest in enumerate(order):
            if turn < number + 1 or turn > number + PLANES:
                continue
            due = turn == number + 1 + jnp.where(dest > z, z, PLANES - 1 - z)
            for w in range(count):
                if parts[w] != "z":
                    continue
                for way in (0, 1):
                    near = dest > z if way == 0 else dest < z
                    has_before = z > 0 if way == 0 else z < PLANES - 1
                    device = (z + (1 if way == 0 else -1), y, place.core, x)
                    copy = plane_copy(w, dest, way, device)

                    @pl.when(due & near & has_before)
                    def _():
                        copy.wait_recv()
                        add_rows(acc[w].at[dest], z_in[w].at[way, dest])

                    pl.when(due & near)(copy.start)
                    if turn == number + 1:
                        finish.append((near, copy))

    def planes_last():
        chosen = [w for w in range(count) if parts[w] == "z"]
        lasts = []
        for w in chosen:
            for way in (0, 1):

                @pl.when(z > 0 if way == 0 else z < PLANES - 1)
                def _():
                    plane_copy(w, z, way, other_core).wait_recv()
                    add_rows(acc[w].at[z], z_in[w].at[way, z])

            copy = remote(
                acc[w].at[z, 1 - y], one_in[w], one_send.at[w, 0, 0], one_recv.at[w, 0, 0], other_y
            )
            copy.start()
            finish.append((None, copy))
            lasts.append(copy)
        for w, copy in zip(chosen, list(lasts)):
            copy.wait_recv()
            add_rows(acc[w].at[z, y], one_in[w])
            more = remote(
                acc[w].at[z, y, :, half(w, 1 - x)],
                two_in[w],
                two_send.at[w, 0],
                two_recv.at[w, 0],
                other_x,
            )
            more.start()
            finish.append((None, more))
            lasts.append(more)
        for w, copy in zip(chosen, lasts[len(chosen) :]):
            copy.wait_recv()
            add_rows(acc[w].at[z, y, :, half(w, x)], two_in[w])

    def z_copy(w, dest, way):
        return remote(
            acc[w].at[dest, y, :, half(w, x)],
            z_in[w].at[way, dest],
            z_send.at[w, way, dest],
            z_recv.at[w, way, dest],
            (z + (1 if way == 0 else -1), y, place.core, x),
        )

    def stage_z(dest):
        for w in range(count):
            if parts[w] == "z":
                continue
            copy = twos[w, dest]
            copy.wait_recv()
            finish.append((None, copy))
            view = acc[w].at[dest, y, :, half(w, x)]
            add_rows(view, two_in[w].at[dest])
            for way in (0, 1):
                near = dest > z if way == 0 else dest < z
                has_before = z > 0 if way == 0 else z < PLANES - 1
                copy = z_copy(w, dest, way)

                @pl.when(near & has_before)
                def _():
                    copy.wait_recv()
                    add_rows(view, z_in[w].at[way, dest])

                pl.when(near)(copy.start)
                finish.append((near, copy))

    for turn in range(PLANES + 2):
        if turn < PLANES:
            stage_one(order[turn])
        if 0 <= turn - 1 < PLANES:
            stage_two(order[turn - 1])
        planes_first(turn)
        if turn >= 2:
            stage_z(order[turn - 2])
    for turn in range(PLANES + 2, 2 * PLANES):
        planes_first(turn)
    planes_last()
    for w in range(count):
        view = acc[w].at[z, y, :, half(w, x)]
        for way in (0, 1) if parts[w] != "z" else ():

            @pl.when(z > 0 if way == 0 else z < PLANES - 1)
            def _():
                remote(
                    view,
                    z_in[w].at[way, z],
                    z_send.at[w, way, z],
                    z_recv.at[w, way, z],
                    other_core,
                ).wait_recv()
                add_rows(view, z_in[w].at[way, z])

        outputs[w][...] = acc[w][z, y, :, half(w, x)].astype(jnp.float32)
    for condition, copy in finish:
        if condition is None:
            copy.wait_send()
        else:
            pl.when(condition)(copy.wait_send)


def sum_weights(grads, parts, call_id):
    count = len(grads)
    bf16, dma = jnp.bfloat16, pltpu.SemaphoreType.DMA
    blocks = [(grad.shape[0] // 16, grad.shape[1]) for grad in grads]
    ones, twos, planes = [], [], []
    for (rows, lanes), part in zip(blocks, parts):
        if part == "z":
            ones.append((rows, lanes))
            twos.append((rows, lanes // 2))
            planes.append((2, PLANES, 2, rows, lanes))
        else:
            ones.append((PLANES, 2, rows, lanes // 2) if part == "xy" else (PLANES, rows, lanes))
            twos.append((PLANES, rows, lanes // 2))
            planes.append((2, PLANES, rows, lanes // 2))
    return pl.pallas_call(
        lambda *refs: sum_weights_body(parts, count, refs),
        in_specs=[pl.BlockSpec(memory_space=pl.ANY)] * count,
        out_specs=[pl.BlockSpec(memory_space=pltpu.VMEM)] * count,
        out_shape=[
            jax.ShapeDtypeStruct((rows, lanes // 2), jnp.float32) for rows, lanes in blocks
        ],
        scratch_shapes=[pltpu.VMEM((PLANES, 2, rows, lanes), bf16) for rows, lanes in blocks]
        + [pltpu.VMEM((PLANES, 2, rows, lanes), bf16) for rows, lanes in blocks]
        + [pltpu.VMEM(shape, bf16) for shape in ones]
        + [pltpu.VMEM(shape, bf16) for shape in twos + planes]
        + [dma((count, PLANES, 2))] * 5
        + [dma((count, PLANES))] * 2
        + [dma((count, 2, PLANES))] * 2,
        compiler_params=pltpu.CompilerParams(
            collective_id=call_id, has_side_effects=True, vmem_limit_bytes=60 * 2**20
        ),
        name="sum_weights",
    )(*grads)


def sample_parallel(
    layer_input,
    labels,
    text_ids,
    noise_seeds,
    penalty_mask,
    class_table,
    token_table,
    sel_weight,
    mod_weight,
    rgb_mod,
    rgb_weight,
    conv_bias,
    noise_strength,
    kernel_bank,
    qk_weight,
    value_weight,
    attn_out,
    cross_query,
    cross_key,
    cross_value,
    cross_out,
    mlp_in,
    mlp_out,
    cot_feat,
    cot_rgb,
    penalty_dir,
):
    mp = lax.axis_index("mp")
    dp = lax.axis_index("dp")
    half_px = layer_input.shape[1]
    slab = kernel_bank.shape[2]
    width_out = kernel_bank.shape[3]
    float32, bfloat16 = jnp.float32, jnp.bfloat16

    input_whole = lax.all_gather(layer_input, "mp", axis=2, tiled=True)
    raw_slabs = to_slabs(input_whole)
    numbers = jnp.concatenate([jnp.pad(labels, (0, 126)), text_ids.reshape(-1)]).reshape(2, 128)
    gathered = gather_weights(
        [
            mlp_in,
            mlp_out.T,
            qk_weight,
            value_weight,
            attn_out.T,
            cross_query,
            cross_out.T,
            cross_key,
            cross_value,
        ],
        jnp.pad(numbers, ((0, 6), (0, 0))),
        1,
    )
    mlp_whole, mout_whole, qk_whole, value_whole, attn_whole, query_whole, cout_whole = gathered[:7]
    key_whole, cval_whole, numbers_all = gathered[7:]
    weights = (
        qk_whole,
        value_whole,
        attn_whole,
        query_whole,
        key_whole,
        cval_whole,
        cout_whole,
        mlp_whole,
        mout_whole,
    )

    numbers_all = numbers_all.reshape(16, 2, 8, 128)[:, 0]
    labels_all = numbers_all[:, 0, :2].reshape(-1)
    ids_all = numbers_all[:, 1].reshape(-1)
    sample_count = labels_all.shape[0]
    classes = jnp.arange(class_table.shape[0], dtype=jnp.int32)
    onehot_class = (labels_all[:, None] == classes[None, :]).astype(bfloat16)
    latent = dot_wide(onehot_class, class_table, 1, 0)
    select_all, select_pull = jax.vjp(last_softmax, dot_wide(latent, sel_weight, 1, 0))
    scales_all = 1.0 + dot_wide(latent, mod_weight, 1, 0)
    rgb_scales_all = 1.0 + dot_wide(latent, rgb_mod, 1, 0)
    me = 2 * dp + mp
    scales = pick(scales_all, me)
    rgb_scales = pick(rgb_scales_all, me)
    scales_slab = lax.dynamic_slice_in_dim(scales_all, dp * slab, slab, 1)
    words = jnp.arange(token_table.shape[0], dtype=jnp.int32)
    text_own = pick(text_ids, mp)
    text_rows = dot_wide((text_own[:, None] == words[None, :]).astype(bfloat16), token_table, 1, 0)
    noise = noise_field(pick(noise_seeds, mp)[None], SIDE * SIDE)[0]
    small = (
        conv_bias.astype(float32),
        noise_strength.astype(float32),
        rgb_scales,
        rgb_weight.astype(float32),
    )

    bank_rows = kernel_bank.reshape(kernel_bank.shape[0], 9 * slab, width_out)
    mix = mix_matrix(select_all)
    scales_two = jnp.broadcast_to(
        (scales_slab * scales_slab)[:, :, None], (sample_count, slab, 128)
    )
    kernel, sums_part = mix_kernels(mix, bank_rows, scales_two)
    place = placing(SIDE // 2)

    input_own = pick(input_whole, mp).astype(float32)
    slabs_x = (raw_slabs.astype(float32) * scales_slab[:, None, :]).astype(bfloat16)
    summed = conv_sum(slabs_x, place, kernel, sums_part, True, 4).astype(float32)
    conv_out, sums = summed[:PIXELS], summed[PIXELS]

    (hidden_four, picture), pull, parts = jax.vjp(
        lambda value: layer_forward(value, sums, text_rows, small, weights, noise),
        conv_out,
        has_aux=True,
    )

    dir_own = pick(penalty_dir, mp).astype(float32)
    grad_conv = pull((jnp.zeros_like(hidden_four), dir_own))[0]
    back_slabs, sides_all = gather_back(
        both_half(grad_conv.astype(bfloat16), mp), place, kernel, half_px, slab, 2
    )
    grad_moduled = from_slabs(back_slabs, mp).astype(bfloat16).astype(float32)
    mask_own = pick(penalty_mask, mp).astype(float32)
    tangent = penalty_weight * mask_own * grad_moduled * scales

    tan_moduled = (tangent * scales).astype(bfloat16)
    tan_other = swap_mp(tan_moduled)
    tan_pair = jnp.stack(
        [jnp.where(mp == 0, tan_moduled, tan_other), jnp.where(mp == 0, tan_other, tan_moduled)]
    )
    slabs_t = to_slabs(tan_pair)
    conv_tan = conv_sum(slabs_t, place, kernel, sums_part, False, 5).astype(float32)

    (ignored_out, ignored_pic, ignored_tan), pull_joint = jax.vjp(
        lambda *given: layer_joint(*given, noise, parts),
        conv_out,
        conv_tan,
        sums,
        text_rows,
        small,
        weights,
    )
    cot_own = own_whole(cot_feat, mp).astype(float32)
    grad_main, _, grad_sums, grad_text, grad_small, grad_weights = pull_joint(
        (cot_own, pick(cot_rgb, mp).astype(float32), dir_own)
    )

    orders = ("xy", "yx", "xy", "yx", "xy", "yx", "z", "z", "z")
    d_qk, d_value, d_attn, d_query, d_key, d_cval, d_cout, d_mlp, d_mout = grad_weights
    mlp_grad, mout_grad, qk_grad, value_grad, attn_grad, query_grad, cout_grad, key_grad, cval_grad = (
        sum_weights(
            [d_mlp, d_mout, d_qk, d_value, d_attn, d_query, d_cout, d_key, d_cval], orders, 6
        )
    )
    big_sums = (
        qk_grad,
        value_grad,
        attn_grad.T,
        query_grad,
        key_grad,
        cval_grad,
        cout_grad.T,
        mlp_grad,
        mout_grad.T,
    )

    lines = jnp.broadcast_to(grad_sums[None], (CHUNK,) + grad_sums.shape)
    wide = jnp.concatenate([grad_main.astype(bfloat16), lines.astype(bfloat16)], axis=0)
    grad_kernel, back_slabs, scale_sums = gather_second(
        slabs_x, slabs_t, place, kernel, both_half(wide, mp), sides_all, scales_two, 3
    )
    grad_scales_slab = 2.0 * scales_slab * scale_sums[:, :, 0]
    bank_grad, select_products = unmix_kernels(mix, bank_rows, grad_kernel)
    bank_grad = bank_grad.reshape(kernel_bank.shape)
    grad_select = jnp.einsum(
        "brkr->bk", select_products.reshape(sample_count, CHUNK, -1, CHUNK)
    )
    back_main = from_slabs(back_slabs, mp).astype(bfloat16).astype(float32)
    input_grad = back_main * scales
    grad_scales = jnp.sum(back_main * input_own + grad_moduled * tangent, axis=0)

    grad_bias, grad_strength, grad_rgb_scales, grad_rgb_weight = grad_small
    row = jnp.concatenate(
        [
            grad_scales,
            grad_rgb_scales,
            grad_rgb_weight.reshape(-1),
            grad_bias,
            grad_strength,
            grad_scales_slab.reshape(-1),
            grad_select.reshape(-1),
        ]
    ).reshape(-1, 128)
    rows_all = lax.all_gather(row, ("dp", "mp"), axis=0, tiled=False).reshape(sample_count, -1)
    channels = scales.shape[0]
    scale_terms = rows_all[:, :channels]
    rgb_terms = rows_all[:, channels : 2 * channels]
    sums_all = jnp.sum(rows_all[:, 2 * channels : 7 * channels], axis=0)
    slab_terms = rows_all[:, 7 * channels : 7 * channels + sample_count * slab]
    slab_terms = slab_terms.reshape(-1, 2, sample_count, slab).sum(axis=1)
    scale_terms = scale_terms + slab_terms.transpose(1, 0, 2).reshape(sample_count, channels)
    select_terms = jnp.sum(rows_all[:, 7 * channels + sample_count * slab :], axis=0)
    logit_terms = select_pull(select_terms.reshape(sample_count, -1))[0]
    latent_terms = (
        matmul_high(scale_terms, mod_weight.astype(float32).T)
        + matmul_high(rgb_terms, rgb_mod.astype(float32).T)
        + matmul_high(logit_terms, sel_weight.astype(float32).T)
    )
    class_grad = matmul_high(onehot_class.astype(float32).T, latent_terms)
    sel_grad = matmul_high(latent.T, logit_terms)
    mod_grad = matmul_high(latent.T, scale_terms)
    rgb_mod_grad = matmul_high(latent.T, rgb_terms)
    text_all = lax.all_gather(grad_text.astype(bfloat16), ("dp", "mp"), axis=0, tiled=True)
    token_grad = dot_wide((ids_all[:, None] == words[None, :]).astype(bfloat16), text_all, 0, 0)

    picture_other = swap_mp(picture)
    pictures = jnp.stack(
        [jnp.where(mp == 0, picture, picture_other), jnp.where(mp == 0, picture_other, picture)]
    )
    return (
        both_half(hidden_four, mp),
        pictures,
        both_half(input_grad, mp),
        class_grad,
        token_grad,
        sel_grad,
        mod_grad,
        rgb_mod_grad,
        sums_all[: 3 * channels].reshape(3, channels),
        sums_all[3 * channels : 4 * channels],
        sums_all[4 * channels :],
        bank_grad,
    ) + big_sums


def solution(mesh):
    in_specs = (
        P("dp", None, "mp"),
        P("dp"),
        P("dp", None),
        P("dp"),
        P("dp"),
        P(),
        P(),
        P(),
        P(),
        P(),
        P(),
        P(),
        P(),
        P(None, None, "dp", "mp"),
        P("dp", "mp"),
        P("dp", "mp"),
        P("mp", "dp"),
        P("dp", "mp"),
        P("dp", "mp"),
        P("dp", "mp"),
        P("mp", "dp"),
        P("dp", "mp"),
        P("mp", "dp"),
        P("dp", None, "mp"),
        P("dp", None, None),
        P("dp", None, None),
    )
    out_specs = (
        P("dp", None, "mp"),
        P("dp", None, None),
        P("dp", None, "mp"),
        P(),
        P(),
        P(),
        P(),
        P(),
        P(),
        P(),
        P(),
        P(None, None, "dp", "mp"),
        P("dp", "mp"),
        P("dp", "mp"),
        P("mp", "dp"),
        P("dp", "mp"),
        P("dp", "mp"),
        P("dp", "mp"),
        P("mp", "dp"),
        P("dp", "mp"),
        P("mp", "dp"),
    )
    return jax.shard_map(
        sample_parallel if fits_samples(mesh) else tensor_parallel,
        mesh=mesh, in_specs=in_specs, out_specs=out_specs, check_vma=False
    )
```

```python
import jax
import jax.numpy as jnp
import numpy as np
from jax import lax
from jax.experimental import pallas as pl
from jax.experimental.pallas import tpu as pltpu
from jax.sharding import PartitionSpec as P

HEAD = 64
SIDE = 16


penalty_weight = 1.0


def rounded(values):
    return lax.optimization_barrier(values.astype(jnp.bfloat16)).astype(jnp.float32)


def matmul_high(left, right):
    return jnp.matmul(left, right, precision=lax.Precision.HIGHEST)


def einsum_high(form, *operands):
    return jnp.einsum(form, *operands, precision=lax.Precision.HIGHEST)


def einsum_low(form, left, right):
    return jnp.einsum(
        form,
        left.astype(jnp.bfloat16),
        right.astype(jnp.bfloat16),
        preferred_element_type=jnp.float32,
    )


def noise_field(seed_ids, pixel_count):
    pixel_ids = jnp.arange(pixel_count, dtype=jnp.int32)
    mixed = seed_ids[:, None] * 1103515245 + pixel_ids[None, :] * 40503
    mixed = jnp.bitwise_xor(mixed, jnp.right_shift(mixed, 13)) * 1664525 + 1013904223
    levels = jnp.bitwise_and(jnp.right_shift(mixed, 8), 65535)
    return levels.astype(jnp.float32) / 65536.0 - 0.5


def patches_of(flat_rows, side_len):
    samples_here, pixels, width_here = flat_rows.shape
    half_side = side_len // 2
    picture = flat_rows.reshape(samples_here, half_side, half_side, width_here)
    picture = jnp.repeat(jnp.repeat(picture, 2, axis=1), 2, axis=2)
    padded = jnp.pad(picture, ((0, 0), (1, 1), (1, 1), (0, 0)))
    pieces = [
        padded[:, shift_row : shift_row + side_len, shift_col : shift_col + side_len, :]
        for shift_row in range(3)
        for shift_col in range(3)
    ]
    return jnp.concatenate(pieces, axis=-1).reshape(
        samples_here, side_len * side_len, 9 * width_here
    )


def rms_norm(values):
    return values * lax.rsqrt(jnp.mean(values * values, axis=-1, keepdims=True) + 1e-06)


def conv_part(gathered, kernel, scales, bias_local, strength_local, noise_map):
    samples_here = gathered.shape[0]
    width_out = kernel.shape[2]
    columns = patches_of(gathered, SIDE)
    conv_out = einsum_low("bpr,bro->bpo", columns, kernel)
    squares = jnp.sum((kernel * kernel).reshape(samples_here, 9, -1, width_out), axis=1)
    demodulate = lax.rsqrt(einsum_high("bi,bio->bo", scales * scales, squares) + 1e-08)
    before = conv_out * demodulate[:, None, :] + bias_local + noise_map[:, :, None] * strength_local
    return jax.nn.silu(before)


def self_attention(active, qk_w, value_w, out_w):
    normed = rounded(rms_norm(active))
    queries = rounded(matmul_high(normed, qk_w))
    values = rounded(matmul_high(normed, value_w))
    samples_here, pixels, width_here = queries.shape
    heads_here = width_here // HEAD
    q_heads = queries.reshape(samples_here, pixels, heads_here, HEAD)
    v_heads = values.reshape(samples_here, pixels, heads_here, HEAD)
    lengths = jnp.transpose(jnp.sum(q_heads * q_heads, axis=-1), (0, 2, 1))
    scores = (
        2.0 * einsum_low("bphd,bqhd->bhpq", q_heads, q_heads) - lengths[:, :, None, :]
    ) * HEAD ** (-0.5)
    soft_weights = rounded(jax.nn.softmax(scores, axis=-1))
    mixture = rounded(
        einsum_low("bhpq,bqhd->bphd", soft_weights, v_heads).reshape(
            samples_here, pixels, width_here
        )
    )
    return matmul_high(mixture, out_w)


def cross_attention(active, text_rows, query_w, key_w, value_w, out_w):
    normed = rounded(rms_norm(active))
    queries = rounded(matmul_high(normed, query_w))
    key_rows = rounded(matmul_high(text_rows, key_w))
    values = rounded(matmul_high(text_rows, value_w))
    samples_here, pixels, width_here = queries.shape
    tokens = key_rows.shape[1]
    heads_here = width_here // HEAD
    q_heads = queries.reshape(samples_here, pixels, heads_here, HEAD)
    k_heads = key_rows.reshape(samples_here, tokens, heads_here, HEAD)
    v_heads = values.reshape(samples_here, tokens, heads_here, HEAD)
    scores = einsum_low("bphd,bthd->bhpt", q_heads, k_heads) * HEAD ** (-0.5)
    soft_weights = rounded(jax.nn.softmax(scores, axis=-1))
    mixture = rounded(
        einsum_low("bhpt,bthd->bphd", soft_weights, v_heads).reshape(
            samples_here, pixels, width_here
        )
    )
    return matmul_high(mixture, out_w)


def feed_forward(active, weight_in, weight_out):
    normed = rounded(rms_norm(active))
    inner = rounded(jax.nn.gelu(matmul_high(normed, weight_in)))
    return matmul_high(inner, weight_out)


def tree_add(first, second):
    return jax.tree.map(jnp.add, first, second)


def tensor_parallel(
    layer_input,
    labels,
    text_ids,
    noise_seeds,
    penalty_mask,
    class_table,
    token_table,
    sel_weight,
    mod_weight,
    rgb_mod,
    rgb_weight,
    conv_bias,
    noise_strength,
    kernel_bank,
    qk_weight,
    value_weight,
    attn_out,
    cross_query,
    cross_key,
    cross_value,
    cross_out,
    mlp_in,
    mlp_out,
    cot_feat,
    cot_rgb,
    penalty_dir,
):
    width_local = layer_input.shape[2]
    offset = lax.axis_index("mp") * width_local
    small_params = tuple(
        (
            entry.astype(jnp.float32)
            for entry in (
                class_table,
                token_table,
                sel_weight,
                mod_weight,
                rgb_mod,
                rgb_weight,
                conv_bias,
                noise_strength,
            )
        )
    )

    def fetch_proj():
        fetched = (
            lax.all_gather(qk_weight, "dp", axis=0, tiled=True),
            lax.all_gather(value_weight, "dp", axis=0, tiled=True),
            lax.all_gather(attn_out, "dp", axis=1, tiled=True),
            lax.all_gather(cross_query, "dp", axis=0, tiled=True),
            lax.all_gather(cross_key, "dp", axis=0, tiled=True),
            lax.all_gather(cross_value, "dp", axis=0, tiled=True),
            lax.all_gather(cross_out, "dp", axis=1, tiled=True),
            lax.all_gather(mlp_in, "dp", axis=0, tiled=True),
            lax.all_gather(mlp_out, "dp", axis=1, tiled=True),
        )
        return tuple((entry.astype(jnp.float32) for entry in fetched))

    def style_part(param_set):
        table_class, table_word, select_w, modul_w, rgbmod_w, rgbout_w, bias_w, strength_w = (
            param_set
        )
        onehot_class = (
            labels[:, None] == jnp.arange(table_class.shape[0], dtype=jnp.int32)[None, :]
        ).astype(jnp.float32)
        latent = matmul_high(onehot_class, table_class)
        onehot_word = (
            text_ids[:, :, None] == jnp.arange(table_word.shape[0], dtype=jnp.int32)
        ).astype(jnp.float32)
        text_rows = matmul_high(onehot_word, table_word)
        select = jax.nn.softmax(matmul_high(latent, select_w), axis=-1)
        scales = 1.0 + matmul_high(latent, modul_w)
        rgb_scales = 1.0 + matmul_high(
            latent, lax.dynamic_slice_in_dim(rgbmod_w, offset, width_local, 1)
        )
        bias_local = lax.dynamic_slice_in_dim(bias_w, offset, width_local, 0)
        strength_local = lax.dynamic_slice_in_dim(strength_w, offset, width_local, 0)
        colour_local = lax.dynamic_slice_in_dim(rgbout_w, offset, width_local, 1)
        return (select, scales, rgb_scales, text_rows, bias_local, strength_local, colour_local)

    styles, style_pull = jax.vjp(style_part, small_params)
    noise_map = noise_field(noise_seeds, SIDE * SIDE)

    def owned_sets():
        proj_set = fetch_proj()
        conv_set = (lax.all_gather(kernel_bank, "dp", axis=2, tiled=True).astype(jnp.float32),)
        return ((), conv_set, proj_set[0:3], proj_set[3:7], proj_set[7:9], ())

    def seg_in(active, styles_in, own_set):
        return active * lax.dynamic_slice_in_dim(styles_in[1], offset, width_local, 1)[:, None, :]

    def seg_conv(active, styles_in, own_set):
        bank_full = own_set[0]
        kernel = rounded(matmul_high(styles_in[0], bank_full.reshape(bank_full.shape[0], -1)))
        kernel = kernel.reshape(active.shape[0], -1, bank_full.shape[3])
        return conv_part(active, kernel, styles_in[1], styles_in[4], styles_in[5], noise_map)

    def seg_self(active, styles_in, own_set):
        return self_attention(active, own_set[0], own_set[1], own_set[2])

    def seg_cross(active, styles_in, own_set):
        return cross_attention(active, styles_in[3], own_set[0], own_set[1], own_set[2], own_set[3])

    def seg_mlp(active, styles_in, own_set):
        return feed_forward(active, own_set[0], own_set[1])

    def seg_rgb(active, styles_in, own_set):
        return einsum_high("bpc,bc,kc->bkp", active, styles_in[2], styles_in[6])

    def spread(stacked):
        return lax.all_gather(stacked, "mp", axis=3, tiled=True)

    def collect(stacked):
        return lax.psum_scatter(
            stacked.astype(jnp.bfloat16), "mp", scatter_dimension=3, tiled=True
        ).astype(jnp.float32)

    def spread_one(values):
        return spread(values.astype(jnp.bfloat16)[None])[0].astype(jnp.float32)

    def collect_one(values):
        return collect(values[None])[0]

    own_first = owned_sets()
    input_full = layer_input.astype(jnp.float32)
    gathered_x = spread_one(seg_in(input_full, styles, own_first[0]))
    hidden_one = seg_conv(gathered_x, styles, own_first[1])
    gathered_one = spread_one(hidden_one)
    hidden_two = hidden_one + collect_one(seg_self(gathered_one, styles, own_first[2]))
    gathered_two = spread_one(hidden_two)
    hidden_three = hidden_two + collect_one(seg_cross(gathered_two, styles, own_first[3]))
    gathered_three = spread_one(hidden_three)
    hidden_four = hidden_three + collect_one(seg_mlp(gathered_three, styles, own_first[4]))
    picture = lax.psum(seg_rgb(hidden_four, styles, own_first[5]), "mp")
    own_second = owned_sets()

    def pull_act(segment, active, own_set, cotan):
        return jax.vjp(lambda inner_x: segment(inner_x, styles, own_set), active)[1](cotan)[0]

    grad_four = pull_act(seg_rgb, hidden_four, own_second[5], penalty_dir.astype(jnp.float32))
    back_three = pull_act(seg_mlp, gathered_three, own_second[4], spread_one(grad_four))
    grad_three = grad_four + rounded(collect_one(back_three))
    back_two = pull_act(seg_cross, gathered_two, own_second[3], spread_one(grad_three))
    grad_two = grad_three + rounded(collect_one(back_two))
    back_one = pull_act(seg_self, gathered_one, own_second[2], spread_one(grad_two))
    grad_one = grad_two + rounded(collect_one(back_one))
    grad_moduled = rounded(collect_one(pull_act(seg_conv, gathered_x, own_second[1], grad_one)))
    penalty_grad = pull_act(seg_in, input_full, own_second[0], grad_moduled)
    tangent = penalty_weight * penalty_mask.astype(jnp.float32)[:, None, None] * penalty_grad
    own_third = owned_sets()

    def push(segment, active, own_set, tangent_in):
        return jax.jvp(lambda inner_x: segment(inner_x, styles, own_set), (active,), (tangent_in,))[
            1
        ]

    tan_x = spread_one(push(seg_in, input_full, own_third[0], tangent))
    tan_one = push(seg_conv, gathered_x, own_third[1], tan_x)
    tan_g1 = spread_one(tan_one)
    tan_two = tan_one + collect_one(push(seg_self, gathered_one, own_third[2], tan_g1))
    tan_g2 = spread_one(tan_two)
    tan_three = tan_two + collect_one(push(seg_cross, gathered_two, own_third[3], tan_g2))
    tan_g3 = spread_one(tan_three)
    tan_four = tan_three + collect_one(push(seg_mlp, gathered_three, own_third[4], tan_g3))
    own_fourth = owned_sets()

    def pull_both(segment, active, tangent_in, own_set, cotan, cotan_tangent):

        def joint(inner_x, inner_tangent, styles_in, own_in):
            return jax.jvp(
                lambda value_x: segment(value_x, styles_in, own_in), (inner_x,), (inner_tangent,)
            )

        return jax.vjp(joint, active, tangent_in, styles, own_set)[1]((cotan, cotan_tangent))

    grad_act, grad_tan, style_acc, ignored = pull_both(
        seg_rgb,
        hidden_four,
        tan_four,
        own_fourth[5],
        cot_rgb.astype(jnp.float32),
        penalty_dir.astype(jnp.float32),
    )
    main_now = cot_feat.astype(jnp.float32) + grad_act
    side_now = grad_tan
    layer_grads = []
    for segment, active, tangent_in, own_set in (
        (seg_mlp, gathered_three, tan_g3, own_fourth[4]),
        (seg_cross, gathered_two, tan_g2, own_fourth[3]),
        (seg_self, gathered_one, tan_g1, own_fourth[2]),
    ):
        both_wide = spread(jnp.stack([main_now, side_now]).astype(jnp.bfloat16)).astype(jnp.float32)
        grad_act, grad_tan, grad_sty, grad_own = pull_both(
            segment, active, tangent_in, own_set, both_wide[0], both_wide[1]
        )
        style_acc = tree_add(style_acc, grad_sty)
        layer_grads.append(grad_own)
        both_sums = collect(jnp.stack([grad_act, grad_tan]))
        main_now = main_now + rounded(both_sums[0])
        side_now = side_now + rounded(both_sums[1])
    grad_act, grad_tan, grad_sty, grads_conv = pull_both(
        seg_conv, gathered_x, tan_x, own_fourth[1], main_now, side_now
    )
    style_acc = tree_add(style_acc, grad_sty)
    both_sums = collect(jnp.stack([grad_act, grad_tan]))
    grad_act, grad_tan, grad_sty, ignored = pull_both(
        seg_in, input_full, tangent, own_fourth[0], rounded(both_sums[0]), rounded(both_sums[1])
    )
    style_acc = tree_add(style_acc, grad_sty)
    proj_terms = layer_grads[2] + layer_grads[1] + layer_grads[0]
    big_terms = grads_conv + proj_terms
    big_sums = (
        lax.psum_scatter(
            big_terms[0].astype(jnp.bfloat16), "dp", scatter_dimension=2, tiled=True
        ).astype(jnp.float32),
        lax.psum_scatter(
            big_terms[1].astype(jnp.bfloat16), "dp", scatter_dimension=0, tiled=True
        ).astype(jnp.float32),
        lax.psum_scatter(
            big_terms[2].astype(jnp.bfloat16), "dp", scatter_dimension=0, tiled=True
        ).astype(jnp.float32),
        lax.psum_scatter(
            big_terms[3].astype(jnp.bfloat16), "dp", scatter_dimension=1, tiled=True
        ).astype(jnp.float32),
        lax.psum_scatter(
            big_terms[4].astype(jnp.bfloat16), "dp", scatter_dimension=0, tiled=True
        ).astype(jnp.float32),
        lax.psum_scatter(
            big_terms[5].astype(jnp.bfloat16), "dp", scatter_dimension=0, tiled=True
        ).astype(jnp.float32),
        lax.psum_scatter(
            big_terms[6].astype(jnp.bfloat16), "dp", scatter_dimension=0, tiled=True
        ).astype(jnp.float32),
        lax.psum_scatter(
            big_terms[7].astype(jnp.bfloat16), "dp", scatter_dimension=1, tiled=True
        ).astype(jnp.float32),
        lax.psum_scatter(
            big_terms[8].astype(jnp.bfloat16), "dp", scatter_dimension=0, tiled=True
        ).astype(jnp.float32),
        lax.psum_scatter(
            big_terms[9].astype(jnp.bfloat16), "dp", scatter_dimension=1, tiled=True
        ).astype(jnp.float32),
    )
    small_terms = style_pull(style_acc)[0]
    small_sums = lax.psum(
        (
            small_terms[0],
            small_terms[1],
            small_terms[2],
            small_terms[3],
            small_terms[4],
            small_terms[5],
            small_terms[6],
            small_terms[7],
        ),
        ("dp", "mp"),
    )
    return (hidden_four, picture, grad_act) + tuple(small_sums) + tuple(big_sums)


def fits_samples(mesh):
    return mesh.shape["dp"] == 16 and mesh.shape["mp"] == 2


def dot_wide(left, right, left_dim, right_dim):
    return lax.dot_general(
        left.astype(jnp.bfloat16),
        right.astype(jnp.bfloat16),
        (((left_dim,), (right_dim,)), ((), ())),
        preferred_element_type=jnp.float32,
    )


def make_products(flip):
    depth = 1 if flip else 0

    def weight_grad(rows, cotan):
        if flip:
            return dot_wide(cotan, rows, 0, 0).astype(jnp.bfloat16)
        return dot_wide(rows, cotan, 0, 0).astype(jnp.bfloat16)

    @jax.custom_vjp
    def single(rows, weight):
        return dot_wide(rows, weight, 1, depth)

    def single_fwd(rows, weight):
        return single(rows, weight), (rows, weight)

    def single_bwd(kept, cotan):
        rows, weight = kept
        return dot_wide(cotan, weight, 1, 1 - depth), weight_grad(rows, cotan)

    single.defvjp(single_fwd, single_bwd)

    @jax.custom_vjp
    def pair(rows, tangents, weight):
        return dot_wide(rows, weight, 1, depth), dot_wide(tangents, weight, 1, depth)

    def pair_fwd(rows, tangents, weight):
        return pair(rows, tangents, weight), (rows, tangents, weight)

    def pair_bwd(kept, cotans):
        rows, tangents, weight = kept
        count = rows.shape[0]
        both = jnp.concatenate([entry.astype(jnp.bfloat16) for entry in cotans], axis=0)
        inputs = jnp.concatenate(
            [rows.astype(jnp.bfloat16), tangents.astype(jnp.bfloat16)], axis=0
        )
        back = dot_wide(both, weight, 1, 1 - depth)
        return back[:count], back[count:], weight_grad(inputs, both)

    pair.defvjp(pair_fwd, pair_bwd)
    return single, pair


product, product_pair = make_products(False)
product_flip, product_flip_pair = make_products(True)


def with_tangent(fun, value, tangent):
    return jax.jvp(fun, (value,), (tangent,))


def last_softmax(scores):
    return jax.nn.softmax(scores, axis=-1)


def post_conv(conv_out, sums, bias, strength, noise):
    demodulate = lax.rsqrt(sums + 1e-08)
    return jax.nn.silu(conv_out * demodulate[None] + bias[None] + noise[:, None] * strength[None])


def picture_of(hidden, rgb_scales, rgb_weight):
    return einsum_high("pc,kc->kp", hidden, rgb_scales[None] * rgb_weight)


CHUNK = 16
PAD_ROWS = (SIDE + 2) * SIDE
PIXELS = SIDE * SIDE


def placing(half_side):
    side = 2 * half_side
    table = np.zeros((side + 2, side, 3, half_side * half_side), np.float32)
    for row in range(1, side + 1):
        for col in range(side):
            for shift in range(3):
                at = col + shift - 1
                if 0 <= at < side:
                    table[row, col, shift, (row - 1) // 2 * half_side + at // 2] = 1.0
    return jnp.asarray(table.reshape((side + 2) * side, -1), jnp.bfloat16)


def dot_f32(left, right, left_dim, right_dim):
    return lax.dot_general(
        left, right, (((left_dim,), (right_dim,)), ((), ())), preferred_element_type=jnp.float32
    )


def mix_matrix(select):
    high = select.astype(jnp.bfloat16)
    low = (select - high.astype(jnp.float32)).astype(jnp.bfloat16)
    eye = jnp.eye(CHUNK, dtype=jnp.bfloat16)
    parts = jnp.stack([high, low], axis=1)
    wide = parts[:, None, :, :, None] * eye[None, :, None, None, :]
    return wide.reshape(select.shape[0] * CHUNK, -1)


def lanes_wide(column, width):
    return jnp.concatenate([column] * (width // column.shape[-1]), axis=-1)


def mix_body(pieces, mix_ref, bank_ref, squares_ref, kernel_ref, sums_ref):
    step = pl.program_id(0)

    @pl.when(step == 0)
    def _():
        sums_ref[...] = jnp.zeros_like(sums_ref)

    kernels, rows, width = bank_ref.shape
    samples = kernel_ref.shape[0]
    per_tap = squares_ref.shape[1]
    for piece in range(pieces):
        part = bank_ref[:, piece * CHUNK : (piece + 1) * CHUNK, :].reshape(kernels * CHUNK, width)
        mixed = dot_f32(mix_ref[...], jnp.concatenate([part, part], axis=0), 1, 0)
        mixed = mixed.astype(jnp.bfloat16).reshape(samples, CHUNK, width)
        kernel_ref[:, piece * CHUNK : (piece + 1) * CHUNK, :] = mixed
        first = lax.rem(step * rows + piece * CHUNK, per_tap)
        factor = squares_ref[:, pl.ds(pl.multiple_of(first, CHUNK), CHUNK), :]
        wide = mixed.astype(jnp.float32)
        sums_ref[...] += jnp.sum(wide * wide * lanes_wide(factor, width), axis=1)


def mix_kernels(mix, bank_rows, squares):
    kernels, depth, width = bank_rows.shape
    samples = squares.shape[0]
    pieces = 4
    rows = pieces * CHUNK
    return pl.pallas_call(
        lambda *refs: mix_body(pieces, *refs),
        grid=(depth // rows,),
        in_specs=[
            pl.BlockSpec(mix.shape, lambda step: (0, 0)),
            pl.BlockSpec((kernels, rows, width), lambda step: (0, step, 0)),
            pl.BlockSpec(squares.shape, lambda step: (0, 0, 0)),
        ],
        out_specs=[
            pl.BlockSpec((samples, rows, width), lambda step: (0, step, 0)),
            pl.BlockSpec((samples, width), lambda step: (0, 0)),
        ],
        out_shape=[
            jax.ShapeDtypeStruct((samples, depth, width), jnp.bfloat16),
            jax.ShapeDtypeStruct((samples, width), jnp.float32),
        ],
        compiler_params=pltpu.CompilerParams(vmem_limit_bytes=48 * 2**20),
        name="mix_kernels",
    )(mix, bank_rows, squares)


def place_rows(slab, place_ref, spot_ref):
    pixels, width = slab.shape
    for shift in range(3):
        spot_ref[
            shift * pixels : (shift + 1) * pixels, shift * width : (shift + 1) * width
        ] = slab
    return dot_f32(place_ref[...], spot_ref[...], 1, 0).astype(jnp.bfloat16)


def conv_step(extra, sample, slab_ref, place_ref, kernel_ref, sums_ref, out_ref, spot_ref):
    rows = place_rows(slab_ref[0], place_ref, spot_ref)
    depth = rows.shape[1]
    total = None
    for shift in range(3):
        term = dot_f32(
            rows[shift * SIDE : shift * SIDE + PIXELS],
            kernel_ref[0, shift * depth : (shift + 1) * depth, :],
            1,
            0,
        )
        total = term if total is None else total + term
    out_ref[0, :PIXELS, :] = total.astype(jnp.bfloat16)
    if extra:
        line = sums_ref[pl.ds(sample, 1), :]
        out_ref[0, PIXELS:, :] = jnp.broadcast_to(line, (CHUNK, line.shape[1])).astype(jnp.bfloat16)


def fold_back(cotan, place_ref, kernel_ref, wide_ref, pixels, width):
    depth = 3 * width
    wide_ref[...] = jnp.zeros_like(wide_ref)
    for shift in range(3):
        wide_ref[shift * SIDE : shift * SIDE + PIXELS, :] += dot_f32(
            cotan, kernel_ref[0, shift * depth : (shift + 1) * depth, :], 1, 1
        )
    back = dot_f32(place_ref[...], wide_ref[...].astype(jnp.bfloat16), 0, 0)
    total = None
    for shift in range(3):
        term = back[shift * pixels : (shift + 1) * pixels, shift * width : (shift + 1) * width]
        total = term if total is None else total + term
    return total.astype(jnp.bfloat16)


def second_step(
    slab_ref,
    tan_ref,
    place_ref,
    kernel_ref,
    cotan_ref,
    side_ref,
    squares_ref,
    grad_ref,
    back_ref,
    scale_ref,
    spot_ref,
    wide_ref,
):
    pixels, width = slab_ref.shape[1:]
    depth = 3 * width
    rows = place_rows(slab_ref[0], place_ref, spot_ref)
    tan_rows = place_rows(tan_ref[0], place_ref, spot_ref)
    line = cotan_ref[0, PIXELS : PIXELS + CHUNK, :][:1].astype(jnp.float32)
    factor = 2.0 * lanes_wide(squares_ref[0], line.shape[1]) * line
    totals = None
    for shift in range(3):
        span = slice(shift * SIDE, shift * SIDE + PIXELS)
        grad = dot_f32(rows[span], cotan_ref[0, :PIXELS, :], 0, 0)
        grad = grad + dot_f32(tan_rows[span], side_ref[0], 0, 0)
        for tap in range(3):
            at = shift * depth + tap * width
            own = kernel_ref[0, at : at + width, :].astype(jnp.float32)
            grad_ref[0, at : at + width, :] = (
                grad[tap * width : (tap + 1) * width] + own * factor
            ).astype(jnp.bfloat16)
            term = own * own
            totals = term if totals is None else totals + term
    summed = jnp.sum(totals * line, axis=1, keepdims=True)
    scale_ref[0] = jnp.broadcast_to(summed, scale_ref.shape[1:])
    back_ref[0] = fold_back(
        cotan_ref[0, :PIXELS, :], place_ref, kernel_ref, wide_ref, pixels, width
    )


def unmix_body(pieces, mix_ref, bank_ref, grad_ref, out_ref, select_ref):
    @pl.when(pl.program_id(0) == 0)
    def _():
        select_ref[...] = jnp.zeros_like(select_ref)

    kernels, _, width = bank_ref.shape
    samples = grad_ref.shape[0]
    for piece in range(pieces):
        span = slice(piece * CHUNK, (piece + 1) * CHUNK)
        grad = grad_ref[:, span, :].reshape(samples * CHUNK, width)
        mixed = dot_f32(mix_ref[...], grad, 0, 0)
        count = kernels * CHUNK
        out_ref[:, span, :] = (mixed[:count] + mixed[count:]).reshape(kernels, CHUNK, width)
        part = bank_ref[:, span, :].reshape(count, width)
        select_ref[...] += dot_f32(grad, part, 1, 1)


def unmix_kernels(mix, bank_rows, grad):
    kernels, depth, width = bank_rows.shape
    samples = grad.shape[0]
    pieces = 4
    rows = pieces * CHUNK
    return pl.pallas_call(
        lambda *refs: unmix_body(pieces, *refs),
        grid=(depth // rows,),
        in_specs=[
            pl.BlockSpec(mix.shape, lambda step: (0, 0)),
            pl.BlockSpec((kernels, rows, width), lambda step: (0, step, 0)),
            pl.BlockSpec((samples, rows, width), lambda step: (0, step, 0)),
        ],
        out_specs=[
            pl.BlockSpec((kernels, rows, width), lambda step: (0, step, 0)),
            pl.BlockSpec((samples * CHUNK, kernels * CHUNK), lambda step: (0, 0)),
        ],
        out_shape=[
            jax.ShapeDtypeStruct((kernels, depth, width), jnp.float32),
            jax.ShapeDtypeStruct((samples * CHUNK, kernels * CHUNK), jnp.float32),
        ],
        compiler_params=pltpu.CompilerParams(vmem_limit_bytes=48 * 2**20),
        name="unmix_kernels",
    )(mix, bank_rows, grad)


@jax.custom_vjp
def row_products(left, right):
    return dot_f32(left.astype(jnp.bfloat16), right.astype(jnp.bfloat16), 1, 1)


def row_products_fwd(left, right):
    return row_products(left, right), (left, right)


def row_products_bwd(kept, cotan):
    left, right = (entry.astype(jnp.bfloat16) for entry in kept)
    short = cotan.astype(jnp.bfloat16)
    return dot_f32(short, right, 1, 0), dot_f32(short, left, 0, 0)


row_products.defvjp(row_products_fwd, row_products_bwd)


@jax.custom_vjp
def mixed_rows(soft, values):
    return dot_f32(soft.astype(jnp.bfloat16), values.astype(jnp.bfloat16), 1, 0)


def mixed_rows_fwd(soft, values):
    return mixed_rows(soft, values), (soft, values)


def mixed_rows_bwd(kept, cotan):
    soft, values = (entry.astype(jnp.bfloat16) for entry in kept)
    short = cotan.astype(jnp.bfloat16)
    return dot_f32(short, values, 1, 1), dot_f32(soft, short, 0, 0)


mixed_rows.defvjp(mixed_rows_fwd, mixed_rows_bwd)


@jax.custom_vjp
def as_row(column):
    count = column.shape[0]
    lane = lax.broadcasted_iota(jnp.int32, (count, 128), 1)
    rest, parts = column, jnp.zeros((count, 128), jnp.float32)
    for place in range(3):
        short = rest.astype(jnp.bfloat16).astype(jnp.float32)
        parts = jnp.where(lane == place, short, parts)
        rest = rest - short
    ones = jnp.ones((count, 128), jnp.bfloat16)
    return dot_f32(ones, parts.astype(jnp.bfloat16), 1, 1)


def as_row_fwd(column):
    return as_row(column), None


def as_row_bwd(kept, cotan):
    ones = jnp.ones((cotan.shape[0], 128), jnp.bfloat16)
    return (dot_f32(cotan.astype(jnp.bfloat16), ones, 0, 0)[:, :1],)


as_row.defvjp(as_row_fwd, as_row_bwd)


def soft_of(scores):
    top = lax.stop_gradient(jnp.max(scores, axis=1, keepdims=True))
    powers = jnp.exp(scores - top)
    return powers / jnp.sum(powers, axis=1, keepdims=True)


def soft_tangent(soft, tangent):
    return soft * (tangent - jnp.sum(soft * tangent, axis=1, keepdims=True))


def squared(left, right):
    return jnp.sum(left * right, axis=1, keepdims=True)


def self_head(queries, values):
    scores = 2.0 * row_products(queries, queries) - as_row(squared(queries, queries))
    return (mixed_rows(soft_of(scores * HEAD ** (-0.5)), values),)


def self_head_joint(queries, tan_queries, values, tan_values):
    scores = 2.0 * row_products(queries, queries) - as_row(squared(queries, queries))
    tan_scores = row_products(tan_queries, queries) + row_products(queries, tan_queries)
    tan_scores = 2.0 * (tan_scores - as_row(squared(queries, tan_queries)))
    soft = soft_of(scores * HEAD ** (-0.5))
    tan_soft = soft_tangent(soft, tan_scores * HEAD ** (-0.5))
    return (
        mixed_rows(soft, values),
        mixed_rows(tan_soft, values) + mixed_rows(soft, tan_values),
    )


def cross_head(queries, keys, values):
    return (mixed_rows(soft_of(row_products(queries, keys) * HEAD ** (-0.5)), values),)


def cross_head_joint(queries, tan_queries, keys, values):
    soft = soft_of(row_products(queries, keys) * HEAD ** (-0.5))
    tan_soft = soft_tangent(soft, row_products(tan_queries, keys) * HEAD ** (-0.5))
    return mixed_rows(soft, values), mixed_rows(tan_soft, values)


def per_head(fun, arrays, shapes, name):
    lanes = 2 * HEAD

    def body(*refs):
        inputs, outputs = refs[: len(arrays)], refs[len(arrays) :]
        for head in range(2):
            span = slice(head * HEAD, (head + 1) * HEAD)
            results = fun(*[ref[:, span].astype(jnp.float32) for ref in inputs])
            for ref, result in zip(outputs, results):
                ref[:, span] = result.astype(jnp.bfloat16)

    return pl.pallas_call(
        body,
        grid=(arrays[0].shape[1] // lanes,),
        in_specs=[pl.BlockSpec((entry.shape[0], lanes), lambda step: (0, step)) for entry in arrays],
        out_specs=[pl.BlockSpec((shape[0], lanes), lambda step: (0, step)) for shape in shapes],
        out_shape=[jax.ShapeDtypeStruct(shape, jnp.bfloat16) for shape in shapes],
        compiler_params=pltpu.CompilerParams(vmem_limit_bytes=32 * 2**20),
        name=name,
    )(*arrays)


def make_attention(fun, count, name):
    @jax.custom_vjp
    def attend(*arrays):
        return tuple(per_head(fun, arrays, [arrays[0].shape] * count, name))

    def attend_fwd(*arrays):
        return attend(*arrays), arrays

    def attend_bwd(arrays, cotans):
        def pull(*given):
            return jax.vjp(fun, *given[: len(arrays)])[1](tuple(given[len(arrays) :]))

        shapes = [entry.shape for entry in arrays]
        return tuple(per_head(pull, list(arrays) + list(cotans), shapes, name + "_pull"))

    attend.defvjp(attend_fwd, attend_bwd)
    return attend


self_attend = make_attention(self_head, 1, "self_heads")
self_attend_joint = make_attention(self_head_joint, 2, "self_heads_joint")
cross_attend = make_attention(cross_head, 1, "cross_heads")
cross_attend_joint = make_attention(cross_head_joint, 2, "cross_heads_joint")


def short_of(*arrays):
    return [entry.astype(jnp.bfloat16) for entry in arrays]


def gelu_parts(value):
    scale, cubic = (2.0 / np.pi) ** 0.5, 0.044715
    bend = jnp.tanh(scale * (value + cubic * value * value * value))
    slope = scale * (1.0 + 3.0 * cubic * value * value)
    steep = 1.0 - bend * bend
    once = steep * slope
    twice = steep * (6.0 * cubic * scale) * value - 2.0 * bend * once * slope
    return (
        0.5 * value * (1.0 + bend),
        0.5 * (1.0 + bend) + 0.5 * value * once,
        once + 0.5 * value * twice,
    )


@jax.custom_vjp
def gelu_kept(value):
    return gelu_parts(value)


def gelu_kept_fwd(value):
    result, first, second = lax.optimization_barrier(gelu_parts(value))
    return (result, first, second), first


def gelu_kept_bwd(first, cotans):
    return (cotans[0] * first,)


gelu_kept.defvjp(gelu_kept_fwd, gelu_kept_bwd)


@jax.custom_vjp
def gelu_joint(value, tangent, parts):
    return parts[0], tangent * parts[1]


def gelu_joint_fwd(value, tangent, parts):
    return gelu_joint(value, tangent, parts), (tangent, parts)


def gelu_joint_bwd(kept, cotans):
    tangent, parts = kept
    main, side = cotans
    back = main * parts[1] + side * tangent * parts[2]
    return back, side * parts[1], tuple(jnp.zeros_like(part) for part in parts)


gelu_joint.defvjp(gelu_joint_fwd, gelu_joint_bwd)


def layer_forward(conv_out, sums, text_rows, small, weights, noise):
    bias, strength, rgb_scales, rgb_weight = small
    qk_w, value_w, attn_w, query_w, key_w, cval_w, cout_w, mlp_w, mout_w = weights
    hidden_one = post_conv(conv_out, sums, bias, strength, noise)
    normed = rms_norm(hidden_one)
    (mixture,) = self_attend(*short_of(product(normed, qk_w), product(normed, value_w)))
    hidden_two = hidden_one + product_flip(mixture.astype(jnp.float32), attn_w)
    normed = rms_norm(hidden_two)
    (mixture,) = cross_attend(
        *short_of(
            product(normed, query_w), product(text_rows, key_w), product(text_rows, cval_w)
        )
    )
    hidden_three = hidden_two + product_flip(mixture.astype(jnp.float32), cout_w)
    normed = rms_norm(hidden_three)
    parts = gelu_kept(product(normed, mlp_w))
    hidden_four = hidden_three + product_flip(parts[0], mout_w)
    return (hidden_four, picture_of(hidden_four, rgb_scales, rgb_weight)), parts


def layer_joint(conv_out, conv_tan, sums, text_rows, small, weights, noise, parts):
    bias, strength, rgb_scales, rgb_weight = small
    qk_w, value_w, attn_w, query_w, key_w, cval_w, cout_w, mlp_w, mout_w = weights
    hidden_one, tan_one = with_tangent(
        lambda value: post_conv(value, sums, bias, strength, noise), conv_out, conv_tan
    )
    normed, tan_normed = with_tangent(rms_norm, hidden_one, tan_one)
    queries, tan_queries = product_pair(normed, tan_normed, qk_w)
    values, tan_values = product_pair(normed, tan_normed, value_w)
    mixture, tan_mixture = self_attend_joint(*short_of(queries, tan_queries, values, tan_values))
    added, tan_added = product_flip_pair(
        mixture.astype(jnp.float32), tan_mixture.astype(jnp.float32), attn_w
    )
    hidden_two, tan_two = hidden_one + added, tan_one + tan_added
    normed, tan_normed = with_tangent(rms_norm, hidden_two, tan_two)
    queries, tan_queries = product_pair(normed, tan_normed, query_w)
    mixture, tan_mixture = cross_attend_joint(
        *short_of(queries, tan_queries, product(text_rows, key_w), product(text_rows, cval_w))
    )
    added, tan_added = product_flip_pair(
        mixture.astype(jnp.float32), tan_mixture.astype(jnp.float32), cout_w
    )
    hidden_three, tan_three = hidden_two + added, tan_two + tan_added
    normed, tan_normed = with_tangent(rms_norm, hidden_three, tan_three)
    before, tan_before = product_pair(normed, tan_normed, mlp_w)
    inner, tan_inner = gelu_joint(before, tan_before, parts)
    added, tan_added = product_flip_pair(inner, tan_inner, mout_w)
    hidden_four, tan_four = hidden_three + added, tan_three + tan_added
    return (
        hidden_four,
        picture_of(hidden_four, rgb_scales, rgb_weight),
        picture_of(tan_four, rgb_scales, rgb_weight),
    )


SWAP = ((0, 1), (1, 0))


def swap_mp(values):
    return lax.ppermute(values, "mp", SWAP)


def pick(values, index):
    return lax.dynamic_index_in_dim(values, index, 0, keepdims=False)


def own_whole(values, mp):
    mine, other = pick(values, mp), swap_mp(pick(values, 1 - mp))
    first = jnp.where(mp == 0, mine, other)
    second = jnp.where(mp == 0, other, mine)
    return jnp.concatenate([first, second], axis=-1)


def both_half(whole, mp):
    half = whole.shape[-1] // 2
    mine = lax.dynamic_slice_in_dim(whole, mp * half, half, whole.ndim - 1)
    other = swap_mp(lax.dynamic_slice_in_dim(whole, (1 - mp) * half, half, whole.ndim - 1))
    first = jnp.where(mp == 0, mine, other)
    second = jnp.where(mp == 0, other, mine)
    return jnp.stack([first, second])


def to_slabs(both):
    devices = lax.axis_size("dp")
    parts = both.reshape(2, both.shape[1], devices, -1).transpose(2, 0, 1, 3)
    parts = lax.all_to_all(parts, "dp", 0, 0, tiled=True)
    return parts.reshape(2 * devices, both.shape[1], -1)


def from_slabs(slabs, mp):
    devices = lax.axis_size("dp")
    rows = slabs.shape[1]
    parts = slabs.astype(jnp.bfloat16).reshape((devices, 2) + slabs.shape[1:])
    parts = lax.all_to_all(parts, "dp", 0, 0, tiled=True)
    parts = parts.transpose(1, 2, 0, 3).reshape(2, rows, -1)
    other = swap_mp(pick(parts, 1 - mp))
    return pick(parts, mp).astype(jnp.float32) + other.astype(jnp.float32)


PLANES = 4


class Place:
    def __init__(self):
        dp = lax.axis_index("dp")
        self.z, self.y, self.core = dp // 4, lax.rem(dp // 2, 2), lax.rem(dp, 2)
        self.x = lax.axis_index("mp")


def greet(place, axes):
    barrier = pltpu.get_barrier_semaphore()

    def tell(**there):
        at = dict(z=place.z, y=place.y, core=place.core, x=place.x)
        at.update(there)
        pl.semaphore_signal(
            barrier,
            inc=1,
            device_id=((at["z"] * 2 + at["y"]) * 2 + at["core"], at["x"]),
            device_id_type=pl.DeviceIdType.MESH,
        )

    tell(core=1 - place.core)
    count = 1
    for name in ("y", "x"):
        if name in axes:
            tell(**{name: 1 - getattr(place, name)})
            count += 1

    @pl.when(place.z > 0)
    def _():
        tell(z=place.z - 1)

    @pl.when(place.z < PLANES - 1)
    def _():
        tell(z=place.z + 1)

    between = (place.z > 0) & (place.z < PLANES - 1)
    pl.semaphore_wait(barrier, count + jnp.where(between, 2, 1))


def gather_body(pieces, inputs, outputs, axes, send_sem, recv_sem, own_sem):
    place = Place()
    greet(place, axes)
    sends = []

    def spot(z, y, core, x):
        return (z * 2 + y) * 2 + core, x

    def chip(z, y, x):
        return (z * 2 + y) * 2 + x

    def send(number, piece, source, target, slot, parity, first, condition):
        sz, sy, sx = source
        dp, mp = spot(sz, sy, place.core, sx)
        there = piece["to"](outputs, dp, mp)
        copy = pltpu.make_async_remote_copy(
            src_ref=piece["of"](inputs) if first else there,
            dst_ref=there,
            send_sem=send_sem.at[number, chip(sz, sy, sx), slot],
            recv_sem=recv_sem.at[number, chip(sz, sy, sx), parity],
            device_id=spot(*target),
            device_id_type=pl.DeviceIdType.MESH,
        )

        if condition is None:
            copy.start()
        else:
            pl.when(condition)(copy.start)
        sends.append((condition, copy))

    def onward(number, piece, source, came, first, condition):
        def both(more):
            if condition is None:
                return more
            return condition if more is None else condition & more

        order = piece["order"]
        later = order if came is None else order[order.index(came[0]) :]
        for name in later:
            here = dict(z=place.z, y=place.y, core=place.core, x=place.x)
            if name == "z":
                for way, slot in ((1, 0), (-1, 1)):
                    if came is not None and came[0] == "z" and came[1] != way:
                        continue
                    fits = place.z < PLANES - 1 if way == 1 else place.z > 0
                    target = (place.z + way, place.y, place.core, place.x)
                    send(number, piece, source, target, slot, 0, first, both(fits))
            elif came is None or came[0] != name:
                here[name] = 1 - here[name]
                target = (here["z"], here["y"], here["core"], here["x"])
                slot = 2 if name == "y" else 3
                send(number, piece, source, target, slot, 0, first, both(None))
        target = (place.z, place.y, 1 - place.core, place.x)
        send(number, piece, source, target, 4, 1, first, both(None))

    def arrive(number, piece, source, parity, condition):
        sz, sy, sx = source
        core = place.core if parity == 0 else 1 - place.core
        there = piece["to"](outputs, *spot(sz, sy, core, sx))

        def wait():
            pltpu.make_async_remote_copy(
                src_ref=there,
                dst_ref=there,
                send_sem=send_sem.at[number, chip(sz, sy, sx), 0],
                recv_sem=recv_sem.at[number, chip(sz, sy, sx), parity],
                device_id=spot(place.z, place.y, 1 - place.core, place.x),
                device_id_type=pl.DeviceIdType.MESH,
            ).wait_recv()

        if condition is None:
            wait()
        else:
            pl.when(condition)(wait)

    own = []
    for number, piece in enumerate(pieces):
        onward(number, piece, (place.z, place.y, place.x), None, True, None)
        copy = pltpu.make_async_copy(
            piece["of"](inputs),
            piece["to"](outputs, *spot(place.z, place.y, place.core, place.x)),
            own_sem.at[number],
        )
        copy.start()
        own.append(copy)
    flips = [(fy, fx) for fy in (0, 1) for fx in ((0, 1) if "x" in axes else (0,))]
    blocks = [(dz, fy, fx) for dz in (0, 1, -1, 2, -2, 3, -3) for fy, fx in flips]
    blocks = sorted(blocks, key=lambda block: abs(block[0]) + block[1] + block[2])
    for dz, fy, fx in blocks:
        if (dz, fy, fx) == (0, 0, 0):
            continue
        condition = None
        if dz > 0:
            condition = place.z >= dz
        elif dz < 0:
            condition = place.z < PLANES + dz
        source = (
            place.z - dz,
            1 - place.y if fy else place.y,
            1 - place.x if fx else place.x,
        )
        for number, piece in enumerate(pieces):
            arrive(number, piece, source, 0, condition)
            moved = dict(z=dz, y=fy, x=fx)
            last = [name for name in piece["order"] if moved[name]][-1]
            came = (last, (1 if dz > 0 else -1) if last == "z" else 0)
            onward(number, piece, source, came, False, condition)
    for number, piece in enumerate(pieces):
        for sz in range(PLANES):
            for sy in range(2):
                for sx in (0, 1) if "x" in axes else (place.x,):
                    arrive(number, piece, (sz, sy, sx), 1, None)
    for condition, copy in sends:
        if condition is None:
            copy.wait_send()
        else:
            pl.when(condition)(copy.wait_send)
    for copy in own:
        copy.wait()


def gather_call(pieces, axes, arrays, shapes, call_id, name):
    count = len(arrays)

    def body(*refs):
        inputs, outputs = refs[:count], refs[count : count + len(shapes)]
        gather_body(pieces, inputs, outputs, axes, *refs[count + len(shapes) :])

    return pl.pallas_call(
        body,
        in_specs=[pl.BlockSpec(memory_space=pl.ANY)] * count,
        out_specs=[pl.BlockSpec(memory_space=pl.ANY)] * len(shapes),
        out_shape=[
            jax.ShapeDtypeStruct(shape, entry.dtype) for shape, entry in zip(shapes, arrays)
        ],
        scratch_shapes=[
            pltpu.SemaphoreType.DMA((len(pieces), 16, 5)),
            pltpu.SemaphoreType.DMA((len(pieces), 16, 2)),
            pltpu.SemaphoreType.DMA((len(pieces),)),
        ],
        compiler_params=pltpu.CompilerParams(collective_id=call_id, has_side_effects=True),
        name=name,
    )(*arrays)


def rows_at(index, rows):
    return pl.ds(pl.multiple_of(index * rows, rows), rows)


def lanes_at(index, lanes):
    return pl.ds(pl.multiple_of(index * lanes, lanes), lanes)


def gather_weights(shards, numbers, call_id):
    orders = dict(x=("z", "y", "x"), y=("z", "x", "y"), z=("x", "y", "z"))
    turns = ("x", "y", "x", "y", "x", "z", "z", "y", "z")

    def piece(number, turn):
        rows, lanes = arrays[number].shape
        stacked = number == len(shards)

        def to(refs, dp, mp):
            if stacked:
                return refs[number].at[rows_at(dp * 2 + mp, rows)]
            return refs[number].at[rows_at(dp, rows), lanes_at(mp, lanes)]

        return dict(order=orders[turn], of=lambda refs: refs[number], to=to)

    arrays = list(shards) + [numbers]
    pieces = [piece(len(shards), "x")]
    pieces += [piece(number, turn) for number, turn in enumerate(turns)]
    shapes = [(entry.shape[0] * 16, entry.shape[1] * 2) for entry in shards]
    shapes.append((numbers.shape[0] * 32, numbers.shape[1]))
    return gather_call(pieces, ("z", "y", "x"), arrays, shapes, call_id, "gather_weights")


def plane_of(z, turn):
    low = jnp.where(turn < 2, 1 - turn, turn)
    high = jnp.where(turn < 2, 2 + turn, 3 - turn)
    between = jnp.where(z == 1, low, high)
    return jnp.where(z == 0, turn, jnp.where(z == PLANES - 1, PLANES - 1 - turn, between))


class Stream:
    def __init__(self, source, slots, sem, where):
        self.source, self.slots, self.sem, self.where = source, slots, sem, where

    def copy(self, turn):
        slot = lax.rem(turn, 2)
        return pltpu.make_async_copy(
            self.source.at[self.where(turn)], self.slots.at[slot], self.sem.at[slot]
        )

    def take(self, turn, count):
        self.copy(turn).wait()

        @pl.when(turn + 1 < count)
        def _():
            self.copy(turn + 1).start()

        return lax.rem(turn, 2)


def consume_body(cut, samples, value_ref, landing, kernel_ref, slots, sems, work):
    kernel_sem, send_sem, recv_sem, own_sem = sems
    place = Place()
    z, y, core, x = place.z, place.y, place.core, place.x
    lanes = landing.shape[-1]
    pieces = [(s, slice(0, cut), "zy") for s in range(samples)]
    pieces += [(s, slice(cut, lanes), "yz") for s in range(samples)]
    blocks = 2 * PLANES
    count = 2 * samples * blocks

    def chip_at(block):
        return plane_of(z, block // 2), jnp.where(lax.rem(block, 2) == 1, 1 - y, y)

    def first_sample(block, parity):
        plane, row = chip_at(block)
        other = jnp.where(parity == 1, 1 - core, core)
        return ((plane * 2 + row) * 2 + other) * samples

    def sample_at(turn):
        block = turn // (2 * samples)
        return first_sample(block, lax.rem(turn // samples, 2)) + lax.rem(turn, samples)

    def sends(block, act):
        plane, row = chip_at(block)
        same_row = lax.rem(block, 2) == 0
        up, down = (plane <= z) & (z < PLANES - 1), (plane >= z) & (z > 0)
        for number, (s, span, order) in enumerate(pieces):
            view = landing.at[first_sample(block, 0) + s, :, span]
            if order == "zy":
                ways = (up & same_row, down & same_row, same_row)
            else:
                ways = (up, down, block == 0)
            targets = (
                (z + 1, y, core, 0),
                (z - 1, y, core, 0),
                (z, 1 - y, core, 0),
                (z, y, 1 - core, 1),
            )
            for slot, (dz, dy, dcore, parity) in enumerate(targets):
                copy = pltpu.make_async_remote_copy(
                    src_ref=view,
                    dst_ref=view,
                    send_sem=send_sem.at[block, number, slot],
                    recv_sem=recv_sem.at[plane * 2 + row, number, parity],
                    device_id=((dz * 2 + dy) * 2 + dcore, x),
                    device_id_type=pl.DeviceIdType.MESH,
                )
                if slot < 3:
                    pl.when(ways[slot])(lambda copy=copy: act(copy))
                else:
                    act(copy)

    def arrive(block, parity):
        plane, row = chip_at(block)
        for number, (s, span, order) in enumerate(pieces):
            view = landing.at[first_sample(block, parity) + s, :, span]
            pltpu.make_async_remote_copy(
                src_ref=view,
                dst_ref=view,
                send_sem=send_sem.at[block, number, 3],
                recv_sem=recv_sem.at[plane * 2 + row, number, parity],
                device_id=((z * 2 + y) * 2 + 1 - core, x),
                device_id_type=pl.DeviceIdType.MESH,
            ).wait_recv()

    stream = Stream(kernel_ref, slots, kernel_sem, sample_at)
    stream.copy(0).start()
    own = pltpu.make_async_copy(
        value_ref, landing.at[pl.ds(first_sample(0, 0), samples)], own_sem
    )
    own.start()
    greet(place, ("z", "y"))
    own.wait()
    sends(0, lambda copy: copy.start())

    @pl.loop(0, count)
    def _(turn):
        block = turn // (2 * samples)
        step = lax.rem(turn, 2 * samples)

        @pl.when((step == 0) & (block > 0))
        def _():
            arrive(block, 0)
            sends(block, lambda copy: copy.start())

        @pl.when(step == samples)
        def _():
            arrive(block, 1)

        slot = stream.take(turn, count)
        work(turn, sample_at(turn), slot, sample_at)

    @pl.loop(0, blocks)
    def _(block):
        sends(block, lambda copy: copy.wait_send())


def consume_scratch(samples, rows, lanes, kernel):
    dma = pltpu.SemaphoreType.DMA
    pieces = 2 * samples
    return [
        pltpu.VMEM((16 * samples, rows, lanes), jnp.bfloat16),
        pltpu.VMEM((2,) + kernel.shape[1:], jnp.bfloat16),
        dma((2,)),
        dma((2 * PLANES, pieces, 4)),
        dma((2 * PLANES, pieces, 2)),
        dma,
    ]


def whole_specs(count):
    return [pl.BlockSpec(memory_space=pltpu.VMEM)] * count


HBM = pl.BlockSpec(memory_space=pl.ANY)


def gather_back(cotan, place, kernel, pixels, width, call_id):
    samples, rows, lanes = cotan.shape
    total = kernel.shape[0]

    def body(
        cotan_ref,
        kernel_ref,
        place_ref,
        out_ref,
        all_ref,
        landing,
        slots,
        s0,
        s1,
        s2,
        s3,
        wide_ref,
        all_sem,
    ):
        def work(turn, sample, slot, sample_at):
            out_ref[sample] = fold_back(
                landing[sample], place_ref, slots.at[pl.ds(slot, 1)], wide_ref, pixels, width
            )

        consume_body(
            lanes * 3 // 4,
            samples,
            cotan_ref,
            landing,
            kernel_ref,
            slots,
            (s0, s1, s2, s3),
            work,
        )
        keep = pltpu.make_async_copy(landing, all_ref, all_sem)
        keep.start()
        keep.wait()

    return pl.pallas_call(
        body,
        in_specs=[HBM, HBM] + whole_specs(1),
        out_specs=whole_specs(1) + [HBM],
        out_shape=[
            jax.ShapeDtypeStruct((total, pixels, width), jnp.bfloat16),
            jax.ShapeDtypeStruct((total, rows, lanes), jnp.bfloat16),
        ],
        scratch_shapes=consume_scratch(samples, rows, lanes, kernel)
        + [pltpu.VMEM((PAD_ROWS, 3 * width), jnp.float32), pltpu.SemaphoreType.DMA],
        compiler_params=pltpu.CompilerParams(
            collective_id=call_id, has_side_effects=True, vmem_limit_bytes=40 * 2**20
        ),
        name="gather_back",
    )(cotan, kernel, place)


def gather_second(slabs, tans, place, kernel, cotan, sides, squares, call_id):
    samples, rows, lanes = cotan.shape
    total, pixels, width = slabs.shape

    def body(
        cotan_ref,
        kernel_ref,
        sides_ref,
        slab_ref,
        tan_ref,
        place_ref,
        squares_ref,
        grad_ref,
        back_ref,
        scale_ref,
        landing,
        slots,
        s0,
        s1,
        s2,
        s3,
        side_slots,
        side_sem,
        grad_slots,
        grad_sem,
        spot_ref,
        wide_ref,
    ):
        spot_ref[...] = jnp.zeros_like(spot_ref)

        def leave(slot, sample):
            return pltpu.make_async_copy(
                grad_slots.at[slot], grad_ref.at[sample], grad_sem.at[slot]
            )

        def work(turn, sample, slot, sample_at):
            sides = Stream(sides_ref, side_slots, side_sem, sample_at)
            pl.when(turn == 0)(lambda: sides.copy(0).start())
            sides.take(turn, total)

            @pl.when(turn >= 2)
            def _():
                leave(slot, sample).wait()

            one = pl.ds(sample, 1)
            second_step(
                slab_ref.at[one],
                tan_ref.at[one],
                place_ref,
                slots.at[pl.ds(slot, 1)],
                landing.at[one],
                side_slots.at[pl.ds(slot, 1)],
                squares_ref.at[one],
                grad_slots.at[pl.ds(slot, 1)],
                back_ref.at[one],
                scale_ref.at[one],
                spot_ref,
                wide_ref,
            )
            leave(slot, sample).start()

        consume_body(
            lanes * 3 // 4,
            samples,
            cotan_ref,
            landing,
            kernel_ref,
            slots,
            (s0, s1, s2, s3),
            work,
        )
        for slot in range(2):
            leave(slot, 0).wait()

    return pl.pallas_call(
        body,
        in_specs=[HBM, HBM, HBM] + whole_specs(4),
        out_specs=[HBM] + whole_specs(2),
        out_shape=[
            jax.ShapeDtypeStruct(kernel.shape, jnp.bfloat16),
            jax.ShapeDtypeStruct((total, pixels, width), jnp.bfloat16),
            jax.ShapeDtypeStruct(squares.shape, jnp.float32),
        ],
        scratch_shapes=consume_scratch(samples, rows, lanes, kernel)
        + [
            pltpu.VMEM((2,) + sides.shape[1:], jnp.bfloat16),
            pltpu.SemaphoreType.DMA((2,)),
            pltpu.VMEM((2,) + kernel.shape[1:], jnp.bfloat16),
            pltpu.SemaphoreType.DMA((2,)),
            pltpu.VMEM((3 * pixels, 3 * width), jnp.bfloat16),
            pltpu.VMEM((PAD_ROWS, 3 * width), jnp.float32),
        ],
        compiler_params=pltpu.CompilerParams(
            collective_id=call_id, has_side_effects=True, vmem_limit_bytes=48 * 2**20
        ),
        name="gather_second",
    )(cotan, kernel, sides, slabs, tans, place, squares)


def add_rows(total, part):
    shape = total.shape[:-2]
    for number in range(int(np.prod(shape))):
        spot = tuple(int(place) for place in np.unravel_index(number, shape))
        total[spot] = (total[spot].astype(jnp.float32) + part[spot].astype(jnp.float32)).astype(
            jnp.bfloat16
        )


def sum_body(
    cut,
    extra,
    kernel_ref,
    slab_ref,
    place_ref,
    sums_ref,
    out_ref,
    slots,
    kernel_sem,
    spot_ref,
    acc,
    core_out,
    core_in,
    y_in,
    y_last,
    z_first,
    z_second,
    x_in,
    core_send,
    core_recv,
    y_send,
    y_recv,
    z_send,
    z_recv,
    x_send,
    x_recv,
):
    place = Place()
    z, y, x = place.z, place.y, place.x
    spot_ref[...] = jnp.zeros_like(spot_ref)
    wide, narrow = slice(0, cut), slice(cut, acc.shape[-1])

    def spot(z, y, core, x):
        return (z * 2 + y) * 2 + core, x

    def remote(source, target, send, recv, device):
        return pltpu.make_async_remote_copy(
            src_ref=source,
            dst_ref=target,
            send_sem=send,
            recv_sem=recv,
            device_id=spot(*device),
            device_id_type=pl.DeviceIdType.MESH,
        )

    other_core = (z, y, 1 - place.core, x)
    other_y = (z, 1 - y, place.core, x)
    other_x = (z, y, place.core, 1 - x)

    order = (3, 0, 2, 1)

    def chunk_at(chunk):
        turn = chunk // 2
        dest = jnp.where(turn == 0, 3, jnp.where(turn == 1, 0, 4 - turn))
        return dest, jnp.where(lax.rem(chunk, 2) == 0, 1 - y, y)

    def sample_at(turn):
        dest, side = chunk_at(turn // 4)
        step = lax.rem(turn, 4)
        owner = jnp.where(step < 2, 1 - place.core, place.core)
        return ((dest * 2 + side) * 2 + owner) * 2 + lax.rem(step, 2)

    stream = Stream(kernel_ref, slots, kernel_sem, sample_at)
    stream.copy(0).start()
    greet(place, ("z", "y", "x"))

    def core_copy(chunk):
        dest, side = chunk_at(chunk)
        return remote(
            core_out.at[dest, side],
            core_in.at[dest, side],
            core_send.at[chunk],
            core_recv.at[chunk],
            other_core,
        )

    def y_copy(dest):
        return remote(
            acc.at[dest, 1 - y, :, :, wide], y_in.at[dest], y_send.at[dest], y_recv.at[dest], other_y
        )

    def one_sample(turn):
        chunk, step = turn // 4, lax.rem(turn, 4)
        dest, side = chunk_at(chunk)
        sample = sample_at(turn)
        slot = stream.take(turn, 16 * 2)

        def convolve(target):
            conv_step(
                extra,
                sample,
                slab_ref.at[pl.ds(sample, 1)],
                place_ref,
                slots.at[pl.ds(slot, 1)],
                sums_ref,
                target.at[dest, side, pl.ds(lax.rem(step, 2), 1)],
                spot_ref,
            )

        pl.when(step < 2)(lambda: convolve(core_out))
        pl.when(step >= 2)(lambda: convolve(acc))
        pl.when(step == 1)(lambda: core_copy(chunk).start())

        @pl.when(step == 3)
        def _():
            core_copy(chunk).wait_recv()
            add_rows(acc.at[dest, side], core_in.at[dest, side])
            pl.when(lax.rem(chunk, 2) == 0)(lambda: y_copy(dest).start())

    views = (
        lambda dest: acc.at[dest, y, :, :, wide],
        lambda dest: acc.at[dest, :, :, :, narrow],
    )
    landings = (z_first, z_second)

    def z_copy(slot, way, dest, device):
        return remote(
            views[slot](dest),
            landings[slot].at[way, dest],
            z_send.at[slot, way, dest],
            z_recv.at[slot, way, dest],
            device,
        )

    def take_y(dest):
        y_copy(dest).wait_recv()
        add_rows(views[0](dest), y_in.at[dest])

    def along_z(slot, dest, act):
        for way in (0, 1):
            near = dest > z if way == 0 else dest < z
            has_before = z > 0 if way == 0 else z < PLANES - 1
            copy = z_copy(slot, way, dest, (z + (1 if way == 0 else -1), y, place.core, x))
            if act:

                @pl.when(near & has_before)
                def _():
                    copy.wait_recv()
                    add_rows(views[slot](dest), landings[slot].at[way, dest])

                pl.when(near)(copy.start)
            else:
                pl.when(near)(copy.wait_send)

    def end_z(slot):
        for way in (0, 1):

            @pl.when(z > 0 if way == 0 else z < PLANES - 1)
            def _():
                z_copy(slot, way, z, other_core).wait_recv()
                add_rows(views[slot](z), landings[slot].at[way, z])

    @pl.loop(0, 2 * PLANES)
    def _(turn):
        @pl.when(turn < PLANES)
        def _():
            pl.loop(0, 8)(lambda step: one_sample(turn * 8 + step))

        for number, dest in enumerate(order):
            due = number + jnp.where(dest > z, z, PLANES - 1 - z)

            @pl.when((turn == due) & (dest != z))
            def _():
                along_z(1, dest, True)

            @pl.when((turn == due + 1) & (dest != z))
            def _():
                take_y(dest)
                along_z(0, dest, True)

    take_y(z)
    end_z(1)
    last = remote(
        acc.at[z, 1 - y, :, :, narrow], y_last, y_send.at[PLANES], y_recv.at[PLANES], other_y
    )
    last.start()
    end_z(0)
    last.wait_recv()
    add_rows(acc.at[z, y, :, :, narrow], y_last)
    swap = remote(acc.at[z, y, 1 - x], x_in, x_send, x_recv, other_x)
    swap.start()
    lanes = acc.shape[-1]
    out_ref[:, lanes_at(x, lanes)] = acc[z, y, x]
    swap.wait_recv()
    out_ref[:, lanes_at(1 - x, lanes)] = x_in[...]
    swap.wait_send()
    last.wait_send()
    for dest in range(PLANES):
        y_copy(dest).wait_send()
        for slot in (0, 1):
            along_z(slot, dest, False)

    @pl.loop(0, 2 * PLANES)
    def _(chunk):
        core_copy(chunk).wait_send()


def conv_sum(slabs, place, kernel, sums, extra, call_id):
    _, pixels, width = slabs.shape
    rows, lanes = PIXELS + (CHUNK if extra else 0), kernel.shape[2]
    cut = lanes * 3 // 4
    bf16, dma = jnp.bfloat16, pltpu.SemaphoreType.DMA
    return pl.pallas_call(
        lambda *refs: sum_body(cut, extra, *refs),
        in_specs=[HBM] + whole_specs(3),
        out_specs=pl.BlockSpec(memory_space=pltpu.VMEM),
        out_shape=jax.ShapeDtypeStruct((rows, 2 * lanes), bf16),
        scratch_shapes=[
            pltpu.VMEM((2,) + kernel.shape[1:], bf16),
            dma((2,)),
            pltpu.VMEM((3 * pixels, 3 * width), bf16),
            pltpu.VMEM((PLANES, 2, 2, rows, lanes), bf16),
            pltpu.VMEM((PLANES, 2, 2, rows, lanes), bf16),
            pltpu.VMEM((PLANES, 2, 2, rows, lanes), bf16),
            pltpu.VMEM((PLANES, 2, rows, cut), bf16),
            pltpu.VMEM((2, rows, lanes - cut), bf16),
            pltpu.VMEM((2, PLANES, 2, rows, cut), bf16),
            pltpu.VMEM((2, PLANES, 2, 2, rows, lanes - cut), bf16),
            pltpu.VMEM((rows, lanes), bf16),
            dma((8,)),
            dma((8,)),
            dma((PLANES + 1,)),
            dma((PLANES + 1,)),
            dma((2, 2, PLANES)),
            dma((2, 2, PLANES)),
            dma,
            dma,
        ],
        compiler_params=pltpu.CompilerParams(
            collective_id=call_id, has_side_effects=True, vmem_limit_bytes=48 * 2**20
        ),
        name="conv_sum",
    )(kernel, slabs, place, sums)


def sum_weights_body(parts, count, refs):
    inputs, outputs, rest = refs[:count], refs[count : 2 * count], refs[2 * count :]
    acc, core_in, one_in, two_in, z_in = (rest[k * count : (k + 1) * count] for k in range(5))
    (
        load_sem,
        core_send,
        core_recv,
        one_send,
        one_recv,
        two_send,
        two_recv,
        z_send,
        z_recv,
    ) = rest[5 * count :]
    place = Place()
    greet(place, ("z", "y", "x"))
    z, y, x = place.z, place.y, place.x
    order = (3, 0, 2, 1)
    finish = []

    def remote(source, target, send, recv, device):
        dz, dy, core, dx = device
        return pltpu.make_async_remote_copy(
            src_ref=source,
            dst_ref=target,
            send_sem=send,
            recv_sem=recv,
            device_id=((dz * 2 + dy) * 2 + core, dx),
            device_id_type=pl.DeviceIdType.MESH,
        )

    other_core = (z, y, 1 - place.core, x)
    other_y = (z, 1 - y, place.core, x)
    other_x = (z, y, place.core, 1 - x)
    sides = (1 - y, y)

    first = {}
    for dest in order:
        for w in range(count):
            rows = acc[w].shape[2]
            for turn, side in enumerate(sides):
                at = ((dest * 2 + side) * 2 + (1 - place.core)) * rows
                mine = ((dest * 2 + side) * 2 + place.core) * rows
                sent = remote(
                    inputs[w].at[pl.ds(pl.multiple_of(at, rows), rows)],
                    core_in[w].at[dest, side],
                    core_send.at[w, dest, turn],
                    core_recv.at[w, dest, turn],
                    other_core,
                )
                sent.start()
                load = pltpu.make_async_copy(
                    inputs[w].at[pl.ds(pl.multiple_of(mine, rows), rows)],
                    acc[w].at[dest, side],
                    load_sem.at[w, dest, turn],
                )
                load.start()
                first[w, dest, turn] = (sent, load)

    def half(w, index):
        lanes = acc[w].shape[-1] // 2
        return lanes_at(index, lanes)

    ones, twos = {}, {}

    def stage_one(dest):
        for w in range(count):
            for turn, side in enumerate(sides):
                sent, load = first[w, dest, turn]
                load.wait()
                sent.wait_recv()
                finish.append((None, sent))
                add_rows(acc[w].at[dest, side], core_in[w].at[dest, side])
                if parts[w] == "z":
                    continue
                if parts[w] == "xy":
                    copy = remote(
                        acc[w].at[dest, side, :, half(w, 1 - x)],
                        one_in[w].at[dest, side],
                        one_send.at[w, dest, turn],
                        one_recv.at[w, dest, turn],
                        other_x,
                    )
                elif turn == 0:
                    copy = remote(
                        acc[w].at[dest, side],
                        one_in[w].at[dest],
                        one_send.at[w, dest, turn],
                        one_recv.at[w, dest, turn],
                        other_y,
                    )
                else:
                    continue
                copy.start()
                ones[w, dest, turn] = copy

    def stage_two(dest):
        for w in range(count):
            if parts[w] == "z":
                continue
            if parts[w] == "xy":
                for turn, side in enumerate(sides):
                    copy = ones[w, dest, turn]
                    copy.wait_recv()
                    finish.append((None, copy))
                    view = acc[w].at[dest, side, :, half(w, x)]
                    add_rows(view, one_in[w].at[dest, side])
                    if turn == 0:
                        twos[w, dest] = remote(
                            view,
                            two_in[w].at[dest],
                            two_send.at[w, dest],
                            two_recv.at[w, dest],
                            other_y,
                        )
                        twos[w, dest].start()
            else:
                copy = ones[w, dest, 0]
                copy.wait_recv()
                finish.append((None, copy))
                add_rows(acc[w].at[dest, y], one_in[w].at[dest])
                twos[w, dest] = remote(
                    acc[w].at[dest, y, :, half(w, 1 - x)],
                    two_in[w].at[dest],
                    two_send.at[w, dest],
                    two_recv.at[w, dest],
                    other_x,
                )
                twos[w, dest].start()

    def plane_copy(w, dest, way, device):
        return remote(
            acc[w].at[dest],
            z_in[w].at[way, dest],
            z_send.at[w, way, dest],
            z_recv.at[w, way, dest],
            device,
        )

    def planes_first(turn):
        for number, dest in enumerate(order):
            if turn < number + 1 or turn > number + PLANES:
                continue
            due = turn == number + 1 + jnp.where(dest > z, z, PLANES - 1 - z)
            for w in range(count):
                if parts[w] != "z":
                    continue
                for way in (0, 1):
                    near = dest > z if way == 0 else dest < z
                    has_before = z > 0 if way == 0 else z < PLANES - 1
                    device = (z + (1 if way == 0 else -1), y, place.core, x)
                    copy = plane_copy(w, dest, way, device)

                    @pl.when(due & near & has_before)
                    def _():
                        copy.wait_recv()
                        add_rows(acc[w].at[dest], z_in[w].at[way, dest])

                    pl.when(due & near)(copy.start)
                    if turn == number + 1:
                        finish.append((near, copy))

    def planes_last():
        chosen = [w for w in range(count) if parts[w] == "z"]
        lasts = []
        for w in chosen:
            for way in (0, 1):

                @pl.when(z > 0 if way == 0 else z < PLANES - 1)
                def _():
                    plane_copy(w, z, way, other_core).wait_recv()
                    add_rows(acc[w].at[z], z_in[w].at[way, z])

            copy = remote(
                acc[w].at[z, 1 - y], one_in[w], one_send.at[w, 0, 0], one_recv.at[w, 0, 0], other_y
            )
            copy.start()
            finish.append((None, copy))
            lasts.append(copy)
        for w, copy in zip(chosen, list(lasts)):
            copy.wait_recv()
            add_rows(acc[w].at[z, y], one_in[w])
            more = remote(
                acc[w].at[z, y, :, half(w, 1 - x)],
                two_in[w],
                two_send.at[w, 0],
                two_recv.at[w, 0],
                other_x,
            )
            more.start()
            finish.append((None, more))
            lasts.append(more)
        for w, copy in zip(chosen, lasts[len(chosen) :]):
            copy.wait_recv()
            add_rows(acc[w].at[z, y, :, half(w, x)], two_in[w])

    def z_copy(w, dest, way):
        return remote(
            acc[w].at[dest, y, :, half(w, x)],
            z_in[w].at[way, dest],
            z_send.at[w, way, dest],
            z_recv.at[w, way, dest],
            (z + (1 if way == 0 else -1), y, place.core, x),
        )

    def stage_z(dest):
        for w in range(count):
            if parts[w] == "z":
                continue
            copy = twos[w, dest]
            copy.wait_recv()
            finish.append((None, copy))
            view = acc[w].at[dest, y, :, half(w, x)]
            add_rows(view, two_in[w].at[dest])
            for way in (0, 1):
                near = dest > z if way == 0 else dest < z
                has_before = z > 0 if way == 0 else z < PLANES - 1
                copy = z_copy(w, dest, way)

                @pl.when(near & has_before)
                def _():
                    copy.wait_recv()
                    add_rows(view, z_in[w].at[way, dest])

                pl.when(near)(copy.start)
                finish.append((near, copy))

    for turn in range(PLANES + 2):
        if turn < PLANES:
            stage_one(order[turn])
        if 0 <= turn - 1 < PLANES:
            stage_two(order[turn - 1])
        planes_first(turn)
        if turn >= 2:
            stage_z(order[turn - 2])
    for turn in range(PLANES + 2, 2 * PLANES):
        planes_first(turn)
    planes_last()
    for w in range(count):
        view = acc[w].at[z, y, :, half(w, x)]
        for way in (0, 1) if parts[w] != "z" else ():

            @pl.when(z > 0 if way == 0 else z < PLANES - 1)
            def _():
                remote(
                    view,
                    z_in[w].at[way, z],
                    z_send.at[w, way, z],
                    z_recv.at[w, way, z],
                    other_core,
                ).wait_recv()
                add_rows(view, z_in[w].at[way, z])

        outputs[w][...] = acc[w][z, y, :, half(w, x)].astype(jnp.float32)
    for condition, copy in finish:
        if condition is None:
            copy.wait_send()
        else:
            pl.when(condition)(copy.wait_send)


def sum_weights(grads, parts, call_id):
    count = len(grads)
    bf16, dma = jnp.bfloat16, pltpu.SemaphoreType.DMA
    blocks = [(grad.shape[0] // 16, grad.shape[1]) for grad in grads]
    ones, twos, planes = [], [], []
    for (rows, lanes), part in zip(blocks, parts):
        if part == "z":
            ones.append((rows, lanes))
            twos.append((rows, lanes // 2))
            planes.append((2, PLANES, 2, rows, lanes))
        else:
            ones.append((PLANES, 2, rows, lanes // 2) if part == "xy" else (PLANES, rows, lanes))
            twos.append((PLANES, rows, lanes // 2))
            planes.append((2, PLANES, rows, lanes // 2))
    return pl.pallas_call(
        lambda *refs: sum_weights_body(parts, count, refs),
        in_specs=[pl.BlockSpec(memory_space=pl.ANY)] * count,
        out_specs=[pl.BlockSpec(memory_space=pltpu.VMEM)] * count,
        out_shape=[
            jax.ShapeDtypeStruct((rows, lanes // 2), jnp.float32) for rows, lanes in blocks
        ],
        scratch_shapes=[pltpu.VMEM((PLANES, 2, rows, lanes), bf16) for rows, lanes in blocks]
        + [pltpu.VMEM((PLANES, 2, rows, lanes), bf16) for rows, lanes in blocks]
        + [pltpu.VMEM(shape, bf16) for shape in ones]
        + [pltpu.VMEM(shape, bf16) for shape in twos + planes]
        + [dma((count, PLANES, 2))] * 5
        + [dma((count, PLANES))] * 2
        + [dma((count, 2, PLANES))] * 2,
        compiler_params=pltpu.CompilerParams(
            collective_id=call_id, has_side_effects=True, vmem_limit_bytes=60 * 2**20
        ),
        name="sum_weights",
    )(*grads)


def sample_parallel(
    layer_input,
    labels,
    text_ids,
    noise_seeds,
    penalty_mask,
    class_table,
    token_table,
    sel_weight,
    mod_weight,
    rgb_mod,
    rgb_weight,
    conv_bias,
    noise_strength,
    kernel_bank,
    qk_weight,
    value_weight,
    attn_out,
    cross_query,
    cross_key,
    cross_value,
    cross_out,
    mlp_in,
    mlp_out,
    cot_feat,
    cot_rgb,
    penalty_dir,
):
    mp = lax.axis_index("mp")
    dp = lax.axis_index("dp")
    half_px = layer_input.shape[1]
    slab = kernel_bank.shape[2]
    width_out = kernel_bank.shape[3]
    float32, bfloat16 = jnp.float32, jnp.bfloat16

    input_whole = lax.all_gather(layer_input, "mp", axis=2, tiled=True)
    raw_slabs = to_slabs(input_whole)
    numbers = jnp.concatenate([jnp.pad(labels, (0, 126)), text_ids.reshape(-1)]).reshape(2, 128)
    gathered = gather_weights(
        [
            mlp_in,
            mlp_out.T,
            qk_weight,
            value_weight,
            attn_out.T,
            cross_query,
            cross_out.T,
            cross_key,
            cross_value,
        ],
        jnp.pad(numbers, ((0, 6), (0, 0))),
        1,
    )
    mlp_whole, mout_whole, qk_whole, value_whole, attn_whole, query_whole, cout_whole = gathered[:7]
    key_whole, cval_whole, numbers_all = gathered[7:]
    weights = (
        qk_whole,
        value_whole,
        attn_whole,
        query_whole,
        key_whole,
        cval_whole,
        cout_whole,
        mlp_whole,
        mout_whole,
    )

    numbers_all = numbers_all.reshape(16, 2, 8, 128)[:, 0]
    labels_all = numbers_all[:, 0, :2].reshape(-1)
    ids_all = numbers_all[:, 1].reshape(-1)
    sample_count = labels_all.shape[0]
    classes = jnp.arange(class_table.shape[0], dtype=jnp.int32)
    onehot_class = (labels_all[:, None] == classes[None, :]).astype(bfloat16)
    latent = dot_wide(onehot_class, class_table, 1, 0)
    select_all, select_pull = jax.vjp(last_softmax, dot_wide(latent, sel_weight, 1, 0))
    scales_all = 1.0 + dot_wide(latent, mod_weight, 1, 0)
    rgb_scales_all = 1.0 + dot_wide(latent, rgb_mod, 1, 0)
    me = 2 * dp + mp
    scales = pick(scales_all, me)
    rgb_scales = pick(rgb_scales_all, me)
    scales_slab = lax.dynamic_slice_in_dim(scales_all, dp * slab, slab, 1)
    words = jnp.arange(token_table.shape[0], dtype=jnp.int32)
    text_own = pick(text_ids, mp)
    text_rows = dot_wide((text_own[:, None] == words[None, :]).astype(bfloat16), token_table, 1, 0)
    noise = noise_field(pick(noise_seeds, mp)[None], SIDE * SIDE)[0]
    small = (
        conv_bias.astype(float32),
        noise_strength.astype(float32),
        rgb_scales,
        rgb_weight.astype(float32),
    )

    bank_rows = kernel_bank.reshape(kernel_bank.shape[0], 9 * slab, width_out)
    mix = mix_matrix(select_all)
    scales_two = jnp.broadcast_to(
        (scales_slab * scales_slab)[:, :, None], (sample_count, slab, 128)
    )
    kernel, sums_part = mix_kernels(mix, bank_rows, scales_two)
    place = placing(SIDE // 2)

    input_own = pick(input_whole, mp).astype(float32)
    slabs_x = (raw_slabs.astype(float32) * scales_slab[:, None, :]).astype(bfloat16)
    summed = conv_sum(slabs_x, place, kernel, sums_part, True, 4).astype(float32)
    conv_out, sums = summed[:PIXELS], summed[PIXELS]

    (hidden_four, picture), pull, parts = jax.vjp(
        lambda value: layer_forward(value, sums, text_rows, small, weights, noise),
        conv_out,
        has_aux=True,
    )

    dir_own = pick(penalty_dir, mp).astype(float32)
    grad_conv = pull((jnp.zeros_like(hidden_four), dir_own))[0]
    back_slabs, sides_all = gather_back(
        both_half(grad_conv.astype(bfloat16), mp), place, kernel, half_px, slab, 2
    )
    grad_moduled = from_slabs(back_slabs, mp).astype(bfloat16).astype(float32)
    mask_own = pick(penalty_mask, mp).astype(float32)
    tangent = penalty_weight * mask_own * grad_moduled * scales

    tan_moduled = (tangent * scales).astype(bfloat16)
    tan_other = swap_mp(tan_moduled)
    tan_pair = jnp.stack(
        [jnp.where(mp == 0, tan_moduled, tan_other), jnp.where(mp == 0, tan_other, tan_moduled)]
    )
    slabs_t = to_slabs(tan_pair)
    conv_tan = conv_sum(slabs_t, place, kernel, sums_part, False, 5).astype(float32)

    (ignored_out, ignored_pic, ignored_tan), pull_joint = jax.vjp(
        lambda *given: layer_joint(*given, noise, parts),
        conv_out,
        conv_tan,
        sums,
        text_rows,
        small,
        weights,
    )
    cot_own = own_whole(cot_feat, mp).astype(float32)
    grad_main, _, grad_sums, grad_text, grad_small, grad_weights = pull_joint(
        (cot_own, pick(cot_rgb, mp).astype(float32), dir_own)
    )

    orders = ("xy", "yx", "xy", "yx", "xy", "yx", "z", "z", "z")
    d_qk, d_value, d_attn, d_query, d_key, d_cval, d_cout, d_mlp, d_mout = grad_weights
    mlp_grad, mout_grad, qk_grad, value_grad, attn_grad, query_grad, cout_grad, key_grad, cval_grad = (
        sum_weights(
            [d_mlp, d_mout, d_qk, d_value, d_attn, d_query, d_cout, d_key, d_cval], orders, 6
        )
    )
    big_sums = (
        qk_grad,
        value_grad,
        attn_grad.T,
        query_grad,
        key_grad,
        cval_grad,
        cout_grad.T,
        mlp_grad,
        mout_grad.T,
    )

    lines = jnp.broadcast_to(grad_sums[None], (CHUNK,) + grad_sums.shape)
    wide = jnp.concatenate([grad_main.astype(bfloat16), lines.astype(bfloat16)], axis=0)
    grad_kernel, back_slabs, scale_sums = gather_second(
        slabs_x, slabs_t, place, kernel, both_half(wide, mp), sides_all, scales_two, 3
    )
    grad_scales_slab = 2.0 * scales_slab * scale_sums[:, :, 0]
    bank_grad, select_products = unmix_kernels(mix, bank_rows, grad_kernel)
    bank_grad = bank_grad.reshape(kernel_bank.shape)
    grad_select = jnp.einsum(
        "brkr->bk", select_products.reshape(sample_count, CHUNK, -1, CHUNK)
    )
    back_main = from_slabs(back_slabs, mp).astype(bfloat16).astype(float32)
    input_grad = back_main * scales
    grad_scales = jnp.sum(back_main * input_own + grad_moduled * tangent, axis=0)

    grad_bias, grad_strength, grad_rgb_scales, grad_rgb_weight = grad_small
    row = jnp.concatenate(
        [
            grad_scales,
            grad_rgb_scales,
            grad_rgb_weight.reshape(-1),
            grad_bias,
            grad_strength,
            grad_scales_slab.reshape(-1),
            grad_select.reshape(-1),
        ]
    ).reshape(-1, 128)
    rows_all = lax.all_gather(row, ("dp", "mp"), axis=0, tiled=False).reshape(sample_count, -1)
    channels = scales.shape[0]
    scale_terms = rows_all[:, :channels]
    rgb_terms = rows_all[:, channels : 2 * channels]
    sums_all = jnp.sum(rows_all[:, 2 * channels : 7 * channels], axis=0)
    slab_terms = rows_all[:, 7 * channels : 7 * channels + sample_count * slab]
    slab_terms = slab_terms.reshape(-1, 2, sample_count, slab).sum(axis=1)
    scale_terms = scale_terms + slab_terms.transpose(1, 0, 2).reshape(sample_count, channels)
    select_terms = jnp.sum(rows_all[:, 7 * channels + sample_count * slab :], axis=0)
    logit_terms = select_pull(select_terms.reshape(sample_count, -1))[0]
    latent_terms = (
        matmul_high(scale_terms, mod_weight.astype(float32).T)
        + matmul_high(rgb_terms, rgb_mod.astype(float32).T)
        + matmul_high(logit_terms, sel_weight.astype(float32).T)
    )
    class_grad = matmul_high(onehot_class.astype(float32).T, latent_terms)
    sel_grad = matmul_high(latent.T, logit_terms)
    mod_grad = matmul_high(latent.T, scale_terms)
    rgb_mod_grad = matmul_high(latent.T, rgb_terms)
    text_all = lax.all_gather(grad_text.astype(bfloat16), ("dp", "mp"), axis=0, tiled=True)
    token_grad = dot_wide((ids_all[:, None] == words[None, :]).astype(bfloat16), text_all, 0, 0)

    picture_other = swap_mp(picture)
    pictures = jnp.stack(
        [jnp.where(mp == 0, picture, picture_other), jnp.where(mp == 0, picture_other, picture)]
    )
    return (
        both_half(hidden_four, mp),
        pictures,
        both_half(input_grad, mp),
        class_grad,
        token_grad,
        sel_grad,
        mod_grad,
        rgb_mod_grad,
        sums_all[: 3 * channels].reshape(3, channels),
        sums_all[3 * channels : 4 * channels],
        sums_all[4 * channels :],
        bank_grad,
    ) + big_sums


def solution(mesh):
    in_specs = (
        P("dp", None, "mp"),
        P("dp"),
        P("dp", None),
        P("dp"),
        P("dp"),
        P(),
        P(),
        P(),
        P(),
        P(),
        P(),
        P(),
        P(),
        P(None, None, "dp", "mp"),
        P("dp", "mp"),
        P("dp", "mp"),
        P("mp", "dp"),
        P("dp", "mp"),
        P("dp", "mp"),
        P("dp", "mp"),
        P("mp", "dp"),
        P("dp", "mp"),
        P("mp", "dp"),
        P("dp", None, "mp"),
        P("dp", None, None),
        P("dp", None, None),
    )
    out_specs = (
        P("dp", None, "mp"),
        P("dp", None, None),
        P("dp", None, "mp"),
        P(),
        P(),
        P(),
        P(),
        P(),
        P(),
        P(),
        P(),
        P(None, None, "dp", "mp"),
        P("dp", "mp"),
        P("dp", "mp"),
        P("mp", "dp"),
        P("dp", "mp"),
        P("dp", "mp"),
        P("dp", "mp"),
        P("mp", "dp"),
        P("dp", "mp"),
        P("mp", "dp"),
    )
    return jax.shard_map(
        sample_parallel if fits_samples(mesh) else tensor_parallel,
        mesh=mesh, in_specs=in_specs, out_specs=out_specs, check_vma=False
    )
```
